256 devices in a mesh: mesh: 32 (over x_hi, z, core), inst: 8 (over y, x_lo).
Axes of the slice: x: 4 (x_hi: 2, x_lo: 2; x = x_hi * 2 + x_lo), y: 4, z: 8, core: 2. Of those that a mesh axis runs over, the one named last changes fastest.
Arguments:
- displacement: float32 [16, 3, 128, 32, 128], P('inst', None, 'mesh'), may hold values from -6 to 6
- direction: float32 [16, 3, 128, 32, 128], P('inst', None, 'mesh'), may hold values from -6 to 6
- forcing: float32 [16, 3, 128, 32, 128], P('inst', None, 'mesh'), may hold values from -6 to 6
- material_ids: int32 [128, 32, 128], P('mesh'), may hold values from 0 to 15
- materials: float32 [16, 4], replicated, may hold values from 0.5 to 4
- joint_owner: int32 [65536, 1], P('mesh'), may hold values from 0 to 31, as said below
- joint_local: int32 [65536], P('mesh'), may hold values from 0 to 16383
- joint_remote: int32 [65536], P('mesh'), may hold values from 0 to 16383
- joint_kind: int32 [65536], P('mesh'), may hold values 0 or 1
Outputs:
- residual: float32 [16, 3, 128, 32, 128], P('inst', None, 'mesh')
- jacobian: float32 [16, 3, 128, 32, 128], P('inst', None, 'mesh')
The draws below stay inside these ranges and needn't reach their ends.
Inputs may be any that keep to these rules, and one draw needn't show every extreme that they name: `joint_owner`: of the 2048 joints listed by slab p, exactly 256 have their partner in slab p, 256 in slab p + 1 and 256 in slab p - 1, 128 each in slabs p + 2 and p - 2 (slab numbers taken modulo the number of slabs), and the rest spread evenly in turn over the other slabs, in a drawn order; so no slab's list names any one slab more than 256 times.
All inputs are finite; a program needn't handle non-finite values. No bound on the sum of `joint_kind` on one device may be relied on, other than what follows from the above.
Results may differ from the reference program's by a relative error of at most 0.000088.
Values sent between devices are 32-bit elements; how exact they have to be, the bound alone decides.
No kernel may reach another device: no remote copies, remote signals or barrier semaphores. Data moves between devices by JAX's collectives and lax.ppermute only.
A program may use at most 128 MiB of HBM per device.

```python
import math
import jax
import jax.numpy as jnp
from jax import lax

NT = 16
MAT = 16
CX = 4
CY = 32
CZ = 128
JDEV = 2048
NX = 128
NODES_DEV = 16384
JOINTS = 65536
CAP = 256
N_MESH = 32


def draw_joint_owner(key, part):
    key = jax.random.fold_in(key, 11)
    half_cap = CAP // 2
    rest_count = JDEV - 4 * CAP
    base = jnp.concatenate([jnp.zeros((CAP,), jnp.int32), jnp.ones((CAP,), jnp.int32), jnp.full((CAP,), -1, jnp.int32), jnp.full((half_cap,), 2, jnp.int32), jnp.full((half_cap,), -2, jnp.int32), 3 + jnp.arange(rest_count, dtype=jnp.int32) % (N_MESH - 5)])
    slab_keys = jax.random.split(key, N_MESH)
    shuffled = jax.vmap(lambda single: jax.random.permutation(single, base))(slab_keys)
    slabs = jnp.arange(N_MESH, dtype=jnp.int32)[:, None]
    owners = (slabs + shuffled) % N_MESH
    return owners.reshape(JOINTS, 1).astype(jnp.int32)


def with_ends(drawn, key, low, top_value):
    longest = drawn.shape.index(max(drawn.shape))
    spots = []
    for shift in (0, 1):
        where = [jax.random.randint(jax.random.fold_in(key, axis), (), 0, length) for axis, length in enumerate(drawn.shape)]
        where[longest] = (where[longest] + shift) % drawn.shape[longest]
        spots.append(tuple(where))
    return drawn.at[spots[0]].set(low).at[spots[1]].set(top_value)


def levels(rng, shape, cuts, smallest, top_value):
    def one(axis_at, parts):
        steps = jax.random.uniform(jax.random.fold_in(jax.random.fold_in(rng, 6), axis_at), (parts,), jnp.float32, smallest / len(cuts), top_value / len(cuts))
        return jnp.repeat(jnp.exp(steps), shape[axis_at] // parts).reshape((-1,) + (1,) * (len(shape) - axis_at - 1))

    gain = one(*cuts[0])
    for cut in cuts[1:]:
        gain = gain * one(*cut)
    return gain


def bell_draw(own_key, extent, width, reach, cuts=(), held_as=jnp.bfloat16):
    values = width * jax.random.normal(own_key, extent, jnp.float32)
    if cuts:
        values = values * levels(own_key, extent, cuts, -0.22, 0.18)
    return jnp.clip(values, -reach, reach).astype(held_as)


def setup_inputs(seed: int = 0) -> dict:
    splits = jax.random.split(jax.random.key(seed), 10)
    displacement = bell_draw(splits[0], (NT, 3, NX, CY, CZ), 1.0, 6.0, ((0, 8), (2, 32)), jnp.float32)
    direction = bell_draw(splits[1], (NT, 3, NX, CY, CZ), 1.0, 6.0, ((0, 8), (2, 32)), jnp.float32)
    forcing = bell_draw(splits[2], (NT, 3, NX, CY, CZ), 1.0, 6.0, ((0, 8), (2, 32)), jnp.float32)
    material_ids = with_ends(jax.random.randint(splits[3], (NX, CY, CZ), 0, MAT), jax.random.fold_in(splits[3], 1), 0, MAT - 1).astype(jnp.int32)
    materials = jnp.clip(jnp.exp(jax.random.uniform(splits[4], (MAT, 4), jnp.float32, math.log(0.5), math.log(4.0))), 0.5, 4.0)
    joint_owner = draw_joint_owner(jax.random.fold_in(splits[9], 71), 0)
    joint_local = with_ends(jax.random.randint(splits[6], (JOINTS,), 0, NODES_DEV), jax.random.fold_in(splits[6], 1), 0, NODES_DEV - 1).astype(jnp.int32)
    joint_remote = with_ends(jax.random.randint(splits[7], (JOINTS,), 0, NODES_DEV), jax.random.fold_in(splits[7], 1), 0, NODES_DEV - 1).astype(jnp.int32)
    joint_kind = with_ends((jax.random.randint(splits[8], (JOINTS,), 0, 2) < 1).astype(jnp.int32), jax.random.fold_in(splits[8], 1), 0, 1)
    return dict(displacement=displacement, direction=direction, forcing=forcing, material_ids=material_ids, materials=materials, joint_owner=joint_owner, joint_local=joint_local, joint_remote=joint_remote, joint_kind=joint_kind)


frequency = 0.6
damping = 0.3
bolt_stiff = 2.0
slip_force = 1.0
slip_speed = 0.5
stop_stiff = 3.0
clearance = 0.3


def spectral(instance_count):
    offsets = jnp.arange(instance_count, dtype=jnp.int32)[:, None] - jnp.arange(instance_count, dtype=jnp.int32)[None, :]
    signs = jnp.where(offsets % 2 == 0, 1.0, -1.0).astype(jnp.float32)
    angles = jnp.pi * offsets.astype(jnp.float32) / instance_count
    tangent = jnp.where(offsets == 0, 1.0, jnp.tan(angles)).astype(jnp.float32)
    first_table = (jnp.where(offsets == 0, 0.0, 0.5 * signs / tangent) * frequency).astype(jnp.float32)
    second_table = jnp.dot(first_table, first_table, precision=lax.Precision.HIGHEST)
    return first_table, second_table


def pad_axis(array, axis_id):
    widths = [(0, 0)] * array.ndim
    widths[axis_id] = (1, 1)
    return jnp.pad(array, widths)


def apply_stiff(fields, stiff_pad, stiff_y, stiff_z):
    centre = fields[:, 1:-1]
    stiff_x = stiff_pad[1:-1]
    summed = 0.5 * (stiff_x + stiff_pad[2:]) * (centre - fields[:, 2:])
    summed = summed + 0.5 * (stiff_x + stiff_pad[:-2]) * (centre - fields[:, :-2])
    for axis_id, stiff_axis in ((2, stiff_y), (3, stiff_z)):
        padded = pad_axis(centre, axis_id)
        padded_stiff = pad_axis(stiff_axis, axis_id - 1)
        length = centre.shape[axis_id]
        for lower in (0, 2):
            beside = lax.slice_in_dim(padded, lower, lower + length, axis=axis_id)
            stiff_beside = lax.slice_in_dim(padded_stiff, lower, lower + length, axis=axis_id - 1)
            summed = summed + 0.5 * (stiff_axis + stiff_beside) * (centre - beside)
    return summed


def joint_forces(own_side, far_side, bolted):
    gap = own_side - far_side
    slide = jnp.tanh(gap[1] / slip_speed)
    opened = jnp.tanh(gap[0] / clearance)
    friction = bolt_stiff * gap[0] + slip_force * slide
    contact = stop_stiff * (gap[0] - clearance * opened)
    joint_force = bolted * friction + (1.0 - bolted) * contact
    tangent_friction = bolt_stiff * gap[2] + slip_force * (1.0 - slide * slide) / slip_speed * gap[3]
    tangent_contact = stop_stiff * opened * opened * gap[2]
    joint_tangent = bolted * tangent_friction + (1.0 - bolted) * tangent_contact
    return joint_force, joint_tangent


def reference(displacement, direction, forcing, material_ids, materials, joint_owner, joint_local, joint_remote, joint_kind):
    first_table, second_table = spectral(NT)
    highest = lax.Precision.HIGHEST
    node_total = NX * CY * CZ
    node_dev = CX * CY * CZ
    disp = displacement.reshape(NT, 3, node_total)
    dirs = direction.reshape(NT, 3, node_total)
    rate_disp = jnp.einsum("ts,scn->tcn", first_table, disp, precision=highest)
    accel_disp = jnp.einsum("ts,scn->tcn", second_table, disp, precision=highest)
    rate_dir = jnp.einsum("ts,scn->tcn", first_table, dirs, precision=highest)
    accel_dir = jnp.einsum("ts,scn->tcn", second_table, dirs, precision=highest)
    properties = jnp.take(materials, material_ids, axis=0)
    stiff_pad = pad_axis(properties[..., 0], 0)
    stiff_y = properties[..., 1]
    stiff_z = properties[..., 2]
    masses = properties[..., 3].reshape(node_total)
    stiff_disp = apply_stiff(pad_axis(displacement.reshape(NT * 3, NX, CY, CZ), 1), stiff_pad, stiff_y, stiff_z).reshape(NT, 3, node_total)
    stiff_dir = apply_stiff(pad_axis(direction.reshape(NT * 3, NX, CY, CZ), 1), stiff_pad, stiff_y, stiff_z).reshape(NT, 3, node_total)
    residual = masses * (accel_disp + damping * rate_disp) + stiff_disp - forcing.reshape(NT, 3, node_total)
    jacobian = masses * (accel_dir + damping * rate_dir) + stiff_dir
    owners = joint_owner[:, 0]
    holders = jnp.arange(JOINTS, dtype=jnp.int32) // JDEV
    near_nodes = (holders * node_dev + joint_local).astype(jnp.int32)
    far_nodes = (owners * node_dev + joint_remote).astype(jnp.int32)
    fields_all = jnp.stack([disp, rate_disp, dirs, rate_dir])
    own_side = fields_all[:, :, :, near_nodes]
    far_side = fields_all[:, :, :, far_nodes]
    joint_force, joint_tangent = joint_forces(own_side, far_side, joint_kind.astype(jnp.float32))
    residual = residual.at[:, :, near_nodes].add(joint_force).at[:, :, far_nodes].add(-joint_force)
    jacobian = jacobian.at[:, :, near_nodes].add(joint_tangent).at[:, :, far_nodes].add(-joint_tangent)
    return residual.reshape(NT, 3, NX, CY, CZ), jacobian.reshape(NT, 3, NX, CY, CZ)
```

```python
import jax
import jax.numpy as jnp
import numpy as np
from jax import lax
from jax.experimental import pallas as pl
from jax.experimental.pallas import tpu as pltpu
from jax.sharding import PartitionSpec as P

frequency = 0.6
damping = 0.3
bolt_stiff = 2.0
slip_force = 1.0
slip_speed = 0.5
stop_stiff = 3.0
clearance = 0.3

SLABS = 32
PARTS = 8
SIDE = 18
SEG = 42
f32 = jnp.float32
bf16 = jnp.bfloat16
i32 = jnp.int32


def tables(count):
    offsets = np.arange(count)[:, None] - np.arange(count)[None, :]
    tangent = np.where(offsets == 0, 1.0, np.tan(np.pi * offsets / count))
    first = np.where(offsets == 0, 0.0, 0.5 * np.where(offsets % 2 == 0, 1.0, -1.0) / tangent) * frequency
    return first, first @ first


FIRST, SECOND = tables(2 * PARTS)


def far_place(offset):
    return 8 + (offset - 3) // 3, SEG * ((offset - 3) % 3)


def place(offset):
    return {2: (6, 0), 30: (7, 0)}.get(offset) or far_place(offset)


def lane_roll(x, shift):
    shift = shift % 128
    return pltpu.roll(x, shift, x.ndim - 1) if shift else x


def lanes(rows):
    return lax.broadcasted_iota(i32, (rows, 128), 1)


def merge_far(read, rows, fill):
    lane = lanes(rows)
    tiles = []
    for k in range(9):
        parts = [lane_roll(read(3 + 3 * k + s), SEG * s) for s in range(3)]
        tile = jnp.where(lane < SEG, parts[0], jnp.where(lane < 2 * SEG, parts[1], parts[2]))
        tiles.append(jnp.where(lane < 3 * SEG, tile, fill))
    return tiles


def prep_kernel(p_ref, owner_ref, local_ref, remote_ref, kind_ref, tab_ref, chunk_ref, up_ref, down_ref):
    p = p_ref[0]
    count = owner_ref.shape[1]
    offset = (owner_ref[...] - p) & (SLABS - 1)
    hit = (lax.broadcasted_iota(i32, (SLABS, count), 0) == offset).astype(f32)
    hit16 = hit.astype(bf16)
    before = (lax.broadcasted_iota(i32, (128, 128), 0) < lax.broadcasted_iota(i32, (128, 128), 1)).astype(f32).astype(bf16)
    row = lax.broadcasted_iota(i32, (SLABS, 1), 0)
    far = row - 3
    group = (far * 171) >> 9
    start = 1024 + group * 128 + (far - 3 * group) * SEG
    for value, at in ((0, 0), (1, 256), (SLABS - 1, 512), (2, 768), (SLABS - 2, 896)):
        start = jnp.where(row == value, at, start)
    run = start.astype(f32)
    places = []
    for b in range(count // 128):
        block = hit[:, 128 * b : 128 * (b + 1)]
        earlier = jnp.dot(hit16[:, 128 * b : 128 * (b + 1)], before, preferred_element_type=f32)
        places.append(jnp.sum(block * (earlier + run), axis=0, keepdims=True))
        run = run + jnp.sum(block, axis=1, keepdims=True)
    slot = jnp.concatenate(places, axis=1).astype(i32)
    in_tile = lax.broadcasted_iota(i32, (24, count), 0) == (slot >> 7)
    in_lane = (lax.broadcasted_iota(i32, (128, count), 0) == (slot & 127)).astype(f32).astype(bf16)
    local = local_ref[...]
    remote = remote_ref[...]
    values = (local >> 7, local & 127, remote >> 7, remote & 127, kind_ref[...], jnp.ones_like(local))
    spread = jnp.concatenate([jnp.where(in_tile, v.astype(f32), 0.0) for v in values], axis=0).astype(bf16)
    got = lax.dot_general(spread, in_lane, (((1,), (1,)), ((), ())), preferred_element_type=f32)
    got = [got[24 * k : 24 * (k + 1)] for k in range(6)]
    empty = got[5] - 1.0
    tab_ref[0:24] = got[0] * 128.0 + got[1] + empty
    tab_ref[24:48] = got[2] * 128.0 + got[3] + empty
    tab_ref[48:72] = got[4]
    chunk_ref[...] = jnp.zeros(chunk_ref.shape, f32)
    for d in range(2, SLABS - 1):
        tile, seg = place(d)
        pair = jnp.concatenate([tab_ref[24 + tile : 25 + tile], tab_ref[48 + tile : 49 + tile]], axis=0)
        chunk_ref[(p + d) & (SLABS - 1), 0:2, :] = lane_roll(pair, -seg)
    for ref, tile in ((up_ref, 2), (down_ref, 4)):
        ref[0:2] = tab_ref[24 + tile : 26 + tile]
        ref[2:4] = tab_ref[48 + tile : 50 + tile]
        ref[4:8] = jnp.zeros((4, 128), f32)


def gather_rows(hi_ref, lo_ref, idx_ref, here_ref):
    def step(k, carry):
        idx = jnp.concatenate([idx_ref[pl.ds(2 * k, 1), :], idx_ref[pl.ds(2 * k + 1, 1), :]], axis=1)
        code = ((idx >> 12) << 7) | (idx & 127)
        pick = (lax.broadcasted_iota(i32, (512, 256), 0) == code).astype(f32).astype(bf16)
        rows = jnp.dot(hi_ref[...], pick, preferred_element_type=f32)
        rows = rows + jnp.dot(lo_ref[...], pick, preferred_element_type=f32)
        in_y = lax.broadcasted_iota(i32, (32, 256), 0) == ((idx >> 7) & 31)
        got = jnp.sum(jnp.where(in_y[None], rows.reshape(12, 32, 256), 0.0), axis=1)
        here_ref[2 * k] = got[:, :128]
        here_ref[2 * k + 1] = got[:, 128:]
        return carry

    lax.fori_loop(0, SIDE, step, 0)


def split_store(hi_ref, lo_ref, at_rows, at_lanes, value):
    hi = value.astype(bf16)
    hi_ref[at_rows, at_lanes] = hi
    lo_ref[at_rows, at_lanes] = (value - hi.astype(f32)).astype(bf16)


def send_rows(p, here_ref, chunk_ref, up_ref, down_ref):
    for d in (0, 1, SLABS - 1):
        chunk_ref[(p + d) & (SLABS - 1)] = jnp.zeros((24, 128), f32)
    for d in range(2, SLABS - 1):
        tile, seg = place(d)
        chunk_ref[(p + d) & (SLABS - 1), 0:12, :] = lane_roll(here_ref[tile], -seg)
        tile, seg = place(SLABS - d)
        chunk_ref[(p + d) & (SLABS - 1), 12:24, :] = lane_roll(here_ref[SIDE + tile], -seg)
    for k in range(2):
        up_ref[k] = here_ref[2 + k]
        up_ref[2 + k] = here_ref[SIDE + 4 + k]
        down_ref[k] = here_ref[4 + k]
        down_ref[2 + k] = here_ref[SIDE + 2 + k]


def there_rows(p, here_ref, chunk_ref, up_ref, down_ref):
    def listed(d):
        return chunk_ref[(p + d) & (SLABS - 1), 12:24, :]

    def asked(d):
        return chunk_ref[(p - d) & (SLABS - 1), 0:12, :]

    empty = jnp.zeros((12, 128), f32)
    out = [here_ref[SIDE], here_ref[SIDE + 1], down_ref[2], down_ref[3], up_ref[2], up_ref[3]]
    out += [listed(2), listed(SLABS - 2)] + merge_far(listed, 12, 0.0) + [empty]
    out += [here_ref[0], here_ref[1], up_ref[0], up_ref[1], down_ref[0], down_ref[1]]
    out += [asked(2), asked(SLABS - 2)] + merge_far(asked, 12, 0.0) + [empty]
    return out


def early_kernel(p_ref, tab_ref, chunk_in, up_in, down_in, disp_ref, dir_ref,
                 idx_ref, kind_ref, here_ref, chunk_ref, up_ref, down_ref, hi_ref, lo_ref):
    p = p_ref[0]

    def asked(row):
        def read(d):
            return chunk_in[(p - d) & (SLABS - 1), row : row + 1, :]

        return read

    for row, out_ref, base, fill in ((0, idx_ref, 24, -1.0), (1, kind_ref, 48, 0.0)):
        empty = jnp.full((1, 128), fill, f32)
        mine = tab_ref[base - 24 * (1 - row) : base - 24 * (1 - row) + 17]
        theirs = [tab_ref[base : base + 2], up_in[2 * row : 2 * row + 2], down_in[2 * row : 2 * row + 2]]
        read = asked(row)
        theirs += [read(2), read(SLABS - 2)] + merge_far(read, 1, fill) + [empty]
        whole = jnp.concatenate([mine, empty] + theirs + [jnp.full((4, 128), fill, f32)], axis=0)
        out_ref[...] = whole.astype(out_ref.dtype)
    for field, ref in enumerate((disp_ref, dir_ref)):
        for x in range(4):
            value = ref[:, x].reshape(6 * 32, 128)
            split_store(hi_ref, lo_ref, slice(192 * field, 192 * (field + 1)), slice(128 * x, 128 * (x + 1)), value)
    gather_rows(hi_ref, lo_ref, idx_ref, here_ref)
    send_rows(p, here_ref, chunk_ref, up_ref, down_ref)


def late_kernel(p_ref, idx_ref, rate_ref, here_ref, chunk_ref, up_ref, down_ref, hi_ref, lo_ref):
    for x in range(4):
        value = jnp.concatenate([rate_ref[2 * x], rate_ref[2 * x + 1]], axis=1).reshape(12 * 32, 128)
        split_store(hi_ref, lo_ref, slice(0, 384), slice(128 * x, 128 * (x + 1)), value)
    gather_rows(hi_ref, lo_ref, idx_ref, here_ref)
    send_rows(p_ref[0], here_ref, chunk_ref, up_ref, down_ref)


def time_kernel(in_ref, rate_ref, acc_ref):
    count = 2 * PARTS

    def step(g, carry):
        field = g // 3
        row = 6 * field + (g - 3 * field)
        x = [in_ref[t // 2, row + 3 * (t % 2)] for t in range(count)]
        for t in range(count):
            rate = None
            acc = None
            for s in range(count):
                c2 = float(SECOND[t, s])
                acc = x[s] * c2 if acc is None else acc + x[s] * c2
                c1 = float(FIRST[t, s])
                if abs(c1) > 1e-12:
                    rate = x[s] * c1 if rate is None else rate + x[s] * c1
            rate_ref[t // 2, row + 3 * (t % 2)] = rate
            acc_ref[t // 2, row + 3 * (t % 2)] = acc + damping * rate
        return carry

    lax.fori_loop(0, 6, step, 0)


def lookup(ids, mat_ref, column, count):
    out = jnp.zeros(ids.shape, f32)
    for m in range(count):
        out = jnp.where(ids == m, mat_ref[m, column], out)
    return out


def stiff_kernel(mat_ref, ids_ref, disp_ref, dir_ref, forcing_ref, low_ref, high_ref, out_ref, mass_ref, *, materials):
    ids = ids_ref[...]
    kx, ky, kz, mass = [lookup(ids, mat_ref, col, materials) for col in range(4)]
    mass_ref[...] = mass
    kx_low = lookup(low_ref[12].astype(i32) - 1, mat_ref, 0, materials)
    kx_high = lookup(high_ref[12].astype(i32) - 1, mat_ref, 0, materials)
    shape = ids.shape
    y = lax.broadcasted_iota(i32, shape, 1)
    z = lax.broadcasted_iota(i32, shape, 2)
    xm = 0.5 * (kx + jnp.concatenate([kx_low[None], kx[:-1]], axis=0))
    xp = 0.5 * (kx + jnp.concatenate([kx[1:], kx_high[None]], axis=0))
    total = xm + xp
    sides = []
    for k, pos, axis in ((ky, y, 1), (kz, z, 2)):
        size = shape[axis]
        for shift, edge in ((1, 0), (size - 1, size - 1)):
            inside = pos != edge
            near = jnp.where(inside, pltpu.roll(k, shift, axis), 0.0)
            side = 0.5 * (k + near)
            total = total + side
            sides.append((jnp.where(inside, side, 0.0), shift, axis))
    for field, ref in enumerate((disp_ref, dir_ref)):
        for c in range(6):
            w = ref[c]
            down = jnp.concatenate([low_ref[6 * field + c][None], w[:-1]], axis=0)
            up = jnp.concatenate([w[1:], high_ref[6 * field + c][None]], axis=0)
            out = total * w - xm * down - xp * up
            for side, shift, axis in sides:
                out = out - side * pltpu.roll(w, shift, axis)
            if field == 0:
                out = out - forcing_ref[c]
            out_ref[6 * field + c] = out


def final_kernel(p_ref, idx_ref, kind_ref, here0_ref, chunk0_ref, up0_ref, down0_ref, here1_ref, chunk1_ref, up1_ref, down1_ref,
                 acc_ref, lin_ref, mass_ref, res_ref, jac_ref, gap_ref, rate_ref, val_ref, sum_ref):
    p = p_ref[0]
    for out_ref, here, chunk, up, down in (
        (gap_ref, here0_ref, chunk0_ref, up0_ref, down0_ref),
        (rate_ref, here1_ref, chunk1_ref, up1_ref, down1_ref),
    ):
        for tile, other in enumerate(there_rows(p, here, chunk, up, down)):
            out_ref[tile] = here[tile] - other
    bolted = kind_ref[0 : 2 * SIDE][:, None, :]
    r = gap_ref[:, 0:6, :]
    dr = gap_ref[:, 6:12, :]
    w = rate_ref[:, 0:6, :]
    dw = rate_ref[:, 6:12, :]
    slide = jnp.tanh(w / slip_speed)
    opened = jnp.tanh(r / clearance)
    friction = bolt_stiff * r + slip_force * slide
    contact = stop_stiff * (r - clearance * opened)
    val_ref[:, 0:6, :] = bolted * friction + (1.0 - bolted) * contact
    tangent_friction = bolt_stiff * dr + slip_force * (1.0 - slide * slide) / slip_speed * dw
    tangent_contact = stop_stiff * opened * opened * dr
    val_ref[:, 6:12, :] = bolted * tangent_friction + (1.0 - bolted) * tangent_contact
    sum_ref[...] = jnp.zeros(sum_ref.shape, f32)

    def step(k, carry):
        idx = jnp.concatenate([idx_ref[pl.ds(2 * k, 1), :], idx_ref[pl.ds(2 * k + 1, 1), :]], axis=1)
        code = ((idx >> 12) << 7) | (idx & 127)
        pick = (lax.broadcasted_iota(i32, (512, 256), 0) == code).astype(f32).astype(bf16)
        in_y = lax.broadcasted_iota(i32, (32, 256), 0) == ((idx >> 7) & 31)
        value = jnp.concatenate([val_ref[2 * k], val_ref[2 * k + 1]], axis=1)
        hi = value.astype(bf16).astype(f32)
        lo = value - hi
        spread = [
            jnp.where(in_y[None], part[:, None, :], 0.0).reshape(384, 256).astype(bf16) for part in (hi, lo)
        ]
        dims = (((1,), (1,)), ((), ()))
        got = lax.dot_general(spread[0], pick, dims, preferred_element_type=f32)
        got = got + lax.dot_general(spread[1], pick, dims, preferred_element_type=f32)
        sum_ref[...] = sum_ref[...] + got
        return carry

    lax.fori_loop(0, SIDE, step, 0)
    for x in range(4):
        added = sum_ref[:, 128 * x : 128 * (x + 1)].reshape(12, 32, 128)
        acc = jnp.concatenate([acc_ref[2 * x], acc_ref[2 * x + 1]], axis=1)
        out = mass_ref[x][None] * acc + lin_ref[:, x] + added
        res_ref[:, x] = out[0:6]
        jac_ref[:, x] = out[6:12]


VMEM = 48 * 1024 * 1024


def call(kernel, outs, *args, smem=(0,), scratch=()):
    specs = [pl.BlockSpec(memory_space=pltpu.SMEM if k in smem else pltpu.VMEM) for k in range(len(args))]
    return pl.pallas_call(
        kernel,
        out_shape=[jax.ShapeDtypeStruct(s, d) for s, d in outs],
        in_specs=specs,
        out_specs=[pl.BlockSpec(memory_space=pltpu.VMEM) for _ in outs],
        scratch_shapes=list(scratch),
        compiler_params=pltpu.CompilerParams(vmem_limit_bytes=VMEM),
    )(*args)


def shift(x, by, wrap=True):
    pairs = [(i, (i + by) % SLABS) for i in range(SLABS) if wrap or 0 <= i + by < SLABS]
    return lax.ppermute(x, "mesh", pairs)


def exchange(chunk, up, down):
    chunk = lax.all_to_all(chunk, "mesh", split_axis=0, concat_axis=0, tiled=True)
    return chunk, shift(up, 1), shift(down, -1)


def on_device(displacement, direction, forcing, material_ids, materials, joint_owner, joint_local, joint_remote, joint_kind):
    shape = displacement.shape
    fields = (6, 4, 32, 128)
    disp = displacement.reshape(fields)
    dire = direction.reshape(fields)
    count = joint_local.shape[0]
    p = lax.axis_index("mesh").astype(i32).reshape(1)

    both = jnp.concatenate([disp, dire], axis=0).reshape(12, PARTS, 16, 128)
    blocks = lax.all_to_all(both.swapaxes(0, 1), "inst", split_axis=0, concat_axis=0, tiled=True)

    tab, chunk, up, down = call(
        prep_kernel,
        [((72, 128), f32), ((SLABS, 8, 128), f32), ((8, 128), f32), ((8, 128), f32)],
        p,
        joint_owner.reshape(1, count),
        joint_local.reshape(1, count),
        joint_remote.reshape(1, count),
        joint_kind.reshape(1, count),
    )
    chunk, up, down = exchange(chunk, up, down)

    ids_plus = (material_ids + 1).astype(f32)
    low = shift(jnp.concatenate([disp[:, 3], dire[:, 3], ids_plus[3:4]], axis=0), 1, wrap=False)
    high = shift(jnp.concatenate([disp[:, 0], dire[:, 0], ids_plus[0:1]], axis=0), -1, wrap=False)

    rate, acc = call(time_kernel, [((PARTS, 12, 16, 128), f32)] * 2, blocks, smem=())
    rate = lax.all_to_all(rate, "inst", split_axis=0, concat_axis=0, tiled=True)
    acc = lax.all_to_all(acc, "inst", split_axis=0, concat_axis=0, tiled=True)

    message = [((SLABS, 24, 128), f32), ((4, 12, 128), f32), ((4, 12, 128), f32)]
    split = [pltpu.VMEM((384, 512), bf16)] * 2
    rows = ((2 * SIDE, 12, 128), f32)
    idx, kind, here0, *sent0 = call(
        early_kernel,
        [((40, 128), i32), ((40, 128), f32), rows] + message,
        p, tab, chunk, up, down, disp, dire,
        scratch=split,
    )
    got0 = exchange(*sent0)

    lin, mass = call(
        lambda *refs: stiff_kernel(*refs, materials=materials.shape[0]),
        [((12, 4, 32, 128), f32), ((4, 32, 128), f32)],
        materials, material_ids, disp, dire, forcing.reshape(fields), low, high,
    )

    here1, *sent1 = call(late_kernel, [rows] + message, p, idx, rate, scratch=split)
    got1 = exchange(*sent1)

    residual, jacobian = call(
        final_kernel,
        [(fields, f32)] * 2,
        p, idx, kind, here0, *got0, here1, *got1, acc, lin, mass,
        scratch=[pltpu.VMEM((2 * SIDE, 12, 128), f32)] * 3 + [pltpu.VMEM((384, 512), f32)],
    )
    return residual.reshape(shape), jacobian.reshape(shape)


def solution(mesh):
    field = P("inst", None, "mesh", None, None)
    placed = (field, field, field, P("mesh", None, None), P(), P("mesh", None), P("mesh"), P("mesh"), P("mesh"))
    return jax.shard_map(on_device, mesh=mesh, in_specs=placed, out_specs=(field, field), check_vma=False)
```

```python
import jax
import jax.numpy as jnp
import numpy as np
from jax import lax
from jax.experimental import pallas as pl
from jax.experimental.pallas import tpu as pltpu
from jax.sharding import PartitionSpec as P

frequency = 0.6
damping = 0.3
bolt_stiff = 2.0
slip_force = 1.0
slip_speed = 0.5
stop_stiff = 3.0
clearance = 0.3

SLABS = 32
PARTS = 8
SIDE = 18
SEG = 42
f32 = jnp.float32
bf16 = jnp.bfloat16
i32 = jnp.int32


def tables(count):
    offsets = np.arange(count)[:, None] - np.arange(count)[None, :]
    tangent = np.where(offsets == 0, 1.0, np.tan(np.pi * offsets / count))
    first = np.where(offsets == 0, 0.0, 0.5 * np.where(offsets % 2 == 0, 1.0, -1.0) / tangent) * frequency
    return first, first @ first


FIRST, SECOND = tables(2 * PARTS)
MIXED = (SECOND + damping * FIRST).astype(np.float32)
SPREAD = np.kron(FIRST, np.eye(3)).astype(np.float32)


def far_place(offset):
    return 8 + (offset - 3) // 3, SEG * ((offset - 3) % 3)


def place(offset):
    return {2: (6, 0), 30: (7, 0)}.get(offset) or far_place(offset)


def lane_roll(x, shift):
    shift = shift % 128
    return pltpu.roll(x, shift, x.ndim - 1) if shift else x


def lanes(rows):
    return lax.broadcasted_iota(i32, (rows, 128), 1)


def merge_far(read, rows, fill):
    lane = lanes(rows)
    tiles = []
    for k in range(9):
        parts = [lane_roll(read(3 + 3 * k + s), SEG * s) for s in range(3)]
        tile = jnp.where(lane < SEG, parts[0], jnp.where(lane < 2 * SEG, parts[1], parts[2]))
        tiles.append(jnp.where(lane < 3 * SEG, tile, fill))
    return tiles


def slot_tables(p, owner_ref, local_ref, remote_ref, kind_ref):
    count = owner_ref.shape[1]
    offset = (owner_ref[...] - p) & (SLABS - 1)
    hit = (lax.broadcasted_iota(i32, (SLABS, count), 0) == offset).astype(f32)
    hit16 = hit.astype(bf16)
    before = (lax.broadcasted_iota(i32, (128, 128), 0) < lax.broadcasted_iota(i32, (128, 128), 1)).astype(f32).astype(bf16)
    row = lax.broadcasted_iota(i32, (SLABS, 1), 0)
    far = row - 3
    group = (far * 171) >> 9
    start = 1024 + group * 128 + (far - 3 * group) * SEG
    for value, at in ((0, 0), (1, 256), (SLABS - 1, 512), (2, 768), (SLABS - 2, 896)):
        start = jnp.where(row == value, at, start)
    run = start.astype(f32)
    places = []
    for b in range(count // 128):
        block = hit[:, 128 * b : 128 * (b + 1)]
        earlier = jnp.dot(hit16[:, 128 * b : 128 * (b + 1)], before, preferred_element_type=f32)
        places.append(jnp.sum(block * (earlier + run), axis=0, keepdims=True))
        run = run + jnp.sum(block, axis=1, keepdims=True)
    slot = jnp.concatenate(places, axis=1).astype(i32)
    in_tile = lax.broadcasted_iota(i32, (24, count), 0) == (slot >> 7)
    in_lane = (lax.broadcasted_iota(i32, (128, count), 0) == (slot & 127)).astype(f32).astype(bf16)
    local = local_ref[...]
    remote = remote_ref[...]
    values = (local >> 7, local & 127, remote >> 7, remote & 127, kind_ref[...], jnp.ones_like(local))
    spread = jnp.concatenate([jnp.where(in_tile, v.astype(f32), 0.0) for v in values], axis=0).astype(bf16)
    got = lax.dot_general(spread, in_lane, (((1,), (1,)), ((), ())), preferred_element_type=f32)
    got = [got[24 * k : 24 * (k + 1)] for k in range(6)]
    empty = got[5] - 1.0
    return got[0] * 128.0 + got[1] + empty, got[2] * 128.0 + got[3] + empty, got[4]


def picks(idx_ref, k):
    idx = jnp.concatenate([idx_ref[pl.ds(2 * k, 1), :], idx_ref[pl.ds(2 * k + 1, 1), :]], axis=1)
    code = ((idx >> 12) << 7) | (idx & 127)
    pick = (lax.broadcasted_iota(i32, (512, 256), 0) == code).astype(f32).astype(bf16)
    return pick, lax.broadcasted_iota(i32, (32, 256), 0) == ((idx >> 7) & 31)


def split_fields(disp_ref, dir_ref, hi_ref, lo_ref):
    for field, ref in enumerate((disp_ref, dir_ref)):
        for x in range(4):
            value = ref[:, x].reshape(6 * 32, 128)
            hi = value.astype(bf16)
            at = (slice(192 * field, 192 * (field + 1)), slice(128 * x, 128 * (x + 1)))
            hi_ref[at] = hi
            lo_ref[at] = (value - hi.astype(f32)).astype(bf16)


def gather_rows(hi_ref, lo_ref, idx_ref, here_ref):
    def step(k, carry):
        pick, in_y = picks(idx_ref, k)
        rows = jnp.dot(hi_ref[...], pick, preferred_element_type=f32)
        rows = rows + jnp.dot(lo_ref[...], pick, preferred_element_type=f32)
        got = jnp.sum(jnp.where(in_y[None], rows.reshape(12, 32, 256), 0.0), axis=1)
        here_ref[2 * k, 0:12, :] = got[:, :128]
        here_ref[2 * k + 1, 0:12, :] = got[:, 128:]
        return carry

    lax.fori_loop(0, SIDE // 2, step, 0)


def scatter_rows(val_ref, idx_ref, sum_ref):
    sum_ref[...] = jnp.zeros(sum_ref.shape, f32)
    dims = (((1,), (1,)), ((), ()))

    def step(k, carry):
        pick, in_y = picks(idx_ref, k)
        value = jnp.concatenate([val_ref[2 * k], val_ref[2 * k + 1]], axis=1)
        hi = value.astype(bf16).astype(f32)
        spread = [
            jnp.where(in_y[None], part[:, None, :], 0.0).reshape(384, 256).astype(bf16) for part in (hi, value - hi)
        ]
        got = lax.dot_general(spread[0], pick, dims, preferred_element_type=f32)
        got = got + lax.dot_general(spread[1], pick, dims, preferred_element_type=f32)
        sum_ref[...] = sum_ref[...] + got
        return carry

    lax.fori_loop(0, SIDE // 2, step, 0)


def list_kernel(p_ref, owner_ref, local_ref, remote_ref, kind_ref, disp_ref, dir_ref,
                idx_ref, chunk_ref, up_ref, down_ref, self_ref, hi_ref, lo_ref, rows_ref):
    p = p_ref[0]
    split_fields(disp_ref, dir_ref, hi_ref, lo_ref)
    mine, theirs, kind = slot_tables(p, owner_ref, local_ref, remote_ref, kind_ref)
    idx_ref[...] = mine.astype(i32)
    for tile in range(SIDE):
        rows_ref[tile, 12:13, :] = theirs[tile : tile + 1]
        rows_ref[tile, 13:14, :] = kind[tile : tile + 1]
        rows_ref[tile, 14:16, :] = jnp.zeros((2, 128), f32)
    gather_rows(hi_ref, lo_ref, idx_ref, rows_ref)
    for d in (0, 1, SLABS - 1):
        chunk_ref[(p + d) & (SLABS - 1)] = jnp.zeros((16, 128), f32)
    for d in range(2, SLABS - 1):
        tile, seg = place(d)
        chunk_ref[(p + d) & (SLABS - 1)] = lane_roll(rows_ref[tile], -seg)
    self_ref[...] = rows_ref[0:2]
    up_ref[...] = rows_ref[2:4]
    down_ref[...] = rows_ref[4:6]


def gap_kernel(p_ref, chunk_ref, up_ref, down_ref, self_ref, disp_ref, dir_ref,
               idx_ref, kind_ref, gap_ref, hi_ref, lo_ref, here_ref):
    p = p_ref[0]
    split_fields(disp_ref, dir_ref, hi_ref, lo_ref)

    def asked(d):
        return chunk_ref[(p - d) & (SLABS - 1)]

    tiles = [self_ref[0], self_ref[1], up_ref[0], up_ref[1], down_ref[0], down_ref[1], asked(2), asked(SLABS - 2)]
    tiles += merge_far(asked, 16, 0.0)
    beyond = lanes(1) >= 3 * SEG
    rows = [t[12:13] for t in tiles[:8]] + [jnp.where(beyond, -1.0, t[12:13]) for t in tiles[8:]]
    idx_ref[...] = jnp.concatenate(rows + [jnp.full((7, 128), -1.0, f32)], axis=0).astype(i32)
    kind_ref[...] = jnp.concatenate([t[13:14] for t in tiles] + [jnp.zeros((7, 128), f32)], axis=0)
    gather_rows(hi_ref, lo_ref, idx_ref, here_ref)
    for tile in range(24):
        gap = tiles[tile][0:12] - here_ref[tile] if tile < 17 else jnp.zeros((12, 128), f32)
        gap_ref[tile // 3, :, 128 * (tile % 3) : 128 * (tile % 3 + 1)] = gap


def force_kernel(me_ref, kind_ref, spread_ref, gap_ref, out_ref, r_ref, d_ref, f_ref, t_ref):
    me = me_ref[0]
    for k in range(PARTS):
        r_ref[6 * k : 6 * k + 6] = gap_ref[k, 0:6, :]
        d_ref[6 * k : 6 * k + 6] = gap_ref[k, 6:12, :]
    r = r_ref[...]
    dr = d_ref[...]
    w = jnp.dot(spread_ref[...], r, precision=lax.Precision.HIGHEST, preferred_element_type=f32)
    dw = jnp.dot(spread_ref[...], dr, precision=lax.Precision.HIGHEST, preferred_element_type=f32)
    bolted = jnp.concatenate([kind_ref[pl.ds(3 * me + k, 1), :] for k in range(3)], axis=1)
    slide = jnp.tanh(w / slip_speed)
    opened = jnp.tanh(r / clearance)
    friction = bolt_stiff * r + slip_force * slide
    contact = stop_stiff * (r - clearance * opened)
    f_ref[...] = bolted * friction + (1.0 - bolted) * contact
    tangent_friction = bolt_stiff * dr + slip_force * (1.0 - slide * slide) / slip_speed * dw
    tangent_contact = stop_stiff * opened * opened * dr
    t_ref[...] = bolted * tangent_friction + (1.0 - bolted) * tangent_contact
    for k in range(PARTS):
        out_ref[k, 0:6, :] = f_ref[6 * k : 6 * k + 6]
        out_ref[k, 6:12, :] = t_ref[6 * k : 6 * k + 6]


def reply_kernel(p_ref, force_ref, chunk_ref, up_ref, down_ref, self_ref):
    p = p_ref[0]

    def force(tile):
        return force_ref[tile // 3, :, 128 * (tile % 3) : 128 * (tile % 3 + 1)]

    for d in (0, 1, SLABS - 1):
        chunk_ref[(p - d) & (SLABS - 1)] = jnp.zeros((12, 128), f32)
    for d in range(2, SLABS - 1):
        tile, seg = place(d)
        chunk_ref[(p - d) & (SLABS - 1)] = lane_roll(force(tile), -seg)
    for k in range(2):
        self_ref[k] = force(k)
        down_ref[k] = force(2 + k)
        up_ref[k] = force(4 + k)


def partner_kernel(me_ref, idx_ref, force_ref, lin_ref, mass_ref, *refs):
    acc_refs, (out_ref, val_ref, sum_ref) = refs[:PARTS], refs[PARTS:]
    for tile in range(17):
        val_ref[tile] = -force_ref[tile // 3, :, 128 * (tile % 3) : 128 * (tile % 3 + 1)]
    val_ref[17] = jnp.zeros((12, 128), f32)
    scatter_rows(val_ref, idx_ref, sum_ref)
    for x in range(4):
        out_ref[:, x] = lin_ref[:, x] + sum_ref[:, 128 * x : 128 * (x + 1)].reshape(12, 32, 128)
    me = me_ref[0]
    for k, acc in enumerate(acc_refs):
        block = me ^ k
        x = block >> 1
        rows = pl.ds(pl.multiple_of(16 * (block & 1), 16), 16)
        out_ref[:, x, rows, :] = out_ref[:, x, rows, :] + mass_ref[x, rows, :][None] * acc[...]


def final_kernel(p_ref, idx_ref, chunk_ref, up_ref, down_ref, self_ref, part_ref, res_ref, jac_ref, val_ref, sum_ref):
    p = p_ref[0]

    def listed(d):
        return chunk_ref[(p + d) & (SLABS - 1)]

    tiles = [self_ref[0], self_ref[1], down_ref[0], down_ref[1], up_ref[0], up_ref[1], listed(2), listed(SLABS - 2)]
    tiles += merge_far(listed, 12, 0.0) + [jnp.zeros((12, 128), f32)]
    for k, tile in enumerate(tiles):
        val_ref[k] = tile
    scatter_rows(val_ref, idx_ref, sum_ref)
    for x in range(4):
        out = part_ref[:, x] + sum_ref[:, 128 * x : 128 * (x + 1)].reshape(12, 32, 128)
        res_ref[:, x] = out[0:6]
        jac_ref[:, x] = out[6:12]


def piece_kernel(me_ref, disp_ref, dir_ref, *out_refs):
    me = me_ref[0]
    for k, out in enumerate(out_refs):
        block = me ^ k
        rows = pl.ds(pl.multiple_of(16 * (block & 1), 16), 16)
        out[0:6] = disp_ref[:, block >> 1, rows, :]
        out[6:12] = dir_ref[:, block >> 1, rows, :]


def time_kernel(me_ref, table_ref, *refs):
    ins, outs = refs[:PARTS], refs[PARTS:]
    me = me_ref[0]

    def step(g, carry):
        field = g // 3
        row = 6 * field + (g - 3 * field)
        x = [[ins[k][row + 3 * t] for t in range(2)] for k in range(PARTS)]
        for k in range(PARTS):
            for t in range(2):
                acc = None
                for j in range(PARTS):
                    for s in range(2):
                        term = x[j][s] * table_ref[2 * (me ^ k) + t, 2 * (me ^ j) + s]
                        acc = term if acc is None else acc + term
                outs[k][row + 3 * t] = acc
        return carry

    lax.fori_loop(0, 6, step, 0)


def lookup(ids, mat_ref, column, count):
    out = jnp.zeros(ids.shape, f32)
    for m in range(count):
        out = jnp.where(ids == m, mat_ref[m, column], out)
    return out


def stiff_kernel(mat_ref, ids_ref, disp_ref, dir_ref, forcing_ref, low_ref, high_ref, out_ref, mass_ref, *, materials):
    ids = ids_ref[...]
    kx, ky, kz, mass = [lookup(ids, mat_ref, col, materials) for col in range(4)]
    mass_ref[...] = mass
    kx_low = lookup(low_ref[12].astype(i32) - 1, mat_ref, 0, materials)
    kx_high = lookup(high_ref[12].astype(i32) - 1, mat_ref, 0, materials)
    shape = ids.shape
    y = lax.broadcasted_iota(i32, shape, 1)
    z = lax.broadcasted_iota(i32, shape, 2)
    xm = 0.5 * (kx + jnp.concatenate([kx_low[None], kx[:-1]], axis=0))
    xp = 0.5 * (kx + jnp.concatenate([kx[1:], kx_high[None]], axis=0))
    total = xm + xp
    sides = []
    for k, pos, axis in ((ky, y, 1), (kz, z, 2)):
        size = shape[axis]
        for shift, edge in ((1, 0), (size - 1, size - 1)):
            inside = pos != edge
            near = jnp.where(inside, pltpu.roll(k, shift, axis), 0.0)
            side = 0.5 * (k + near)
            total = total + side
            sides.append((jnp.where(inside, side, 0.0), shift, axis))
    for field, ref in enumerate((disp_ref, dir_ref)):
        for c in range(6):
            w = ref[c]
            down = jnp.concatenate([low_ref[6 * field + c][None], w[:-1]], axis=0)
            up = jnp.concatenate([w[1:], high_ref[6 * field + c][None]], axis=0)
            out = total * w - xm * down - xp * up
            for side, shift, axis in sides:
                out = out - side * pltpu.roll(w, shift, axis)
            if field == 0:
                out = out - forcing_ref[c]
            out_ref[6 * field + c] = out


VMEM = 48 * 1024 * 1024


def call(kernel, outs, *args, smem=(0,), scratch=()):
    specs = [pl.BlockSpec(memory_space=pltpu.SMEM if k in smem else pltpu.VMEM) for k in range(len(args))]
    return pl.pallas_call(
        kernel,
        out_shape=[jax.ShapeDtypeStruct(s, d) for s, d in outs],
        in_specs=specs,
        out_specs=[pl.BlockSpec(memory_space=pltpu.VMEM) for _ in outs],
        scratch_shapes=list(scratch),
        compiler_params=pltpu.CompilerParams(vmem_limit_bytes=VMEM),
    )(*args)


def shift(x, by, wrap=True):
    pairs = [(i, (i + by) % SLABS) for i in range(SLABS) if wrap or 0 <= i + by < SLABS]
    return lax.ppermute(x, "mesh", pairs)


def exchange(chunk, up, down):
    up, down = shift(up, 1), shift(down, -1)
    return lax.all_to_all(chunk, "mesh", split_axis=0, concat_axis=0, tiled=True), up, down


def swap(pieces):
    return [pieces[0]] + [lax.ppermute(pieces[k], "inst", [(i, i ^ k) for i in range(PARTS)]) for k in range(1, PARTS)]


def inst_split(x):
    return lax.all_to_all(x, "inst", split_axis=0, concat_axis=0, tiled=True)


def on_device(displacement, direction, forcing, material_ids, materials, joint_owner, joint_local, joint_remote, joint_kind):
    shape = displacement.shape
    fields = (6, 4, 32, 128)
    whole = (12, 4, 32, 128)
    disp = displacement.reshape(fields)
    dire = direction.reshape(fields)
    count = joint_local.shape[0]
    p = lax.axis_index("mesh").astype(i32).reshape(1)
    me = lax.axis_index("inst").astype(i32).reshape(1)
    split = [pltpu.VMEM((384, 512), bf16)] * 2
    index = ((24, 128), i32)

    own_idx, chunk, up, down, own = call(
        list_kernel,
        [index, ((SLABS, 16, 128), f32)] + [((2, 16, 128), f32)] * 3,
        p,
        joint_owner.reshape(1, count),
        joint_local.reshape(1, count),
        joint_remote.reshape(1, count),
        joint_kind.reshape(1, count),
        disp,
        dire,
        scratch=split + [pltpu.VMEM((SIDE, 16, 128), f32)],
    )
    chunk, up, down = exchange(chunk, up, down)

    pieces = swap(call(piece_kernel, [((12, 16, 128), f32)] * PARTS, me, disp, dire))
    pieces = swap(call(time_kernel, [((12, 16, 128), f32)] * PARTS, me, jnp.asarray(MIXED), *pieces, smem=(0, 1)))

    ids_plus = (material_ids + 1).astype(f32)
    low = shift(jnp.concatenate([disp[:, 3], dire[:, 3], ids_plus[3:4]], axis=0), 1, wrap=False)
    high = shift(jnp.concatenate([disp[:, 0], dire[:, 0], ids_plus[0:1]], axis=0), -1, wrap=False)
    lin, mass = call(
        lambda *refs: stiff_kernel(*refs, materials=materials.shape[0]),
        [(whole, f32), ((4, 32, 128), f32)],
        materials, material_ids, disp, dire, forcing.reshape(fields), low, high,
    )

    part = ((PARTS, 12, 384), f32)
    far_idx, kind, gap = call(
        gap_kernel,
        [index, ((24, 128), f32), part],
        p, chunk, up, down, own, disp, dire,
        scratch=split + [pltpu.VMEM((SIDE, 12, 128), f32)],
    )
    force = call(
        force_kernel, [part], me, kind, jnp.asarray(SPREAD), inst_split(gap), scratch=[pltpu.VMEM((48, 384), f32)] * 4
    )[0]
    force = inst_split(force)
    chunk, up, down, own = call(
        reply_kernel, [((SLABS, 12, 128), f32)] + [((2, 12, 128), f32)] * 3, p, force
    )
    chunk, up, down = exchange(chunk, up, down)

    adding = [pltpu.VMEM((SIDE, 12, 128), f32), pltpu.VMEM((384, 512), f32)]
    partial = call(partner_kernel, [(whole, f32)], me, far_idx, force, lin, mass, *pieces, scratch=adding)[0]
    residual, jacobian = call(
        final_kernel, [(fields, f32)] * 2, p, own_idx, chunk, up, down, own, partial, scratch=adding
    )
    return residual.reshape(shape), jacobian.reshape(shape)


def solution(mesh):
    field = P("inst", None, "mesh", None, None)
    placed = (field, field, field, P("mesh", None, None), P(), P("mesh", None), P("mesh"), P("mesh"), P("mesh"))
    return jax.shard_map(on_device, mesh=mesh, in_specs=placed, out_specs=(field, field), check_vma=False)
```

```python
import jax
import jax.numpy as jnp
import numpy as np
from jax import lax
from jax.experimental import pallas as pl
from jax.experimental.pallas import tpu as pltpu
from jax.sharding import PartitionSpec as P

frequency = 0.6
damping = 0.3
bolt_stiff = 2.0
slip_force = 1.0
slip_speed = 0.5
stop_stiff = 3.0
clearance = 0.3

SLABS = 32
PARTS = 8
SIDE = 18
SEG = 42
f32 = jnp.float32
bf16 = jnp.bfloat16
i32 = jnp.int32


def tables(count):
    offsets = np.arange(count)[:, None] - np.arange(count)[None, :]
    tangent = np.where(offsets == 0, 1.0, np.tan(np.pi * offsets / count))
    first = np.where(offsets == 0, 0.0, 0.5 * np.where(offsets % 2 == 0, 1.0, -1.0) / tangent) * frequency
    return first, first @ first


FIRST, SECOND = tables(2 * PARTS)
MIXED = (SECOND + damping * FIRST).astype(np.float32)
SPREAD = np.kron(FIRST, np.eye(3)).astype(np.float32)


def far_place(offset):
    return 8 + (offset - 3) // 3, SEG * ((offset - 3) % 3)


def place(offset):
    return {2: (6, 0), 30: (7, 0)}.get(offset) or far_place(offset)


def lane_roll(x, shift):
    shift = shift % 128
    return pltpu.roll(x, shift, x.ndim - 1) if shift else x


def lanes(rows):
    return lax.broadcasted_iota(i32, (rows, 128), 1)


def merge_far(read, rows, fill):
    lane = lanes(rows)
    tiles = []
    for k in range(9):
        parts = [lane_roll(read(3 + 3 * k + s), SEG * s) for s in range(3)]
        tile = jnp.where(lane < SEG, parts[0], jnp.where(lane < 2 * SEG, parts[1], parts[2]))
        tiles.append(jnp.where(lane < 3 * SEG, tile, fill))
    return tiles


def slot_tables(p, owner_ref, local_ref, remote_ref, kind_ref):
    count = owner_ref.shape[1]
    offset = (owner_ref[...] - p) & (SLABS - 1)
    hit = (lax.broadcasted_iota(i32, (SLABS, count), 0) == offset).astype(f32)
    hit16 = hit.astype(bf16)
    before = (lax.broadcasted_iota(i32, (128, 128), 0) < lax.broadcasted_iota(i32, (128, 128), 1)).astype(f32).astype(bf16)
    row = lax.broadcasted_iota(i32, (SLABS, 1), 0)
    far = row - 3
    group = (far * 171) >> 9
    start = 1024 + group * 128 + (far - 3 * group) * SEG
    for value, at in ((0, 0), (1, 256), (SLABS - 1, 512), (2, 768), (SLABS - 2, 896)):
        start = jnp.where(row == value, at, start)
    run = start.astype(f32)
    places = []
    for b in range(count // 128):
        block = hit[:, 128 * b : 128 * (b + 1)]
        earlier = jnp.dot(hit16[:, 128 * b : 128 * (b + 1)], before, preferred_element_type=f32)
        places.append(jnp.sum(block * (earlier + run), axis=0, keepdims=True))
        run = run + jnp.sum(block, axis=1, keepdims=True)
    slot = jnp.concatenate(places, axis=1).astype(i32)
    in_tile = lax.broadcasted_iota(i32, (24, count), 0) == (slot >> 7)
    in_lane = (lax.broadcasted_iota(i32, (128, count), 0) == (slot & 127)).astype(f32).astype(bf16)
    local = local_ref[...]
    remote = remote_ref[...]
    values = (local >> 7, local & 127, remote >> 7, remote & 127, kind_ref[...], jnp.ones_like(local))
    spread = jnp.concatenate([jnp.where(in_tile, v.astype(f32), 0.0) for v in values], axis=0).astype(bf16)
    got = lax.dot_general(spread, in_lane, (((1,), (1,)), ((), ())), preferred_element_type=f32)
    got = [got[24 * k : 24 * (k + 1)] for k in range(6)]
    empty = got[5] - 1.0
    return got[0] * 128.0 + got[1] + empty, got[2] * 128.0 + got[3] + empty, got[4]


def picks(idx_ref, k):
    idx = jnp.concatenate([idx_ref[pl.ds(2 * k, 1), :], idx_ref[pl.ds(2 * k + 1, 1), :]], axis=1)
    code = ((idx >> 12) << 7) | (idx & 127)
    pick = (lax.broadcasted_iota(i32, (512, 256), 0) == code).astype(f32).astype(bf16)
    return pick, lax.broadcasted_iota(i32, (32, 256), 0) == ((idx >> 7) & 31)


def split_fields(disp_ref, dir_ref, hi_ref, lo_ref):
    for field, ref in enumerate((disp_ref, dir_ref)):
        for x in range(4):
            value = ref[:, x].reshape(6 * 32, 128)
            hi = value.astype(bf16)
            at = (slice(192 * field, 192 * (field + 1)), slice(128 * x, 128 * (x + 1)))
            hi_ref[at] = hi
            lo_ref[at] = (value - hi.astype(f32)).astype(bf16)


def gather_rows(hi_ref, lo_ref, idx_ref, here_ref):
    def step(k, carry):
        pick, in_y = picks(idx_ref, k)
        rows = jnp.dot(hi_ref[...], pick, preferred_element_type=f32)
        rows = rows + jnp.dot(lo_ref[...], pick, preferred_element_type=f32)
        got = jnp.sum(jnp.where(in_y[None], rows.reshape(12, 32, 256), 0.0), axis=1)
        here_ref[2 * k, 0:12, :] = got[:, :128]
        here_ref[2 * k + 1, 0:12, :] = got[:, 128:]
        return carry

    lax.fori_loop(0, SIDE // 2, step, 0)


def scatter_rows(val_ref, idx_ref, sum_ref):
    sum_ref[...] = jnp.zeros(sum_ref.shape, f32)
    dims = (((1,), (1,)), ((), ()))

    def step(k, carry):
        pick, in_y = picks(idx_ref, k)
        value = jnp.concatenate([val_ref[2 * k], val_ref[2 * k + 1]], axis=1)
        hi = value.astype(bf16).astype(f32)
        spread = [
            jnp.where(in_y[None], part[:, None, :], 0.0).reshape(384, 256).astype(bf16) for part in (hi, value - hi)
        ]
        got = lax.dot_general(spread[0], pick, dims, preferred_element_type=f32)
        got = got + lax.dot_general(spread[1], pick, dims, preferred_element_type=f32)
        sum_ref[...] = sum_ref[...] + got
        return carry

    lax.fori_loop(0, SIDE // 2, step, 0)


def list_kernel(p_ref, me_ref, owner_hbm, local_hbm, remote_hbm, kind_hbm, disp_hbm, dir_hbm, ids_hbm,
                idx_ref, chunk_ref, up_ref, down_ref, self_ref, same_ref, other_ref,
                hi_ref, lo_ref, rows_ref, owner_ref, local_ref, remote_ref, kind_ref, disp_ref, dir_ref, ids_ref, sems):
    p = p_ref[0]
    pairs = ((owner_hbm, owner_ref), (local_hbm, local_ref), (remote_hbm, remote_ref), (kind_hbm, kind_ref),
             (disp_hbm, disp_ref), (dir_hbm, dir_ref), (ids_hbm, ids_ref))
    copies = [pltpu.make_async_copy(a, b, sems.at[k]) for k, (a, b) in enumerate(pairs)]
    for copy in copies:
        copy.start()
    for copy in copies[:4]:
        copy.wait()
    mine, theirs, kind = slot_tables(p, owner_ref, local_ref, remote_ref, kind_ref)
    idx_ref[...] = mine.astype(i32)
    for tile in range(SIDE):
        rows_ref[tile, 12:13, :] = theirs[tile : tile + 1]
        rows_ref[tile, 13:14, :] = kind[tile : tile + 1]
        rows_ref[tile, 14:16, :] = jnp.zeros((2, 128), f32)
    for copy in copies[4:]:
        copy.wait()
    split_fields(disp_ref, dir_ref, hi_ref, lo_ref)
    for ref, x in ((up_ref, 3), (down_ref, 0)):
        ref[2:14] = disp_ref[:, x].reshape(12, 16, 128)
        ref[14:26] = dir_ref[:, x].reshape(12, 16, 128)
        ref[26:28] = (ids_ref[x] + 1).astype(f32).reshape(2, 16, 128)
    for k in range(PARTS):
        block = me_ref[0] ^ k
        rows = pl.ds(pl.multiple_of(16 * (block & 1), 16), 16)
        out = (same_ref, other_ref)[k % 2].at[k // 2]
        out[0:6] = disp_ref[:, block >> 1, rows, :]
        out[6:12] = dir_ref[:, block >> 1, rows, :]
    gather_rows(hi_ref, lo_ref, idx_ref, rows_ref)
    for d in (0, 1, SLABS - 1):
        chunk_ref[(p + d) & (SLABS - 1)] = jnp.zeros((16, 128), f32)
    for d in range(2, SLABS - 1):
        tile, seg = place(d)
        chunk_ref[(p + d) & (SLABS - 1)] = lane_roll(rows_ref[tile], -seg)
    self_ref[...] = rows_ref[0:2]
    up_ref[0:2] = rows_ref[2:4]
    down_ref[0:2] = rows_ref[4:6]


def gap_kernel(p_ref, chunk_ref, up_ref, down_ref, self_ref, disp_ref, dir_ref, after_ref,
               idx_ref, kind_ref, gap_ref, hi_ref, lo_ref, here_ref):
    p = p_ref[0]
    split_fields(disp_ref, dir_ref, hi_ref, lo_ref)

    def asked(d):
        return chunk_ref[(p - d) & (SLABS - 1)]

    tiles = [self_ref[0], self_ref[1], up_ref[0], up_ref[1], down_ref[0], down_ref[1], asked(2), asked(SLABS - 2)]
    tiles += merge_far(asked, 16, 0.0)
    beyond = lanes(1) >= 3 * SEG
    rows = [t[12:13] for t in tiles[:8]] + [jnp.where(beyond, -1.0, t[12:13]) for t in tiles[8:]]
    idx_ref[...] = jnp.concatenate(rows + [jnp.full((7, 128), -1.0, f32)], axis=0).astype(i32)
    kind_ref[...] = jnp.concatenate([t[13:14] for t in tiles] + [jnp.zeros((7, 128), f32)], axis=0)
    gather_rows(hi_ref, lo_ref, idx_ref, here_ref)
    for tile in range(24):
        gap = tiles[tile][0:12] - here_ref[tile] if tile < 17 else jnp.zeros((12, 128), f32)
        gap_ref[tile // 3, :, 128 * (tile % 3) : 128 * (tile % 3 + 1)] = gap


def force_kernel(me_ref, kind_ref, spread_ref, gap_ref, after_ref, out_ref, r_ref, d_ref, f_ref, t_ref):
    me = me_ref[0]
    for k in range(PARTS):
        r_ref[6 * k : 6 * k + 6] = gap_ref[k, 0:6, :]
        d_ref[6 * k : 6 * k + 6] = gap_ref[k, 6:12, :]
    r = r_ref[...]
    dr = d_ref[...]
    w = jnp.dot(spread_ref[...], r, precision=lax.Precision.HIGHEST, preferred_element_type=f32)
    dw = jnp.dot(spread_ref[...], dr, precision=lax.Precision.HIGHEST, preferred_element_type=f32)
    bolted = jnp.concatenate([kind_ref[pl.ds(3 * me + k, 1), :] for k in range(3)], axis=1)
    slide = jnp.tanh(w / slip_speed)
    opened = jnp.tanh(r / clearance)
    friction = bolt_stiff * r + slip_force * slide
    contact = stop_stiff * (r - clearance * opened)
    f_ref[...] = bolted * friction + (1.0 - bolted) * contact
    tangent_friction = bolt_stiff * dr + slip_force * (1.0 - slide * slide) / slip_speed * dw
    tangent_contact = stop_stiff * opened * opened * dr
    t_ref[...] = bolted * tangent_friction + (1.0 - bolted) * tangent_contact
    for k in range(PARTS):
        out_ref[k, 0:6, :] = f_ref[6 * k : 6 * k + 6]
        out_ref[k, 6:12, :] = t_ref[6 * k : 6 * k + 6]


def reply_kernel(p_ref, force_ref, after1, after2, after3, chunk_ref, up_ref, down_ref, self_ref):
    p = p_ref[0]

    def force(tile):
        return force_ref[tile // 3, :, 128 * (tile % 3) : 128 * (tile % 3 + 1)]

    for d in (0, 1, SLABS - 1):
        chunk_ref[(p - d) & (SLABS - 1)] = jnp.zeros((12, 128), f32)
    for d in range(2, SLABS - 1):
        tile, seg = place(d)
        chunk_ref[(p - d) & (SLABS - 1)] = lane_roll(force(tile), -seg)
    for k in range(2):
        self_ref[k] = force(k)
        down_ref[k] = force(2 + k)
        up_ref[k] = force(4 + k)


def partner_kernel(me_ref, idx_ref, force_ref, lin_ref, mass_ref, own_ref, y1_ref, y2_ref, y3_ref, x_ref,
                   out_ref, val_ref, sum_ref):
    for tile in range(17):
        val_ref[tile] = -force_ref[tile // 3, :, 128 * (tile % 3) : 128 * (tile % 3 + 1)]
    val_ref[17] = jnp.zeros((12, 128), f32)
    scatter_rows(val_ref, idx_ref, sum_ref)
    for x in range(4):
        out_ref[:, x] = lin_ref[:, x] + sum_ref[:, 128 * x : 128 * (x + 1)].reshape(12, 32, 128)
    me = me_ref[0]
    for k in range(PARTS):
        acc = x_ref[k // 2] if k % 2 else (own_ref, y1_ref, y2_ref, y3_ref)[k // 2][0]
        block = me ^ k
        x = block >> 1
        rows = pl.ds(pl.multiple_of(16 * (block & 1), 16), 16)
        out_ref[:, x, rows, :] = out_ref[:, x, rows, :] + mass_ref[x, rows, :][None] * acc


def final_kernel(p_ref, idx_ref, chunk_ref, up_ref, down_ref, self_ref, part_ref, res_ref, jac_ref, val_ref, sum_ref):
    p = p_ref[0]

    def listed(d):
        return chunk_ref[(p + d) & (SLABS - 1)]

    tiles = [self_ref[0], self_ref[1], down_ref[0], down_ref[1], up_ref[0], up_ref[1], listed(2), listed(SLABS - 2)]
    tiles += merge_far(listed, 12, 0.0) + [jnp.zeros((12, 128), f32)]
    for k, tile in enumerate(tiles):
        val_ref[k] = tile
    scatter_rows(val_ref, idx_ref, sum_ref)
    for x in range(4):
        out = part_ref[:, x] + sum_ref[:, 128 * x : 128 * (x + 1)].reshape(12, 32, 128)
        res_ref[:, x] = out[0:6]
        jac_ref[:, x] = out[6:12]


def join_kernel(same_ref, other_ref, *out_refs):
    for k, out in enumerate(out_refs):
        out[0] = same_ref[k + 1]
        out[1] = other_ref[k + 1]


def turn_kernel(own_ref, y1_ref, y2_ref, y3_ref, out_ref):
    for k, ref in enumerate((own_ref, y1_ref, y2_ref, y3_ref)):
        out_ref[k] = ref[1]


def time_kernel(me_ref, table_ref, same_ref, other_ref, y1_ref, y2_ref, y3_ref, *outs):
    me = me_ref[0]
    ins = [same_ref.at[0], other_ref.at[0]] + [ref.at[b] for ref in (y1_ref, y2_ref, y3_ref) for b in range(2)]

    def step(g, carry):
        field = g // 3
        row = 6 * field + (g - 3 * field)
        x = [[ins[k][row + 3 * t] for t in range(2)] for k in range(PARTS)]
        for k in range(PARTS):
            for t in range(2):
                acc = None
                for j in range(PARTS):
                    for s in range(2):
                        term = x[j][s] * table_ref[2 * (me ^ k) + t, 2 * (me ^ j) + s]
                        acc = term if acc is None else acc + term
                outs[k // 2][k % 2, row + 3 * t] = acc
        return carry

    lax.fori_loop(0, 6, step, 0)


def lookup(ids, mat_ref, column, count):
    out = jnp.zeros(ids.shape, f32)
    for m in range(count):
        out = jnp.where(ids == m, mat_ref[m, column], out)
    return out


def stiff_kernel(p_ref, mat_ref, ids_ref, disp_ref, dir_ref, forcing_ref, up_ref, down_ref, out_ref, mass_ref, *, materials):
    p = p_ref[0]
    low = jnp.where(p > 0, up_ref[2:28], 0.0).reshape(13, 32, 128)
    high = jnp.where(p < SLABS - 1, down_ref[2:28], 0.0).reshape(13, 32, 128)
    ids = ids_ref[...]
    kx, ky, kz, mass = [lookup(ids, mat_ref, col, materials) for col in range(4)]
    mass_ref[...] = mass
    kx_low = lookup(low[12].astype(i32) - 1, mat_ref, 0, materials)
    kx_high = lookup(high[12].astype(i32) - 1, mat_ref, 0, materials)
    shape = ids.shape
    y = lax.broadcasted_iota(i32, shape, 1)
    z = lax.broadcasted_iota(i32, shape, 2)
    xm = 0.5 * (kx + jnp.concatenate([kx_low[None], kx[:-1]], axis=0))
    xp = 0.5 * (kx + jnp.concatenate([kx[1:], kx_high[None]], axis=0))
    total = xm + xp
    sides = []
    for k, pos, axis in ((ky, y, 1), (kz, z, 2)):
        size = shape[axis]
        for shift, edge in ((1, 0), (size - 1, size - 1)):
            inside = pos != edge
            near = jnp.where(inside, pltpu.roll(k, shift, axis), 0.0)
            side = 0.5 * (k + near)
            total = total + side
            sides.append((jnp.where(inside, side, 0.0), shift, axis))
    for field, ref in enumerate((disp_ref, dir_ref)):
        for c in range(6):
            w = ref[c]
            down = jnp.concatenate([low[6 * field + c][None], w[:-1]], axis=0)
            up = jnp.concatenate([w[1:], high[6 * field + c][None]], axis=0)
            out = total * w - xm * down - xp * up
            for side, shift, axis in sides:
                out = out - side * pltpu.roll(w, shift, axis)
            if field == 0:
                out = out - forcing_ref[c]
            out_ref[6 * field + c] = out


VMEM = 24 * 1024 * 1024


def call(kernel, outs, *args, smem=(0,), away=(), scratch=(), limit=VMEM):
    spaces = [pltpu.SMEM if k in smem else pl.ANY if k in away else pltpu.VMEM for k in range(len(args))]
    specs = [pl.BlockSpec(memory_space=space) for space in spaces]
    return pl.pallas_call(
        kernel,
        out_shape=[jax.ShapeDtypeStruct(s, d) for s, d in outs],
        in_specs=specs,
        out_specs=[pl.BlockSpec(memory_space=pltpu.VMEM) for _ in outs],
        scratch_shapes=list(scratch),
        compiler_params=pltpu.CompilerParams(vmem_limit_bytes=limit),
    )(*args)


def shift(x, by):
    return lax.ppermute(x, "mesh", [(i, (i + by) % SLABS) for i in range(SLABS)])


def exchange(chunk, up, down):
    up, down = shift(up, 1), shift(down, -1)
    return lax.all_to_all(chunk, "mesh", split_axis=0, concat_axis=0, tiled=True), up, down


def swap(x, bit):
    return lax.ppermute(x, "inst", [(i, i ^ bit) for i in range(PARTS)])


def inst_split(x):
    return lax.all_to_all(x, "inst", split_axis=0, concat_axis=0, tiled=True)


def on_device(displacement, direction, forcing, material_ids, materials, joint_owner, joint_local, joint_remote, joint_kind):
    shape = displacement.shape
    fields = (6, 4, 32, 128)
    whole = (12, 4, 32, 128)
    disp = displacement.reshape(fields)
    dire = direction.reshape(fields)
    count = joint_local.shape[0]
    p = lax.axis_index("mesh").astype(i32).reshape(1)
    me = lax.axis_index("inst").astype(i32).reshape(1)
    split = [pltpu.VMEM((384, 512), bf16)] * 2
    index = ((24, 128), i32)
    half = ((4, 12, 16, 128), f32)

    own_idx, chunk, up, down, own, same, other = call(
        list_kernel,
        [index, ((SLABS, 16, 128), f32), ((28, 16, 128), f32), ((28, 16, 128), f32), ((2, 16, 128), f32), half, half],
        p,
        me,
        joint_owner.reshape(1, count),
        joint_local.reshape(1, count),
        joint_remote.reshape(1, count),
        joint_kind.reshape(1, count),
        disp,
        dire,
        material_ids,
        smem=(0, 1),
        away=range(2, 9),
        limit=60 * 1024 * 1024,
        scratch=split
        + [pltpu.VMEM((SIDE, 16, 128), f32)]
        + [pltpu.VMEM((1, count), i32)] * 4
        + [pltpu.VMEM(fields, f32)] * 2
        + [pltpu.VMEM((4, 32, 128), i32), pltpu.SemaphoreType.DMA((7,))],
    )
    chunk, up, down = exchange(chunk, up, down)

    pair = ((2, 12, 16, 128), f32)
    other = swap(other, 1)
    joined = call(join_kernel, [pair] * 3, same, other, smem=())
    turned = [swap(x, 2 * k + 2) for k, x in enumerate(joined)]
    inertia = call(time_kernel, [pair] * 4, me, jnp.asarray(MIXED), same, other, *turned, smem=(0, 1))

    part = ((PARTS, 12, 384), f32)
    far_idx, kind, gap = call(
        gap_kernel,
        [index, ((24, 128), f32), part],
        p, chunk, up, down, own, disp, dire, joined[0],
        away=(7,),
        scratch=split + [pltpu.VMEM((SIDE, 12, 128), f32)],
    )
    force = call(
        force_kernel,
        [part],
        me, kind, jnp.asarray(SPREAD), inst_split(gap), inertia[0],
        away=(4,),
        scratch=[pltpu.VMEM((48, 384), f32)] * 4,
    )[0]
    force = inst_split(force)
    turned = [inertia[0]] + [swap(inertia[k], 2 * k) for k in (1, 2, 3)]
    messages = [((SLABS, 12, 128), f32)] + [((2, 12, 128), f32)] * 3
    chunk, up2, down2, own = call(reply_kernel, messages, p, force, *turned[1:], away=(2, 3, 4))
    chunk, up2, down2 = exchange(chunk, up2, down2)

    lin, mass = call(
        lambda *refs: stiff_kernel(*refs, materials=materials.shape[0]),
        [(whole, f32), ((4, 32, 128), f32)],
        p, materials, material_ids, disp, dire, forcing.reshape(fields), up, down,
        smem=(0, 1),
    )
    other = swap(call(turn_kernel, [half], *turned, smem=())[0], 1)
    adding = [pltpu.VMEM((SIDE, 12, 128), f32), pltpu.VMEM((384, 512), f32)]
    partial = call(partner_kernel, [(whole, f32)], me, far_idx, force, lin, mass, *turned, other, scratch=adding)[0]
    residual, jacobian = call(
        final_kernel, [(fields, f32)] * 2, p, own_idx, chunk, up2, down2, own, partial, scratch=adding
    )
    return residual.reshape(shape), jacobian.reshape(shape)


def solution(mesh):
    field = P("inst", None, "mesh", None, None)
    placed = (field, field, field, P("mesh", None, None), P(), P("mesh", None), P("mesh"), P("mesh"), P("mesh"))
    return jax.shard_map(on_device, mesh=mesh, in_specs=placed, out_specs=(field, field), check_vma=False)
```

```python
import jax
import jax.numpy as jnp
import numpy as np
from jax import lax
from jax.experimental import pallas as pl
from jax.experimental.pallas import tpu as pltpu
from jax.sharding import PartitionSpec as P

frequency = 0.6
damping = 0.3
bolt_stiff = 2.0
slip_force = 1.0
slip_speed = 0.5
stop_stiff = 3.0
clearance = 0.3

SLABS = 32
PARTS = 8
SIDE = 18
SEG = 42
f32 = jnp.float32
bf16 = jnp.bfloat16
i32 = jnp.int32


def tables(count):
    offsets = np.arange(count)[:, None] - np.arange(count)[None, :]
    tangent = np.where(offsets == 0, 1.0, np.tan(np.pi * offsets / count))
    first = np.where(offsets == 0, 0.0, 0.5 * np.where(offsets % 2 == 0, 1.0, -1.0) / tangent) * frequency
    return first, first @ first


FIRST, SECOND = tables(2 * PARTS)
MIXED = (SECOND + damping * FIRST).astype(np.float32)
SPREAD = np.kron(FIRST, np.eye(3)).astype(np.float32)


def far_place(offset):
    return 8 + (offset - 3) // 3, SEG * ((offset - 3) % 3)


def place(offset):
    return {2: (6, 0), 30: (7, 0)}.get(offset) or far_place(offset)


def lane_roll(x, shift):
    shift = shift % 128
    return pltpu.roll(x, shift, x.ndim - 1) if shift else x


def lanes(rows):
    return lax.broadcasted_iota(i32, (rows, 128), 1)


def merge_far(read, rows, fill):
    lane = lanes(rows)
    tiles = []
    for k in range(9):
        parts = [lane_roll(read(3 + 3 * k + s), SEG * s) for s in range(3)]
        tile = jnp.where(lane < SEG, parts[0], jnp.where(lane < 2 * SEG, parts[1], parts[2]))
        tiles.append(jnp.where(lane < 3 * SEG, tile, fill))
    return tiles


def slot_tables(p, owner_ref, local_ref, remote_ref, kind_ref):
    count = owner_ref.shape[1]
    offset = (owner_ref[...] - p) & (SLABS - 1)
    hit = (lax.broadcasted_iota(i32, (SLABS, count), 0) == offset).astype(f32)
    hit16 = hit.astype(bf16)
    before = (lax.broadcasted_iota(i32, (128, 128), 0) < lax.broadcasted_iota(i32, (128, 128), 1)).astype(f32).astype(bf16)
    row = lax.broadcasted_iota(i32, (SLABS, 1), 0)
    far = row - 3
    group = (far * 171) >> 9
    start = 1024 + group * 128 + (far - 3 * group) * SEG
    for value, at in ((0, 0), (1, 256), (SLABS - 1, 512), (2, 768), (SLABS - 2, 896)):
        start = jnp.where(row == value, at, start)
    run = start.astype(f32)
    places = []
    for b in range(count // 128):
        block = hit[:, 128 * b : 128 * (b + 1)]
        earlier = jnp.dot(hit16[:, 128 * b : 128 * (b + 1)], before, preferred_element_type=f32)
        places.append(jnp.sum(block * (earlier + run), axis=0, keepdims=True))
        run = run + jnp.sum(block, axis=1, keepdims=True)
    slot = jnp.concatenate(places, axis=1).astype(i32)
    in_tile = lax.broadcasted_iota(i32, (24, count), 0) == (slot >> 7)
    in_lane = (lax.broadcasted_iota(i32, (128, count), 0) == (slot & 127)).astype(f32).astype(bf16)
    local = local_ref[...]
    remote = remote_ref[...]
    values = (local >> 7, local & 127, remote >> 7, remote & 127, kind_ref[...], jnp.ones_like(local))
    spread = jnp.concatenate([jnp.where(in_tile, v.astype(f32), 0.0) for v in values], axis=0).astype(bf16)
    got = lax.dot_general(spread, in_lane, (((1,), (1,)), ((), ())), preferred_element_type=f32)
    got = [got[24 * k : 24 * (k + 1)] for k in range(6)]
    empty = got[5] - 1.0
    return got[0] * 128.0 + got[1] + empty, got[2] * 128.0 + got[3] + empty, got[4]


def picks(idx_ref, k):
    idx = jnp.concatenate([idx_ref[pl.ds(2 * k, 1), :], idx_ref[pl.ds(2 * k + 1, 1), :]], axis=1)
    code = ((idx >> 12) << 7) | (idx & 127)
    pick = (lax.broadcasted_iota(i32, (512, 256), 0) == code).astype(f32).astype(bf16)
    return pick, lax.broadcasted_iota(i32, (32, 256), 0) == ((idx >> 7) & 31)


def split_fields(disp_ref, dir_ref, parts_ref):
    for field, ref in enumerate((disp_ref, dir_ref)):
        for x in range(4):
            value = ref[:, x].reshape(6 * 32, 128)
            hi = value.astype(bf16)
            cols = slice(128 * x, 128 * (x + 1))
            parts_ref[192 * field : 192 * (field + 1), cols] = hi
            parts_ref[384 + 192 * field : 384 + 192 * (field + 1), cols] = (value - hi.astype(f32)).astype(bf16)


def split_kernel(disp_ref, dir_ref, parts_ref):
    split_fields(disp_ref, dir_ref, parts_ref)


def gather_rows(parts_ref, idx_ref, here_ref):
    def step(k, carry):
        pick, in_y = picks(idx_ref, k)
        rows = jnp.dot(parts_ref[...], pick, preferred_element_type=f32)
        rows = (rows[:384] + rows[384:]).reshape(12, 32, 256)
        got = jnp.sum(jnp.where(in_y[None], rows, 0.0), axis=1)
        here_ref[2 * k, 0:12, :] = got[:, :128]
        here_ref[2 * k + 1, 0:12, :] = got[:, 128:]
        return carry

    lax.fori_loop(0, SIDE // 2, step, 0, unroll=3)


def scatter_rows(val_ref, idx_ref, sum_ref):
    sum_ref[...] = jnp.zeros(sum_ref.shape, f32)
    dims = (((1,), (1,)), ((), ()))

    def step(k, carry):
        pick, in_y = picks(idx_ref, k)
        value = jnp.concatenate([val_ref[2 * k], val_ref[2 * k + 1]], axis=1)
        hi = value.astype(bf16).astype(f32)
        spread = [
            jnp.where(in_y[None], part[:, None, :], 0.0).reshape(384, 256).astype(bf16) for part in (hi, value - hi)
        ]
        got = lax.dot_general(spread[0], pick, dims, preferred_element_type=f32)
        got = got + lax.dot_general(spread[1], pick, dims, preferred_element_type=f32)
        sum_ref[...] = sum_ref[...] + got
        return carry

    lax.fori_loop(0, SIDE // 2, step, 0, unroll=3)


def list_kernel(p_ref, me_ref, owner_hbm, local_hbm, remote_hbm, kind_hbm, disp_hbm, dir_hbm, ids_hbm,
                idx_ref, chunk_ref, up_hbm, down_hbm, self_ref, same_hbm, other_hbm,
                parts_ref, rows_ref, owner_ref, local_ref, remote_ref, kind_ref, disp_ref, dir_ref, ids_ref, near_ref,
                sems, more_sems):
    p = p_ref[0]
    pairs = ((owner_hbm, owner_ref), (local_hbm, local_ref), (remote_hbm, remote_ref), (kind_hbm, kind_ref),
             (disp_hbm, disp_ref), (dir_hbm, dir_ref), (ids_hbm, ids_ref))
    copies = [pltpu.make_async_copy(a, b, sems.at[k]) for k, (a, b) in enumerate(pairs)]
    for copy in copies:
        copy.start()
    moves = []
    for field, hbm in enumerate((disp_hbm, dir_hbm)):
        part = pl.ds(6 * field, 6)
        for k in range(PARTS):
            block = me_ref[0] ^ k
            rows = pl.ds(pl.multiple_of(16 * (block & 1), 16), 16)
            moves.append((hbm.at[:, block >> 1, rows, :], (same_hbm, other_hbm)[k % 2].at[k // 2, part]))
        moves.append((hbm.at[:, 3], up_hbm.at[pl.ds(1 + 6 * field, 6)]))
        moves.append((hbm.at[:, 0], down_hbm.at[pl.ds(1 + 6 * field, 6)]))
    moves = [pltpu.make_async_copy(a, b, more_sems.at[k]) for k, (a, b) in enumerate(moves)]
    for move in moves:
        move.start()
    for copy in copies[:4]:
        copy.wait()
    mine, theirs, kind = slot_tables(p, owner_ref, local_ref, remote_ref, kind_ref)
    idx_ref[...] = mine.astype(i32)
    for tile in range(SIDE):
        rows_ref[tile, 12:13, :] = theirs[tile : tile + 1]
        rows_ref[tile, 13:14, :] = kind[tile : tile + 1]
        rows_ref[tile, 14:16, :] = jnp.zeros((2, 128), f32)
    for copy in copies[4:]:
        copy.wait()
    split_fields(disp_ref, dir_ref, parts_ref)
    near_ref[2] = (ids_ref[3] + 1).astype(f32)
    near_ref[3] = (ids_ref[0] + 1).astype(f32)
    gather_rows(parts_ref, idx_ref, rows_ref)
    for k in range(2):
        near_ref[k] = rows_ref[2 + 2 * k : 4 + 2 * k].reshape(32, 128)
    ends = ((near_ref.at[0], up_hbm.at[0]), (near_ref.at[1], down_hbm.at[0]),
            (near_ref.at[2], up_hbm.at[13]), (near_ref.at[3], down_hbm.at[13]))
    ends = [pltpu.make_async_copy(a, b, sems.at[7 + k]) for k, (a, b) in enumerate(ends)]
    for end in ends:
        end.start()
    for d in (0, 1, SLABS - 1):
        chunk_ref[(p + d) & (SLABS - 1)] = jnp.zeros((16, 128), f32)
    for d in range(2, SLABS - 1):
        tile, seg = place(d)
        chunk_ref[(p + d) & (SLABS - 1)] = lane_roll(rows_ref[tile], -seg)
    self_ref[...] = rows_ref[0:2]
    for move in moves + ends:
        move.wait()


def gap_kernel(p_ref, chunk_ref, up_ref, down_ref, self_ref, parts_ref, after_ref,
               idx_ref, kind_ref, gap_ref, here_ref):
    p = p_ref[0]

    def asked(d):
        return chunk_ref[(p - d) & (SLABS - 1)]

    near = [ref[0, 16 * k : 16 * (k + 1), :] for ref in (up_ref, down_ref) for k in range(2)]
    tiles = [self_ref[0], self_ref[1]] + near + [asked(2), asked(SLABS - 2)]
    tiles += merge_far(asked, 16, 0.0)
    beyond = lanes(1) >= 3 * SEG
    rows = [t[12:13] for t in tiles[:8]] + [jnp.where(beyond, -1.0, t[12:13]) for t in tiles[8:]]
    idx_ref[...] = jnp.concatenate(rows + [jnp.full((7, 128), -1.0, f32)], axis=0).astype(i32)
    kind_ref[...] = jnp.concatenate([t[13:14] for t in tiles] + [jnp.zeros((7, 128), f32)], axis=0)
    gather_rows(parts_ref, idx_ref, here_ref)
    for tile in range(24):
        gap = tiles[tile][0:12] - here_ref[tile] if tile < 17 else jnp.zeros((12, 128), f32)
        gap_ref[tile // 3, :, 128 * (tile % 3) : 128 * (tile % 3 + 1)] = gap


def force_kernel(me_ref, kind_ref, spread_ref, gap_ref, after_ref, out_ref, r_ref, d_ref, f_ref, t_ref):
    me = me_ref[0]
    for k in range(PARTS):
        r_ref[6 * k : 6 * k + 6] = gap_ref[k, 0:6, :]
        d_ref[6 * k : 6 * k + 6] = gap_ref[k, 6:12, :]
    r = r_ref[...]
    dr = d_ref[...]
    w = jnp.dot(spread_ref[...], r, precision=lax.Precision.HIGHEST, preferred_element_type=f32)
    dw = jnp.dot(spread_ref[...], dr, precision=lax.Precision.HIGHEST, preferred_element_type=f32)
    bolted = jnp.concatenate([kind_ref[pl.ds(3 * me + k, 1), :] for k in range(3)], axis=1)
    slide = jnp.tanh(w / slip_speed)
    opened = jnp.tanh(r / clearance)
    friction = bolt_stiff * r + slip_force * slide
    contact = stop_stiff * (r - clearance * opened)
    f_ref[...] = bolted * friction + (1.0 - bolted) * contact
    tangent_friction = bolt_stiff * dr + slip_force * (1.0 - slide * slide) / slip_speed * dw
    tangent_contact = stop_stiff * opened * opened * dr
    t_ref[...] = bolted * tangent_friction + (1.0 - bolted) * tangent_contact
    for k in range(PARTS):
        out_ref[k, 0:6, :] = f_ref[6 * k : 6 * k + 6]
        out_ref[k, 6:12, :] = t_ref[6 * k : 6 * k + 6]


def reply_kernel(p_ref, force_ref, after1, after2, after3, chunk_ref, up_ref, down_ref, self_ref):
    p = p_ref[0]

    def force(tile):
        return force_ref[tile // 3, :, 128 * (tile % 3) : 128 * (tile % 3 + 1)]

    for d in (0, 1, SLABS - 1):
        chunk_ref[(p - d) & (SLABS - 1)] = jnp.zeros((12, 128), f32)
    for d in range(2, SLABS - 1):
        tile, seg = place(d)
        chunk_ref[(p - d) & (SLABS - 1)] = lane_roll(force(tile), -seg)
    for k in range(2):
        self_ref[k] = force(k)
        down_ref[k] = force(2 + k)
        up_ref[k] = force(4 + k)


def partner_kernel(me_ref, idx_ref, force_ref, lin_ref, mass_ref, own_ref, y1_ref, y2_ref, y3_ref, x_ref,
                   out_ref, val_ref, sum_ref):
    for tile in range(17):
        val_ref[tile] = -force_ref[tile // 3, :, 128 * (tile % 3) : 128 * (tile % 3 + 1)]
    val_ref[17] = jnp.zeros((12, 128), f32)
    scatter_rows(val_ref, idx_ref, sum_ref)
    for x in range(4):
        out_ref[:, x] = lin_ref[:, x] + sum_ref[:, 128 * x : 128 * (x + 1)].reshape(12, 32, 128)
    me = me_ref[0]
    for k in range(PARTS):
        acc = x_ref[k // 2] if k % 2 else (own_ref, y1_ref, y2_ref, y3_ref)[k // 2][0]
        block = me ^ k
        x = block >> 1
        rows = pl.ds(pl.multiple_of(16 * (block & 1), 16), 16)
        out_ref[:, x, rows, :] = out_ref[:, x, rows, :] + mass_ref[x, rows, :][None] * acc


def final_kernel(p_ref, idx_ref, chunk_ref, up_ref, down_ref, self_ref, part_ref, res_ref, jac_ref, val_ref, sum_ref):
    p = p_ref[0]

    def listed(d):
        return chunk_ref[(p + d) & (SLABS - 1)]

    tiles = [self_ref[0], self_ref[1], down_ref[0], down_ref[1], up_ref[0], up_ref[1], listed(2), listed(SLABS - 2)]
    tiles += merge_far(listed, 12, 0.0) + [jnp.zeros((12, 128), f32)]
    for k, tile in enumerate(tiles):
        val_ref[k] = tile
    scatter_rows(val_ref, idx_ref, sum_ref)
    for x in range(4):
        out = part_ref[:, x] + sum_ref[:, 128 * x : 128 * (x + 1)].reshape(12, 32, 128)
        res_ref[:, x] = out[0:6]
        jac_ref[:, x] = out[6:12]


def join_kernel(same_ref, other_ref, *out_refs):
    for k, out in enumerate(out_refs):
        out[0] = same_ref[k + 1]
        out[1] = other_ref[k + 1]


def turn_kernel(own_ref, y1_ref, y2_ref, y3_ref, out_ref):
    for k, ref in enumerate((own_ref, y1_ref, y2_ref, y3_ref)):
        out_ref[k] = ref[1]


def time_kernel(me_ref, same_ref, other_ref, y1_ref, y2_ref, y3_ref, *refs):
    outs, in_ref, out_ref = refs[:4], refs[4], refs[5]
    me = me_ref[0]
    in_ref[0] = same_ref[0]
    in_ref[1] = other_ref[0]
    for k, ref in enumerate((y1_ref, y2_ref, y3_ref)):
        in_ref[2 * k + 2 : 2 * k + 4] = ref[...]
    at = [me ^ ((me + k) & (PARTS - 1)) for k in range(PARTS)]
    count = 2 * PARTS

    def step(g, carry):
        field = g // 3
        row = 6 * field + (g - 3 * field)
        x = [in_ref[at[t // 2], row + 3 * (t % 2)] for t in range(count)]
        for t in range(count):
            acc = x[0] * float(MIXED[t, 0])
            for s in range(1, count):
                acc = acc + x[s] * float(MIXED[(t - s) % count, 0])
            out_ref[at[t // 2], row + 3 * (t % 2)] = acc
        return carry

    lax.fori_loop(0, 6, step, 0)
    for k, out in enumerate(outs):
        out[...] = out_ref[2 * k : 2 * k + 2]


def lookup(ids, mat_ref, column, count):
    out = jnp.zeros(ids.shape, f32)
    for m in range(count):
        out = jnp.where(ids == m, mat_ref[m, column], out)
    return out


def stiff_kernel(p_ref, mat_ref, ids_ref, disp_ref, dir_ref, forcing_ref, up_ref, down_ref, out_ref, mass_ref, *, materials):
    p = p_ref[0]
    low = jnp.where(p > 0, up_ref[1:14], 0.0)
    high = jnp.where(p < SLABS - 1, down_ref[1:14], 0.0)
    ids = ids_ref[...]
    kx, ky, kz, mass = [lookup(ids, mat_ref, col, materials) for col in range(4)]
    mass_ref[...] = mass
    kx_low = lookup(low[12].astype(i32) - 1, mat_ref, 0, materials)
    kx_high = lookup(high[12].astype(i32) - 1, mat_ref, 0, materials)
    shape = ids.shape
    y = lax.broadcasted_iota(i32, shape, 1)
    z = lax.broadcasted_iota(i32, shape, 2)
    xm = 0.5 * (kx + jnp.concatenate([kx_low[None], kx[:-1]], axis=0))
    xp = 0.5 * (kx + jnp.concatenate([kx[1:], kx_high[None]], axis=0))
    total = xm + xp
    sides = []
    for k, pos, axis in ((ky, y, 1), (kz, z, 2)):
        size = shape[axis]
        for shift, edge in ((1, 0), (size - 1, size - 1)):
            inside = pos != edge
            near = jnp.where(inside, pltpu.roll(k, shift, axis), 0.0)
            side = 0.5 * (k + near)
            total = total + side
            sides.append((jnp.where(inside, side, 0.0), shift, axis))
    for field, ref in enumerate((disp_ref, dir_ref)):
        for c in range(6):
            w = ref[c]
            down = jnp.concatenate([low[6 * field + c][None], w[:-1]], axis=0)
            up = jnp.concatenate([w[1:], high[6 * field + c][None]], axis=0)
            out = total * w - xm * down - xp * up
            for side, shift, axis in sides:
                out = out - side * pltpu.roll(w, shift, axis)
            if field == 0:
                out = out - forcing_ref[c]
            out_ref[6 * field + c] = out


VMEM = 16 * 1024 * 1024


def call(kernel, outs, *args, smem=(0,), away=(), scratch=(), kept=(), limit=VMEM):
    spaces = [pltpu.SMEM if k in smem else pl.ANY if k in away else pltpu.VMEM for k in range(len(args))]
    specs = [pl.BlockSpec(memory_space=space) for space in spaces]
    return pl.pallas_call(
        kernel,
        out_shape=[jax.ShapeDtypeStruct(s, d) for s, d in outs],
        in_specs=specs,
        out_specs=[pl.BlockSpec(memory_space=pl.ANY if k in kept else pltpu.VMEM) for k in range(len(outs))],
        scratch_shapes=list(scratch),
        compiler_params=pltpu.CompilerParams(vmem_limit_bytes=limit),
    )(*args)


def shift(x, by):
    return lax.ppermute(x, "mesh", [(i, (i + by) % SLABS) for i in range(SLABS)])


def exchange(chunk, up, down):
    up, down = shift(up, 1), shift(down, -1)
    return lax.all_to_all(chunk, "mesh", split_axis=0, concat_axis=0, tiled=True), up, down


def swap(x, bit):
    return lax.ppermute(x, "inst", [(i, i ^ bit) for i in range(PARTS)])


def inst_split(x):
    return lax.all_to_all(x, "inst", split_axis=0, concat_axis=0, tiled=True)


def on_device(displacement, direction, forcing, material_ids, materials, joint_owner, joint_local, joint_remote, joint_kind):
    shape = displacement.shape
    fields = (6, 4, 32, 128)
    whole = (12, 4, 32, 128)
    disp = displacement.reshape(fields)
    dire = direction.reshape(fields)
    count = joint_local.shape[0]
    p = lax.axis_index("mesh").astype(i32).reshape(1)
    me = lax.axis_index("inst").astype(i32).reshape(1)
    parts = (768, 512)
    index = ((24, 128), i32)
    half = ((4, 12, 16, 128), f32)
    near = ((14, 32, 128), f32)

    own_idx, chunk, up, down, own, same, other = call(
        list_kernel,
        [index, ((SLABS, 16, 128), f32), near, near, ((2, 16, 128), f32), half, half],
        p,
        me,
        joint_owner.reshape(1, count),
        joint_local.reshape(1, count),
        joint_remote.reshape(1, count),
        joint_kind.reshape(1, count),
        disp,
        dire,
        material_ids,
        smem=(0, 1),
        away=range(2, 9),
        limit=60 * 1024 * 1024,
        kept=(2, 3, 5, 6),
        scratch=[pltpu.VMEM(parts, bf16), pltpu.VMEM((SIDE, 16, 128), f32)]
        + [pltpu.VMEM((1, count), i32)] * 4
        + [pltpu.VMEM(fields, f32)] * 2
        + [pltpu.VMEM((4, 32, 128), i32), pltpu.VMEM((4, 32, 128), f32)]
        + [pltpu.SemaphoreType.DMA((11,)), pltpu.SemaphoreType.DMA((20,))],
    )
    chunk, up, down = exchange(chunk, up, down)

    pair = ((2, 12, 16, 128), f32)
    other = swap(other, 1)
    joined = call(join_kernel, [pair] * 3, same, other, smem=())
    turned = [swap(x, 2 * k + 2) for k, x in enumerate(joined)]
    blocks = [pltpu.VMEM((PARTS, 12, 16, 128), f32)] * 2
    inertia = call(time_kernel, [pair] * 4, me, same, other, *turned, scratch=blocks)

    part = ((PARTS, 12, 384), f32)
    fields_parts = call(split_kernel, [(parts, bf16)], disp, dire, smem=())[0]
    far_idx, kind, gap = call(
        gap_kernel,
        [index, ((24, 128), f32), part],
        p, chunk, up, down, own, fields_parts, joined[0],
        away=(6,),
        scratch=[pltpu.VMEM((SIDE, 12, 128), f32)],
    )
    force = call(
        force_kernel,
        [part],
        me, kind, jnp.asarray(SPREAD), inst_split(gap), inertia[0],
        away=(4,),
        scratch=[pltpu.VMEM((48, 384), f32)] * 4,
    )[0]
    force = inst_split(force)
    turned = [inertia[0]] + [swap(inertia[k], 2 * k) for k in (1, 2, 3)]
    messages = [((SLABS, 12, 128), f32)] + [((2, 12, 128), f32)] * 3
    chunk, up2, down2, own = call(reply_kernel, messages, p, force, *turned[1:], away=(2, 3, 4))
    chunk, up2, down2 = exchange(chunk, up2, down2)

    lin, mass = call(
        lambda *refs: stiff_kernel(*refs, materials=materials.shape[0]),
        [(whole, f32), ((4, 32, 128), f32)],
        p, materials, material_ids, disp, dire, forcing.reshape(fields), up, down,
        smem=(0, 1),
    )
    other = swap(call(turn_kernel, [half], *turned, smem=())[0], 1)
    adding = [pltpu.VMEM((SIDE, 12, 128), f32), pltpu.VMEM((384, 512), f32)]
    partial = call(partner_kernel, [(whole, f32)], me, far_idx, force, lin, mass, *turned, other, scratch=adding)[0]
    residual, jacobian = call(
        final_kernel, [(fields, f32)] * 2, p, own_idx, chunk, up2, down2, own, partial, scratch=adding
    )
    return residual.reshape(shape), jacobian.reshape(shape)


def solution(mesh):
    field = P("inst", None, "mesh", None, None)
    placed = (field, field, field, P("mesh", None, None), P(), P("mesh", None), P("mesh"), P("mesh"), P("mesh"))
    return jax.shard_map(on_device, mesh=mesh, in_specs=placed, out_specs=(field, field), check_vma=False)
```

```python
import jax
import jax.numpy as jnp
import numpy as np
from jax import lax
from jax.experimental import pallas as pl
from jax.experimental.pallas import tpu as pltpu
from jax.sharding import PartitionSpec as P

frequency = 0.6
damping = 0.3
bolt_stiff = 2.0
slip_force = 1.0
slip_speed = 0.5
stop_stiff = 3.0
clearance = 0.3

SLABS = 32
PARTS = 8
SIDE = 18
SEG = 42
f32 = jnp.float32
bf16 = jnp.bfloat16
i32 = jnp.int32


def tables(count):
    offsets = np.arange(count)[:, None] - np.arange(count)[None, :]
    tangent = np.where(offsets == 0, 1.0, np.tan(np.pi * offsets / count))
    first = np.where(offsets == 0, 0.0, 0.5 * np.where(offsets % 2 == 0, 1.0, -1.0) / tangent) * frequency
    return first, first @ first


FIRST, SECOND = tables(2 * PARTS)
MIXED = (SECOND + damping * FIRST).astype(np.float32)
SPREAD = np.kron(FIRST, np.eye(3)).astype(np.float32)


def far_place(offset):
    return 8 + (offset - 3) // 3, SEG * ((offset - 3) % 3)


def place(offset):
    return {2: (6, 0), 30: (7, 0)}.get(offset) or far_place(offset)


def lane_roll(x, shift):
    shift = shift % 128
    return pltpu.roll(x, shift, x.ndim - 1) if shift else x


def lanes(rows):
    return lax.broadcasted_iota(i32, (rows, 128), 1)


def merge_far(read, rows, fill):
    lane = lanes(rows)
    tiles = []
    for k in range(9):
        parts = [lane_roll(read(3 + 3 * k + s), SEG * s) for s in range(3)]
        tile = jnp.where(lane < SEG, parts[0], jnp.where(lane < 2 * SEG, parts[1], parts[2]))
        tiles.append(jnp.where(lane < 3 * SEG, tile, fill))
    return tiles


def slot_tables(p, owner_ref, local_ref, remote_ref, kind_ref):
    count = owner_ref.shape[1]
    offset = (owner_ref[...] - p) & (SLABS - 1)
    hit = (lax.broadcasted_iota(i32, (SLABS, count), 0) == offset).astype(f32)
    hit16 = hit.astype(bf16)
    before = (lax.broadcasted_iota(i32, (128, 128), 0) < lax.broadcasted_iota(i32, (128, 128), 1)).astype(f32).astype(bf16)
    row = lax.broadcasted_iota(i32, (SLABS, 1), 0)
    far = row - 3
    group = (far * 171) >> 9
    start = 1024 + group * 128 + (far - 3 * group) * SEG
    for value, at in ((0, 0), (1, 256), (SLABS - 1, 512), (2, 768), (SLABS - 2, 896)):
        start = jnp.where(row == value, at, start)
    run = start.astype(f32)
    places = []
    for b in range(count // 128):
        block = hit[:, 128 * b : 128 * (b + 1)]
        earlier = jnp.dot(hit16[:, 128 * b : 128 * (b + 1)], before, preferred_element_type=f32)
        places.append(jnp.sum(block * (earlier + run), axis=0, keepdims=True))
        run = run + jnp.sum(block, axis=1, keepdims=True)
    slot = jnp.concatenate(places, axis=1).astype(i32)
    in_tile = lax.broadcasted_iota(i32, (24, count), 0) == (slot >> 7)
    in_lane = (lax.broadcasted_iota(i32, (128, count), 0) == (slot & 127)).astype(f32).astype(bf16)
    local = local_ref[...]
    remote = remote_ref[...]
    values = (local >> 7, local & 127, remote >> 7, remote & 127, kind_ref[...], jnp.ones_like(local))
    spread = jnp.concatenate([jnp.where(in_tile, v.astype(f32), 0.0) for v in values], axis=0).astype(bf16)
    got = lax.dot_general(spread, in_lane, (((1,), (1,)), ((), ())), preferred_element_type=f32)
    got = [got[24 * k : 24 * (k + 1)] for k in range(6)]
    empty = got[5] - 1.0
    return got[0] * 128.0 + got[1] + empty, got[2] * 128.0 + got[3] + empty, got[4]


def picks(idx_ref, k):
    idx = jnp.concatenate([idx_ref[pl.ds(2 * k, 1), :], idx_ref[pl.ds(2 * k + 1, 1), :]], axis=1)
    code = ((idx >> 12) << 7) | (idx & 127)
    pick = (lax.broadcasted_iota(i32, (512, 256), 0) == code).astype(f32).astype(bf16)
    return pick, lax.broadcasted_iota(i32, (32, 256), 0) == ((idx >> 7) & 31)


def split_fields(disp_ref, dir_ref, parts_ref):
    for field, ref in enumerate((disp_ref, dir_ref)):
        for x in range(4):
            value = ref[:, x].reshape(6 * 32, 128)
            hi = value.astype(bf16)
            cols = slice(128 * x, 128 * (x + 1))
            parts_ref[192 * field : 192 * (field + 1), cols] = hi
            parts_ref[384 + 192 * field : 384 + 192 * (field + 1), cols] = (value - hi.astype(f32)).astype(bf16)


def split_kernel(disp_ref, dir_ref, parts_ref):
    split_fields(disp_ref, dir_ref, parts_ref)


def gather_rows(parts_ref, idx_ref, here_ref):
    def step(k, carry):
        pick, in_y = picks(idx_ref, k)
        rows = jnp.dot(parts_ref[...], pick, preferred_element_type=f32)
        rows = (rows[:384] + rows[384:]).reshape(12, 32, 256)
        got = jnp.sum(jnp.where(in_y[None], rows, 0.0), axis=1)
        here_ref[2 * k, 0:12, :] = got[:, :128]
        here_ref[2 * k + 1, 0:12, :] = got[:, 128:]
        return carry

    lax.fori_loop(0, SIDE // 2, step, 0, unroll=3)


def scatter_rows(val_ref, idx_ref, sum_ref):
    sum_ref[...] = jnp.zeros(sum_ref.shape, f32)
    dims = (((1,), (1,)), ((), ()))

    def step(k, carry):
        pick, in_y = picks(idx_ref, k)
        value = jnp.concatenate([val_ref[2 * k], val_ref[2 * k + 1]], axis=1)
        hi = value.astype(bf16).astype(f32)
        spread = [
            jnp.where(in_y[None], part[:, None, :], 0.0).reshape(384, 256).astype(bf16) for part in (hi, value - hi)
        ]
        got = lax.dot_general(spread[0], pick, dims, preferred_element_type=f32)
        got = got + lax.dot_general(spread[1], pick, dims, preferred_element_type=f32)
        sum_ref[...] = sum_ref[...] + got
        return carry

    lax.fori_loop(0, SIDE // 2, step, 0, unroll=3)


def list_kernel(p_ref, me_ref, owner_hbm, local_hbm, remote_hbm, kind_hbm, disp_hbm, dir_hbm, ids_hbm,
                idx_ref, chunk_ref, up_hbm, down_hbm, self_ref, same_hbm, other_hbm,
                parts_ref, rows_ref, owner_ref, local_ref, remote_ref, kind_ref, disp_ref, dir_ref, ids_ref, near_ref,
                sems, more_sems):
    p = p_ref[0]
    pairs = ((owner_hbm, owner_ref), (local_hbm, local_ref), (remote_hbm, remote_ref), (kind_hbm, kind_ref),
             (disp_hbm, disp_ref), (dir_hbm, dir_ref), (ids_hbm, ids_ref))
    copies = [pltpu.make_async_copy(a, b, sems.at[k]) for k, (a, b) in enumerate(pairs)]
    for copy in copies:
        copy.start()
    for copy in copies[:4]:
        copy.wait()
    mine, theirs, kind = slot_tables(p, owner_ref, local_ref, remote_ref, kind_ref)
    idx_ref[...] = mine.astype(i32)
    for tile in range(SIDE):
        rows_ref[tile, 12:13, :] = theirs[tile : tile + 1]
        rows_ref[tile, 13:14, :] = kind[tile : tile + 1]
        rows_ref[tile, 14:16, :] = jnp.zeros((2, 128), f32)
    for copy in copies[4:]:
        copy.wait()
    moves = []
    for field, ref in enumerate((disp_ref, dir_ref)):
        part = pl.ds(6 * field, 6)
        for k in range(PARTS):
            block = me_ref[0] ^ k
            rows = pl.ds(pl.multiple_of(16 * (block & 1), 16), 16)
            moves.append((ref.at[:, block >> 1, rows, :], (same_hbm, other_hbm)[k % 2].at[k // 2, part]))
        moves.append((ref.at[:, 3], up_hbm.at[pl.ds(1 + 6 * field, 6)]))
        moves.append((ref.at[:, 0], down_hbm.at[pl.ds(1 + 6 * field, 6)]))
    moves = [pltpu.make_async_copy(a, b, more_sems.at[k]) for k, (a, b) in enumerate(moves)]
    for move in moves:
        move.start()
    split_fields(disp_ref, dir_ref, parts_ref)
    near_ref[2] = (ids_ref[3] + 1).astype(f32)
    near_ref[3] = (ids_ref[0] + 1).astype(f32)
    gather_rows(parts_ref, idx_ref, rows_ref)
    for k in range(2):
        near_ref[k] = rows_ref[2 + 2 * k : 4 + 2 * k].reshape(32, 128)
    ends = ((near_ref.at[0], up_hbm.at[0]), (near_ref.at[1], down_hbm.at[0]),
            (near_ref.at[2], up_hbm.at[13]), (near_ref.at[3], down_hbm.at[13]))
    ends = [pltpu.make_async_copy(a, b, sems.at[7 + k]) for k, (a, b) in enumerate(ends)]
    for end in ends:
        end.start()
    for d in (0, 1, SLABS - 1):
        chunk_ref[(p + d) & (SLABS - 1)] = jnp.zeros((16, 128), f32)
    for d in range(2, SLABS - 1):
        tile, seg = place(d)
        chunk_ref[(p + d) & (SLABS - 1)] = lane_roll(rows_ref[tile], -seg)
    self_ref[...] = rows_ref[0:2]
    for move in moves + ends:
        move.wait()


def gap_kernel(p_ref, chunk_ref, up_ref, down_ref, self_ref, parts_ref, after_ref,
               idx_ref, kind_ref, gap_ref, here_ref):
    p = p_ref[0]

    def asked(d):
        return chunk_ref[(p - d) & (SLABS - 1)]

    near = [ref[0, 16 * k : 16 * (k + 1), :] for ref in (up_ref, down_ref) for k in range(2)]
    tiles = [self_ref[0], self_ref[1]] + near + [asked(2), asked(SLABS - 2)]
    tiles += merge_far(asked, 16, 0.0)
    beyond = lanes(1) >= 3 * SEG
    rows = [t[12:13] for t in tiles[:8]] + [jnp.where(beyond, -1.0, t[12:13]) for t in tiles[8:]]
    idx_ref[...] = jnp.concatenate(rows + [jnp.full((7, 128), -1.0, f32)], axis=0).astype(i32)
    kind_ref[...] = jnp.concatenate([t[13:14] for t in tiles] + [jnp.zeros((7, 128), f32)], axis=0)
    gather_rows(parts_ref, idx_ref, here_ref)
    for tile in range(24):
        gap = tiles[tile][0:12] - here_ref[tile] if tile < 17 else jnp.zeros((12, 128), f32)
        gap_ref[tile // 3, :, 128 * (tile % 3) : 128 * (tile % 3 + 1)] = gap


def force_kernel(me_ref, kind_ref, spread_ref, gap_ref, after_ref, out_ref, r_ref, d_ref, f_ref, t_ref):
    me = me_ref[0]
    for k in range(PARTS):
        r_ref[6 * k : 6 * k + 6] = gap_ref[k, 0:6, :]
        d_ref[6 * k : 6 * k + 6] = gap_ref[k, 6:12, :]
    r = r_ref[...]
    dr = d_ref[...]
    w = jnp.dot(spread_ref[...], r, precision=lax.Precision.HIGHEST, preferred_element_type=f32)
    dw = jnp.dot(spread_ref[...], dr, precision=lax.Precision.HIGHEST, preferred_element_type=f32)
    bolted = jnp.concatenate([kind_ref[pl.ds(3 * me + k, 1), :] for k in range(3)], axis=1)
    slide = jnp.tanh(w / slip_speed)
    opened = jnp.tanh(r / clearance)
    friction = bolt_stiff * r + slip_force * slide
    contact = stop_stiff * (r - clearance * opened)
    f_ref[...] = bolted * friction + (1.0 - bolted) * contact
    tangent_friction = bolt_stiff * dr + slip_force * (1.0 - slide * slide) / slip_speed * dw
    tangent_contact = stop_stiff * opened * opened * dr
    t_ref[...] = bolted * tangent_friction + (1.0 - bolted) * tangent_contact
    for k in range(PARTS):
        out_ref[k, 0:6, :] = f_ref[6 * k : 6 * k + 6]
        out_ref[k, 6:12, :] = t_ref[6 * k : 6 * k + 6]


def reply_kernel(p_ref, force_ref, chunk_ref, up_ref, down_ref, self_ref):
    p = p_ref[0]

    def force(tile):
        return force_ref[tile // 3, :, 128 * (tile % 3) : 128 * (tile % 3 + 1)]

    for d in (0, 1, SLABS - 1):
        chunk_ref[(p - d) & (SLABS - 1)] = jnp.zeros((12, 128), f32)
    for d in range(2, SLABS - 1):
        tile, seg = place(d)
        chunk_ref[(p - d) & (SLABS - 1)] = lane_roll(force(tile), -seg)
    for k in range(2):
        self_ref[k] = force(k)
        down_ref[k] = force(2 + k)
        up_ref[k] = force(4 + k)


def partner_kernel(idx_ref, force_ref, lin_ref, out_ref, val_ref, sum_ref):
    for tile in range(17):
        val_ref[tile] = -force_ref[tile // 3, :, 128 * (tile % 3) : 128 * (tile % 3 + 1)]
    val_ref[17] = jnp.zeros((12, 128), f32)
    scatter_rows(val_ref, idx_ref, sum_ref)
    for x in range(4):
        out_ref[:, x] = lin_ref[:, x] + sum_ref[:, 128 * x : 128 * (x + 1)].reshape(12, 32, 128)


def final_kernel(p_ref, me_ref, idx_ref, chunk_ref, up_ref, down_ref, self_ref, part_ref, mass_ref,
                 own_ref, y1_ref, y2_ref, y3_ref, x_ref, res_ref, jac_ref, val_ref, sum_ref, acc_ref):
    p = p_ref[0]

    def listed(d):
        return chunk_ref[(p + d) & (SLABS - 1)]

    tiles = [self_ref[0], self_ref[1], down_ref[0], down_ref[1], up_ref[0], up_ref[1], listed(2), listed(SLABS - 2)]
    tiles += merge_far(listed, 12, 0.0) + [jnp.zeros((12, 128), f32)]
    for k, tile in enumerate(tiles):
        val_ref[k] = tile
    for k in range(PARTS):
        acc = x_ref[k // 2] if k % 2 else (own_ref, y1_ref, y2_ref, y3_ref)[k // 2][0]
        acc_ref[me_ref[0] ^ k] = acc
    scatter_rows(val_ref, idx_ref, sum_ref)
    for x in range(4):
        acc = jnp.concatenate([acc_ref[2 * x], acc_ref[2 * x + 1]], axis=1)
        added = sum_ref[:, 128 * x : 128 * (x + 1)].reshape(12, 32, 128)
        out = part_ref[:, x] + mass_ref[x][None] * acc + added
        res_ref[:, x] = out[0:6]
        jac_ref[:, x] = out[6:12]


def join_kernel(same_ref, other_ref, *out_refs):
    for k, out in enumerate(out_refs):
        out[0] = same_ref[k + 1]
        out[1] = other_ref[k + 1]


def turn_kernel(own_ref, y1_ref, y2_ref, y3_ref, out_ref):
    for k, ref in enumerate((own_ref, y1_ref, y2_ref, y3_ref)):
        out_ref[k] = ref[1]


def time_kernel(me_ref, same_ref, other_ref, y1_ref, y2_ref, y3_ref, *refs):
    outs, in_ref, out_ref = refs[:4], refs[4], refs[5]
    me = me_ref[0]
    in_ref[0] = same_ref[0]
    in_ref[1] = other_ref[0]
    for k, ref in enumerate((y1_ref, y2_ref, y3_ref)):
        in_ref[2 * k + 2 : 2 * k + 4] = ref[...]
    at = [me ^ ((me + k) & (PARTS - 1)) for k in range(PARTS)]
    count = 2 * PARTS

    def step(g, carry):
        field = g // 3
        row = 6 * field + (g - 3 * field)
        x = [in_ref[at[t // 2], row + 3 * (t % 2)] for t in range(count)]
        for t in range(count):
            acc = x[0] * float(MIXED[t, 0])
            for s in range(1, count):
                acc = acc + x[s] * float(MIXED[(t - s) % count, 0])
            out_ref[at[t // 2], row + 3 * (t % 2)] = acc
        return carry

    lax.fori_loop(0, 6, step, 0)
    for k, out in enumerate(outs):
        out[...] = out_ref[2 * k : 2 * k + 2]


def lookup(ids, mat_ref, column, count):
    out = jnp.zeros(ids.shape, f32)
    for m in range(count):
        out = jnp.where(ids == m, mat_ref[m, column], out)
    return out


def stiff_kernel(p_ref, mat_ref, ids_ref, disp_ref, dir_ref, forcing_ref, up_ref, down_ref, out_ref, mass_ref, *, materials):
    p = p_ref[0]
    low = jnp.where(p > 0, up_ref[1:14], 0.0)
    high = jnp.where(p < SLABS - 1, down_ref[1:14], 0.0)
    ids = ids_ref[...]
    kx, ky, kz, mass = [lookup(ids, mat_ref, col, materials) for col in range(4)]
    mass_ref[...] = mass
    kx_low = lookup(low[12].astype(i32) - 1, mat_ref, 0, materials)
    kx_high = lookup(high[12].astype(i32) - 1, mat_ref, 0, materials)
    shape = ids.shape
    y = lax.broadcasted_iota(i32, shape, 1)
    z = lax.broadcasted_iota(i32, shape, 2)
    xm = 0.5 * (kx + jnp.concatenate([kx_low[None], kx[:-1]], axis=0))
    xp = 0.5 * (kx + jnp.concatenate([kx[1:], kx_high[None]], axis=0))
    total = xm + xp
    sides = []
    for k, pos, axis in ((ky, y, 1), (kz, z, 2)):
        size = shape[axis]
        for shift, edge in ((1, 0), (size - 1, size - 1)):
            inside = pos != edge
            near = jnp.where(inside, pltpu.roll(k, shift, axis), 0.0)
            side = 0.5 * (k + near)
            total = total + side
            sides.append((jnp.where(inside, side, 0.0), shift, axis))
    for field, ref in enumerate((disp_ref, dir_ref)):
        for c in range(6):
            w = ref[c]
            down = jnp.concatenate([low[6 * field + c][None], w[:-1]], axis=0)
            up = jnp.concatenate([w[1:], high[6 * field + c][None]], axis=0)
            out = total * w - xm * down - xp * up
            for side, shift, axis in sides:
                out = out - side * pltpu.roll(w, shift, axis)
            if field == 0:
                out = out - forcing_ref[c]
            out_ref[6 * field + c] = out


VMEM = 16 * 1024 * 1024


def call(kernel, outs, *args, smem=(0,), away=(), scratch=(), kept=(), limit=VMEM):
    spaces = [pltpu.SMEM if k in smem else pl.ANY if k in away else pltpu.VMEM for k in range(len(args))]
    specs = [pl.BlockSpec(memory_space=space) for space in spaces]
    return pl.pallas_call(
        kernel,
        out_shape=[jax.ShapeDtypeStruct(s, d) for s, d in outs],
        in_specs=specs,
        out_specs=[pl.BlockSpec(memory_space=pl.ANY if k in kept else pltpu.VMEM) for k in range(len(outs))],
        scratch_shapes=list(scratch),
        compiler_params=pltpu.CompilerParams(vmem_limit_bytes=limit),
    )(*args)


def shift(x, by):
    return lax.ppermute(x, "mesh", [(i, (i + by) % SLABS) for i in range(SLABS)])


def exchange(chunk, up, down):
    up, down = shift(up, 1), shift(down, -1)
    return lax.all_to_all(chunk, "mesh", split_axis=0, concat_axis=0, tiled=True), up, down


def swap(x, bit):
    return lax.ppermute(x, "inst", [(i, i ^ bit) for i in range(PARTS)])


def inst_split(x):
    return lax.all_to_all(x, "inst", split_axis=0, concat_axis=0, tiled=True)


def on_device(displacement, direction, forcing, material_ids, materials, joint_owner, joint_local, joint_remote, joint_kind):
    shape = displacement.shape
    fields = (6, 4, 32, 128)
    whole = (12, 4, 32, 128)
    disp = displacement.reshape(fields)
    dire = direction.reshape(fields)
    count = joint_local.shape[0]
    p = lax.axis_index("mesh").astype(i32).reshape(1)
    me = lax.axis_index("inst").astype(i32).reshape(1)
    parts = (768, 512)
    index = ((24, 128), i32)
    half = ((4, 12, 16, 128), f32)
    near = ((14, 32, 128), f32)

    own_idx, chunk, up, down, own, same, other = call(
        list_kernel,
        [index, ((SLABS, 16, 128), f32), near, near, ((2, 16, 128), f32), half, half],
        p,
        me,
        joint_owner.reshape(1, count),
        joint_local.reshape(1, count),
        joint_remote.reshape(1, count),
        joint_kind.reshape(1, count),
        disp,
        dire,
        material_ids,
        smem=(0, 1),
        away=range(2, 9),
        limit=60 * 1024 * 1024,
        kept=(2, 3, 5, 6),
        scratch=[pltpu.VMEM(parts, bf16), pltpu.VMEM((SIDE, 16, 128), f32)]
        + [pltpu.VMEM((1, count), i32)] * 4
        + [pltpu.VMEM(fields, f32)] * 2
        + [pltpu.VMEM((4, 32, 128), i32), pltpu.VMEM((4, 32, 128), f32)]
        + [pltpu.SemaphoreType.DMA((11,)), pltpu.SemaphoreType.DMA((20,))],
    )
    chunk, up, down = exchange(chunk, up, down)

    pair = ((2, 12, 16, 128), f32)
    other = swap(other, 1)
    joined = call(join_kernel, [pair] * 3, same, other, smem=())
    turned = [swap(x, 2 * k + 2) for k, x in enumerate(joined)]
    blocks = [pltpu.VMEM((PARTS, 12, 16, 128), f32)] * 2
    inertia = call(time_kernel, [pair] * 4, me, same, other, *turned, scratch=blocks)

    part = ((PARTS, 12, 384), f32)
    fields_parts = call(split_kernel, [(parts, bf16)], disp, dire, smem=())[0]
    far_idx, kind, gap = call(
        gap_kernel,
        [index, ((24, 128), f32), part],
        p, chunk, up, down, own, fields_parts, joined[0],
        away=(6,),
        scratch=[pltpu.VMEM((SIDE, 12, 128), f32)],
    )
    force = call(
        force_kernel,
        [part],
        me, kind, jnp.asarray(SPREAD), inst_split(gap), inertia[0],
        away=(4,),
        scratch=[pltpu.VMEM((48, 384), f32)] * 4,
    )[0]
    force = inst_split(force)
    turned = [inertia[0]] + [swap(inertia[k], 2 * k) for k in (1, 2, 3)]
    messages = [((SLABS, 12, 128), f32)] + [((2, 12, 128), f32)] * 3
    chunk, up2, down2, own = call(reply_kernel, messages, p, force)
    chunk, up2, down2 = exchange(chunk, up2, down2)

    lin, mass = call(
        lambda *refs: stiff_kernel(*refs, materials=materials.shape[0]),
        [(whole, f32), ((4, 32, 128), f32)],
        p, materials, material_ids, disp, dire, forcing.reshape(fields), up, down,
        smem=(0, 1),
    )
    other = swap(call(turn_kernel, [half], *turned, smem=())[0], 1)
    adding = [pltpu.VMEM((SIDE, 12, 128), f32), pltpu.VMEM((384, 512), f32)]
    partial = call(partner_kernel, [(whole, f32)], far_idx, force, lin, smem=(), scratch=adding)[0]
    residual, jacobian = call(
        final_kernel,
        [(fields, f32)] * 2,
        p, me, own_idx, chunk, up2, down2, own, partial, mass, *turned, other,
        smem=(0, 1),
        scratch=adding + blocks[:1],
    )
    return residual.reshape(shape), jacobian.reshape(shape)


def solution(mesh):
    field = P("inst", None, "mesh", None, None)
    placed = (field, field, field, P("mesh", None, None), P(), P("mesh", None), P("mesh"), P("mesh"), P("mesh"))
    return jax.shard_map(on_device, mesh=mesh, in_specs=placed, out_specs=(field, field), check_vma=False)
```

```python
import jax
import jax.numpy as jnp
import numpy as np
from jax import lax
from jax.experimental import pallas as pl
from jax.experimental.pallas import tpu as pltpu
from jax.sharding import PartitionSpec as P

frequency = 0.6
damping = 0.3
bolt_stiff = 2.0
slip_force = 1.0
slip_speed = 0.5
stop_stiff = 3.0
clearance = 0.3

SLABS = 32
PARTS = 8
SIDE = 18
SEG = 42
f32 = jnp.float32
bf16 = jnp.bfloat16
i32 = jnp.int32


def tables(count):
    offsets = np.arange(count)[:, None] - np.arange(count)[None, :]
    tangent = np.where(offsets == 0, 1.0, np.tan(np.pi * offsets / count))
    first = np.where(offsets == 0, 0.0, 0.5 * np.where(offsets % 2 == 0, 1.0, -1.0) / tangent) * frequency
    return first, first @ first


FIRST, SECOND = tables(2 * PARTS)
MIXED = (SECOND + damping * FIRST).astype(np.float32)
SPREAD = np.kron(FIRST, np.eye(3)).astype(np.float32)


def far_place(offset):
    return 8 + (offset - 3) // 3, SEG * ((offset - 3) % 3)


def pack(rows, seg):
    return jnp.where(lanes(8) < 64, lane_roll(rows[:8], -seg), lane_roll(rows[8:], 64 - seg))


def unpack(chunk):
    return jnp.concatenate([chunk, lane_roll(chunk, 64)], axis=0)


def lane_roll(x, shift):
    shift = shift % 128
    return pltpu.roll(x, shift, x.ndim - 1) if shift else x


def lanes(rows):
    return lax.broadcasted_iota(i32, (rows, 128), 1)


def merge_far(read, rows, fill):
    lane = lanes(rows)
    tiles = []
    for k in range(9):
        parts = [lane_roll(read(3 + 3 * k + s), SEG * s) for s in range(3)]
        tile = jnp.where(lane < SEG, parts[0], jnp.where(lane < 2 * SEG, parts[1], parts[2]))
        tiles.append(jnp.where(lane < 3 * SEG, tile, fill))
    return tiles


def slot_tables(p, owner_ref, local_ref, remote_ref, kind_ref):
    count = owner_ref.shape[1]
    offset = (owner_ref[...] - p) & (SLABS - 1)
    hit = (lax.broadcasted_iota(i32, (SLABS, count), 0) == offset).astype(f32)
    hit16 = hit.astype(bf16)
    before = (lax.broadcasted_iota(i32, (128, 128), 0) < lax.broadcasted_iota(i32, (128, 128), 1)).astype(f32).astype(bf16)
    row = lax.broadcasted_iota(i32, (SLABS, 1), 0)
    far = row - 3
    group = (far * 171) >> 9
    start = 1024 + group * 128 + (far - 3 * group) * SEG
    for value, at in ((0, 0), (1, 256), (SLABS - 1, 512), (2, 768), (SLABS - 2, 896)):
        start = jnp.where(row == value, at, start)
    run = start.astype(f32)
    places = []
    for b in range(count // 128):
        block = hit[:, 128 * b : 128 * (b + 1)]
        earlier = jnp.dot(hit16[:, 128 * b : 128 * (b + 1)], before, preferred_element_type=f32)
        places.append(jnp.sum(block * (earlier + run), axis=0, keepdims=True))
        run = run + jnp.sum(block, axis=1, keepdims=True)
    slot = jnp.concatenate(places, axis=1).astype(i32)
    in_tile = lax.broadcasted_iota(i32, (24, count), 0) == (slot >> 7)
    in_lane = (lax.broadcasted_iota(i32, (128, count), 0) == (slot & 127)).astype(f32).astype(bf16)
    local = local_ref[...]
    remote = remote_ref[...]
    values = (local >> 7, local & 127, remote >> 7, remote & 127, kind_ref[...], jnp.ones_like(local))
    spread = jnp.concatenate([jnp.where(in_tile, v.astype(f32), 0.0) for v in values], axis=0).astype(bf16)
    got = lax.dot_general(spread, in_lane, (((1,), (1,)), ((), ())), preferred_element_type=f32)
    got = [got[24 * k : 24 * (k + 1)] for k in range(6)]
    empty = got[5] - 1.0
    return got[0] * 128.0 + got[1] + empty, got[2] * 128.0 + got[3] + empty, got[4]


def picks(idx_ref, k):
    idx = jnp.concatenate([idx_ref[pl.ds(2 * k, 1), :], idx_ref[pl.ds(2 * k + 1, 1), :]], axis=1)
    code = ((idx >> 12) << 7) | (idx & 127)
    pick = (lax.broadcasted_iota(i32, (512, 256), 0) == code).astype(f32).astype(bf16)
    return pick, lax.broadcasted_iota(i32, (32, 256), 0) == ((idx >> 7) & 31)


def split_fields(disp_ref, dir_ref, parts_ref):
    for field, ref in enumerate((disp_ref, dir_ref)):
        for x in range(4):
            value = ref[:, x].reshape(6 * 32, 128)
            hi = value.astype(bf16)
            cols = slice(128 * x, 128 * (x + 1))
            parts_ref[192 * field : 192 * (field + 1), cols] = hi
            parts_ref[384 + 192 * field : 384 + 192 * (field + 1), cols] = (value - hi.astype(f32)).astype(bf16)


def split_kernel(disp_ref, dir_ref, parts_ref):
    split_fields(disp_ref, dir_ref, parts_ref)


def gather_rows(parts_ref, idx_ref, here_ref):
    def step(k, carry):
        pick, in_y = picks(idx_ref, k)
        rows = jnp.dot(parts_ref[...], pick, preferred_element_type=f32)
        rows = (rows[:384] + rows[384:]).reshape(12, 32, 256)
        got = jnp.sum(jnp.where(in_y[None], rows, 0.0), axis=1)
        here_ref[2 * k, 0:12, :] = got[:, :128]
        here_ref[2 * k + 1, 0:12, :] = got[:, 128:]
        return carry

    lax.fori_loop(0, SIDE // 2, step, 0, unroll=3)


def scatter_rows(val_ref, idx_ref, sum_ref):
    sum_ref[...] = jnp.zeros(sum_ref.shape, f32)
    dims = (((1,), (1,)), ((), ()))

    def step(k, carry):
        pick, in_y = picks(idx_ref, k)
        value = jnp.concatenate([val_ref[2 * k], val_ref[2 * k + 1]], axis=1)
        hi = value.astype(bf16).astype(f32)
        spread = [
            jnp.where(in_y[None], part[:, None, :], 0.0).reshape(384, 256).astype(bf16) for part in (hi, value - hi)
        ]
        got = lax.dot_general(spread[0], pick, dims, preferred_element_type=f32)
        got = got + lax.dot_general(spread[1], pick, dims, preferred_element_type=f32)
        sum_ref[...] = sum_ref[...] + got
        return carry

    lax.fori_loop(0, SIDE // 2, step, 0, unroll=3)


def list_kernel(p_ref, me_ref, owner_hbm, local_hbm, remote_hbm, kind_hbm, disp_hbm, dir_hbm, ids_hbm,
                idx_ref, chunk_ref, up_hbm, down_hbm, up2_ref, down2_ref, self_ref, same_hbm, other_hbm,
                parts_ref, rows_ref, owner_ref, local_ref, remote_ref, kind_ref, disp_ref, dir_ref, ids_ref, near_ref,
                sems, more_sems):
    p = p_ref[0]
    pairs = ((owner_hbm, owner_ref), (local_hbm, local_ref), (remote_hbm, remote_ref), (kind_hbm, kind_ref),
             (disp_hbm, disp_ref), (dir_hbm, dir_ref), (ids_hbm, ids_ref))
    copies = [pltpu.make_async_copy(a, b, sems.at[k]) for k, (a, b) in enumerate(pairs)]
    for copy in copies:
        copy.start()
    for copy in copies[:4]:
        copy.wait()
    mine, theirs, kind = slot_tables(p, owner_ref, local_ref, remote_ref, kind_ref)
    idx_ref[...] = mine.astype(i32)
    for tile in range(SIDE):
        rows_ref[tile, 12:13, :] = theirs[tile : tile + 1]
        rows_ref[tile, 13:14, :] = kind[tile : tile + 1]
        rows_ref[tile, 14:16, :] = jnp.zeros((2, 128), f32)
    for copy in copies[4:]:
        copy.wait()
    moves = []
    for field, ref in enumerate((disp_ref, dir_ref)):
        part = pl.ds(6 * field, 6)
        for k in range(PARTS):
            block = me_ref[0] ^ k
            rows = pl.ds(pl.multiple_of(16 * (block & 1), 16), 16)
            moves.append((ref.at[:, block >> 1, rows, :], (same_hbm, other_hbm)[k % 2].at[k // 2, part]))
        moves.append((ref.at[:, 3], up_hbm.at[pl.ds(1 + 6 * field, 6)]))
        moves.append((ref.at[:, 0], down_hbm.at[pl.ds(1 + 6 * field, 6)]))
    moves = [pltpu.make_async_copy(a, b, more_sems.at[k]) for k, (a, b) in enumerate(moves)]
    for move in moves:
        move.start()
    split_fields(disp_ref, dir_ref, parts_ref)
    near_ref[2] = (ids_ref[3] + 1).astype(f32)
    near_ref[3] = (ids_ref[0] + 1).astype(f32)
    gather_rows(parts_ref, idx_ref, rows_ref)
    for k in range(2):
        near_ref[k] = rows_ref[2 + 2 * k : 4 + 2 * k].reshape(32, 128)
    ends = ((near_ref.at[0], up_hbm.at[0]), (near_ref.at[1], down_hbm.at[0]),
            (near_ref.at[2], up_hbm.at[13]), (near_ref.at[3], down_hbm.at[13]))
    ends = [pltpu.make_async_copy(a, b, sems.at[7 + k]) for k, (a, b) in enumerate(ends)]
    for end in ends:
        end.start()
    for d in (0, 1, 2, SLABS - 2, SLABS - 1):
        chunk_ref[(p + d) & (SLABS - 1)] = jnp.zeros((8, 128), f32)
    for d in range(3, SLABS - 2):
        tile, seg = far_place(d)
        chunk_ref[(p + d) & (SLABS - 1)] = pack(rows_ref[tile], seg)
    up2_ref[...] = rows_ref[6]
    down2_ref[...] = rows_ref[7]
    self_ref[...] = rows_ref[0:2]
    for move in moves + ends:
        move.wait()


def gap_kernel(p_ref, chunk_ref, up_ref, down_ref, up2_ref, down2_ref, self_ref, parts_ref, after_ref,
               idx_ref, kind_ref, gap_ref, here_ref):
    p = p_ref[0]

    def asked(d):
        return unpack(chunk_ref[(p - d) & (SLABS - 1)])

    near = [ref[0, 16 * k : 16 * (k + 1), :] for ref in (up_ref, down_ref) for k in range(2)]
    tiles = [self_ref[0], self_ref[1]] + near + [up2_ref[...], down2_ref[...]]
    tiles += merge_far(asked, 16, 0.0)
    beyond = lanes(1) >= 3 * SEG
    rows = [t[12:13] for t in tiles[:8]] + [jnp.where(beyond, -1.0, t[12:13]) for t in tiles[8:]]
    idx_ref[...] = jnp.concatenate(rows + [jnp.full((7, 128), -1.0, f32)], axis=0).astype(i32)
    kind_ref[...] = jnp.concatenate([t[13:14] for t in tiles] + [jnp.zeros((7, 128), f32)], axis=0)
    gather_rows(parts_ref, idx_ref, here_ref)
    for tile in range(24):
        gap = tiles[tile][0:12] - here_ref[tile] if tile < 17 else jnp.zeros((12, 128), f32)
        gap_ref[tile // 3, :, 128 * (tile % 3) : 128 * (tile % 3 + 1)] = gap


def force_kernel(me_ref, kind_ref, spread_ref, gap_ref, after_ref, out_ref, r_ref, d_ref, f_ref, t_ref):
    me = me_ref[0]
    for k in range(PARTS):
        r_ref[6 * k : 6 * k + 6] = gap_ref[k, 0:6, :]
        d_ref[6 * k : 6 * k + 6] = gap_ref[k, 6:12, :]
    r = r_ref[...]
    dr = d_ref[...]
    w = jnp.dot(spread_ref[...], r, precision=lax.Precision.HIGHEST, preferred_element_type=f32)
    dw = jnp.dot(spread_ref[...], dr, precision=lax.Precision.HIGHEST, preferred_element_type=f32)
    bolted = jnp.concatenate([kind_ref[pl.ds(3 * me + k, 1), :] for k in range(3)], axis=1)
    slide = jnp.tanh(w / slip_speed)
    opened = jnp.tanh(r / clearance)
    friction = bolt_stiff * r + slip_force * slide
    contact = stop_stiff * (r - clearance * opened)
    f_ref[...] = bolted * friction + (1.0 - bolted) * contact
    tangent_friction = bolt_stiff * dr + slip_force * (1.0 - slide * slide) / slip_speed * dw
    tangent_contact = stop_stiff * opened * opened * dr
    t_ref[...] = bolted * tangent_friction + (1.0 - bolted) * tangent_contact
    for k in range(PARTS):
        out_ref[k, 0:6, :] = f_ref[6 * k : 6 * k + 6]
        out_ref[k, 6:12, :] = t_ref[6 * k : 6 * k + 6]


def reply_kernel(p_ref, force_ref, chunk_ref, up_ref, down_ref, self_ref):
    p = p_ref[0]

    def force(tile):
        return force_ref[tile // 3, :, 128 * (tile % 3) : 128 * (tile % 3 + 1)]

    for d in (0, 1, SLABS - 1):
        chunk_ref[(p - d) & (SLABS - 1)] = jnp.zeros((12, 128), f32)
    for d, tile in ((2, 6), (SLABS - 2, 7)):
        chunk_ref[(p - d) & (SLABS - 1)] = force(tile)
    for d in range(3, SLABS - 2):
        tile, seg = far_place(d)
        chunk_ref[(p - d) & (SLABS - 1)] = lane_roll(force(tile), -seg)
    for k in range(2):
        self_ref[k] = force(k)
        down_ref[k] = force(2 + k)
        up_ref[k] = force(4 + k)


def partner_kernel(idx_ref, force_ref, lin_ref, out_ref, val_ref, sum_ref):
    for tile in range(17):
        val_ref[tile] = -force_ref[tile // 3, :, 128 * (tile % 3) : 128 * (tile % 3 + 1)]
    val_ref[17] = jnp.zeros((12, 128), f32)
    scatter_rows(val_ref, idx_ref, sum_ref)
    for x in range(4):
        out_ref[:, x] = lin_ref[:, x] + sum_ref[:, 128 * x : 128 * (x + 1)].reshape(12, 32, 128)


def final_kernel(p_ref, me_ref, idx_ref, chunk_ref, up_ref, down_ref, self_ref, part_ref, mass_ref,
                 own_ref, y1_ref, y2_ref, y3_ref, x_ref, res_ref, jac_ref, val_ref, sum_ref, acc_ref, sems):
    p = p_ref[0]
    copies = []
    for k in range(PARTS):
        source = x_ref.at[k // 2] if k % 2 else (own_ref, y1_ref, y2_ref, y3_ref)[k // 2].at[0]
        copies.append(pltpu.make_async_copy(source, acc_ref.at[me_ref[0] ^ k], sems.at[k]))
    for copy in copies:
        copy.start()

    def listed(d):
        return chunk_ref[(p + d) & (SLABS - 1)]

    tiles = [self_ref[0], self_ref[1], down_ref[0], down_ref[1], up_ref[0], up_ref[1], listed(2), listed(SLABS - 2)]
    tiles += merge_far(listed, 12, 0.0) + [jnp.zeros((12, 128), f32)]
    for k, tile in enumerate(tiles):
        val_ref[k] = tile
    scatter_rows(val_ref, idx_ref, sum_ref)
    for copy in copies:
        copy.wait()
    for x in range(4):
        acc = jnp.concatenate([acc_ref[2 * x], acc_ref[2 * x + 1]], axis=1)
        added = sum_ref[:, 128 * x : 128 * (x + 1)].reshape(12, 32, 128)
        out = part_ref[:, x] + mass_ref[x][None] * acc + added
        res_ref[:, x] = out[0:6]
        jac_ref[:, x] = out[6:12]


def join_kernel(same_ref, other_ref, *out_refs):
    for k, out in enumerate(out_refs):
        out[0] = same_ref[k + 1]
        out[1] = other_ref[k + 1]


def turn_kernel(own_ref, y1_ref, y2_ref, y3_ref, out_ref):
    for k, ref in enumerate((own_ref, y1_ref, y2_ref, y3_ref)):
        out_ref[k] = ref[1]


def time_kernel(me_ref, same_ref, other_ref, y1_ref, y2_ref, y3_ref, *refs):
    outs, in_ref, out_ref, sems = refs[:4], refs[4], refs[5], refs[6]
    me = me_ref[0]
    pairs = [(same_ref.at[0], in_ref.at[0]), (other_ref.at[0], in_ref.at[1])]
    pairs += [(ref, in_ref.at[pl.ds(2 * k + 2, 2)]) for k, ref in enumerate((y1_ref, y2_ref, y3_ref))]
    copies = [pltpu.make_async_copy(a, b, sems.at[k]) for k, (a, b) in enumerate(pairs)]
    for copy in copies:
        copy.start()
    for copy in copies:
        copy.wait()
    at = [me ^ ((me + k) & (PARTS - 1)) for k in range(PARTS)]
    count = 2 * PARTS

    def step(g, carry):
        field = g // 3
        row = 6 * field + (g - 3 * field)
        x = [in_ref[at[t // 2], row + 3 * (t % 2)] for t in range(count)]
        for t in range(count):
            acc = x[0] * float(MIXED[t, 0])
            for s in range(1, count):
                acc = acc + x[s] * float(MIXED[(t - s) % count, 0])
            out_ref[at[t // 2], row + 3 * (t % 2)] = acc
        return carry

    lax.fori_loop(0, 6, step, 0)
    for k, out in enumerate(outs):
        out[...] = out_ref[2 * k : 2 * k + 2]


def lookup(ids, mat_ref, column, count):
    out = jnp.zeros(ids.shape, f32)
    for m in range(count):
        out = jnp.where(ids == m, mat_ref[m, column], out)
    return out


def stiff_kernel(p_ref, mat_ref, ids_ref, disp_ref, dir_ref, forcing_ref, up_ref, down_ref, out_ref, mass_ref, *, materials):
    p = p_ref[0]
    low = jnp.where(p > 0, up_ref[1:14], 0.0)
    high = jnp.where(p < SLABS - 1, down_ref[1:14], 0.0)
    ids = ids_ref[...]
    kx, ky, kz, mass = [lookup(ids, mat_ref, col, materials) for col in range(4)]
    mass_ref[...] = mass
    kx_low = lookup(low[12].astype(i32) - 1, mat_ref, 0, materials)
    kx_high = lookup(high[12].astype(i32) - 1, mat_ref, 0, materials)
    shape = ids.shape
    y = lax.broadcasted_iota(i32, shape, 1)
    z = lax.broadcasted_iota(i32, shape, 2)
    xm = 0.5 * (kx + jnp.concatenate([kx_low[None], kx[:-1]], axis=0))
    xp = 0.5 * (kx + jnp.concatenate([kx[1:], kx_high[None]], axis=0))
    total = xm + xp
    sides = []
    for k, pos, axis in ((ky, y, 1), (kz, z, 2)):
        size = shape[axis]
        for shift, edge in ((1, 0), (size - 1, size - 1)):
            inside = pos != edge
            near = jnp.where(inside, pltpu.roll(k, shift, axis), 0.0)
            side = 0.5 * (k + near)
            total = total + side
            sides.append((jnp.where(inside, side, 0.0), shift, axis))
    for field, ref in enumerate((disp_ref, dir_ref)):
        for c in range(6):
            w = ref[c]
            down = jnp.concatenate([low[6 * field + c][None], w[:-1]], axis=0)
            up = jnp.concatenate([w[1:], high[6 * field + c][None]], axis=0)
            out = total * w - xm * down - xp * up
            for side, shift, axis in sides:
                out = out - side * pltpu.roll(w, shift, axis)
            if field == 0:
                out = out - forcing_ref[c]
            out_ref[6 * field + c] = out


VMEM = 16 * 1024 * 1024


def call(kernel, outs, *args, smem=(0,), away=(), scratch=(), kept=(), limit=VMEM):
    spaces = [pltpu.SMEM if k in smem else pl.ANY if k in away else pltpu.VMEM for k in range(len(args))]
    specs = [pl.BlockSpec(memory_space=space) for space in spaces]
    return pl.pallas_call(
        kernel,
        out_shape=[jax.ShapeDtypeStruct(s, d) for s, d in outs],
        in_specs=specs,
        out_specs=[pl.BlockSpec(memory_space=pl.ANY if k in kept else pltpu.VMEM) for k in range(len(outs))],
        scratch_shapes=list(scratch),
        compiler_params=pltpu.CompilerParams(vmem_limit_bytes=limit),
    )(*args)


def shift(x, by):
    return lax.ppermute(x, "mesh", [(i, (i + by) % SLABS) for i in range(SLABS)])


def exchange(chunk, *near):
    near = [shift(x, by) for x, by in zip(near, (1, -1, 2, -2))]
    return lax.all_to_all(chunk, "mesh", split_axis=0, concat_axis=0, tiled=True), *near


def swap(x, bit):
    return lax.ppermute(x, "inst", [(i, i ^ bit) for i in range(PARTS)])


def inst_split(x):
    return lax.all_to_all(x, "inst", split_axis=0, concat_axis=0, tiled=True)


def on_device(displacement, direction, forcing, material_ids, materials, joint_owner, joint_local, joint_remote, joint_kind):
    shape = displacement.shape
    fields = (6, 4, 32, 128)
    whole = (12, 4, 32, 128)
    disp = displacement.reshape(fields)
    dire = direction.reshape(fields)
    count = joint_local.shape[0]
    p = lax.axis_index("mesh").astype(i32).reshape(1)
    me = lax.axis_index("inst").astype(i32).reshape(1)
    parts = (768, 512)
    index = ((24, 128), i32)
    half = ((4, 12, 16, 128), f32)
    near = ((14, 32, 128), f32)
    tile = ((16, 128), f32)

    own_idx, chunk, *sides, own, same, other = call(
        list_kernel,
        [index, ((SLABS, 8, 128), f32), near, near, tile, tile, ((2, 16, 128), f32), half, half],
        p,
        me,
        joint_owner.reshape(1, count),
        joint_local.reshape(1, count),
        joint_remote.reshape(1, count),
        joint_kind.reshape(1, count),
        disp,
        dire,
        material_ids,
        smem=(0, 1),
        away=range(2, 9),
        limit=60 * 1024 * 1024,
        kept=(2, 3, 7, 8),
        scratch=[pltpu.VMEM(parts, bf16), pltpu.VMEM((SIDE, 16, 128), f32)]
        + [pltpu.VMEM((1, count), i32)] * 4
        + [pltpu.VMEM(fields, f32)] * 2
        + [pltpu.VMEM((4, 32, 128), i32), pltpu.VMEM((4, 32, 128), f32)]
        + [pltpu.SemaphoreType.DMA((11,)), pltpu.SemaphoreType.DMA((20,))],
    )
    chunk, *sides = exchange(chunk, *sides)

    pair = ((2, 12, 16, 128), f32)
    other = swap(other, 1)
    joined = call(join_kernel, [pair] * 3, same, other, smem=())
    turned = [swap(x, 2 * k + 2) for k, x in enumerate(joined)]
    blocks = [pltpu.VMEM((PARTS, 12, 16, 128), f32)] * 2
    inertia = call(time_kernel, [pair] * 4, me, same, other, *turned, away=range(1, 6), scratch=blocks + [pltpu.SemaphoreType.DMA((5,))])

    part = ((PARTS, 12, 384), f32)
    fields_parts = call(split_kernel, [(parts, bf16)], disp, dire, smem=())[0]
    far_idx, kind, gap = call(
        gap_kernel,
        [index, ((24, 128), f32), part],
        p, chunk, *sides, own, fields_parts, joined[0],
        away=(8,),
        scratch=[pltpu.VMEM((SIDE, 12, 128), f32)],
    )
    force = call(
        force_kernel,
        [part],
        me, kind, jnp.asarray(SPREAD), inst_split(gap), inertia[0],
        away=(4,),
        scratch=[pltpu.VMEM((48, 384), f32)] * 4,
    )[0]
    force = inst_split(force)
    turned = [inertia[0]] + [swap(inertia[k], 2 * k) for k in (1, 2, 3)]
    two = ((2, 12, 128), f32)
    chunk, *replies, own = call(reply_kernel, [((SLABS, 12, 128), f32), two, two, two], p, force)
    chunk, *replies = exchange(chunk, *replies)

    lin, mass = call(
        lambda *refs: stiff_kernel(*refs, materials=materials.shape[0]),
        [(whole, f32), ((4, 32, 128), f32)],
        p, materials, material_ids, disp, dire, forcing.reshape(fields), *sides[:2],
        smem=(0, 1),
    )
    other = swap(call(turn_kernel, [half], *turned, smem=())[0], 1)
    adding = [pltpu.VMEM((SIDE, 12, 128), f32), pltpu.VMEM((384, 512), f32)]
    partial = call(partner_kernel, [(whole, f32)], far_idx, force, lin, smem=(), scratch=adding)[0]
    residual, jacobian = call(
        final_kernel,
        [(fields, f32)] * 2,
        p, me, own_idx, chunk, *replies, own, partial, mass, *turned, other,
        smem=(0, 1),
        away=range(9, 14),
        scratch=adding + blocks[:1] + [pltpu.SemaphoreType.DMA((PARTS,))],
    )
    return residual.reshape(shape), jacobian.reshape(shape)


def solution(mesh):
    field = P("inst", None, "mesh", None, None)
    placed = (field, field, field, P("mesh", None, None), P(), P("mesh", None), P("mesh"), P("mesh"), P("mesh"))
    return jax.shard_map(on_device, mesh=mesh, in_specs=placed, out_specs=(field, field), check_vma=False)
```

```python
import jax
import jax.numpy as jnp
import numpy as np
from jax import lax
from jax.experimental import pallas as pl
from jax.experimental.pallas import tpu as pltpu
from jax.sharding import PartitionSpec as P

frequency = 0.6
damping = 0.3
bolt_stiff = 2.0
slip_force = 1.0
slip_speed = 0.5
stop_stiff = 3.0
clearance = 0.3

SLABS = 32
PARTS = 8
SIDE = 18
SEG = 42
f32 = jnp.float32
bf16 = jnp.bfloat16
i32 = jnp.int32


def tables(count):
    offsets = np.arange(count)[:, None] - np.arange(count)[None, :]
    tangent = np.where(offsets == 0, 1.0, np.tan(np.pi * offsets / count))
    first = np.where(offsets == 0, 0.0, 0.5 * np.where(offsets % 2 == 0, 1.0, -1.0) / tangent) * frequency
    return first, first @ first


FIRST, SECOND = tables(2 * PARTS)
MIXED = (SECOND + damping * FIRST).astype(np.float32)
SPREAD = np.kron(FIRST, np.eye(3)).astype(np.float32)


def far_place(offset):
    return 8 + (offset - 3) // 3, SEG * ((offset - 3) % 3)


def lane_roll(x, shift):
    shift = shift % 128
    return pltpu.roll(x, shift, x.ndim - 1) if shift else x


def lanes(rows):
    return lax.broadcasted_iota(i32, (rows, 128), 1)


def merge_far(read, rows, fill):
    lane = lanes(rows)
    tiles = []
    for k in range(9):
        parts = [lane_roll(read(3 + 3 * k + s), SEG * s) for s in range(3)]
        tile = jnp.where(lane < SEG, parts[0], jnp.where(lane < 2 * SEG, parts[1], parts[2]))
        tiles.append(jnp.where(lane < 3 * SEG, tile, fill))
    return tiles


def slot_tables(p, owner_ref, local_ref, remote_ref, kind_ref):
    count = owner_ref.shape[1]
    offset = (owner_ref[...] - p) & (SLABS - 1)
    hit = (lax.broadcasted_iota(i32, (SLABS, count), 0) == offset).astype(f32)
    hit16 = hit.astype(bf16)
    before = (lax.broadcasted_iota(i32, (128, 128), 0) < lax.broadcasted_iota(i32, (128, 128), 1)).astype(f32).astype(bf16)
    row = lax.broadcasted_iota(i32, (SLABS, 1), 0)
    far = row - 3
    group = (far * 171) >> 9
    start = 1024 + group * 128 + (far - 3 * group) * SEG
    for value, at in ((0, 0), (1, 256), (SLABS - 1, 512), (2, 768), (SLABS - 2, 896)):
        start = jnp.where(row == value, at, start)
    run = start.astype(f32)
    places = []
    for b in range(count // 128):
        block = hit[:, 128 * b : 128 * (b + 1)]
        earlier = jnp.dot(hit16[:, 128 * b : 128 * (b + 1)], before, preferred_element_type=f32)
        places.append(jnp.sum(block * (earlier + run), axis=0, keepdims=True))
        run = run + jnp.sum(block, axis=1, keepdims=True)
    slot = jnp.concatenate(places, axis=1).astype(i32)
    in_tile = lax.broadcasted_iota(i32, (24, count), 0) == (slot >> 7)
    in_lane = (lax.broadcasted_iota(i32, (128, count), 0) == (slot & 127)).astype(f32).astype(bf16)
    local = local_ref[...]
    remote = remote_ref[...]
    values = (local >> 7, local & 127, remote >> 7, remote & 127, kind_ref[...], jnp.ones_like(local))
    spread = jnp.concatenate([jnp.where(in_tile, v.astype(f32), 0.0) for v in values], axis=0).astype(bf16)
    got = lax.dot_general(spread, in_lane, (((1,), (1,)), ((), ())), preferred_element_type=f32)
    got = [got[24 * k : 24 * (k + 1)] for k in range(6)]
    empty = got[5] - 1.0
    return got[0] * 128.0 + got[1] + empty, got[2] * 128.0 + got[3] + empty, got[4]


def picks(idx_ref, k):
    idx = jnp.concatenate([idx_ref[pl.ds(2 * k, 1), :], idx_ref[pl.ds(2 * k + 1, 1), :]], axis=1)
    code = ((idx >> 12) << 7) | (idx & 127)
    pick = (lax.broadcasted_iota(i32, (512, 256), 0) == code).astype(f32).astype(bf16)
    return pick, lax.broadcasted_iota(i32, (32, 256), 0) == ((idx >> 7) & 31)


def split_fields(disp_ref, dir_ref, parts_ref):
    for field, ref in enumerate((disp_ref, dir_ref)):
        for x in range(4):
            value = ref[:, x].reshape(6 * 32, 128)
            hi = value.astype(bf16)
            cols = slice(128 * x, 128 * (x + 1))
            parts_ref[192 * field : 192 * (field + 1), cols] = hi
            parts_ref[384 + 192 * field : 384 + 192 * (field + 1), cols] = (value - hi.astype(f32)).astype(bf16)


def split_kernel(disp_ref, dir_ref, parts_ref):
    split_fields(disp_ref, dir_ref, parts_ref)


def gather_rows(parts_ref, idx_ref, here_ref):
    def step(k, carry):
        pick, in_y = picks(idx_ref, k)
        rows = jnp.dot(parts_ref[...], pick, preferred_element_type=f32)
        rows = (rows[:384] + rows[384:]).reshape(12, 32, 256)
        got = jnp.sum(jnp.where(in_y[None], rows, 0.0), axis=1)
        here_ref[2 * k, 0:12, :] = got[:, :128]
        here_ref[2 * k + 1, 0:12, :] = got[:, 128:]
        return carry

    lax.fori_loop(0, SIDE // 2, step, 0, unroll=3)


def scatter_rows(val_ref, idx_ref, sum_ref):
    sum_ref[...] = jnp.zeros(sum_ref.shape, f32)
    dims = (((1,), (1,)), ((), ()))

    def step(k, carry):
        pick, in_y = picks(idx_ref, k)
        value = jnp.concatenate([val_ref[2 * k], val_ref[2 * k + 1]], axis=1)
        hi = value.astype(bf16).astype(f32)
        spread = [
            jnp.where(in_y[None], part[:, None, :], 0.0).reshape(384, 256).astype(bf16) for part in (hi, value - hi)
        ]
        got = lax.dot_general(spread[0], pick, dims, preferred_element_type=f32)
        got = got + lax.dot_general(spread[1], pick, dims, preferred_element_type=f32)
        sum_ref[...] = sum_ref[...] + got
        return carry

    lax.fori_loop(0, SIDE // 2, step, 0, unroll=3)


def list_kernel(p_ref, me_ref, owner_hbm, local_hbm, remote_hbm, kind_hbm, disp_hbm, dir_hbm, ids_hbm,
                idx_ref, chunk_ref, up_ref, down_ref, self_ref, same_hbm, other_hbm, high_hbm, low_hbm,
                parts_ref, rows_ref, owner_ref, local_ref, remote_ref, kind_ref, disp_ref, dir_ref, ids_ref, edge_ref,
                sems, more_sems):
    p = p_ref[0]
    pairs = ((owner_hbm, owner_ref), (local_hbm, local_ref), (remote_hbm, remote_ref), (kind_hbm, kind_ref),
             (disp_hbm, disp_ref), (dir_hbm, dir_ref), (ids_hbm, ids_ref))
    copies = [pltpu.make_async_copy(a, b, sems.at[k]) for k, (a, b) in enumerate(pairs)]
    for copy in copies:
        copy.start()
    for copy in copies[:4]:
        copy.wait()
    mine, theirs, kind = slot_tables(p, owner_ref, local_ref, remote_ref, kind_ref)
    idx_ref[...] = mine.astype(i32)
    for tile in range(SIDE):
        rows_ref[tile, 12:13, :] = theirs[tile : tile + 1]
        rows_ref[tile, 13:14, :] = kind[tile : tile + 1]
        rows_ref[tile, 14:16, :] = jnp.zeros((2, 128), f32)
    for copy in copies[4:]:
        copy.wait()
    moves = []
    for field, ref in enumerate((disp_ref, dir_ref)):
        part = pl.ds(6 * field, 6)
        for k in range(PARTS):
            block = me_ref[0] ^ k
            rows = pl.ds(pl.multiple_of(16 * (block & 1), 16), 16)
            moves.append((ref.at[:, block >> 1, rows, :], (same_hbm, other_hbm)[k % 2].at[k // 2, part]))
        moves.append((ref.at[:, 3], high_hbm.at[pl.ds(6 * field, 6)]))
        moves.append((ref.at[:, 0], low_hbm.at[pl.ds(6 * field, 6)]))
    moves = [pltpu.make_async_copy(a, b, more_sems.at[k]) for k, (a, b) in enumerate(moves)]
    for move in moves:
        move.start()
    split_fields(disp_ref, dir_ref, parts_ref)
    ends = []
    for k, (x, hbm) in enumerate(((3, high_hbm), (0, low_hbm))):
        edge_ref[k] = (ids_ref[x] + 1).astype(f32)
        ends.append(pltpu.make_async_copy(edge_ref.at[k], hbm.at[12], sems.at[7 + k]))
    for end in ends:
        end.start()
    gather_rows(parts_ref, idx_ref, rows_ref)
    for d in (0, 1, SLABS - 1):
        chunk_ref[(p + d) & (SLABS - 1)] = jnp.zeros((16, 128), f32)
    for d, tile in ((2, 6), (SLABS - 2, 7)):
        chunk_ref[(p + d) & (SLABS - 1)] = rows_ref[tile]
    for d in range(3, SLABS - 2):
        tile, seg = far_place(d)
        chunk_ref[(p + d) & (SLABS - 1)] = lane_roll(rows_ref[tile], -seg)
    self_ref[...] = rows_ref[0:2]
    up_ref[...] = rows_ref[2:4]
    down_ref[...] = rows_ref[4:6]
    for move in moves + ends:
        move.wait()


def gap_kernel(p_ref, chunk_ref, up_ref, down_ref, self_ref, parts_ref, after_ref,
               idx_ref, kind_ref, gap_ref, here_ref):
    p = p_ref[0]

    def asked(d):
        return chunk_ref[(p - d) & (SLABS - 1)]

    tiles = [self_ref[0], self_ref[1], up_ref[0], up_ref[1], down_ref[0], down_ref[1], asked(2), asked(SLABS - 2)]
    tiles += merge_far(asked, 16, 0.0)
    beyond = lanes(1) >= 3 * SEG
    rows = [t[12:13] for t in tiles[:8]] + [jnp.where(beyond, -1.0, t[12:13]) for t in tiles[8:]]
    idx_ref[...] = jnp.concatenate(rows + [jnp.full((7, 128), -1.0, f32)], axis=0).astype(i32)
    kind_ref[...] = jnp.concatenate([t[13:14] for t in tiles] + [jnp.zeros((7, 128), f32)], axis=0)
    gather_rows(parts_ref, idx_ref, here_ref)
    for tile in range(24):
        gap = tiles[tile][0:12] - here_ref[tile] if tile < 17 else jnp.zeros((12, 128), f32)
        gap_ref[tile // 3, :, 128 * (tile % 3) : 128 * (tile % 3 + 1)] = gap


def force_kernel(me_ref, kind_ref, spread_ref, gap_ref, after_ref, out_ref, r_ref, d_ref, f_ref, t_ref):
    me = me_ref[0]
    for k in range(PARTS):
        r_ref[6 * k : 6 * k + 6] = gap_ref[k, 0:6, :]
        d_ref[6 * k : 6 * k + 6] = gap_ref[k, 6:12, :]
    r = r_ref[...]
    dr = d_ref[...]
    w = jnp.dot(spread_ref[...], r, precision=lax.Precision.HIGHEST, preferred_element_type=f32)
    dw = jnp.dot(spread_ref[...], dr, precision=lax.Precision.HIGHEST, preferred_element_type=f32)
    bolted = jnp.concatenate([kind_ref[pl.ds(3 * me + k, 1), :] for k in range(3)], axis=1)
    slide = jnp.tanh(w / slip_speed)
    opened = jnp.tanh(r / clearance)
    friction = bolt_stiff * r + slip_force * slide
    contact = stop_stiff * (r - clearance * opened)
    f_ref[...] = bolted * friction + (1.0 - bolted) * contact
    tangent_friction = bolt_stiff * dr + slip_force * (1.0 - slide * slide) / slip_speed * dw
    tangent_contact = stop_stiff * opened * opened * dr
    t_ref[...] = bolted * tangent_friction + (1.0 - bolted) * tangent_contact
    for k in range(PARTS):
        out_ref[k, 0:6, :] = f_ref[6 * k : 6 * k + 6]
        out_ref[k, 6:12, :] = t_ref[6 * k : 6 * k + 6]


def reply_kernel(p_ref, force_ref, chunk_ref, up_ref, down_ref, self_ref):
    p = p_ref[0]

    def force(tile):
        return force_ref[tile // 3, :, 128 * (tile % 3) : 128 * (tile % 3 + 1)]

    for d in (0, 1, SLABS - 1):
        chunk_ref[(p - d) & (SLABS - 1)] = jnp.zeros((12, 128), f32)
    for d, tile in ((2, 6), (SLABS - 2, 7)):
        chunk_ref[(p - d) & (SLABS - 1)] = force(tile)
    for d in range(3, SLABS - 2):
        tile, seg = far_place(d)
        chunk_ref[(p - d) & (SLABS - 1)] = lane_roll(force(tile), -seg)
    for k in range(2):
        self_ref[k] = force(k)
        down_ref[k] = force(2 + k)
        up_ref[k] = force(4 + k)


def partner_kernel(idx_ref, force_ref, lin_ref, out_ref, val_ref, sum_ref):
    for tile in range(17):
        val_ref[tile] = -force_ref[tile // 3, :, 128 * (tile % 3) : 128 * (tile % 3 + 1)]
    val_ref[17] = jnp.zeros((12, 128), f32)
    scatter_rows(val_ref, idx_ref, sum_ref)
    for x in range(4):
        out_ref[:, x] = lin_ref[:, x] + sum_ref[:, 128 * x : 128 * (x + 1)].reshape(12, 32, 128)


def final_kernel(p_ref, me_ref, idx_ref, chunk_ref, up_ref, down_ref, self_ref, part_ref, mass_ref,
                 own_ref, y1_ref, y2_ref, y3_ref, x_ref, res_ref, jac_ref, val_ref, sum_ref, acc_ref, sems):
    p = p_ref[0]
    copies = []
    for k in range(PARTS):
        source = x_ref.at[k // 2] if k % 2 else (own_ref, y1_ref, y2_ref, y3_ref)[k // 2].at[0]
        copies.append(pltpu.make_async_copy(source, acc_ref.at[me_ref[0] ^ k], sems.at[k]))
    for copy in copies:
        copy.start()

    def listed(d):
        return chunk_ref[(p + d) & (SLABS - 1)]

    tiles = [self_ref[0], self_ref[1], down_ref[0], down_ref[1], up_ref[0], up_ref[1], listed(2), listed(SLABS - 2)]
    tiles += merge_far(listed, 12, 0.0) + [jnp.zeros((12, 128), f32)]
    for k, tile in enumerate(tiles):
        val_ref[k] = tile
    scatter_rows(val_ref, idx_ref, sum_ref)
    for copy in copies:
        copy.wait()
    for x in range(4):
        acc = jnp.concatenate([acc_ref[2 * x], acc_ref[2 * x + 1]], axis=1)
        added = sum_ref[:, 128 * x : 128 * (x + 1)].reshape(12, 32, 128)
        out = part_ref[:, x] + mass_ref[x][None] * acc + added
        res_ref[:, x] = out[0:6]
        jac_ref[:, x] = out[6:12]


def join_kernel(same_ref, other_ref, *out_refs):
    for k, out in enumerate(out_refs):
        out[0] = same_ref[k + 1]
        out[1] = other_ref[k + 1]


def turn_kernel(own_ref, y1_ref, y2_ref, y3_ref, out_ref):
    for k, ref in enumerate((own_ref, y1_ref, y2_ref, y3_ref)):
        out_ref[k] = ref[1]


def time_kernel(me_ref, same_ref, other_ref, y1_ref, y2_ref, y3_ref, *refs):
    outs, in_ref, out_ref, sems = refs[:4], refs[4], refs[5], refs[6]
    me = me_ref[0]
    pairs = [(same_ref.at[0], in_ref.at[0]), (other_ref.at[0], in_ref.at[1])]
    pairs += [(ref, in_ref.at[pl.ds(2 * k + 2, 2)]) for k, ref in enumerate((y1_ref, y2_ref, y3_ref))]
    copies = [pltpu.make_async_copy(a, b, sems.at[k]) for k, (a, b) in enumerate(pairs)]
    for copy in copies:
        copy.start()
    for copy in copies:
        copy.wait()
    at = [me ^ ((me + k) & (PARTS - 1)) for k in range(PARTS)]
    count = 2 * PARTS

    def step(g, carry):
        field = g // 3
        row = 6 * field + (g - 3 * field)
        x = [in_ref[at[t // 2], row + 3 * (t % 2)] for t in range(count)]
        for t in range(count):
            acc = x[0] * float(MIXED[t, 0])
            for s in range(1, count):
                acc = acc + x[s] * float(MIXED[(t - s) % count, 0])
            out_ref[at[t // 2], row + 3 * (t % 2)] = acc
        return carry

    lax.fori_loop(0, 6, step, 0)
    for k, out in enumerate(outs):
        out[...] = out_ref[2 * k : 2 * k + 2]


def lookup(ids, mat_ref, column, count):
    out = jnp.zeros(ids.shape, f32)
    for m in range(count):
        out = jnp.where(ids == m, mat_ref[m, column], out)
    return out


def stiff_kernel(p_ref, mat_ref, ids_ref, disp_ref, dir_ref, forcing_ref, low_ref, high_ref, out_ref, mass_ref, *, materials):
    p = p_ref[0]
    low = jnp.where(p > 0, low_ref[...], 0.0)
    high = jnp.where(p < SLABS - 1, high_ref[...], 0.0)
    ids = ids_ref[...]
    kx, ky, kz, mass = [lookup(ids, mat_ref, col, materials) for col in range(4)]
    mass_ref[...] = mass
    kx_low = lookup(low[12].astype(i32) - 1, mat_ref, 0, materials)
    kx_high = lookup(high[12].astype(i32) - 1, mat_ref, 0, materials)
    shape = ids.shape
    y = lax.broadcasted_iota(i32, shape, 1)
    z = lax.broadcasted_iota(i32, shape, 2)
    xm = 0.5 * (kx + jnp.concatenate([kx_low[None], kx[:-1]], axis=0))
    xp = 0.5 * (kx + jnp.concatenate([kx[1:], kx_high[None]], axis=0))
    total = xm + xp
    sides = []
    for k, pos, axis in ((ky, y, 1), (kz, z, 2)):
        size = shape[axis]
        for shift, edge in ((1, 0), (size - 1, size - 1)):
            inside = pos != edge
            near = jnp.where(inside, pltpu.roll(k, shift, axis), 0.0)
            side = 0.5 * (k + near)
            total = total + side
            sides.append((jnp.where(inside, side, 0.0), shift, axis))
    for field, ref in enumerate((disp_ref, dir_ref)):
        for c in range(6):
            w = ref[c]
            down = jnp.concatenate([low[6 * field + c][None], w[:-1]], axis=0)
            up = jnp.concatenate([w[1:], high[6 * field + c][None]], axis=0)
            out = total * w - xm * down - xp * up
            for side, shift, axis in sides:
                out = out - side * pltpu.roll(w, shift, axis)
            if field == 0:
                out = out - forcing_ref[c]
            out_ref[6 * field + c] = out


VMEM = 16 * 1024 * 1024


def call(kernel, outs, *args, smem=(0,), away=(), scratch=(), kept=(), limit=VMEM):
    spaces = [pltpu.SMEM if k in smem else pl.ANY if k in away else pltpu.VMEM for k in range(len(args))]
    specs = [pl.BlockSpec(memory_space=space) for space in spaces]
    return pl.pallas_call(
        kernel,
        out_shape=[jax.ShapeDtypeStruct(s, d) for s, d in outs],
        in_specs=specs,
        out_specs=[pl.BlockSpec(memory_space=pl.ANY if k in kept else pltpu.VMEM) for k in range(len(outs))],
        scratch_shapes=list(scratch),
        compiler_params=pltpu.CompilerParams(vmem_limit_bytes=limit),
    )(*args)


def shift(x, by, wrap=True):
    pairs = [(i, (i + by) % SLABS) for i in range(SLABS) if wrap or 0 <= i + by < SLABS]
    return lax.ppermute(x, "mesh", pairs)


def exchange(chunk, *near):
    near = [shift(x, by) for x, by in zip(near, (1, -1))]
    return lax.all_to_all(chunk, "mesh", split_axis=0, concat_axis=0, tiled=True), *near


def swap(x, bit):
    return lax.ppermute(x, "inst", [(i, i ^ bit) for i in range(PARTS)])


def inst_split(x):
    return lax.all_to_all(x, "inst", split_axis=0, concat_axis=0, tiled=True)


def on_device(displacement, direction, forcing, material_ids, materials, joint_owner, joint_local, joint_remote, joint_kind):
    shape = displacement.shape
    fields = (6, 4, 32, 128)
    whole = (12, 4, 32, 128)
    disp = displacement.reshape(fields)
    dire = direction.reshape(fields)
    count = joint_local.shape[0]
    p = lax.axis_index("mesh").astype(i32).reshape(1)
    me = lax.axis_index("inst").astype(i32).reshape(1)
    parts = (768, 512)
    index = ((24, 128), i32)
    half = ((4, 12, 16, 128), f32)
    halo = ((13, 32, 128), f32)

    own_idx, chunk, up, down, own, same, other, high, low = call(
        list_kernel,
        [index, ((SLABS, 16, 128), f32)] + [((2, 16, 128), f32)] * 3 + [half, half, halo, halo],
        p,
        me,
        joint_owner.reshape(1, count),
        joint_local.reshape(1, count),
        joint_remote.reshape(1, count),
        joint_kind.reshape(1, count),
        disp,
        dire,
        material_ids,
        smem=(0, 1),
        away=range(2, 9),
        limit=60 * 1024 * 1024,
        kept=(5, 6, 7, 8),
        scratch=[pltpu.VMEM(parts, bf16), pltpu.VMEM((SIDE, 16, 128), f32)]
        + [pltpu.VMEM((1, count), i32)] * 4
        + [pltpu.VMEM(fields, f32)] * 2
        + [pltpu.VMEM((4, 32, 128), i32), pltpu.VMEM((2, 32, 128), f32)]
        + [pltpu.SemaphoreType.DMA((9,)), pltpu.SemaphoreType.DMA((20,))],
    )
    chunk, up, down = exchange(chunk, up, down)

    pair = ((2, 12, 16, 128), f32)
    other = swap(other, 1)
    joined = call(join_kernel, [pair] * 3, same, other, smem=())
    turned = [swap(x, 2 * k + 2) for k, x in enumerate(joined)]
    blocks = [pltpu.VMEM((PARTS, 12, 16, 128), f32)] * 2
    inertia = call(time_kernel, [pair] * 4, me, same, other, *turned, away=range(1, 6), scratch=blocks + [pltpu.SemaphoreType.DMA((5,))])

    part = ((PARTS, 12, 384), f32)
    fields_parts = call(split_kernel, [(parts, bf16)], disp, dire, smem=())[0]
    far_idx, kind, gap = call(
        gap_kernel,
        [index, ((24, 128), f32), part],
        p, chunk, up, down, own, fields_parts, joined[0],
        away=(6,),
        scratch=[pltpu.VMEM((SIDE, 12, 128), f32)],
    )
    force = call(
        force_kernel,
        [part],
        me, kind, jnp.asarray(SPREAD), inst_split(gap), inertia[0],
        away=(4,),
        scratch=[pltpu.VMEM((48, 384), f32)] * 4,
    )[0]
    force = inst_split(force)
    turned = [inertia[0]] + [swap(inertia[k], 2 * k) for k in (1, 2, 3)]
    two = ((2, 12, 128), f32)
    chunk, *replies, own = call(reply_kernel, [((SLABS, 12, 128), f32), two, two, two], p, force)
    chunk, *replies = exchange(chunk, *replies)

    lin, mass = call(
        lambda *refs: stiff_kernel(*refs, materials=materials.shape[0]),
        [(whole, f32), ((4, 32, 128), f32)],
        p, materials, material_ids, disp, dire, forcing.reshape(fields), shift(high, 1, False), shift(low, -1, False),
        smem=(0, 1),
    )
    other = swap(call(turn_kernel, [half], *turned, smem=())[0], 1)
    adding = [pltpu.VMEM((SIDE, 12, 128), f32), pltpu.VMEM((384, 512), f32)]
    partial = call(partner_kernel, [(whole, f32)], far_idx, force, lin, smem=(), scratch=adding)[0]
    residual, jacobian = call(
        final_kernel,
        [(fields, f32)] * 2,
        p, me, own_idx, chunk, *replies, own, partial, mass, *turned, other,
        smem=(0, 1),
        away=range(9, 14),
        scratch=adding + blocks[:1] + [pltpu.SemaphoreType.DMA((PARTS,))],
    )
    return residual.reshape(shape), jacobian.reshape(shape)


def solution(mesh):
    field = P("inst", None, "mesh", None, None)
    placed = (field, field, field, P("mesh", None, None), P(), P("mesh", None), P("mesh"), P("mesh"), P("mesh"))
    return jax.shard_map(on_device, mesh=mesh, in_specs=placed, out_specs=(field, field), check_vma=False)
```

```python
import jax
import jax.numpy as jnp
import numpy as np
from jax import lax
from jax.experimental import pallas as pl
from jax.experimental.pallas import tpu as pltpu
from jax.sharding import PartitionSpec as P

frequency = 0.6
damping = 0.3
bolt_stiff = 2.0
slip_force = 1.0
slip_speed = 0.5
stop_stiff = 3.0
clearance = 0.3

SLABS = 32
PARTS = 8
SIDE = 18
SEG = 42
f32 = jnp.float32
bf16 = jnp.bfloat16
i32 = jnp.int32


def tables(count):
    offsets = np.arange(count)[:, None] - np.arange(count)[None, :]
    tangent = np.where(offsets == 0, 1.0, np.tan(np.pi * offsets / count))
    first = np.where(offsets == 0, 0.0, 0.5 * np.where(offsets % 2 == 0, 1.0, -1.0) / tangent) * frequency
    return first, first @ first


FIRST, SECOND = tables(2 * PARTS)
MIXED = (SECOND + damping * FIRST).astype(np.float32)
SPREAD = np.kron(FIRST, np.eye(3)).astype(np.float32)


def far_place(offset):
    return 8 + (offset - 3) // 3, SEG * ((offset - 3) % 3)


def fold(rows):
    return jnp.concatenate([rows[0:4], rows[4:8], rows[8:12]], axis=1)


def unfold(rows):
    width = rows.shape[1] // 3
    return jnp.concatenate([rows[:, width * k : width * (k + 1)] for k in range(3)], axis=0)


def part_tile(ref, tile):
    at = 128 * (tile % 3)
    return jnp.concatenate([ref[tile // 3, :, 384 * k + at : 384 * k + at + 128] for k in range(3)], axis=0)


def lane_roll(x, shift):
    shift = shift % 128
    return pltpu.roll(x, shift, x.ndim - 1) if shift else x


def lanes(rows):
    return lax.broadcasted_iota(i32, (rows, 128), 1)


def merge_far(read, rows, fill):
    lane = lanes(rows)
    tiles = []
    for k in range(9):
        parts = [lane_roll(read(3 + 3 * k + s), SEG * s) for s in range(3)]
        tile = jnp.where(lane < SEG, parts[0], jnp.where(lane < 2 * SEG, parts[1], parts[2]))
        tiles.append(jnp.where(lane < 3 * SEG, tile, fill))
    return tiles


def slot_tables(p, owner_ref, local_ref, remote_ref, kind_ref):
    count = owner_ref.shape[1]
    offset = (owner_ref[...] - p) & (SLABS - 1)
    hit = (lax.broadcasted_iota(i32, (SLABS, count), 0) == offset).astype(f32)
    hit16 = hit.astype(bf16)
    before = (lax.broadcasted_iota(i32, (128, 128), 0) < lax.broadcasted_iota(i32, (128, 128), 1)).astype(f32).astype(bf16)
    row = lax.broadcasted_iota(i32, (SLABS, 1), 0)
    far = row - 3
    group = (far * 171) >> 9
    start = 1024 + group * 128 + (far - 3 * group) * SEG
    for value, at in ((0, 0), (1, 256), (SLABS - 1, 512), (2, 768), (SLABS - 2, 896)):
        start = jnp.where(row == value, at, start)
    run = start.astype(f32)
    places = []
    for b in range(count // 128):
        block = hit[:, 128 * b : 128 * (b + 1)]
        earlier = jnp.dot(hit16[:, 128 * b : 128 * (b + 1)], before, preferred_element_type=f32)
        places.append(jnp.sum(block * (earlier + run), axis=0, keepdims=True))
        run = run + jnp.sum(block, axis=1, keepdims=True)
    slot = jnp.concatenate(places, axis=1).astype(i32)
    in_tile = lax.broadcasted_iota(i32, (24, count), 0) == (slot >> 7)
    in_lane = (lax.broadcasted_iota(i32, (128, count), 0) == (slot & 127)).astype(f32).astype(bf16)
    local = local_ref[...]
    remote = remote_ref[...]
    values = (local >> 7, local & 127, remote >> 7, remote & 127, kind_ref[...], jnp.ones_like(local))
    spread = jnp.concatenate([jnp.where(in_tile, v.astype(f32), 0.0) for v in values], axis=0).astype(bf16)
    got = lax.dot_general(spread, in_lane, (((1,), (1,)), ((), ())), preferred_element_type=f32)
    got = [got[24 * k : 24 * (k + 1)] for k in range(6)]
    empty = got[5] - 1.0
    return got[0] * 128.0 + got[1] + empty, got[2] * 128.0 + got[3] + empty, got[4]


def picks(idx_ref, k):
    idx = jnp.concatenate([idx_ref[pl.ds(2 * k, 1), :], idx_ref[pl.ds(2 * k + 1, 1), :]], axis=1)
    code = ((idx >> 12) << 7) | (idx & 127)
    pick = (lax.broadcasted_iota(i32, (512, 256), 0) == code).astype(f32).astype(bf16)
    return pick, lax.broadcasted_iota(i32, (32, 256), 0) == ((idx >> 7) & 31)


def split_fields(disp_ref, dir_ref, parts_ref):
    for field, ref in enumerate((disp_ref, dir_ref)):
        for x in range(4):
            value = ref[:, x].reshape(6 * 32, 128)
            hi = value.astype(bf16)
            cols = slice(128 * x, 128 * (x + 1))
            parts_ref[192 * field : 192 * (field + 1), cols] = hi
            parts_ref[384 + 192 * field : 384 + 192 * (field + 1), cols] = (value - hi.astype(f32)).astype(bf16)


def split_kernel(disp_ref, dir_ref, parts_ref):
    split_fields(disp_ref, dir_ref, parts_ref)


def gather_rows(parts_ref, idx_ref, here_ref):
    def step(k, carry):
        pick, in_y = picks(idx_ref, k)
        rows = jnp.dot(parts_ref[...], pick, preferred_element_type=f32)
        rows = (rows[:384] + rows[384:]).reshape(12, 32, 256)
        got = jnp.sum(jnp.where(in_y[None], rows, 0.0), axis=1)
        here_ref[2 * k, 0:12, :] = got[:, :128]
        here_ref[2 * k + 1, 0:12, :] = got[:, 128:]
        return carry

    lax.fori_loop(0, SIDE // 2, step, 0, unroll=3)


def scatter_rows(val_ref, idx_ref, sum_ref):
    sum_ref[...] = jnp.zeros(sum_ref.shape, f32)
    dims = (((1,), (1,)), ((), ()))

    def step(k, carry):
        pick, in_y = picks(idx_ref, k)
        value = jnp.concatenate([val_ref[2 * k], val_ref[2 * k + 1]], axis=1)
        hi = value.astype(bf16).astype(f32)
        spread = [
            jnp.where(in_y[None], part[:, None, :], 0.0).reshape(384, 256).astype(bf16) for part in (hi, value - hi)
        ]
        got = lax.dot_general(spread[0], pick, dims, preferred_element_type=f32)
        got = got + lax.dot_general(spread[1], pick, dims, preferred_element_type=f32)
        sum_ref[...] = sum_ref[...] + got
        return carry

    lax.fori_loop(0, SIDE // 2, step, 0, unroll=3)


def list_kernel(p_ref, me_ref, owner_hbm, local_hbm, remote_hbm, kind_hbm, disp_hbm, dir_hbm, ids_hbm,
                idx_ref, chunk_ref, up_hbm, down_hbm, self_ref, same_hbm, other_hbm,
                parts_ref, rows_ref, owner_ref, local_ref, remote_ref, kind_ref, disp_ref, dir_ref, ids_ref, near_ref,
                sems, more_sems):
    p = p_ref[0]
    pairs = ((owner_hbm, owner_ref), (local_hbm, local_ref), (remote_hbm, remote_ref), (kind_hbm, kind_ref),
             (disp_hbm, disp_ref), (dir_hbm, dir_ref), (ids_hbm, ids_ref))
    copies = [pltpu.make_async_copy(a, b, sems.at[k]) for k, (a, b) in enumerate(pairs)]
    for copy in copies:
        copy.start()
    for copy in copies[:4]:
        copy.wait()
    mine, theirs, kind = slot_tables(p, owner_ref, local_ref, remote_ref, kind_ref)
    idx_ref[...] = mine.astype(i32)
    for tile in range(SIDE):
        rows_ref[tile, 12:13, :] = theirs[tile : tile + 1]
        rows_ref[tile, 13:14, :] = kind[tile : tile + 1]
        rows_ref[tile, 14:16, :] = jnp.zeros((2, 128), f32)
    for copy in copies[4:]:
        copy.wait()
    moves = []
    for field, ref in enumerate((disp_ref, dir_ref)):
        part = pl.ds(6 * field, 6)
        for k in range(PARTS):
            block = me_ref[0] ^ k
            rows = pl.ds(pl.multiple_of(16 * (block & 1), 16), 16)
            moves.append((ref.at[:, block >> 1, rows, :], (same_hbm, other_hbm)[k % 2].at[k // 2, part]))
        moves.append((ref.at[:, 3], up_hbm.at[pl.ds(1 + 6 * field, 6)]))
        moves.append((ref.at[:, 0], down_hbm.at[pl.ds(1 + 6 * field, 6)]))
    moves = [pltpu.make_async_copy(a, b, more_sems.at[k]) for k, (a, b) in enumerate(moves)]
    for move in moves:
        move.start()
    split_fields(disp_ref, dir_ref, parts_ref)
    near_ref[2] = (ids_ref[3] + 1).astype(f32)
    near_ref[3] = (ids_ref[0] + 1).astype(f32)
    gather_rows(parts_ref, idx_ref, rows_ref)
    for k in range(2):
        near_ref[k] = rows_ref[2 + 2 * k : 4 + 2 * k].reshape(32, 128)
    ends = ((near_ref.at[0], up_hbm.at[0]), (near_ref.at[1], down_hbm.at[0]),
            (near_ref.at[2], up_hbm.at[13]), (near_ref.at[3], down_hbm.at[13]))
    ends = [pltpu.make_async_copy(a, b, sems.at[7 + k]) for k, (a, b) in enumerate(ends)]
    for end in ends:
        end.start()
    for d in (0, 1, SLABS - 1):
        chunk_ref[(p + d) & (SLABS - 1)] = jnp.zeros((16, 128), f32)
    for d, tile in ((2, 6), (SLABS - 2, 7)):
        chunk_ref[(p + d) & (SLABS - 1)] = rows_ref[tile]
    for d in range(3, SLABS - 2):
        tile, seg = far_place(d)
        chunk_ref[(p + d) & (SLABS - 1)] = lane_roll(rows_ref[tile], -seg)
    self_ref[...] = rows_ref[0:2]
    for move in moves + ends:
        move.wait()


def gap_kernel(p_ref, chunk_ref, up_ref, down_ref, self_ref, parts_ref, after_ref,
               idx_ref, kind_ref, gap_ref, here_ref):
    p = p_ref[0]

    def asked(d):
        return chunk_ref[(p - d) & (SLABS - 1)]

    near = [ref[0, 16 * k : 16 * (k + 1), :] for ref in (up_ref, down_ref) for k in range(2)]
    tiles = [self_ref[0], self_ref[1]] + near + [asked(2), asked(SLABS - 2)]
    tiles += merge_far(asked, 16, 0.0)
    beyond = lanes(1) >= 3 * SEG
    rows = [t[12:13] for t in tiles[:8]] + [jnp.where(beyond, -1.0, t[12:13]) for t in tiles[8:]]
    idx_ref[...] = jnp.concatenate(rows + [jnp.full((7, 128), -1.0, f32)], axis=0).astype(i32)
    kind_ref[...] = jnp.concatenate([t[13:14] for t in tiles] + [jnp.zeros((7, 128), f32)], axis=0)
    gather_rows(parts_ref, idx_ref, here_ref)
    for tile in range(24):
        gap = tiles[tile][0:12] - here_ref[tile] if tile < 17 else jnp.zeros((12, 128), f32)
        at = 128 * (tile % 3)
        for k in range(3):
            gap_ref[tile // 3, :, 384 * k + at : 384 * k + at + 128] = gap[4 * k : 4 * k + 4]


def force_kernel(me_ref, kind_ref, spread_ref, gap_ref, after_ref, out_ref, r_ref, d_ref, f_ref, t_ref):
    me = me_ref[0]
    for k in range(PARTS):
        gap = unfold(gap_ref[k])
        r_ref[6 * k : 6 * k + 6] = gap[0:6]
        d_ref[6 * k : 6 * k + 6] = gap[6:12]
    r = r_ref[...]
    dr = d_ref[...]
    w = jnp.dot(spread_ref[...], r, precision=lax.Precision.HIGHEST, preferred_element_type=f32)
    dw = jnp.dot(spread_ref[...], dr, precision=lax.Precision.HIGHEST, preferred_element_type=f32)
    bolted = jnp.concatenate([kind_ref[pl.ds(3 * me + k, 1), :] for k in range(3)], axis=1)
    slide = jnp.tanh(w / slip_speed)
    opened = jnp.tanh(r / clearance)
    friction = bolt_stiff * r + slip_force * slide
    contact = stop_stiff * (r - clearance * opened)
    f_ref[...] = bolted * friction + (1.0 - bolted) * contact
    tangent_friction = bolt_stiff * dr + slip_force * (1.0 - slide * slide) / slip_speed * dw
    tangent_contact = stop_stiff * opened * opened * dr
    t_ref[...] = bolted * tangent_friction + (1.0 - bolted) * tangent_contact
    for k in range(PARTS):
        out_ref[k] = fold(jnp.concatenate([f_ref[6 * k : 6 * k + 6], t_ref[6 * k : 6 * k + 6]], axis=0))


def reply_kernel(p_ref, force_ref, chunk_ref, up_ref, down_ref, self_ref):
    p = p_ref[0]
    for d in (0, 1, SLABS - 1):
        chunk_ref[(p - d) & (SLABS - 1)] = jnp.zeros((4, 384), f32)
    for d, tile in ((2, 6), (SLABS - 2, 7)):
        chunk_ref[(p - d) & (SLABS - 1)] = fold(part_tile(force_ref, tile))
    for d in range(3, SLABS - 2):
        tile, seg = far_place(d)
        chunk_ref[(p - d) & (SLABS - 1)] = fold(lane_roll(part_tile(force_ref, tile), -seg))
    for k in range(2):
        self_ref[k] = part_tile(force_ref, k)
        down_ref[k] = part_tile(force_ref, 2 + k)
        up_ref[k] = part_tile(force_ref, 4 + k)


def partner_kernel(idx_ref, force_ref, lin_ref, out_ref, val_ref, sum_ref):
    for tile in range(17):
        val_ref[tile] = -part_tile(force_ref, tile)
    val_ref[17] = jnp.zeros((12, 128), f32)
    scatter_rows(val_ref, idx_ref, sum_ref)
    for x in range(4):
        out_ref[:, x] = lin_ref[:, x] + sum_ref[:, 128 * x : 128 * (x + 1)].reshape(12, 32, 128)


def final_kernel(p_ref, me_ref, idx_ref, chunk_ref, up_ref, down_ref, self_ref, part_ref, mass_ref,
                 own_ref, y1_ref, y2_ref, y3_ref, x_ref, res_ref, jac_ref, val_ref, sum_ref, acc_ref, sems):
    p = p_ref[0]
    copies = []
    for k in range(PARTS):
        source = x_ref.at[k // 2] if k % 2 else (own_ref, y1_ref, y2_ref, y3_ref)[k // 2].at[0]
        copies.append(pltpu.make_async_copy(source, acc_ref.at[me_ref[0] ^ k], sems.at[k]))
    for copy in copies:
        copy.start()

    def listed(d):
        return unfold(chunk_ref[(p + d) & (SLABS - 1)])

    tiles = [self_ref[0], self_ref[1], down_ref[0], down_ref[1], up_ref[0], up_ref[1], listed(2), listed(SLABS - 2)]
    tiles += merge_far(listed, 12, 0.0) + [jnp.zeros((12, 128), f32)]
    for k, tile in enumerate(tiles):
        val_ref[k] = tile
    scatter_rows(val_ref, idx_ref, sum_ref)
    for copy in copies:
        copy.wait()
    for x in range(4):
        acc = jnp.concatenate([acc_ref[2 * x], acc_ref[2 * x + 1]], axis=1)
        added = sum_ref[:, 128 * x : 128 * (x + 1)].reshape(12, 32, 128)
        out = part_ref[:, x] + mass_ref[x][None] * acc + added
        res_ref[:, x] = out[0:6]
        jac_ref[:, x] = out[6:12]


def join_kernel(same_ref, other_ref, *out_refs):
    for k, out in enumerate(out_refs):
        out[0] = same_ref[k + 1]
        out[1] = other_ref[k + 1]


def turn_kernel(own_ref, y1_ref, y2_ref, y3_ref, out_ref):
    for k, ref in enumerate((own_ref, y1_ref, y2_ref, y3_ref)):
        out_ref[k] = ref[1]


def time_kernel(me_ref, same_ref, other_ref, y1_ref, y2_ref, y3_ref, *refs):
    outs, in_ref, out_ref, sems = refs[:4], refs[4], refs[5], refs[6]
    me = me_ref[0]
    pairs = [(same_ref.at[0], in_ref.at[0]), (other_ref.at[0], in_ref.at[1])]
    pairs += [(ref, in_ref.at[pl.ds(2 * k + 2, 2)]) for k, ref in enumerate((y1_ref, y2_ref, y3_ref))]
    copies = [pltpu.make_async_copy(a, b, sems.at[k]) for k, (a, b) in enumerate(pairs)]
    for copy in copies:
        copy.start()
    for copy in copies:
        copy.wait()
    at = [me ^ ((me + k) & (PARTS - 1)) for k in range(PARTS)]
    count = 2 * PARTS

    def step(g, carry):
        field = g // 3
        row = 6 * field + (g - 3 * field)
        x = [in_ref[at[t // 2], row + 3 * (t % 2)] for t in range(count)]
        for t in range(count):
            acc = x[0] * float(MIXED[t, 0])
            for s in range(1, count):
                acc = acc + x[s] * float(MIXED[(t - s) % count, 0])
            out_ref[at[t // 2], row + 3 * (t % 2)] = acc
        return carry

    lax.fori_loop(0, 6, step, 0)
    for k, out in enumerate(outs):
        out[...] = out_ref[2 * k : 2 * k + 2]


def lookup(ids, mat_ref, column, count):
    out = jnp.zeros(ids.shape, f32)
    for m in range(count):
        out = jnp.where(ids == m, mat_ref[m, column], out)
    return out


def stiff_kernel(p_ref, mat_ref, ids_ref, disp_ref, dir_ref, forcing_ref, up_ref, down_ref, out_ref, mass_ref, *, materials):
    p = p_ref[0]
    low = jnp.where(p > 0, up_ref[1:14], 0.0)
    high = jnp.where(p < SLABS - 1, down_ref[1:14], 0.0)
    ids = ids_ref[...]
    kx, ky, kz, mass = [lookup(ids, mat_ref, col, materials) for col in range(4)]
    mass_ref[...] = mass
    kx_low = lookup(low[12].astype(i32) - 1, mat_ref, 0, materials)
    kx_high = lookup(high[12].astype(i32) - 1, mat_ref, 0, materials)
    shape = ids.shape
    y = lax.broadcasted_iota(i32, shape, 1)
    z = lax.broadcasted_iota(i32, shape, 2)
    xm = 0.5 * (kx + jnp.concatenate([kx_low[None], kx[:-1]], axis=0))
    xp = 0.5 * (kx + jnp.concatenate([kx[1:], kx_high[None]], axis=0))
    total = xm + xp
    sides = []
    for k, pos, axis in ((ky, y, 1), (kz, z, 2)):
        size = shape[axis]
        for shift, edge in ((1, 0), (size - 1, size - 1)):
            inside = pos != edge
            near = jnp.where(inside, pltpu.roll(k, shift, axis), 0.0)
            side = 0.5 * (k + near)
            total = total + side
            sides.append((jnp.where(inside, side, 0.0), shift, axis))
    for field, ref in enumerate((disp_ref, dir_ref)):
        for c in range(6):
            w = ref[c]
            down = jnp.concatenate([low[6 * field + c][None], w[:-1]], axis=0)
            up = jnp.concatenate([w[1:], high[6 * field + c][None]], axis=0)
            out = total * w - xm * down - xp * up
            for side, shift, axis in sides:
                out = out - side * pltpu.roll(w, shift, axis)
            if field == 0:
                out = out - forcing_ref[c]
            out_ref[6 * field + c] = out


VMEM = 16 * 1024 * 1024


def call(kernel, outs, *args, smem=(0,), away=(), scratch=(), kept=(), limit=VMEM):
    spaces = [pltpu.SMEM if k in smem else pl.ANY if k in away else pltpu.VMEM for k in range(len(args))]
    specs = [pl.BlockSpec(memory_space=space) for space in spaces]
    return pl.pallas_call(
        kernel,
        out_shape=[jax.ShapeDtypeStruct(s, d) for s, d in outs],
        in_specs=specs,
        out_specs=[pl.BlockSpec(memory_space=pl.ANY if k in kept else pltpu.VMEM) for k in range(len(outs))],
        scratch_shapes=list(scratch),
        compiler_params=pltpu.CompilerParams(vmem_limit_bytes=limit),
    )(*args)


def shift(x, by):
    return lax.ppermute(x, "mesh", [(i, (i + by) % SLABS) for i in range(SLABS)])


def exchange(chunk, up, down):
    up, down = shift(up, 1), shift(down, -1)
    return lax.all_to_all(chunk, "mesh", split_axis=0, concat_axis=0, tiled=True), up, down


def swap(x, bit):
    return lax.ppermute(x, "inst", [(i, i ^ bit) for i in range(PARTS)])


def inst_split(x):
    return lax.all_to_all(x, "inst", split_axis=0, concat_axis=0, tiled=True)


def on_device(displacement, direction, forcing, material_ids, materials, joint_owner, joint_local, joint_remote, joint_kind):
    shape = displacement.shape
    fields = (6, 4, 32, 128)
    whole = (12, 4, 32, 128)
    disp = displacement.reshape(fields)
    dire = direction.reshape(fields)
    count = joint_local.shape[0]
    p = lax.axis_index("mesh").astype(i32).reshape(1)
    me = lax.axis_index("inst").astype(i32).reshape(1)
    parts = (768, 512)
    index = ((24, 128), i32)
    half = ((4, 12, 16, 128), f32)
    near = ((14, 32, 128), f32)

    own_idx, chunk, up, down, own, same, other = call(
        list_kernel,
        [index, ((SLABS, 16, 128), f32), near, near, ((2, 16, 128), f32), half, half],
        p,
        me,
        joint_owner.reshape(1, count),
        joint_local.reshape(1, count),
        joint_remote.reshape(1, count),
        joint_kind.reshape(1, count),
        disp,
        dire,
        material_ids,
        smem=(0, 1),
        away=range(2, 9),
        limit=60 * 1024 * 1024,
        kept=(2, 3, 5, 6),
        scratch=[pltpu.VMEM(parts, bf16), pltpu.VMEM((SIDE, 16, 128), f32)]
        + [pltpu.VMEM((1, count), i32)] * 4
        + [pltpu.VMEM(fields, f32)] * 2
        + [pltpu.VMEM((4, 32, 128), i32), pltpu.VMEM((4, 32, 128), f32)]
        + [pltpu.SemaphoreType.DMA((11,)), pltpu.SemaphoreType.DMA((20,))],
    )
    chunk, up, down = exchange(chunk, up, down)

    pair = ((2, 12, 16, 128), f32)
    other = swap(other, 1)
    joined = call(join_kernel, [pair] * 3, same, other, smem=())
    turned = [swap(x, 2 * k + 2) for k, x in enumerate(joined)]
    blocks = [pltpu.VMEM((PARTS, 12, 16, 128), f32)] * 2
    inertia = call(time_kernel, [pair] * 4, me, same, other, *turned, away=range(1, 6), scratch=blocks + [pltpu.SemaphoreType.DMA((5,))])

    part = ((PARTS, 4, 1152), f32)
    fields_parts = call(split_kernel, [(parts, bf16)], disp, dire, smem=())[0]
    far_idx, kind, gap = call(
        gap_kernel,
        [index, ((24, 128), f32), part],
        p, chunk, up, down, own, fields_parts, joined[0],
        away=(6,),
        scratch=[pltpu.VMEM((SIDE, 12, 128), f32)],
    )
    force = call(
        force_kernel,
        [part],
        me, kind, jnp.asarray(SPREAD), inst_split(gap), inertia[0],
        away=(4,),
        scratch=[pltpu.VMEM((48, 384), f32)] * 4,
    )[0]
    force = inst_split(force)
    turned = [inertia[0]] + [swap(inertia[k], 2 * k) for k in (1, 2, 3)]
    two = ((2, 12, 128), f32)
    chunk, up2, down2, own = call(reply_kernel, [((SLABS, 4, 384), f32), two, two, two], p, force)
    chunk, up2, down2 = exchange(chunk, up2, down2)

    lin, mass = call(
        lambda *refs: stiff_kernel(*refs, materials=materials.shape[0]),
        [(whole, f32), ((4, 32, 128), f32)],
        p, materials, material_ids, disp, dire, forcing.reshape(fields), up, down,
        smem=(0, 1),
    )
    other = swap(call(turn_kernel, [half], *turned, smem=())[0], 1)
    adding = [pltpu.VMEM((SIDE, 12, 128), f32), pltpu.VMEM((384, 512), f32)]
    partial = call(partner_kernel, [(whole, f32)], far_idx, force, lin, smem=(), scratch=adding)[0]
    residual, jacobian = call(
        final_kernel,
        [(fields, f32)] * 2,
        p, me, own_idx, chunk, up2, down2, own, partial, mass, *turned, other,
        smem=(0, 1),
        away=range(9, 14),
        scratch=adding + blocks[:1] + [pltpu.SemaphoreType.DMA((PARTS,))],
    )
    return residual.reshape(shape), jacobian.reshape(shape)


def solution(mesh):
    field = P("inst", None, "mesh", None, None)
    placed = (field, field, field, P("mesh", None, None), P(), P("mesh", None), P("mesh"), P("mesh"), P("mesh"))
    return jax.shard_map(on_device, mesh=mesh, in_specs=placed, out_specs=(field, field), check_vma=False)
```

```python
import jax
import jax.numpy as jnp
import numpy as np
from jax import lax
from jax.experimental import pallas as pl
from jax.experimental.pallas import tpu as pltpu
from jax.sharding import PartitionSpec as P

frequency = 0.6
damping = 0.3
bolt_stiff = 2.0
slip_force = 1.0
slip_speed = 0.5
stop_stiff = 3.0
clearance = 0.3

SLABS = 32
PARTS = 8
SIDE = 18
SEG = 42
f32 = jnp.float32
bf16 = jnp.bfloat16
i32 = jnp.int32


def tables(count):
    offsets = np.arange(count)[:, None] - np.arange(count)[None, :]
    tangent = np.where(offsets == 0, 1.0, np.tan(np.pi * offsets / count))
    first = np.where(offsets == 0, 0.0, 0.5 * np.where(offsets % 2 == 0, 1.0, -1.0) / tangent) * frequency
    return first, first @ first


FIRST, SECOND = tables(2 * PARTS)
MIXED = (SECOND + damping * FIRST).astype(np.float32)


def rate_tables():
    table = np.zeros((PARTS, 2, 16, PARTS, 16), np.float32)
    for me in range(PARTS):
        for odd in range(2):
            for row in range(16):
                channel = row if row < 8 else row - 4 * odd
                if channel < 8 and row >= 8 or channel >= 12:
                    continue
                field, s, c = channel // 6, channel // 3 % 2, channel % 3
                for t in range(2):
                    table[me, odd, 6 * field + 3 * t + c, :, row] = FIRST[2 * me + t, s::2]
    return table.reshape(PARTS, 2, 16, 16 * PARTS)


RATES = rate_tables()


def far_place(offset):
    return 8 + (offset - 3) // 3, SEG * ((offset - 3) % 3)


def fold(rows):
    return jnp.concatenate([rows[0:4], rows[4:8], rows[8:12]], axis=1)


def unfold(rows):
    width = rows.shape[1] // 3
    return jnp.concatenate([rows[:, width * k : width * (k + 1)] for k in range(3)], axis=0)


def lane_roll(x, shift):
    shift = shift % 128
    return pltpu.roll(x, shift, x.ndim - 1) if shift else x


def lanes(rows):
    return lax.broadcasted_iota(i32, (rows, 128), 1)


def merge_far(read, rows, fill):
    lane = lanes(rows)
    tiles = []
    for k in range(9):
        parts = [lane_roll(read(3 + 3 * k + s), SEG * s) for s in range(3)]
        tile = jnp.where(lane < SEG, parts[0], jnp.where(lane < 2 * SEG, parts[1], parts[2]))
        tiles.append(jnp.where(lane < 3 * SEG, tile, fill))
    return tiles


def slot_tables(p, owner_ref, local_ref, remote_ref, kind_ref):
    count = owner_ref.shape[1]
    offset = (owner_ref[...] - p) & (SLABS - 1)
    hit = (lax.broadcasted_iota(i32, (SLABS, count), 0) == offset).astype(f32)
    hit16 = hit.astype(bf16)
    before = (lax.broadcasted_iota(i32, (128, 128), 0) < lax.broadcasted_iota(i32, (128, 128), 1)).astype(f32).astype(bf16)
    row = lax.broadcasted_iota(i32, (SLABS, 1), 0)
    far = row - 3
    group = (far * 171) >> 9
    start = 1024 + group * 128 + (far - 3 * group) * SEG
    for value, at in ((0, 0), (1, 256), (SLABS - 1, 512), (2, 768), (SLABS - 2, 896)):
        start = jnp.where(row == value, at, start)
    run = start.astype(f32)
    places = []
    for b in range(count // 128):
        block = hit[:, 128 * b : 128 * (b + 1)]
        earlier = jnp.dot(hit16[:, 128 * b : 128 * (b + 1)], before, preferred_element_type=f32)
        places.append(jnp.sum(block * (earlier + run), axis=0, keepdims=True))
        run = run + jnp.sum(block, axis=1, keepdims=True)
    slot = jnp.concatenate(places, axis=1).astype(i32)
    in_tile = lax.broadcasted_iota(i32, (24, count), 0) == (slot >> 7)
    in_lane = (lax.broadcasted_iota(i32, (128, count), 0) == (slot & 127)).astype(f32).astype(bf16)
    local = local_ref[...]
    remote = remote_ref[...]
    values = (local >> 7, local & 127, remote >> 7, remote & 127, kind_ref[...], jnp.ones_like(local))
    spread = jnp.concatenate([jnp.where(in_tile, v.astype(f32), 0.0) for v in values], axis=0).astype(bf16)
    got = lax.dot_general(spread, in_lane, (((1,), (1,)), ((), ())), preferred_element_type=f32)
    got = [got[24 * k : 24 * (k + 1)] for k in range(6)]
    empty = got[5] - 1.0
    return got[0] * 128.0 + got[1] + empty, got[2] * 128.0 + got[3] + empty, got[4]


def picks(idx_ref, k):
    idx = jnp.concatenate([idx_ref[pl.ds(2 * k, 1), :], idx_ref[pl.ds(2 * k + 1, 1), :]], axis=1)
    code = ((idx >> 12) << 7) | (idx & 127)
    pick = (lax.broadcasted_iota(i32, (512, 256), 0) == code).astype(f32).astype(bf16)
    return pick, lax.broadcasted_iota(i32, (32, 256), 0) == ((idx >> 7) & 31)


def split_fields(disp_ref, dir_ref, parts_ref):
    for field, ref in enumerate((disp_ref, dir_ref)):
        for x in range(4):
            value = ref[:, x].reshape(6 * 32, 128)
            hi = value.astype(bf16)
            cols = slice(128 * x, 128 * (x + 1))
            parts_ref[192 * field : 192 * (field + 1), cols] = hi
            parts_ref[384 + 192 * field : 384 + 192 * (field + 1), cols] = (value - hi.astype(f32)).astype(bf16)


def split_kernel(disp_ref, dir_ref, parts_ref):
    split_fields(disp_ref, dir_ref, parts_ref)


def gather_rows(parts_ref, idx_ref, here_ref):
    def step(k, carry):
        pick, in_y = picks(idx_ref, k)
        rows = jnp.dot(parts_ref[...], pick, preferred_element_type=f32)
        rows = (rows[:384] + rows[384:]).reshape(12, 32, 256)
        got = jnp.sum(jnp.where(in_y[None], rows, 0.0), axis=1)
        here_ref[2 * k, 0:12, :] = got[:, :128]
        here_ref[2 * k + 1, 0:12, :] = got[:, 128:]
        return carry

    lax.fori_loop(0, SIDE // 2, step, 0, unroll=3)


def scatter_rows(val_ref, idx_ref, sum_ref):
    sum_ref[...] = jnp.zeros(sum_ref.shape, f32)
    dims = (((1,), (1,)), ((), ()))

    def step(k, carry):
        pick, in_y = picks(idx_ref, k)
        value = jnp.concatenate([val_ref[2 * k], val_ref[2 * k + 1]], axis=1)
        hi = value.astype(bf16).astype(f32)
        spread = [
            jnp.where(in_y[None], part[:, None, :], 0.0).reshape(384, 256).astype(bf16) for part in (hi, value - hi)
        ]
        got = lax.dot_general(spread[0], pick, dims, preferred_element_type=f32)
        got = got + lax.dot_general(spread[1], pick, dims, preferred_element_type=f32)
        sum_ref[...] = sum_ref[...] + got
        return carry

    lax.fori_loop(0, SIDE // 2, step, 0, unroll=3)


def list_kernel(p_ref, me_ref, owner_hbm, local_hbm, remote_hbm, kind_hbm, disp_hbm, dir_hbm, ids_hbm,
                idx_ref, chunk_ref, up_ref, down_ref, self_ref, same_hbm, other_hbm, high_hbm, low_hbm,
                parts_ref, rows_ref, owner_ref, local_ref, remote_ref, kind_ref, disp_ref, dir_ref, ids_ref, edge_ref,
                sems, more_sems):
    p = p_ref[0]
    pairs = ((owner_hbm, owner_ref), (local_hbm, local_ref), (remote_hbm, remote_ref), (kind_hbm, kind_ref),
             (disp_hbm, disp_ref), (dir_hbm, dir_ref), (ids_hbm, ids_ref))
    copies = [pltpu.make_async_copy(a, b, sems.at[k]) for k, (a, b) in enumerate(pairs)]
    for copy in copies:
        copy.start()
    for copy in copies[:4]:
        copy.wait()
    mine, theirs, kind = slot_tables(p, owner_ref, local_ref, remote_ref, kind_ref)
    idx_ref[...] = mine.astype(i32)
    for tile in range(SIDE):
        rows_ref[tile, 12:13, :] = theirs[tile : tile + 1]
        rows_ref[tile, 13:14, :] = kind[tile : tile + 1]
        rows_ref[tile, 14:16, :] = jnp.zeros((2, 128), f32)
    for copy in copies[4:]:
        copy.wait()
    moves = []
    for field, ref in enumerate((disp_ref, dir_ref)):
        part = pl.ds(6 * field, 6)
        for k in range(PARTS):
            block = me_ref[0] ^ k
            rows = pl.ds(pl.multiple_of(16 * (block & 1), 16), 16)
            moves.append((ref.at[:, block >> 1, rows, :], (same_hbm, other_hbm)[k % 2].at[k // 2, part]))
        moves.append((ref.at[:, 3], high_hbm.at[pl.ds(6 * field, 6)]))
        moves.append((ref.at[:, 0], low_hbm.at[pl.ds(6 * field, 6)]))
    moves = [pltpu.make_async_copy(a, b, more_sems.at[k]) for k, (a, b) in enumerate(moves)]
    for move in moves:
        move.start()
    split_fields(disp_ref, dir_ref, parts_ref)
    ends = []
    for k, (x, hbm) in enumerate(((3, high_hbm), (0, low_hbm))):
        edge_ref[k] = (ids_ref[x] + 1).astype(f32)
        ends.append(pltpu.make_async_copy(edge_ref.at[k], hbm.at[12], sems.at[7 + k]))
    for end in ends:
        end.start()
    gather_rows(parts_ref, idx_ref, rows_ref)
    for d in (0, 1, SLABS - 1):
        chunk_ref[(p + d) & (SLABS - 1)] = jnp.zeros((16, 128), f32)
    for d, tile in ((2, 6), (SLABS - 2, 7)):
        chunk_ref[(p + d) & (SLABS - 1)] = rows_ref[tile]
    for d in range(3, SLABS - 2):
        tile, seg = far_place(d)
        chunk_ref[(p + d) & (SLABS - 1)] = lane_roll(rows_ref[tile], -seg)
    self_ref[...] = rows_ref[0:2]
    up_ref[...] = rows_ref[2:4]
    down_ref[...] = rows_ref[4:6]
    for move in moves + ends:
        move.wait()


def gap_kernel(p_ref, chunk_ref, up_ref, down_ref, self_ref, parts_ref, after1, after2, after3,
               idx_ref, kind_ref, gap_hbm, here_ref, gap_ref, sems):
    p = p_ref[0]

    def asked(d):
        return chunk_ref[(p - d) & (SLABS - 1)]

    tiles = [self_ref[0], self_ref[1], up_ref[0], up_ref[1], down_ref[0], down_ref[1], asked(2), asked(SLABS - 2)]
    tiles += merge_far(asked, 16, 0.0)
    beyond = lanes(1) >= 3 * SEG
    rows = [t[12:13] for t in tiles[:8]] + [jnp.where(beyond, -1.0, t[12:13]) for t in tiles[8:]]
    idx_ref[...] = jnp.concatenate(rows + [jnp.full((7, 128), -1.0, f32)], axis=0).astype(i32)
    kind_ref[...] = jnp.concatenate([t[13:14] for t in tiles] + [jnp.zeros((7, 128), f32)], axis=0)
    gather_rows(parts_ref, idx_ref, here_ref)
    for m in range(9):
        low = []
        for tile in (2 * m, 2 * m + 1):
            gap = tiles[tile][0:12] - here_ref[tile] if tile < 17 else jnp.zeros((12, 128), f32)
            low.append(gap[8:12])
            if tile < 17:
                gap_ref[8 * tile : 8 * tile + 8] = gap[0:8]
        gap_ref[8 * (17 + m) : 8 * (18 + m)] = jnp.concatenate(low, axis=0)
    copies = [pltpu.make_async_copy(gap_ref, gap_hbm.at[k], sems.at[k]) for k in range(PARTS)]
    for copy in copies:
        copy.start()
    for copy in copies:
        copy.wait()


def force_kernel(p_ref, me_ref, kind_ref, rates_ref, gap_ref, after1, after2,
                 val_ref, chunk_ref, up_ref, down_ref, self_ref, all_ref):
    p = p_ref[0]
    me = me_ref[0]
    for odd in range(2):
        count = 9 - odd
        for m in range(count):
            for k in range(PARTS):
                tile = 2 * m + odd
                all_ref[16 * k : 16 * k + 8, 128 * m : 128 * (m + 1)] = gap_ref[k, 8 * tile : 8 * tile + 8]
                all_ref[16 * k + 8 : 16 * k + 16, 128 * m : 128 * (m + 1)] = gap_ref[k, 8 * (17 + m) : 8 * (18 + m)]
        width = 128 * count
        rates = jnp.dot(
            rates_ref[me, odd], all_ref[:, :width], precision=lax.Precision.HIGHEST, preferred_element_type=f32
        )
        mine = all_ref[pl.ds(pl.multiple_of(16 * me, 16), 16), :width]
        mine = jnp.concatenate([mine[0:8], mine[8 + 4 * odd : 12 + 4 * odd]], axis=0)
        r, dr, w, dw = mine[0:6], mine[6:12], rates[0:6], rates[6:12]
        bolted = jnp.concatenate([kind_ref[2 * m + odd : 2 * m + odd + 1] for m in range(count)], axis=1)
        slide = jnp.tanh(w / slip_speed)
        opened = jnp.tanh(r / clearance)
        friction = bolt_stiff * r + slip_force * slide
        contact = stop_stiff * (r - clearance * opened)
        force = bolted * friction + (1.0 - bolted) * contact
        tangent_friction = bolt_stiff * dr + slip_force * (1.0 - slide * slide) / slip_speed * dw
        tangent_contact = stop_stiff * opened * opened * dr
        tangent = bolted * tangent_friction + (1.0 - bolted) * tangent_contact
        both = jnp.concatenate([force, tangent], axis=0)
        for m in range(count):
            val_ref[2 * m + odd] = both[:, 128 * m : 128 * (m + 1)]
    val_ref[17] = jnp.zeros((12, 128), f32)
    for d in (0, 1, SLABS - 1):
        chunk_ref[(p - d) & (SLABS - 1)] = jnp.zeros((4, 384), f32)
    for d, tile in ((2, 6), (SLABS - 2, 7)):
        chunk_ref[(p - d) & (SLABS - 1)] = fold(val_ref[tile])
    for d in range(3, SLABS - 2):
        tile, seg = far_place(d)
        chunk_ref[(p - d) & (SLABS - 1)] = fold(lane_roll(val_ref[tile], -seg))
    self_ref[...] = val_ref[0:2]
    down_ref[...] = val_ref[2:4]
    up_ref[...] = val_ref[4:6]


def partner_kernel(idx_ref, val_ref, lin_ref, out_ref, sum_ref):
    scatter_rows(val_ref, idx_ref, sum_ref)
    for x in range(4):
        out_ref[:, x] = lin_ref[:, x] - sum_ref[:, 128 * x : 128 * (x + 1)].reshape(12, 32, 128)


def final_kernel(p_ref, me_ref, idx_ref, chunk_ref, up_ref, down_ref, self_ref, part_ref, mass_ref,
                 own_ref, y1_ref, y2_ref, y3_ref, x_ref, res_ref, jac_ref, val_ref, sum_ref, acc_ref, sems):
    p = p_ref[0]
    copies = []
    for k in range(PARTS):
        source = x_ref.at[k // 2] if k % 2 else (own_ref, y1_ref, y2_ref, y3_ref)[k // 2].at[0]
        copies.append(pltpu.make_async_copy(source, acc_ref.at[me_ref[0] ^ k], sems.at[k]))
    for copy in copies:
        copy.start()

    def listed(d):
        return unfold(chunk_ref[(p + d) & (SLABS - 1)])

    tiles = [self_ref[0], self_ref[1], down_ref[0], down_ref[1], up_ref[0], up_ref[1], listed(2), listed(SLABS - 2)]
    tiles += merge_far(listed, 12, 0.0) + [jnp.zeros((12, 128), f32)]
    for k, tile in enumerate(tiles):
        val_ref[k] = tile
    scatter_rows(val_ref, idx_ref, sum_ref)
    for copy in copies:
        copy.wait()
    for x in range(4):
        acc = jnp.concatenate([acc_ref[2 * x], acc_ref[2 * x + 1]], axis=1)
        added = sum_ref[:, 128 * x : 128 * (x + 1)].reshape(12, 32, 128)
        out = part_ref[:, x] + mass_ref[x][None] * acc + added
        res_ref[:, x] = out[0:6]
        jac_ref[:, x] = out[6:12]


def join_kernel(same_ref, other_ref, *out_refs):
    for k, out in enumerate(out_refs):
        out[0] = same_ref[k + 1]
        out[1] = other_ref[k + 1]


def turn_kernel(own_ref, y1_ref, y2_ref, y3_ref, out_ref):
    for k, ref in enumerate((own_ref, y1_ref, y2_ref, y3_ref)):
        out_ref[k] = ref[1]


def time_kernel(me_ref, same_ref, other_ref, y1_ref, y2_ref, y3_ref, after_ref, *refs):
    outs, in_ref, out_ref, sems = refs[:4], refs[4], refs[5], refs[6]
    me = me_ref[0]
    pairs = [(same_ref.at[0], in_ref.at[0]), (other_ref.at[0], in_ref.at[1])]
    pairs += [(ref, in_ref.at[pl.ds(2 * k + 2, 2)]) for k, ref in enumerate((y1_ref, y2_ref, y3_ref))]
    copies = [pltpu.make_async_copy(a, b, sems.at[k]) for k, (a, b) in enumerate(pairs)]
    for copy in copies:
        copy.start()
    for copy in copies:
        copy.wait()
    at = [me ^ ((me + k) & (PARTS - 1)) for k in range(PARTS)]
    count = 2 * PARTS

    def step(g, carry):
        field = g // 3
        row = 6 * field + (g - 3 * field)
        x = [in_ref[at[t // 2], row + 3 * (t % 2)] for t in range(count)]
        for t in range(count):
            acc = x[0] * float(MIXED[t, 0])
            for s in range(1, count):
                acc = acc + x[s] * float(MIXED[(t - s) % count, 0])
            out_ref[at[t // 2], row + 3 * (t % 2)] = acc
        return carry

    lax.fori_loop(0, 6, step, 0)
    for k, out in enumerate(outs):
        out[...] = out_ref[2 * k : 2 * k + 2]


def lookup(ids, mat_ref, column, count):
    out = jnp.zeros(ids.shape, f32)
    for m in range(count):
        out = jnp.where(ids == m, mat_ref[m, column], out)
    return out


def stiff_kernel(p_ref, mat_ref, ids_ref, disp_ref, dir_ref, forcing_ref, low_ref, high_ref, out_ref, mass_ref, *, materials):
    p = p_ref[0]
    low = jnp.where(p > 0, low_ref[...], 0.0)
    high = jnp.where(p < SLABS - 1, high_ref[...], 0.0)
    ids = ids_ref[...]
    kx, ky, kz, mass = [lookup(ids, mat_ref, col, materials) for col in range(4)]
    mass_ref[...] = mass
    kx_low = lookup(low[12].astype(i32) - 1, mat_ref, 0, materials)
    kx_high = lookup(high[12].astype(i32) - 1, mat_ref, 0, materials)
    shape = ids.shape
    y = lax.broadcasted_iota(i32, shape, 1)
    z = lax.broadcasted_iota(i32, shape, 2)
    xm = 0.5 * (kx + jnp.concatenate([kx_low[None], kx[:-1]], axis=0))
    xp = 0.5 * (kx + jnp.concatenate([kx[1:], kx_high[None]], axis=0))
    total = xm + xp
    sides = []
    for k, pos, axis in ((ky, y, 1), (kz, z, 2)):
        size = shape[axis]
        for shift, edge in ((1, 0), (size - 1, size - 1)):
            inside = pos != edge
            near = jnp.where(inside, pltpu.roll(k, shift, axis), 0.0)
            side = 0.5 * (k + near)
            total = total + side
            sides.append((jnp.where(inside, side, 0.0), shift, axis))
    for field, ref in enumerate((disp_ref, dir_ref)):
        for c in range(6):
            w = ref[c]
            down = jnp.concatenate([low[6 * field + c][None], w[:-1]], axis=0)
            up = jnp.concatenate([w[1:], high[6 * field + c][None]], axis=0)
            out = total * w - xm * down - xp * up
            for side, shift, axis in sides:
                out = out - side * pltpu.roll(w, shift, axis)
            if field == 0:
                out = out - forcing_ref[c]
            out_ref[6 * field + c] = out


VMEM = 16 * 1024 * 1024


def call(kernel, outs, *args, smem=(0,), away=(), scratch=(), kept=(), limit=VMEM):
    spaces = [pltpu.SMEM if k in smem else pl.ANY if k in away else pltpu.VMEM for k in range(len(args))]
    specs = [pl.BlockSpec(memory_space=space) for space in spaces]
    return pl.pallas_call(
        kernel,
        out_shape=[jax.ShapeDtypeStruct(s, d) for s, d in outs],
        in_specs=specs,
        out_specs=[pl.BlockSpec(memory_space=pltpu.HBM if k in kept else pltpu.VMEM) for k in range(len(outs))],
        scratch_shapes=list(scratch),
        compiler_params=pltpu.CompilerParams(vmem_limit_bytes=limit),
    )(*args)


def shift(x, by, wrap=True):
    pairs = [(i, (i + by) % SLABS) for i in range(SLABS) if wrap or 0 <= i + by < SLABS]
    return lax.ppermute(x, "mesh", pairs)


def exchange(chunk, up, down):
    up, down = shift(up, 1), shift(down, -1)
    return lax.all_to_all(chunk, "mesh", split_axis=0, concat_axis=0, tiled=True), up, down


def swap(x, bit):
    return lax.ppermute(x, "inst", [(i, i ^ bit) for i in range(PARTS)])


def on_device(displacement, direction, forcing, material_ids, materials, joint_owner, joint_local, joint_remote, joint_kind):
    shape = displacement.shape
    fields = (6, 4, 32, 128)
    whole = (12, 4, 32, 128)
    disp = displacement.reshape(fields)
    dire = direction.reshape(fields)
    count = joint_local.shape[0]
    p = lax.axis_index("mesh").astype(i32).reshape(1)
    me = lax.axis_index("inst").astype(i32).reshape(1)
    parts = (768, 512)
    index = ((24, 128), i32)
    half = ((4, 12, 16, 128), f32)
    halo = ((13, 32, 128), f32)

    own_idx, chunk, up, down, own, same, other, high, low = call(
        list_kernel,
        [index, ((SLABS, 16, 128), f32)] + [((2, 16, 128), f32)] * 3 + [half, half, halo, halo],
        p,
        me,
        joint_owner.reshape(1, count),
        joint_local.reshape(1, count),
        joint_remote.reshape(1, count),
        joint_kind.reshape(1, count),
        disp,
        dire,
        material_ids,
        smem=(0, 1),
        away=range(2, 9),
        limit=60 * 1024 * 1024,
        kept=(5, 6, 7, 8),
        scratch=[pltpu.VMEM(parts, bf16), pltpu.VMEM((SIDE, 16, 128), f32)]
        + [pltpu.VMEM((1, count), i32)] * 4
        + [pltpu.VMEM(fields, f32)] * 2
        + [pltpu.VMEM((4, 32, 128), i32), pltpu.VMEM((2, 32, 128), f32)]
        + [pltpu.SemaphoreType.DMA((9,)), pltpu.SemaphoreType.DMA((20,))],
    )
    chunk, up, down = exchange(chunk, up, down)

    pair = ((2, 12, 16, 128), f32)
    other = swap(other, 1)
    joined = call(join_kernel, [pair] * 3, same, other, smem=())
    turned = [swap(x, 2 * k + 2) for k, x in enumerate(joined)]
    fields_parts = call(split_kernel, [(parts, bf16)], disp, dire, smem=())[0]
    far_idx, kind, gap = call(
        gap_kernel,
        [index, ((24, 128), f32), ((PARTS, 8 * 26, 128), f32)],
        p, chunk, up, down, own, fields_parts, *turned,
        away=(6, 7, 8),
        kept=(2,),
        scratch=[
            pltpu.VMEM((SIDE, 12, 128), f32),
            pltpu.VMEM((8 * 26, 128), f32),
            pltpu.SemaphoreType.DMA((PARTS,)),
        ],
    )
    gap = lax.all_to_all(gap, "inst", split_axis=0, concat_axis=0, tiled=True)
    blocks = [pltpu.VMEM((PARTS, 12, 16, 128), f32)] * 2
    inertia = call(time_kernel, [pair] * 4, me, same, other, *turned, far_idx, away=range(1, 7), scratch=blocks + [pltpu.SemaphoreType.DMA((5,))])

    lin, mass = call(
        lambda *refs: stiff_kernel(*refs, materials=materials.shape[0]),
        [(whole, f32), ((4, 32, 128), f32)],
        p, materials, material_ids, disp, dire, forcing.reshape(fields), shift(high, 1, False), shift(low, -1, False),
        smem=(0, 1),
    )
    two = ((2, 12, 128), f32)
    force, chunk, up2, down2, own = call(
        force_kernel,
        [((SIDE, 12, 128), f32), ((SLABS, 4, 384), f32), two, two, two],
        p, me, kind, jnp.asarray(RATES), gap, inertia[0], mass,
        smem=(0, 1),
        away=(5, 6),
        scratch=[pltpu.VMEM((16 * PARTS, 9 * 128), f32)],
    )
    turned = [inertia[0]] + [swap(inertia[k], 2 * k) for k in (1, 2, 3)]
    chunk, up2, down2 = exchange(chunk, up2, down2)

    other = swap(call(turn_kernel, [half], *turned, smem=())[0], 1)
    adding = [pltpu.VMEM((SIDE, 12, 128), f32), pltpu.VMEM((384, 512), f32)]
    partial = call(partner_kernel, [(whole, f32)], far_idx, force, lin, smem=(), scratch=adding[1:])[0]
    residual, jacobian = call(
        final_kernel,
        [(fields, f32)] * 2,
        p, me, own_idx, chunk, up2, down2, own, partial, mass, *turned, other,
        smem=(0, 1),
        away=range(9, 14),
        scratch=adding + blocks[:1] + [pltpu.SemaphoreType.DMA((PARTS,))],
    )
    return residual.reshape(shape), jacobian.reshape(shape)


def solution(mesh):
    field = P("inst", None, "mesh", None, None)
    placed = (field, field, field, P("mesh", None, None), P(), P("mesh", None), P("mesh"), P("mesh"), P("mesh"))
    return jax.shard_map(on_device, mesh=mesh, in_specs=placed, out_specs=(field, field), check_vma=False)
```

```python
import jax
import jax.numpy as jnp
import numpy as np
from jax import lax
from jax.experimental import pallas as pl
from jax.experimental.pallas import tpu as pltpu
from jax.sharding import PartitionSpec as P

frequency = 0.6
damping = 0.3
bolt_stiff = 2.0
slip_force = 1.0
slip_speed = 0.5
stop_stiff = 3.0
clearance = 0.3

SLABS = 32
PARTS = 8
SIDE = 18
SEG = 42
f32 = jnp.float32
bf16 = jnp.bfloat16
i32 = jnp.int32


def tables(count):
    offsets = np.arange(count)[:, None] - np.arange(count)[None, :]
    tangent = np.where(offsets == 0, 1.0, np.tan(np.pi * offsets / count))
    first = np.where(offsets == 0, 0.0, 0.5 * np.where(offsets % 2 == 0, 1.0, -1.0) / tangent) * frequency
    return first, first @ first


FIRST, SECOND = tables(2 * PARTS)
MIXED = (SECOND + damping * FIRST).astype(np.float32)
SPREAD = np.kron(FIRST, np.eye(3)).astype(np.float32)


def far_place(offset):
    return 8 + (offset - 3) // 3, SEG * ((offset - 3) % 3)


def fold(rows):
    return jnp.concatenate([rows[0:4], rows[4:8], rows[8:12]], axis=1)


def unfold(rows):
    width = rows.shape[1] // 3
    return jnp.concatenate([rows[:, width * k : width * (k + 1)] for k in range(3)], axis=0)


def part_tile(ref, tile):
    at = 128 * (tile % 3)
    return jnp.concatenate([ref[tile // 3, :, 384 * k + at : 384 * k + at + 128] for k in range(3)], axis=0)


def lane_roll(x, shift):
    shift = shift % 128
    return pltpu.roll(x, shift, x.ndim - 1) if shift else x


def lanes(rows):
    return lax.broadcasted_iota(i32, (rows, 128), 1)


def merge_far(read, rows, fill):
    lane = lanes(rows)
    tiles = []
    for k in range(9):
        parts = [lane_roll(read(3 + 3 * k + s), SEG * s) for s in range(3)]
        tile = jnp.where(lane < SEG, parts[0], jnp.where(lane < 2 * SEG, parts[1], parts[2]))
        tiles.append(jnp.where(lane < 3 * SEG, tile, fill))
    return tiles


def slot_tables(p, owner_ref, local_ref, remote_ref, kind_ref):
    count = owner_ref.shape[1]
    offset = (owner_ref[...] - p) & (SLABS - 1)
    hit = (lax.broadcasted_iota(i32, (SLABS, count), 0) == offset).astype(f32)
    hit16 = hit.astype(bf16)
    before = (lax.broadcasted_iota(i32, (128, 128), 0) < lax.broadcasted_iota(i32, (128, 128), 1)).astype(f32).astype(bf16)
    row = lax.broadcasted_iota(i32, (SLABS, 1), 0)
    far = row - 3
    group = (far * 171) >> 9
    start = 1024 + group * 128 + (far - 3 * group) * SEG
    for value, at in ((0, 0), (1, 256), (SLABS - 1, 512), (2, 768), (SLABS - 2, 896)):
        start = jnp.where(row == value, at, start)
    run = start.astype(f32)
    places = []
    for b in range(count // 128):
        block = hit[:, 128 * b : 128 * (b + 1)]
        earlier = jnp.dot(hit16[:, 128 * b : 128 * (b + 1)], before, preferred_element_type=f32)
        places.append(jnp.sum(block * (earlier + run), axis=0, keepdims=True))
        run = run + jnp.sum(block, axis=1, keepdims=True)
    slot = jnp.concatenate(places, axis=1).astype(i32)
    in_tile = lax.broadcasted_iota(i32, (24, count), 0) == (slot >> 7)
    in_lane = (lax.broadcasted_iota(i32, (128, count), 0) == (slot & 127)).astype(f32).astype(bf16)
    local = local_ref[...]
    remote = remote_ref[...]
    values = (local >> 7, local & 127, remote >> 7, remote & 127, kind_ref[...], jnp.ones_like(local))
    spread = jnp.concatenate([jnp.where(in_tile, v.astype(f32), 0.0) for v in values], axis=0).astype(bf16)
    got = lax.dot_general(spread, in_lane, (((1,), (1,)), ((), ())), preferred_element_type=f32)
    got = [got[24 * k : 24 * (k + 1)] for k in range(6)]
    empty = got[5] - 1.0
    return got[0] * 128.0 + got[1] + empty, got[2] * 128.0 + got[3] + empty, got[4]


def picks(idx_ref, k):
    idx = jnp.concatenate([idx_ref[pl.ds(2 * k, 1), :], idx_ref[pl.ds(2 * k + 1, 1), :]], axis=1)
    code = ((idx >> 12) << 7) | (idx & 127)
    pick = (lax.broadcasted_iota(i32, (512, 256), 0) == code).astype(f32).astype(bf16)
    return pick, lax.broadcasted_iota(i32, (32, 256), 0) == ((idx >> 7) & 31)


def split_fields(disp_ref, dir_ref, parts_ref):
    for field, ref in enumerate((disp_ref, dir_ref)):
        for x in range(4):
            value = ref[:, x].reshape(6 * 32, 128)
            hi = value.astype(bf16)
            cols = slice(128 * x, 128 * (x + 1))
            parts_ref[192 * field : 192 * (field + 1), cols] = hi
            parts_ref[384 + 192 * field : 384 + 192 * (field + 1), cols] = (value - hi.astype(f32)).astype(bf16)


def split_kernel(disp_ref, dir_ref, parts_ref):
    split_fields(disp_ref, dir_ref, parts_ref)


def gather_rows(parts_ref, idx_ref, here_ref):
    def step(k, carry):
        pick, in_y = picks(idx_ref, k)
        rows = jnp.dot(parts_ref[...], pick, preferred_element_type=f32)
        rows = (rows[:384] + rows[384:]).reshape(12, 32, 256)
        got = jnp.sum(jnp.where(in_y[None], rows, 0.0), axis=1)
        here_ref[2 * k, 0:12, :] = got[:, :128]
        here_ref[2 * k + 1, 0:12, :] = got[:, 128:]
        return carry

    lax.fori_loop(0, SIDE // 2, step, 0, unroll=3)


def scatter_rows(val_ref, idx_ref, sum_ref):
    sum_ref[...] = jnp.zeros(sum_ref.shape, f32)
    dims = (((1,), (1,)), ((), ()))

    def step(k, carry):
        pick, in_y = picks(idx_ref, k)
        value = jnp.concatenate([val_ref[2 * k], val_ref[2 * k + 1]], axis=1)
        hi = value.astype(bf16).astype(f32)
        spread = [
            jnp.where(in_y[None], part[:, None, :], 0.0).reshape(384, 256).astype(bf16) for part in (hi, value - hi)
        ]
        got = lax.dot_general(spread[0], pick, dims, preferred_element_type=f32)
        got = got + lax.dot_general(spread[1], pick, dims, preferred_element_type=f32)
        sum_ref[...] = sum_ref[...] + got
        return carry

    lax.fori_loop(0, SIDE // 2, step, 0, unroll=3)


def list_kernel(p_ref, me_ref, owner_hbm, local_hbm, remote_hbm, kind_hbm, disp_hbm, dir_hbm, ids_hbm,
                idx_ref, chunk_ref, up_hbm, down_hbm, self_ref, same_hbm, other_hbm,
                parts_ref, rows_ref, owner_ref, local_ref, remote_ref, kind_ref, disp_ref, dir_ref, ids_ref, near_ref,
                sems, more_sems):
    p = p_ref[0]
    pairs = ((owner_hbm, owner_ref), (local_hbm, local_ref), (remote_hbm, remote_ref), (kind_hbm, kind_ref),
             (disp_hbm, disp_ref), (dir_hbm, dir_ref), (ids_hbm, ids_ref))
    copies = [pltpu.make_async_copy(a, b, sems.at[k]) for k, (a, b) in enumerate(pairs)]
    for copy in copies:
        copy.start()
    for copy in copies[:4]:
        copy.wait()
    mine, theirs, kind = slot_tables(p, owner_ref, local_ref, remote_ref, kind_ref)
    idx_ref[...] = mine.astype(i32)
    for tile in range(SIDE):
        rows_ref[tile, 12:13, :] = theirs[tile : tile + 1]
        rows_ref[tile, 13:14, :] = kind[tile : tile + 1]
        rows_ref[tile, 14:16, :] = jnp.zeros((2, 128), f32)
    for copy in copies[4:]:
        copy.wait()
    moves = []
    for field, ref in enumerate((disp_ref, dir_ref)):
        part = pl.ds(6 * field, 6)
        for k in range(PARTS):
            block = me_ref[0] ^ k
            rows = pl.ds(pl.multiple_of(16 * (block & 1), 16), 16)
            moves.append((ref.at[:, block >> 1, rows, :], (same_hbm, other_hbm)[k % 2].at[k // 2, part]))
        moves.append((ref.at[:, 3], up_hbm.at[pl.ds(1 + 6 * field, 6)]))
        moves.append((ref.at[:, 0], down_hbm.at[pl.ds(1 + 6 * field, 6)]))
    moves = [pltpu.make_async_copy(a, b, more_sems.at[k]) for k, (a, b) in enumerate(moves)]
    for move in moves:
        move.start()
    split_fields(disp_ref, dir_ref, parts_ref)
    near_ref[2] = (ids_ref[3] + 1).astype(f32)
    near_ref[3] = (ids_ref[0] + 1).astype(f32)
    gather_rows(parts_ref, idx_ref, rows_ref)
    for k in range(2):
        near_ref[k] = rows_ref[2 + 2 * k : 4 + 2 * k].reshape(32, 128)
    ends = ((near_ref.at[0], up_hbm.at[0]), (near_ref.at[1], down_hbm.at[0]),
            (near_ref.at[2], up_hbm.at[13]), (near_ref.at[3], down_hbm.at[13]))
    ends = [pltpu.make_async_copy(a, b, sems.at[7 + k]) for k, (a, b) in enumerate(ends)]
    for end in ends:
        end.start()
    for d in (0, 1, SLABS - 1):
        chunk_ref[(p + d) & (SLABS - 1)] = jnp.zeros((16, 128), f32)
    for d, tile in ((2, 6), (SLABS - 2, 7)):
        chunk_ref[(p + d) & (SLABS - 1)] = rows_ref[tile]
    for d in range(3, SLABS - 2):
        tile, seg = far_place(d)
        chunk_ref[(p + d) & (SLABS - 1)] = lane_roll(rows_ref[tile], -seg)
    self_ref[...] = rows_ref[0:2]
    for move in moves + ends:
        move.wait()


def gap_kernel(p_ref, chunk_ref, up_ref, down_ref, self_ref, parts_ref, after_ref,
               idx_ref, kind_ref, gap_ref, here_ref):
    p = p_ref[0]

    def asked(d):
        return chunk_ref[(p - d) & (SLABS - 1)]

    near = [ref[0, 16 * k : 16 * (k + 1), :] for ref in (up_ref, down_ref) for k in range(2)]
    tiles = [self_ref[0], self_ref[1]] + near + [asked(2), asked(SLABS - 2)]
    tiles += merge_far(asked, 16, 0.0)
    beyond = lanes(1) >= 3 * SEG
    rows = [t[12:13] for t in tiles[:8]] + [jnp.where(beyond, -1.0, t[12:13]) for t in tiles[8:]]
    idx_ref[...] = jnp.concatenate(rows + [jnp.full((7, 128), -1.0, f32)], axis=0).astype(i32)
    kind_ref[...] = jnp.concatenate([t[13:14] for t in tiles] + [jnp.zeros((7, 128), f32)], axis=0)
    gather_rows(parts_ref, idx_ref, here_ref)
    for tile in range(24):
        gap = tiles[tile][0:12] - here_ref[tile] if tile < 17 else jnp.zeros((12, 128), f32)
        at = 128 * (tile % 3)
        for k in range(3):
            gap_ref[tile // 3, :, 384 * k + at : 384 * k + at + 128] = gap[4 * k : 4 * k + 4]


def force_kernel(me_ref, kind_ref, spread_ref, gap_ref, after_ref, out_ref, r_ref, d_ref, f_ref, t_ref):
    me = me_ref[0]
    for k in range(PARTS):
        gap = unfold(gap_ref[k])
        r_ref[6 * k : 6 * k + 6] = gap[0:6]
        d_ref[6 * k : 6 * k + 6] = gap[6:12]
    r = r_ref[...]
    dr = d_ref[...]
    w = jnp.dot(spread_ref[...], r, precision=lax.Precision.HIGHEST, preferred_element_type=f32)
    dw = jnp.dot(spread_ref[...], dr, precision=lax.Precision.HIGHEST, preferred_element_type=f32)
    bolted = jnp.concatenate([kind_ref[pl.ds(3 * me + k, 1), :] for k in range(3)], axis=1)
    slide = jnp.tanh(w / slip_speed)
    opened = jnp.tanh(r / clearance)
    friction = bolt_stiff * r + slip_force * slide
    contact = stop_stiff * (r - clearance * opened)
    f_ref[...] = bolted * friction + (1.0 - bolted) * contact
    tangent_friction = bolt_stiff * dr + slip_force * (1.0 - slide * slide) / slip_speed * dw
    tangent_contact = stop_stiff * opened * opened * dr
    t_ref[...] = bolted * tangent_friction + (1.0 - bolted) * tangent_contact
    for k in range(PARTS):
        out_ref[k] = fold(jnp.concatenate([f_ref[6 * k : 6 * k + 6], t_ref[6 * k : 6 * k + 6]], axis=0))


def reply_kernel(p_ref, force_ref, after_ref, chunk_ref, up_ref, down_ref, self_ref):
    p = p_ref[0]
    for d in (0, 1, SLABS - 1):
        chunk_ref[(p - d) & (SLABS - 1)] = jnp.zeros((4, 384), f32)
    for d, tile in ((2, 6), (SLABS - 2, 7)):
        chunk_ref[(p - d) & (SLABS - 1)] = fold(part_tile(force_ref, tile))
    for d in range(3, SLABS - 2):
        tile, seg = far_place(d)
        chunk_ref[(p - d) & (SLABS - 1)] = fold(lane_roll(part_tile(force_ref, tile), -seg))
    for k in range(2):
        self_ref[k] = part_tile(force_ref, k)
        down_ref[k] = part_tile(force_ref, 2 + k)
        up_ref[k] = part_tile(force_ref, 4 + k)


def partner_kernel(idx_ref, force_ref, lin_ref, out_ref, val_ref, sum_ref):
    for tile in range(17):
        val_ref[tile] = -part_tile(force_ref, tile)
    val_ref[17] = jnp.zeros((12, 128), f32)
    scatter_rows(val_ref, idx_ref, sum_ref)
    for x in range(4):
        out_ref[:, x] = lin_ref[:, x] + sum_ref[:, 128 * x : 128 * (x + 1)].reshape(12, 32, 128)


def final_kernel(p_ref, me_ref, idx_ref, chunk_ref, up_ref, down_ref, self_ref, part_ref, mass_ref,
                 keep_ref, cross_ref, y1_ref, y2_ref, y3_ref, res_ref, jac_ref, val_ref, sum_ref, acc_ref, sems):
    p = p_ref[0]
    copies = []
    for k in range(PARTS):
        source = (y1_ref, y2_ref, y3_ref)[k // 2 - 1].at[k % 2] if k > 1 else (keep_ref, cross_ref)[k].at[0]
        copies.append(pltpu.make_async_copy(source, acc_ref.at[me_ref[0] ^ k], sems.at[k]))
    for copy in copies:
        copy.start()

    def listed(d):
        return unfold(chunk_ref[(p + d) & (SLABS - 1)])

    tiles = [self_ref[0], self_ref[1], down_ref[0], down_ref[1], up_ref[0], up_ref[1], listed(2), listed(SLABS - 2)]
    tiles += merge_far(listed, 12, 0.0) + [jnp.zeros((12, 128), f32)]
    for k, tile in enumerate(tiles):
        val_ref[k] = tile
    scatter_rows(val_ref, idx_ref, sum_ref)
    for copy in copies:
        copy.wait()
    for x in range(4):
        acc = jnp.concatenate([acc_ref[2 * x], acc_ref[2 * x + 1]], axis=1)
        added = sum_ref[:, 128 * x : 128 * (x + 1)].reshape(12, 32, 128)
        out = part_ref[:, x] + mass_ref[x][None] * acc + added
        res_ref[:, x] = out[0:6]
        jac_ref[:, x] = out[6:12]


def join_kernel(same_ref, other_ref, *out_refs):
    for k, out in enumerate(out_refs):
        out[0] = same_ref[k + 1]
        out[1] = other_ref[k + 1]


def time_kernel(me_ref, same_ref, other_ref, y1_ref, y2_ref, y3_ref, *refs):
    keep_ref, cross_ref, in_ref, out_ref, sems = refs
    me = me_ref[0]
    pairs = [(same_ref.at[0], in_ref.at[0]), (other_ref.at[0], in_ref.at[1])]
    pairs += [(ref, in_ref.at[pl.ds(2 * k + 2, 2)]) for k, ref in enumerate((y1_ref, y2_ref, y3_ref))]
    copies = [pltpu.make_async_copy(a, b, sems.at[k]) for k, (a, b) in enumerate(pairs)]
    for copy in copies:
        copy.start()
    for copy in copies:
        copy.wait()
    at = [me ^ ((me + k) & (PARTS - 1)) for k in range(PARTS)]
    count = 2 * PARTS

    def step(g, carry):
        field = g // 3
        row = 6 * field + (g - 3 * field)
        x = [in_ref[at[t // 2], row + 3 * (t % 2)] for t in range(count)]
        for t in range(count):
            acc = x[0] * float(MIXED[t, 0])
            for s in range(1, count):
                acc = acc + x[s] * float(MIXED[(t - s) % count, 0])
            out_ref[at[t // 2], row + 3 * (t % 2)] = acc
        return carry

    lax.fori_loop(0, 6, step, 0)
    for k in range(PARTS):
        (keep_ref, cross_ref)[k % 2][k // 2] = out_ref[k]


def lookup(ids, mat_ref, column, count):
    out = jnp.zeros(ids.shape, f32)
    for m in range(count):
        out = jnp.where(ids == m, mat_ref[m, column], out)
    return out


def stiff_kernel(p_ref, mat_ref, ids_ref, disp_ref, dir_ref, forcing_ref, up_ref, down_ref, out_ref, mass_ref, *, materials):
    p = p_ref[0]
    low = jnp.where(p > 0, up_ref[1:14], 0.0)
    high = jnp.where(p < SLABS - 1, down_ref[1:14], 0.0)
    ids = ids_ref[...]
    kx, ky, kz, mass = [lookup(ids, mat_ref, col, materials) for col in range(4)]
    mass_ref[...] = mass
    kx_low = lookup(low[12].astype(i32) - 1, mat_ref, 0, materials)
    kx_high = lookup(high[12].astype(i32) - 1, mat_ref, 0, materials)
    shape = ids.shape
    y = lax.broadcasted_iota(i32, shape, 1)
    z = lax.broadcasted_iota(i32, shape, 2)
    xm = 0.5 * (kx + jnp.concatenate([kx_low[None], kx[:-1]], axis=0))
    xp = 0.5 * (kx + jnp.concatenate([kx[1:], kx_high[None]], axis=0))
    total = xm + xp
    sides = []
    for k, pos, axis in ((ky, y, 1), (kz, z, 2)):
        size = shape[axis]
        for shift, edge in ((1, 0), (size - 1, size - 1)):
            inside = pos != edge
            near = jnp.where(inside, pltpu.roll(k, shift, axis), 0.0)
            side = 0.5 * (k + near)
            total = total + side
            sides.append((jnp.where(inside, side, 0.0), shift, axis))
    for field, ref in enumerate((disp_ref, dir_ref)):
        for c in range(6):
            w = ref[c]
            down = jnp.concatenate([low[6 * field + c][None], w[:-1]], axis=0)
            up = jnp.concatenate([w[1:], high[6 * field + c][None]], axis=0)
            out = total * w - xm * down - xp * up
            for side, shift, axis in sides:
                out = out - side * pltpu.roll(w, shift, axis)
            if field == 0:
                out = out - forcing_ref[c]
            out_ref[6 * field + c] = out


VMEM = 16 * 1024 * 1024


def call(kernel, outs, *args, smem=(0,), away=(), scratch=(), kept=(), limit=VMEM):
    spaces = [pltpu.SMEM if k in smem else pl.ANY if k in away else pltpu.VMEM for k in range(len(args))]
    specs = [pl.BlockSpec(memory_space=space) for space in spaces]
    return pl.pallas_call(
        kernel,
        out_shape=[jax.ShapeDtypeStruct(s, d) for s, d in outs],
        in_specs=specs,
        out_specs=[pl.BlockSpec(memory_space=pl.ANY if k in kept else pltpu.VMEM) for k in range(len(outs))],
        scratch_shapes=list(scratch),
        compiler_params=pltpu.CompilerParams(vmem_limit_bytes=limit),
    )(*args)


def shift(x, by):
    return lax.ppermute(x, "mesh", [(i, (i + by) % SLABS) for i in range(SLABS)])


def exchange(chunk, up, down):
    up, down = shift(up, 1), shift(down, -1)
    return lax.all_to_all(chunk, "mesh", split_axis=0, concat_axis=0, tiled=True), up, down


def swap(x, bit):
    return lax.ppermute(x, "inst", [(i, i ^ bit) for i in range(PARTS)])


def inst_split(x):
    return lax.all_to_all(x, "inst", split_axis=0, concat_axis=0, tiled=True)


def on_device(displacement, direction, forcing, material_ids, materials, joint_owner, joint_local, joint_remote, joint_kind):
    shape = displacement.shape
    fields = (6, 4, 32, 128)
    whole = (12, 4, 32, 128)
    disp = displacement.reshape(fields)
    dire = direction.reshape(fields)
    count = joint_local.shape[0]
    p = lax.axis_index("mesh").astype(i32).reshape(1)
    me = lax.axis_index("inst").astype(i32).reshape(1)
    parts = (768, 512)
    index = ((24, 128), i32)
    half = ((4, 12, 16, 128), f32)
    near = ((14, 32, 128), f32)

    own_idx, chunk, up, down, own, same, other = call(
        list_kernel,
        [index, ((SLABS, 16, 128), f32), near, near, ((2, 16, 128), f32), half, half],
        p,
        me,
        joint_owner.reshape(1, count),
        joint_local.reshape(1, count),
        joint_remote.reshape(1, count),
        joint_kind.reshape(1, count),
        disp,
        dire,
        material_ids,
        smem=(0, 1),
        away=range(2, 9),
        limit=60 * 1024 * 1024,
        kept=(2, 3, 5, 6),
        scratch=[pltpu.VMEM(parts, bf16), pltpu.VMEM((SIDE, 16, 128), f32)]
        + [pltpu.VMEM((1, count), i32)] * 4
        + [pltpu.VMEM(fields, f32)] * 2
        + [pltpu.VMEM((4, 32, 128), i32), pltpu.VMEM((4, 32, 128), f32)]
        + [pltpu.SemaphoreType.DMA((11,)), pltpu.SemaphoreType.DMA((20,))],
    )
    chunk, up, down = exchange(chunk, up, down)

    pair = ((2, 12, 16, 128), f32)
    other = swap(other, 1)
    joined = call(join_kernel, [pair] * 3, same, other, smem=())
    turned = [swap(x, 2 * k + 2) for k, x in enumerate(joined)]
    blocks = [pltpu.VMEM((PARTS, 12, 16, 128), f32)] * 2
    keep, cross = call(time_kernel, [half] * 2, me, same, other, *turned, away=range(1, 6), scratch=blocks + [pltpu.SemaphoreType.DMA((5,))])

    part = ((PARTS, 4, 1152), f32)
    fields_parts = call(split_kernel, [(parts, bf16)], disp, dire, smem=())[0]
    far_idx, kind, gap = call(
        gap_kernel,
        [index, ((24, 128), f32), part],
        p, chunk, up, down, own, fields_parts, joined[0],
        away=(6,),
        scratch=[pltpu.VMEM((SIDE, 12, 128), f32)],
    )
    force = call(
        force_kernel,
        [part],
        me, kind, jnp.asarray(SPREAD), inst_split(gap), keep,
        away=(4,),
        scratch=[pltpu.VMEM((48, 384), f32)] * 4,
    )[0]
    force = inst_split(force)
    cross = swap(cross, 1)
    joined = call(join_kernel, [pair] * 3, keep, cross, smem=())
    turned = [swap(x, 2 * k + 2) for k, x in enumerate(joined)]
    lin, mass = call(
        lambda *refs: stiff_kernel(*refs, materials=materials.shape[0]),
        [(whole, f32), ((4, 32, 128), f32)],
        p, materials, material_ids, disp, dire, forcing.reshape(fields), up, down,
        smem=(0, 1),
    )
    two = ((2, 12, 128), f32)
    chunk, up2, down2, own = call(reply_kernel, [((SLABS, 4, 384), f32), two, two, two], p, force, mass, away=(2,))
    chunk, up2, down2 = exchange(chunk, up2, down2)

    adding = [pltpu.VMEM((SIDE, 12, 128), f32), pltpu.VMEM((384, 512), f32)]
    partial = call(partner_kernel, [(whole, f32)], far_idx, force, lin, smem=(), scratch=adding)[0]
    residual, jacobian = call(
        final_kernel,
        [(fields, f32)] * 2,
        p, me, own_idx, chunk, up2, down2, own, partial, mass, keep, cross, *turned,
        smem=(0, 1),
        away=range(9, 14),
        scratch=adding + blocks[:1] + [pltpu.SemaphoreType.DMA((PARTS,))],
    )
    return residual.reshape(shape), jacobian.reshape(shape)


def solution(mesh):
    field = P("inst", None, "mesh", None, None)
    placed = (field, field, field, P("mesh", None, None), P(), P("mesh", None), P("mesh"), P("mesh"), P("mesh"))
    return jax.shard_map(on_device, mesh=mesh, in_specs=placed, out_specs=(field, field), check_vma=False)
```

```python
import jax
import jax.numpy as jnp
import numpy as np
from jax import lax
from jax.experimental import pallas as pl
from jax.experimental.pallas import tpu as pltpu
from jax.sharding import PartitionSpec as P

frequency = 0.6
damping = 0.3
bolt_stiff = 2.0
slip_force = 1.0
slip_speed = 0.5
stop_stiff = 3.0
clearance = 0.3

SLABS = 32
PARTS = 8
SIDE = 18
SEG = 42
f32 = jnp.float32
bf16 = jnp.bfloat16
i32 = jnp.int32


def tables(count):
    offsets = np.arange(count)[:, None] - np.arange(count)[None, :]
    tangent = np.where(offsets == 0, 1.0, np.tan(np.pi * offsets / count))
    first = np.where(offsets == 0, 0.0, 0.5 * np.where(offsets % 2 == 0, 1.0, -1.0) / tangent) * frequency
    return first, first @ first


FIRST, SECOND = tables(2 * PARTS)
MIXED = (SECOND + damping * FIRST).astype(np.float32)
SPREAD = np.kron(FIRST, np.eye(3)).astype(np.float32)


def far_place(offset):
    return 8 + (offset - 3) // 3, SEG * ((offset - 3) % 3)


def fold(rows):
    return jnp.concatenate([rows[0:4], rows[4:8], rows[8:12]], axis=1)


def unfold(rows):
    width = rows.shape[1] // 3
    return jnp.concatenate([rows[:, width * k : width * (k + 1)] for k in range(3)], axis=0)


def part_tile(ref, tile):
    at = 128 * (tile % 3)
    return jnp.concatenate([ref[tile // 3, :, 384 * k + at : 384 * k + at + 128] for k in range(3)], axis=0)


def lane_roll(x, shift):
    shift = shift % 128
    return pltpu.roll(x, shift, x.ndim - 1) if shift else x


def lanes(rows):
    return lax.broadcasted_iota(i32, (rows, 128), 1)


def merge_far(read, rows, fill):
    lane = lanes(rows)
    tiles = []
    for k in range(9):
        parts = [lane_roll(read(3 + 3 * k + s), SEG * s) for s in range(3)]
        tile = jnp.where(lane < SEG, parts[0], jnp.where(lane < 2 * SEG, parts[1], parts[2]))
        tiles.append(jnp.where(lane < 3 * SEG, tile, fill))
    return tiles


def slot_tables(p, owner_ref, local_ref, remote_ref, kind_ref):
    count = owner_ref.shape[1]
    offset = (owner_ref[...] - p) & (SLABS - 1)
    hit = (lax.broadcasted_iota(i32, (SLABS, count), 0) == offset).astype(f32)
    hit16 = hit.astype(bf16)
    before = (lax.broadcasted_iota(i32, (128, 128), 0) < lax.broadcasted_iota(i32, (128, 128), 1)).astype(f32).astype(bf16)
    row = lax.broadcasted_iota(i32, (SLABS, 1), 0)
    far = row - 3
    group = (far * 171) >> 9
    start = 1024 + group * 128 + (far - 3 * group) * SEG
    for value, at in ((0, 0), (1, 256), (SLABS - 1, 512), (2, 768), (SLABS - 2, 896)):
        start = jnp.where(row == value, at, start)
    run = start.astype(f32)
    places = []
    for b in range(count // 128):
        block = hit[:, 128 * b : 128 * (b + 1)]
        earlier = jnp.dot(hit16[:, 128 * b : 128 * (b + 1)], before, preferred_element_type=f32)
        places.append(jnp.sum(block * (earlier + run), axis=0, keepdims=True))
        run = run + jnp.sum(block, axis=1, keepdims=True)
    slot = jnp.concatenate(places, axis=1).astype(i32)
    in_tile = lax.broadcasted_iota(i32, (24, count), 0) == (slot >> 7)
    in_lane = (lax.broadcasted_iota(i32, (128, count), 0) == (slot & 127)).astype(f32).astype(bf16)
    local = local_ref[...]
    remote = remote_ref[...]
    values = (local >> 7, local & 127, remote >> 7, remote & 127, kind_ref[...], jnp.ones_like(local))
    spread = jnp.concatenate([jnp.where(in_tile, v.astype(f32), 0.0) for v in values], axis=0).astype(bf16)
    got = lax.dot_general(spread, in_lane, (((1,), (1,)), ((), ())), preferred_element_type=f32)
    got = [got[24 * k : 24 * (k + 1)] for k in range(6)]
    empty = got[5] - 1.0
    return got[0] * 128.0 + got[1] + empty, got[2] * 128.0 + got[3] + empty, got[4]


def picks(idx_ref, k):
    idx = jnp.concatenate([idx_ref[pl.ds(2 * k, 1), :], idx_ref[pl.ds(2 * k + 1, 1), :]], axis=1)
    code = ((idx >> 12) << 7) | (idx & 127)
    pick = (lax.broadcasted_iota(i32, (512, 256), 0) == code).astype(f32).astype(bf16)
    return pick, lax.broadcasted_iota(i32, (32, 256), 0) == ((idx >> 7) & 31)


def split_fields(disp_ref, dir_ref, parts_ref):
    for field, ref in enumerate((disp_ref, dir_ref)):
        for x in range(4):
            value = ref[:, x].reshape(6 * 32, 128)
            hi = value.astype(bf16)
            cols = slice(128 * x, 128 * (x + 1))
            parts_ref[192 * field : 192 * (field + 1), cols] = hi
            parts_ref[384 + 192 * field : 384 + 192 * (field + 1), cols] = (value - hi.astype(f32)).astype(bf16)


def split_kernel(disp_ref, dir_ref, parts_ref):
    split_fields(disp_ref, dir_ref, parts_ref)


def gather_rows(parts_ref, idx_ref, here_ref):
    def step(k, carry):
        pick, in_y = picks(idx_ref, k)
        rows = jnp.dot(parts_ref[...], pick, preferred_element_type=f32)
        rows = (rows[:384] + rows[384:]).reshape(12, 32, 256)
        got = jnp.sum(jnp.where(in_y[None], rows, 0.0), axis=1)
        here_ref[2 * k, 0:12, :] = got[:, :128]
        here_ref[2 * k + 1, 0:12, :] = got[:, 128:]
        return carry

    lax.fori_loop(0, SIDE // 2, step, 0, unroll=3)


def scatter_rows(val_ref, idx_ref, sum_ref):
    dims = (((1,), (1,)), ((), ()))
    total = None
    for group in range(3):
        held, high, low = [], [], []
        for k in range(group * SIDE // 2 // 3, (group + 1) * SIDE // 2 // 3):
            pick, in_y = picks(idx_ref, k)
            value = jnp.concatenate([val_ref[2 * k], val_ref[2 * k + 1]], axis=1)
            hi = value.astype(bf16).astype(f32)
            held.append(pick)
            for out, part in ((high, hi), (low, value - hi)):
                out.append(jnp.where(in_y[None], part[:, None, :], 0.0).reshape(384, 256).astype(bf16))
        held = jnp.concatenate(held, axis=1)
        got = lax.dot_general(jnp.concatenate(high, axis=1), held, dims, preferred_element_type=f32)
        got = got + lax.dot_general(jnp.concatenate(low, axis=1), held, dims, preferred_element_type=f32)
        total = got if total is None else total + got
    sum_ref[...] = total


def list_kernel(p_ref, me_ref, owner_hbm, local_hbm, remote_hbm, kind_hbm, disp_hbm, dir_hbm, ids_hbm,
                idx_ref, chunk_hbm, up_hbm, down_hbm, self_ref, same_hbm, other_hbm,
                parts_ref, rows_ref, owner_ref, local_ref, remote_ref, kind_ref, disp_ref, dir_ref, ids_ref, near_ref,
                chunk_ref, sems, more_sems):
    p = p_ref[0]
    pairs = ((owner_hbm, owner_ref), (local_hbm, local_ref), (remote_hbm, remote_ref), (kind_hbm, kind_ref),
             (disp_hbm, disp_ref), (dir_hbm, dir_ref), (ids_hbm, ids_ref))
    copies = [pltpu.make_async_copy(a, b, sems.at[k]) for k, (a, b) in enumerate(pairs)]
    for copy in copies:
        copy.start()
    for copy in copies[:4]:
        copy.wait()
    mine, theirs, kind = slot_tables(p, owner_ref, local_ref, remote_ref, kind_ref)
    idx_ref[...] = mine.astype(i32)
    for tile in range(SIDE):
        rows_ref[tile, 12:13, :] = theirs[tile : tile + 1]
        rows_ref[tile, 13:14, :] = kind[tile : tile + 1]
        rows_ref[tile, 14:16, :] = jnp.zeros((2, 128), f32)
    for copy in copies[4:]:
        copy.wait()
    moves = []
    for field, ref in enumerate((disp_ref, dir_ref)):
        part = pl.ds(6 * field, 6)
        for k in range(PARTS):
            block = me_ref[0] ^ k
            rows = pl.ds(pl.multiple_of(16 * (block & 1), 16), 16)
            moves.append((ref.at[:, block >> 1, rows, :], (same_hbm, other_hbm)[k % 2].at[k // 2, part]))
        moves.append((ref.at[:, 3], up_hbm.at[pl.ds(1 + 6 * field, 6)]))
        moves.append((ref.at[:, 0], down_hbm.at[pl.ds(1 + 6 * field, 6)]))
    moves = [pltpu.make_async_copy(a, b, more_sems.at[k]) for k, (a, b) in enumerate(moves)]
    for move in moves:
        move.start()
    split_fields(disp_ref, dir_ref, parts_ref)
    near_ref[2] = (ids_ref[3] + 1).astype(f32)
    near_ref[3] = (ids_ref[0] + 1).astype(f32)
    gather_rows(parts_ref, idx_ref, rows_ref)
    for k in range(2):
        near_ref[k] = rows_ref[2 + 2 * k : 4 + 2 * k].reshape(32, 128)
    ends = ((near_ref.at[0], up_hbm.at[0]), (near_ref.at[1], down_hbm.at[0]),
            (near_ref.at[2], up_hbm.at[13]), (near_ref.at[3], down_hbm.at[13]))
    ends = [pltpu.make_async_copy(a, b, sems.at[7 + k]) for k, (a, b) in enumerate(ends)]
    for end in ends:
        end.start()
    for d in (0, 1, SLABS - 1):
        chunk_ref[(p + d) & (SLABS - 1)] = jnp.zeros((16, 128), f32)
    for d, tile in ((2, 6), (SLABS - 2, 7)):
        chunk_ref[(p + d) & (SLABS - 1)] = rows_ref[tile]
    for d in range(3, SLABS - 2):
        tile, seg = far_place(d)
        chunk_ref[(p + d) & (SLABS - 1)] = lane_roll(rows_ref[tile], -seg)
    ends.append(pltpu.make_async_copy(chunk_ref, chunk_hbm, sems.at[11]))
    ends[-1].start()
    self_ref[...] = rows_ref[0:2]
    for move in moves + ends:
        move.wait()


def gap_kernel(p_ref, chunk_ref, up_ref, down_ref, self_ref, parts_ref, after_ref,
               idx_ref, kind_ref, gap_ref, here_ref):
    p = p_ref[0]

    def asked(d):
        return chunk_ref[(p - d) & (SLABS - 1)]

    near = [ref[0, 16 * k : 16 * (k + 1), :] for ref in (up_ref, down_ref) for k in range(2)]
    tiles = [self_ref[0], self_ref[1]] + near + [asked(2), asked(SLABS - 2)]
    tiles += merge_far(asked, 16, 0.0)
    beyond = lanes(1) >= 3 * SEG
    rows = [t[12:13] for t in tiles[:8]] + [jnp.where(beyond, -1.0, t[12:13]) for t in tiles[8:]]
    idx_ref[...] = jnp.concatenate(rows + [jnp.full((7, 128), -1.0, f32)], axis=0).astype(i32)
    kind_ref[...] = jnp.concatenate([t[13:14] for t in tiles] + [jnp.zeros((7, 128), f32)], axis=0)
    gather_rows(parts_ref, idx_ref, here_ref)
    for tile in range(24):
        gap = tiles[tile][0:12] - here_ref[tile] if tile < 17 else jnp.zeros((12, 128), f32)
        at = 128 * (tile % 3)
        for k in range(3):
            gap_ref[tile // 3, :, 384 * k + at : 384 * k + at + 128] = gap[4 * k : 4 * k + 4]


def force_kernel(me_ref, kind_ref, spread_ref, gap_ref, after_ref, out_ref, r_ref, d_ref, f_ref, t_ref):
    me = me_ref[0]
    for k in range(PARTS):
        gap = unfold(gap_ref[k])
        r_ref[6 * k : 6 * k + 6] = gap[0:6]
        d_ref[6 * k : 6 * k + 6] = gap[6:12]
    r = r_ref[...]
    dr = d_ref[...]
    w = jnp.dot(spread_ref[...], r, precision=lax.Precision.HIGHEST, preferred_element_type=f32)
    dw = jnp.dot(spread_ref[...], dr, precision=lax.Precision.HIGHEST, preferred_element_type=f32)
    bolted = jnp.concatenate([kind_ref[pl.ds(3 * me + k, 1), :] for k in range(3)], axis=1)
    slide = jnp.tanh(w / slip_speed)
    opened = jnp.tanh(r / clearance)
    friction = bolt_stiff * r + slip_force * slide
    contact = stop_stiff * (r - clearance * opened)
    f_ref[...] = bolted * friction + (1.0 - bolted) * contact
    tangent_friction = bolt_stiff * dr + slip_force * (1.0 - slide * slide) / slip_speed * dw
    tangent_contact = stop_stiff * opened * opened * dr
    t_ref[...] = bolted * tangent_friction + (1.0 - bolted) * tangent_contact
    for k in range(PARTS):
        out_ref[k] = fold(jnp.concatenate([f_ref[6 * k : 6 * k + 6], t_ref[6 * k : 6 * k + 6]], axis=0))


def reply_kernel(p_ref, force_ref, after_ref, chunk_ref, up_ref, down_ref, self_ref):
    p = p_ref[0]
    for d in (0, 1, SLABS - 1):
        chunk_ref[(p - d) & (SLABS - 1)] = jnp.zeros((4, 384), f32)
    for d, tile in ((2, 6), (SLABS - 2, 7)):
        chunk_ref[(p - d) & (SLABS - 1)] = fold(part_tile(force_ref, tile))
    for d in range(3, SLABS - 2):
        tile, seg = far_place(d)
        chunk_ref[(p - d) & (SLABS - 1)] = fold(lane_roll(part_tile(force_ref, tile), -seg))
    for k in range(2):
        self_ref[k] = part_tile(force_ref, k)
        down_ref[k] = part_tile(force_ref, 2 + k)
        up_ref[k] = part_tile(force_ref, 4 + k)


def partner_kernel(idx_ref, force_ref, lin_ref, out_ref, val_ref, sum_ref):
    for tile in range(17):
        val_ref[tile] = -part_tile(force_ref, tile)
    val_ref[17] = jnp.zeros((12, 128), f32)
    scatter_rows(val_ref, idx_ref, sum_ref)
    for x in range(4):
        out_ref[:, x] = lin_ref[:, x] + sum_ref[:, 128 * x : 128 * (x + 1)].reshape(12, 32, 128)


def final_kernel(p_ref, me_ref, idx_ref, chunk_ref, up_ref, down_ref, self_ref, part_ref, mass_ref,
                 keep_ref, cross_ref, y1_ref, y2_ref, y3_ref, res_ref, jac_ref, val_ref, sum_ref, acc_ref):
    p = p_ref[0]
    for k in range(PARTS):
        acc = (y1_ref, y2_ref, y3_ref)[k // 2 - 1][k % 2] if k > 1 else (keep_ref, cross_ref)[k][0]
        acc_ref[me_ref[0] ^ k] = acc

    def listed(d):
        return unfold(chunk_ref[(p + d) & (SLABS - 1)])

    tiles = [self_ref[0], self_ref[1], down_ref[0], down_ref[1], up_ref[0], up_ref[1], listed(2), listed(SLABS - 2)]
    tiles += merge_far(listed, 12, 0.0) + [jnp.zeros((12, 128), f32)]
    for k, tile in enumerate(tiles):
        val_ref[k] = tile
    scatter_rows(val_ref, idx_ref, sum_ref)
    for x in range(4):
        acc = jnp.concatenate([acc_ref[2 * x], acc_ref[2 * x + 1]], axis=1)
        added = sum_ref[:, 128 * x : 128 * (x + 1)].reshape(12, 32, 128)
        out = part_ref[:, x] + mass_ref[x][None] * acc + added
        res_ref[:, x] = out[0:6]
        jac_ref[:, x] = out[6:12]


def join_kernel(same_ref, other_ref, *out_refs):
    for k, out in enumerate(out_refs):
        out[0] = same_ref[k + 1]
        out[1] = other_ref[k + 1]


def time_kernel(me_ref, same_ref, other_ref, y1_ref, y2_ref, y3_ref, *refs):
    keep_ref, cross_ref, in_ref, out_ref = refs
    me = me_ref[0]
    in_ref[0] = same_ref[0]
    in_ref[1] = other_ref[0]
    for k, ref in enumerate((y1_ref, y2_ref, y3_ref)):
        in_ref[2 * k + 2 : 2 * k + 4] = ref[...]
    at = [me ^ ((me + k) & (PARTS - 1)) for k in range(PARTS)]
    count = 2 * PARTS

    def step(g, carry):
        field = g // 3
        row = 6 * field + (g - 3 * field)
        x = [in_ref[at[t // 2], row + 3 * (t % 2)] for t in range(count)]
        for t in range(count):
            acc = x[0] * float(MIXED[t, 0])
            for s in range(1, count):
                acc = acc + x[s] * float(MIXED[(t - s) % count, 0])
            out_ref[at[t // 2], row + 3 * (t % 2)] = acc
        return carry

    lax.fori_loop(0, 6, step, 0)
    for k in range(PARTS):
        (keep_ref, cross_ref)[k % 2][k // 2] = out_ref[k]


def lookup(ids, mat_ref, column, count):
    out = jnp.zeros(ids.shape, f32)
    for m in range(count):
        out = jnp.where(ids == m, mat_ref[m, column], out)
    return out


def stiff_kernel(p_ref, mat_ref, ids_ref, disp_ref, dir_ref, forcing_ref, up_ref, down_ref, out_ref, mass_ref, *, materials):
    p = p_ref[0]
    low = jnp.where(p > 0, up_ref[1:14], 0.0)
    high = jnp.where(p < SLABS - 1, down_ref[1:14], 0.0)
    ids = ids_ref[...]
    kx, ky, kz, mass = [lookup(ids, mat_ref, col, materials) for col in range(4)]
    mass_ref[...] = mass
    kx_low = lookup(low[12].astype(i32) - 1, mat_ref, 0, materials)
    kx_high = lookup(high[12].astype(i32) - 1, mat_ref, 0, materials)
    shape = ids.shape
    y = lax.broadcasted_iota(i32, shape, 1)
    z = lax.broadcasted_iota(i32, shape, 2)
    xm = 0.5 * (kx + jnp.concatenate([kx_low[None], kx[:-1]], axis=0))
    xp = 0.5 * (kx + jnp.concatenate([kx[1:], kx_high[None]], axis=0))
    total = xm + xp
    sides = []
    for k, pos, axis in ((ky, y, 1), (kz, z, 2)):
        size = shape[axis]
        for shift, edge in ((1, 0), (size - 1, size - 1)):
            inside = pos != edge
            near = jnp.where(inside, pltpu.roll(k, shift, axis), 0.0)
            side = 0.5 * (k + near)
            total = total + side
            sides.append((jnp.where(inside, side, 0.0), shift, axis))
    for field, ref in enumerate((disp_ref, dir_ref)):
        for c in range(6):
            w = ref[c]
            down = jnp.concatenate([low[6 * field + c][None], w[:-1]], axis=0)
            up = jnp.concatenate([w[1:], high[6 * field + c][None]], axis=0)
            out = total * w - xm * down - xp * up
            for side, shift, axis in sides:
                out = out - side * pltpu.roll(w, shift, axis)
            if field == 0:
                out = out - forcing_ref[c]
            out_ref[6 * field + c] = out


VMEM = 16 * 1024 * 1024


def call(kernel, outs, *args, smem=(0,), away=(), scratch=(), kept=(), limit=VMEM):
    spaces = [pltpu.SMEM if k in smem else pl.ANY if k in away else pltpu.VMEM for k in range(len(args))]
    specs = [pl.BlockSpec(memory_space=space) for space in spaces]
    return pl.pallas_call(
        kernel,
        out_shape=[jax.ShapeDtypeStruct(s, d) for s, d in outs],
        in_specs=specs,
        out_specs=[pl.BlockSpec(memory_space=pl.ANY if k in kept else pltpu.VMEM) for k in range(len(outs))],
        scratch_shapes=list(scratch),
        compiler_params=pltpu.CompilerParams(vmem_limit_bytes=limit),
    )(*args)


def shift(x, by):
    return lax.ppermute(x, "mesh", [(i, (i + by) % SLABS) for i in range(SLABS)])


def exchange(chunk, up, down):
    up, down = shift(up, 1), shift(down, -1)
    return lax.all_to_all(chunk, "mesh", split_axis=0, concat_axis=0, tiled=True), up, down


def swap(x, bit):
    return lax.ppermute(x, "inst", [(i, i ^ bit) for i in range(PARTS)])


def inst_split(x):
    return lax.all_to_all(x, "inst", split_axis=0, concat_axis=0, tiled=True)


def on_device(displacement, direction, forcing, material_ids, materials, joint_owner, joint_local, joint_remote, joint_kind):
    shape = displacement.shape
    fields = (6, 4, 32, 128)
    whole = (12, 4, 32, 128)
    disp = displacement.reshape(fields)
    dire = direction.reshape(fields)
    count = joint_local.shape[0]
    p = lax.axis_index("mesh").astype(i32).reshape(1)
    me = lax.axis_index("inst").astype(i32).reshape(1)
    parts = (768, 512)
    index = ((24, 128), i32)
    half = ((4, 12, 16, 128), f32)
    near = ((14, 32, 128), f32)

    own_idx, chunk, up, down, own, same, other = call(
        list_kernel,
        [index, ((SLABS, 16, 128), f32), near, near, ((2, 16, 128), f32), half, half],
        p,
        me,
        joint_owner.reshape(1, count),
        joint_local.reshape(1, count),
        joint_remote.reshape(1, count),
        joint_kind.reshape(1, count),
        disp,
        dire,
        material_ids,
        smem=(0, 1),
        away=range(2, 9),
        limit=60 * 1024 * 1024,
        kept=(1, 2, 3, 5, 6),
        scratch=[pltpu.VMEM(parts, bf16), pltpu.VMEM((SIDE, 16, 128), f32)]
        + [pltpu.VMEM((1, count), i32)] * 4
        + [pltpu.VMEM(fields, f32)] * 2
        + [pltpu.VMEM((4, 32, 128), i32), pltpu.VMEM((4, 32, 128), f32)]
        + [pltpu.VMEM((SLABS, 16, 128), f32), pltpu.SemaphoreType.DMA((12,)), pltpu.SemaphoreType.DMA((20,))],
    )
    chunk, up, down = exchange(chunk, up, down)

    pair = ((2, 12, 16, 128), f32)
    other = swap(other, 1)
    joined = call(join_kernel, [pair] * 3, same, other, smem=())
    turned = [swap(x, 2 * k + 2) for k, x in enumerate(joined)]
    blocks = [pltpu.VMEM((PARTS, 12, 16, 128), f32)] * 2
    keep, cross = call(time_kernel, [half] * 2, me, same, other, *turned, scratch=blocks)

    part = ((PARTS, 4, 1152), f32)
    fields_parts = call(split_kernel, [(parts, bf16)], disp, dire, smem=())[0]
    far_idx, kind, gap = call(
        gap_kernel,
        [index, ((24, 128), f32), part],
        p, chunk, up, down, own, fields_parts, joined[0],
        away=(6,),
        scratch=[pltpu.VMEM((SIDE, 12, 128), f32)],
    )
    force = call(
        force_kernel,
        [part],
        me, kind, jnp.asarray(SPREAD), inst_split(gap), keep,
        away=(4,),
        scratch=[pltpu.VMEM((48, 384), f32)] * 4,
    )[0]
    force = inst_split(force)
    cross = swap(cross, 1)
    joined = call(join_kernel, [pair] * 3, keep, cross, smem=())
    turned = [swap(x, 2 * k + 2) for k, x in enumerate(joined)]
    lin, mass = call(
        lambda *refs: stiff_kernel(*refs, materials=materials.shape[0]),
        [(whole, f32), ((4, 32, 128), f32)],
        p, materials, material_ids, disp, dire, forcing.reshape(fields), up, down,
        smem=(0, 1),
    )
    two = ((2, 12, 128), f32)
    chunk, up2, down2, own = call(reply_kernel, [((SLABS, 4, 384), f32), two, two, two], p, force, mass, away=(2,))
    chunk, up2, down2 = exchange(chunk, up2, down2)

    adding = [pltpu.VMEM((SIDE, 12, 128), f32), pltpu.VMEM((384, 512), f32)]
    partial = call(partner_kernel, [(whole, f32)], far_idx, force, lin, smem=(), scratch=adding)[0]
    residual, jacobian = call(
        final_kernel,
        [(fields, f32)] * 2,
        p, me, own_idx, chunk, up2, down2, own, partial, mass, keep, cross, *turned,
        smem=(0, 1),
        scratch=adding + blocks[:1],
    )
    return residual.reshape(shape), jacobian.reshape(shape)


def solution(mesh):
    field = P("inst", None, "mesh", None, None)
    placed = (field, field, field, P("mesh", None, None), P(), P("mesh", None), P("mesh"), P("mesh"), P("mesh"))
    return jax.shard_map(on_device, mesh=mesh, in_specs=placed, out_specs=(field, field), check_vma=False)
```

```python
import jax
import jax.numpy as jnp
import numpy as np
from jax import lax
from jax.experimental import pallas as pl
from jax.experimental.pallas import tpu as pltpu
from jax.sharding import PartitionSpec as P

frequency = 0.6
damping = 0.3
bolt_stiff = 2.0
slip_force = 1.0
slip_speed = 0.5
stop_stiff = 3.0
clearance = 0.3

SLABS = 32
PARTS = 8
SIDE = 18
SEG = 42
f32 = jnp.float32
bf16 = jnp.bfloat16
i32 = jnp.int32


def tables(count):
    offsets = np.arange(count)[:, None] - np.arange(count)[None, :]
    tangent = np.where(offsets == 0, 1.0, np.tan(np.pi * offsets / count))
    first = np.where(offsets == 0, 0.0, 0.5 * np.where(offsets % 2 == 0, 1.0, -1.0) / tangent) * frequency
    return first, first @ first


FIRST, SECOND = tables(2 * PARTS)
MIXED = (SECOND + damping * FIRST).astype(np.float32)
SPREAD = np.kron(FIRST, np.eye(3)).astype(np.float32)


def far_place(offset):
    return 8 + (offset - 3) // 3, SEG * ((offset - 3) % 3)


def fold(rows):
    return jnp.concatenate([rows[0:4], rows[4:8], rows[8:12]], axis=1)


def unfold(rows):
    width = rows.shape[1] // 3
    return jnp.concatenate([rows[:, width * k : width * (k + 1)] for k in range(3)], axis=0)


def part_tile(ref, tile):
    at = 128 * (tile % 3)
    return jnp.concatenate([ref[tile // 3, :, 384 * k + at : 384 * k + at + 128] for k in range(3)], axis=0)


def lane_roll(x, shift):
    shift = shift % 128
    return pltpu.roll(x, shift, x.ndim - 1) if shift else x


def lanes(rows):
    return lax.broadcasted_iota(i32, (rows, 128), 1)


def merge_far(read, rows, fill):
    lane = lanes(rows)
    tiles = []
    for k in range(9):
        parts = [lane_roll(read(3 + 3 * k + s), SEG * s) for s in range(3)]
        tile = jnp.where(lane < SEG, parts[0], jnp.where(lane < 2 * SEG, parts[1], parts[2]))
        tiles.append(jnp.where(lane < 3 * SEG, tile, fill))
    return tiles


def slot_tables(p, owner_ref, local_ref, remote_ref, kind_ref):
    count = owner_ref.shape[1]
    offset = (owner_ref[...] - p) & (SLABS - 1)
    hit = (lax.broadcasted_iota(i32, (SLABS, count), 0) == offset).astype(f32)
    hit16 = hit.astype(bf16)
    before = (lax.broadcasted_iota(i32, (128, 128), 0) < lax.broadcasted_iota(i32, (128, 128), 1)).astype(f32).astype(bf16)
    row = lax.broadcasted_iota(i32, (SLABS, 1), 0)
    far = row - 3
    group = (far * 171) >> 9
    start = 1024 + group * 128 + (far - 3 * group) * SEG
    for value, at in ((0, 0), (1, 256), (SLABS - 1, 512), (2, 768), (SLABS - 2, 896)):
        start = jnp.where(row == value, at, start)
    run = start.astype(f32)
    places = []
    for b in range(count // 128):
        block = hit[:, 128 * b : 128 * (b + 1)]
        earlier = jnp.dot(hit16[:, 128 * b : 128 * (b + 1)], before, preferred_element_type=f32)
        places.append(jnp.sum(block * (earlier + run), axis=0, keepdims=True))
        run = run + jnp.sum(block, axis=1, keepdims=True)
    slot = jnp.concatenate(places, axis=1).astype(i32)
    in_tile = lax.broadcasted_iota(i32, (24, count), 0) == (slot >> 7)
    in_lane = (lax.broadcasted_iota(i32, (128, count), 0) == (slot & 127)).astype(f32).astype(bf16)
    local = local_ref[...]
    remote = remote_ref[...]
    values = (local >> 7, local & 127, remote >> 7, remote & 127, kind_ref[...], jnp.ones_like(local))
    spread = jnp.concatenate([jnp.where(in_tile, v.astype(f32), 0.0) for v in values], axis=0).astype(bf16)
    got = lax.dot_general(spread, in_lane, (((1,), (1,)), ((), ())), preferred_element_type=f32)
    got = [got[24 * k : 24 * (k + 1)] for k in range(6)]
    empty = got[5] - 1.0
    return got[0] * 128.0 + got[1] + empty, got[2] * 128.0 + got[3] + empty, got[4]


def picks(idx_ref, k):
    idx = jnp.concatenate([idx_ref[pl.ds(2 * k, 1), :], idx_ref[pl.ds(2 * k + 1, 1), :]], axis=1)
    code = ((idx >> 12) << 7) | (idx & 127)
    pick = (lax.broadcasted_iota(i32, (512, 256), 0) == code).astype(f32).astype(bf16)
    return pick, lax.broadcasted_iota(i32, (32, 256), 0) == ((idx >> 7) & 31)


def split_fields(disp_ref, dir_ref, parts_ref):
    for field, ref in enumerate((disp_ref, dir_ref)):
        for x in range(4):
            value = ref[:, x].reshape(6 * 32, 128)
            hi = value.astype(bf16)
            cols = slice(128 * x, 128 * (x + 1))
            parts_ref[192 * field : 192 * (field + 1), cols] = hi
            parts_ref[384 + 192 * field : 384 + 192 * (field + 1), cols] = (value - hi.astype(f32)).astype(bf16)


def split_kernel(disp_ref, dir_ref, parts_ref):
    split_fields(disp_ref, dir_ref, parts_ref)


def gather_rows(parts_ref, idx_ref, here_ref, first, last):
    def step(k, carry):
        pick, in_y = picks(idx_ref, k)
        rows = jnp.dot(parts_ref[...], pick, preferred_element_type=f32)
        rows = (rows[:384] + rows[384:]).reshape(12, 32, 256)
        got = jnp.sum(jnp.where(in_y[None], rows, 0.0), axis=1)
        here_ref[2 * k, 0:12, :] = got[:, :128]
        here_ref[2 * k + 1, 0:12, :] = got[:, 128:]
        return carry

    lax.fori_loop(first, last, step, 0, unroll=3)


def scatter_rows(val_ref, idx_ref, sum_ref):
    dims = (((1,), (1,)), ((), ()))
    total = None
    for group in range(3):
        held, high, low = [], [], []
        for k in range(group * SIDE // 2 // 3, (group + 1) * SIDE // 2 // 3):
            pick, in_y = picks(idx_ref, k)
            value = jnp.concatenate([val_ref[2 * k], val_ref[2 * k + 1]], axis=1)
            hi = value.astype(bf16).astype(f32)
            held.append(pick)
            for out, part in ((high, hi), (low, value - hi)):
                out.append(jnp.where(in_y[None], part[:, None, :], 0.0).reshape(384, 256).astype(bf16))
        held = jnp.concatenate(held, axis=1)
        got = lax.dot_general(jnp.concatenate(high, axis=1), held, dims, preferred_element_type=f32)
        got = got + lax.dot_general(jnp.concatenate(low, axis=1), held, dims, preferred_element_type=f32)
        total = got if total is None else total + got
    sum_ref[...] = total


def list_kernel(p_ref, me_ref, owner_hbm, local_hbm, remote_hbm, kind_hbm, disp_hbm, dir_hbm, ids_hbm,
                idx_ref, chunk_hbm, up_hbm, down_hbm, self_ref, same_hbm, other_hbm,
                parts_ref, rows_ref, owner_ref, local_ref, remote_ref, kind_ref, disp_ref, dir_ref, ids_ref, near_ref,
                chunk_ref, sems, more_sems):
    p = p_ref[0]
    pairs = ((owner_hbm, owner_ref), (local_hbm, local_ref), (remote_hbm, remote_ref), (kind_hbm, kind_ref),
             (disp_hbm, disp_ref), (dir_hbm, dir_ref), (ids_hbm, ids_ref))
    copies = [pltpu.make_async_copy(a, b, sems.at[k]) for k, (a, b) in enumerate(pairs)]
    for copy in copies:
        copy.start()
    for copy in copies[:4]:
        copy.wait()
    mine, theirs, kind = slot_tables(p, owner_ref, local_ref, remote_ref, kind_ref)
    idx_ref[...] = mine.astype(i32)
    for tile in range(SIDE):
        rows_ref[tile, 12:13, :] = theirs[tile : tile + 1]
        rows_ref[tile, 13:14, :] = kind[tile : tile + 1]
        rows_ref[tile, 14:16, :] = jnp.zeros((2, 128), f32)
    for copy in copies[4:]:
        copy.wait()
    moves = []
    for field, ref in enumerate((disp_ref, dir_ref)):
        part = pl.ds(6 * field, 6)
        for k in range(PARTS):
            block = me_ref[0] ^ k
            rows = pl.ds(pl.multiple_of(16 * (block & 1), 16), 16)
            moves.append((ref.at[:, block >> 1, rows, :], (same_hbm, other_hbm)[k % 2].at[k // 2, part]))
        moves.append((ref.at[:, 3], up_hbm.at[pl.ds(1 + 6 * field, 6)]))
        moves.append((ref.at[:, 0], down_hbm.at[pl.ds(1 + 6 * field, 6)]))
    moves = [pltpu.make_async_copy(a, b, more_sems.at[k]) for k, (a, b) in enumerate(moves)]
    for move in moves:
        move.start()
    split_fields(disp_ref, dir_ref, parts_ref)
    near_ref[2] = (ids_ref[3] + 1).astype(f32)
    near_ref[3] = (ids_ref[0] + 1).astype(f32)
    for d in (0, 1, SLABS - 1):
        chunk_ref[(p + d) & (SLABS - 1)] = jnp.zeros((16, 128), f32)
    gather_rows(parts_ref, idx_ref, rows_ref, 3, SIDE // 2)
    for d, tile in ((2, 6), (SLABS - 2, 7)):
        chunk_ref[(p + d) & (SLABS - 1)] = rows_ref[tile]
    for d in range(3, SLABS - 2):
        tile, seg = far_place(d)
        chunk_ref[(p + d) & (SLABS - 1)] = lane_roll(rows_ref[tile], -seg)
    ends = [pltpu.make_async_copy(chunk_ref, chunk_hbm, sems.at[11])]
    ends[0].start()
    gather_rows(parts_ref, idx_ref, rows_ref, 0, 3)
    for k in range(2):
        near_ref[k] = rows_ref[2 + 2 * k : 4 + 2 * k].reshape(32, 128)
    pairs = ((near_ref.at[0], up_hbm.at[0]), (near_ref.at[1], down_hbm.at[0]),
             (near_ref.at[2], up_hbm.at[13]), (near_ref.at[3], down_hbm.at[13]))
    for k, (a, b) in enumerate(pairs):
        ends.append(pltpu.make_async_copy(a, b, sems.at[7 + k]))
        ends[-1].start()
    self_ref[...] = rows_ref[0:2]
    for move in moves + ends:
        move.wait()


def gap_kernel(p_ref, chunk_ref, up_ref, down_ref, self_ref, parts_ref, after_ref,
               idx_ref, kind_ref, gap_hbm, here_ref, gap_ref, sems):
    p = p_ref[0]

    def asked(d):
        return chunk_ref[(p - d) & (SLABS - 1)]

    near = [ref[0, 16 * k : 16 * (k + 1), :] for ref in (up_ref, down_ref) for k in range(2)]
    tiles = [self_ref[0], self_ref[1]] + near + [asked(2), asked(SLABS - 2)]
    tiles += merge_far(asked, 16, 0.0)
    beyond = lanes(1) >= 3 * SEG
    rows = [t[12:13] for t in tiles[:8]] + [jnp.where(beyond, -1.0, t[12:13]) for t in tiles[8:]]
    idx_ref[...] = jnp.concatenate(rows + [jnp.full((7, 128), -1.0, f32)], axis=0).astype(i32)
    kind_ref[...] = jnp.concatenate([t[13:14] for t in tiles] + [jnp.zeros((7, 128), f32)], axis=0)
    copies = [pltpu.make_async_copy(gap_ref.at[pl.ds(2 * g, 2)], gap_hbm.at[pl.ds(2 * g, 2)], sems.at[g]) for g in range(4)]
    gap_ref[6:8] = jnp.zeros((2, 4, 1152), f32)
    copies[3].start()
    for g in range(3):
        gather_rows(parts_ref, idx_ref, here_ref, 3 * g, 3 * g + 3)
        for tile in range(6 * g, 6 * g + 6):
            gap = tiles[tile][0:12] - here_ref[tile] if tile < 17 else jnp.zeros((12, 128), f32)
            at = 128 * (tile % 3)
            for k in range(3):
                gap_ref[tile // 3, :, 384 * k + at : 384 * k + at + 128] = gap[4 * k : 4 * k + 4]
        copies[g].start()
    for copy in copies:
        copy.wait()


def force_kernel(me_ref, kind_ref, spread_ref, gap_ref, after_ref, out_ref, r_ref, d_ref, f_ref, t_ref):
    me = me_ref[0]
    for k in range(PARTS):
        gap = unfold(gap_ref[k])
        r_ref[6 * k : 6 * k + 6] = gap[0:6]
        d_ref[6 * k : 6 * k + 6] = gap[6:12]
    r = r_ref[...]
    dr = d_ref[...]
    w = jnp.dot(spread_ref[...], r, precision=lax.Precision.HIGHEST, preferred_element_type=f32)
    dw = jnp.dot(spread_ref[...], dr, precision=lax.Precision.HIGHEST, preferred_element_type=f32)
    bolted = jnp.concatenate([kind_ref[pl.ds(3 * me + k, 1), :] for k in range(3)], axis=1)
    slide = jnp.tanh(w / slip_speed)
    opened = jnp.tanh(r / clearance)
    friction = bolt_stiff * r + slip_force * slide
    contact = stop_stiff * (r - clearance * opened)
    f_ref[...] = bolted * friction + (1.0 - bolted) * contact
    tangent_friction = bolt_stiff * dr + slip_force * (1.0 - slide * slide) / slip_speed * dw
    tangent_contact = stop_stiff * opened * opened * dr
    t_ref[...] = bolted * tangent_friction + (1.0 - bolted) * tangent_contact
    for k in range(PARTS):
        out_ref[k] = fold(jnp.concatenate([f_ref[6 * k : 6 * k + 6], t_ref[6 * k : 6 * k + 6]], axis=0))


def reply_kernel(p_ref, force_ref, after_ref, chunk_ref, up_ref, down_ref, self_ref):
    p = p_ref[0]
    for d in (0, 1, SLABS - 1):
        chunk_ref[(p - d) & (SLABS - 1)] = jnp.zeros((4, 384), f32)
    for d, tile in ((2, 6), (SLABS - 2, 7)):
        chunk_ref[(p - d) & (SLABS - 1)] = fold(part_tile(force_ref, tile))
    for d in range(3, SLABS - 2):
        tile, seg = far_place(d)
        chunk_ref[(p - d) & (SLABS - 1)] = fold(lane_roll(part_tile(force_ref, tile), -seg))
    for k in range(2):
        self_ref[k] = part_tile(force_ref, k)
        down_ref[k] = part_tile(force_ref, 2 + k)
        up_ref[k] = part_tile(force_ref, 4 + k)


def partner_kernel(idx_ref, force_ref, lin_ref, out_ref, val_ref, sum_ref):
    for tile in range(17):
        val_ref[tile] = -part_tile(force_ref, tile)
    val_ref[17] = jnp.zeros((12, 128), f32)
    scatter_rows(val_ref, idx_ref, sum_ref)
    for x in range(4):
        out_ref[:, x] = lin_ref[:, x] + sum_ref[:, 128 * x : 128 * (x + 1)].reshape(12, 32, 128)


def final_kernel(p_ref, me_ref, idx_ref, chunk_ref, up_ref, down_ref, self_ref, part_ref, mass_ref,
                 keep_ref, cross_ref, y1_ref, y2_ref, y3_ref, res_ref, jac_ref, val_ref, sum_ref, acc_ref):
    p = p_ref[0]
    for k in range(PARTS):
        acc = (y1_ref, y2_ref, y3_ref)[k // 2 - 1][k % 2] if k > 1 else (keep_ref, cross_ref)[k][0]
        acc_ref[me_ref[0] ^ k] = acc

    def listed(d):
        return unfold(chunk_ref[(p + d) & (SLABS - 1)])

    tiles = [self_ref[0], self_ref[1], down_ref[0], down_ref[1], up_ref[0], up_ref[1], listed(2), listed(SLABS - 2)]
    tiles += merge_far(listed, 12, 0.0) + [jnp.zeros((12, 128), f32)]
    for k, tile in enumerate(tiles):
        val_ref[k] = tile
    scatter_rows(val_ref, idx_ref, sum_ref)
    for x in range(4):
        acc = jnp.concatenate([acc_ref[2 * x], acc_ref[2 * x + 1]], axis=1)
        added = sum_ref[:, 128 * x : 128 * (x + 1)].reshape(12, 32, 128)
        out = part_ref[:, x] + mass_ref[x][None] * acc + added
        res_ref[:, x] = out[0:6]
        jac_ref[:, x] = out[6:12]


def join_kernel(same_ref, other_ref, *out_refs):
    for k, out in enumerate(out_refs):
        out[0] = same_ref[k + 1]
        out[1] = other_ref[k + 1]


def rejoin_kernel(keep_ref, cross1_ref, cross2_ref, *out_refs):
    for k, out in enumerate(out_refs):
        out[0] = keep_ref[k + 1]
        out[1] = (cross1_ref, cross2_ref)[(k + 1) // 2][(k + 1) % 2]


def time_kernel(me_ref, same_ref, other_ref, y1_ref, y2_ref, y3_ref, *refs):
    keep_ref, cross1_ref, cross2_ref, in_ref, out_ref = refs
    me = me_ref[0]
    in_ref[0] = same_ref[0]
    in_ref[1] = other_ref[0]
    for k, ref in enumerate((y1_ref, y2_ref, y3_ref)):
        in_ref[2 * k + 2 : 2 * k + 4] = ref[...]
    at = [me ^ ((me + k) & (PARTS - 1)) for k in range(PARTS)]
    count = 2 * PARTS

    def step(g, carry):
        field = g // 3
        row = 6 * field + (g - 3 * field)
        x = [in_ref[at[t // 2], row + 3 * (t % 2)] for t in range(count)]
        for t in range(count):
            acc = x[0] * float(MIXED[t, 0])
            for s in range(1, count):
                acc = acc + x[s] * float(MIXED[(t - s) % count, 0])
            out_ref[at[t // 2], row + 3 * (t % 2)] = acc
        return carry

    lax.fori_loop(0, 6, step, 0)
    for k in range(PARTS):
        ref, at = (keep_ref, k // 2) if k % 2 == 0 else ((cross1_ref, cross2_ref)[k // 4], k // 2 % 2)
        ref[at] = out_ref[k]


def lookup(ids, mat_ref, column, count):
    out = jnp.zeros(ids.shape, f32)
    for m in range(count):
        out = jnp.where(ids == m, mat_ref[m, column], out)
    return out


def stiff_kernel(p_ref, mat_ref, ids_ref, disp_ref, dir_ref, forcing_ref, up_ref, down_ref, after_ref, out_ref, mass_ref, *, materials):
    p = p_ref[0]
    low = jnp.where(p > 0, up_ref[1:14], 0.0)
    high = jnp.where(p < SLABS - 1, down_ref[1:14], 0.0)
    ids = ids_ref[...]
    kx, ky, kz, mass = [lookup(ids, mat_ref, col, materials) for col in range(4)]
    mass_ref[...] = mass
    kx_low = lookup(low[12].astype(i32) - 1, mat_ref, 0, materials)
    kx_high = lookup(high[12].astype(i32) - 1, mat_ref, 0, materials)
    shape = ids.shape
    y = lax.broadcasted_iota(i32, shape, 1)
    z = lax.broadcasted_iota(i32, shape, 2)
    xm = 0.5 * (kx + jnp.concatenate([kx_low[None], kx[:-1]], axis=0))
    xp = 0.5 * (kx + jnp.concatenate([kx[1:], kx_high[None]], axis=0))
    total = xm + xp
    sides = []
    for k, pos, axis in ((ky, y, 1), (kz, z, 2)):
        size = shape[axis]
        for shift, edge in ((1, 0), (size - 1, size - 1)):
            inside = pos != edge
            near = jnp.where(inside, pltpu.roll(k, shift, axis), 0.0)
            side = 0.5 * (k + near)
            total = total + side
            sides.append((jnp.where(inside, side, 0.0), shift, axis))
    for field, ref in enumerate((disp_ref, dir_ref)):
        for c in range(6):
            w = ref[c]
            down = jnp.concatenate([low[6 * field + c][None], w[:-1]], axis=0)
            up = jnp.concatenate([w[1:], high[6 * field + c][None]], axis=0)
            out = total * w - xm * down - xp * up
            for side, shift, axis in sides:
                out = out - side * pltpu.roll(w, shift, axis)
            if field == 0:
                out = out - forcing_ref[c]
            out_ref[6 * field + c] = out


VMEM = 16 * 1024 * 1024


def call(kernel, outs, *args, smem=(0,), away=(), scratch=(), kept=(), limit=VMEM):
    spaces = [pltpu.SMEM if k in smem else pl.ANY if k in away else pltpu.VMEM for k in range(len(args))]
    specs = [pl.BlockSpec(memory_space=space) for space in spaces]
    return pl.pallas_call(
        kernel,
        out_shape=[jax.ShapeDtypeStruct(s, d) for s, d in outs],
        in_specs=specs,
        out_specs=[pl.BlockSpec(memory_space=pltpu.HBM if k in kept else pltpu.VMEM) for k in range(len(outs))],
        scratch_shapes=list(scratch),
        compiler_params=pltpu.CompilerParams(vmem_limit_bytes=limit),
    )(*args)


def shift(x, by):
    return lax.ppermute(x, "mesh", [(i, (i + by) % SLABS) for i in range(SLABS)])


def exchange(chunk, up, down):
    up, down = shift(up, 1), shift(down, -1)
    return lax.all_to_all(chunk, "mesh", split_axis=0, concat_axis=0, tiled=True), up, down


def swap(x, bit):
    return lax.ppermute(x, "inst", [(i, i ^ bit) for i in range(PARTS)])


def inst_split(x):
    return lax.all_to_all(x, "inst", split_axis=0, concat_axis=0, tiled=True)


def on_device(displacement, direction, forcing, material_ids, materials, joint_owner, joint_local, joint_remote, joint_kind):
    shape = displacement.shape
    fields = (6, 4, 32, 128)
    whole = (12, 4, 32, 128)
    disp = displacement.reshape(fields)
    dire = direction.reshape(fields)
    count = joint_local.shape[0]
    p = lax.axis_index("mesh").astype(i32).reshape(1)
    me = lax.axis_index("inst").astype(i32).reshape(1)
    parts = (768, 512)
    index = ((24, 128), i32)
    half = ((4, 12, 16, 128), f32)
    near = ((14, 32, 128), f32)

    own_idx, chunk, up, down, own, same, other = call(
        list_kernel,
        [index, ((SLABS, 16, 128), f32), near, near, ((2, 16, 128), f32), half, half],
        p,
        me,
        joint_owner.reshape(1, count),
        joint_local.reshape(1, count),
        joint_remote.reshape(1, count),
        joint_kind.reshape(1, count),
        disp,
        dire,
        material_ids,
        smem=(0, 1),
        away=range(2, 9),
        limit=60 * 1024 * 1024,
        kept=(1, 2, 3, 5, 6),
        scratch=[pltpu.VMEM(parts, bf16), pltpu.VMEM((SIDE, 16, 128), f32)]
        + [pltpu.VMEM((1, count), i32)] * 4
        + [pltpu.VMEM(fields, f32)] * 2
        + [pltpu.VMEM((4, 32, 128), i32), pltpu.VMEM((4, 32, 128), f32)]
        + [pltpu.VMEM((SLABS, 16, 128), f32), pltpu.SemaphoreType.DMA((12,)), pltpu.SemaphoreType.DMA((20,))],
    )
    chunk, up, down = exchange(chunk, up, down)

    pair = ((2, 12, 16, 128), f32)
    other = swap(other, 1)
    joined = call(join_kernel, [pair] * 3, same, other, smem=())
    turned = [swap(x, 2 * k + 2) for k, x in enumerate(joined)]
    blocks = [pltpu.VMEM((PARTS, 12, 16, 128), f32)] * 2
    keep, *cross = call(time_kernel, [half, pair, pair], me, same, other, *turned, scratch=blocks)

    part = ((PARTS, 4, 1152), f32)
    fields_parts = call(split_kernel, [(parts, bf16)], disp, dire, smem=())[0]
    far_idx, kind, gap = call(
        gap_kernel,
        [index, ((24, 128), f32), part],
        p, chunk, up, down, own, fields_parts, joined[0],
        away=(6,),
        kept=(2,),
        scratch=[pltpu.VMEM((SIDE, 12, 128), f32), pltpu.VMEM(part[0], f32), pltpu.SemaphoreType.DMA((4,))],
    )
    force = call(
        force_kernel,
        [part],
        me, kind, jnp.asarray(SPREAD), inst_split(gap), keep,
        away=(4,),
        scratch=[pltpu.VMEM((48, 384), f32)] * 4,
    )[0]
    force = inst_split(force)
    cross = [swap(x, 1) for x in cross]
    joined = call(rejoin_kernel, [pair] * 3, keep, *cross, smem=())
    turned = [swap(x, 2 * k + 2) for k, x in enumerate(joined)]
    lin, mass = call(
        lambda *refs: stiff_kernel(*refs, materials=materials.shape[0]),
        [(whole, f32), ((4, 32, 128), f32)],
        p, materials, material_ids, disp, dire, forcing.reshape(fields), up, down, joined[0],
        smem=(0, 1),
        away=(8,),
    )
    two = ((2, 12, 128), f32)
    chunk, up2, down2, own = call(reply_kernel, [((SLABS, 4, 384), f32), two, two, two], p, force, mass, away=(2,))
    chunk, up2, down2 = exchange(chunk, up2, down2)

    adding = [pltpu.VMEM((SIDE, 12, 128), f32), pltpu.VMEM((384, 512), f32)]
    partial = call(partner_kernel, [(whole, f32)], far_idx, force, lin, smem=(), scratch=adding)[0]
    residual, jacobian = call(
        final_kernel,
        [(fields, f32)] * 2,
        p, me, own_idx, chunk, up2, down2, own, partial, mass, keep, cross[0], *turned,
        smem=(0, 1),
        scratch=adding + blocks[:1],
    )
    return residual.reshape(shape), jacobian.reshape(shape)


def solution(mesh):
    field = P("inst", None, "mesh", None, None)
    placed = (field, field, field, P("mesh", None, None), P(), P("mesh", None), P("mesh"), P("mesh"), P("mesh"))
    return jax.shard_map(on_device, mesh=mesh, in_specs=placed, out_specs=(field, field), check_vma=False)
```

```python
import jax
import jax.numpy as jnp
import numpy as np
from jax import lax
from jax.experimental import pallas as pl
from jax.experimental.pallas import tpu as pltpu
from jax.sharding import PartitionSpec as P

frequency = 0.6
damping = 0.3
bolt_stiff = 2.0
slip_force = 1.0
slip_speed = 0.5
stop_stiff = 3.0
clearance = 0.3

SLABS = 32
PARTS = 8
SIDE = 18
SEG = 42
f32 = jnp.float32
bf16 = jnp.bfloat16
i32 = jnp.int32


def tables(count):
    offsets = np.arange(count)[:, None] - np.arange(count)[None, :]
    tangent = np.where(offsets == 0, 1.0, np.tan(np.pi * offsets / count))
    first = np.where(offsets == 0, 0.0, 0.5 * np.where(offsets % 2 == 0, 1.0, -1.0) / tangent) * frequency
    return first, first @ first


FIRST, SECOND = tables(2 * PARTS)
MIXED = (SECOND + damping * FIRST).astype(np.float32)
SPREAD = np.kron(FIRST, np.eye(3)).astype(np.float32)


def far_tile(offset):
    return 8 + (offset - 3) // 3


def fold(rows):
    return jnp.concatenate([rows[0:4], rows[4:8], rows[8:12]], axis=1)


def unfold(rows):
    width = rows.shape[1] // 3
    return jnp.concatenate([rows[:, width * k : width * (k + 1)] for k in range(3)], axis=0)


def part_tile(ref, tile):
    at = 128 * (tile % 3)
    return jnp.concatenate([ref[tile // 3, :, 384 * k + at : 384 * k + at + 128] for k in range(3)], axis=0)


def lanes(rows):
    return lax.broadcasted_iota(i32, (rows, 128), 1)


def merge_far(read, rows, fill):
    lane = lanes(rows)
    tiles = []
    for k in range(9):
        parts = [read(3 + 3 * k + s) for s in range(3)]
        tile = jnp.where(lane < SEG, parts[0], jnp.where(lane < 2 * SEG, parts[1], parts[2]))
        tiles.append(jnp.where(lane < 3 * SEG, tile, fill))
    return tiles


def slot_tables(p, owner_ref, local_ref, remote_ref, kind_ref):
    count = owner_ref.shape[1]
    offset = (owner_ref[...] - p) & (SLABS - 1)
    hit = (lax.broadcasted_iota(i32, (SLABS, count), 0) == offset).astype(f32)
    hit16 = hit.astype(bf16)
    before = (lax.broadcasted_iota(i32, (128, 128), 0) < lax.broadcasted_iota(i32, (128, 128), 1)).astype(f32).astype(bf16)
    row = lax.broadcasted_iota(i32, (SLABS, 1), 0)
    far = row - 3
    group = (far * 171) >> 9
    start = 1024 + group * 128 + (far - 3 * group) * SEG
    for value, at in ((0, 0), (1, 256), (SLABS - 1, 512), (2, 768), (SLABS - 2, 896)):
        start = jnp.where(row == value, at, start)
    run = start.astype(f32)
    places = []
    for b in range(count // 128):
        block = hit[:, 128 * b : 128 * (b + 1)]
        earlier = jnp.dot(hit16[:, 128 * b : 128 * (b + 1)], before, preferred_element_type=f32)
        places.append(jnp.sum(block * (earlier + run), axis=0, keepdims=True))
        run = run + jnp.sum(block, axis=1, keepdims=True)
    slot = jnp.concatenate(places, axis=1).astype(i32)
    in_tile = lax.broadcasted_iota(i32, (24, count), 0) == (slot >> 7)
    in_lane = (lax.broadcasted_iota(i32, (128, count), 0) == (slot & 127)).astype(f32).astype(bf16)
    local = local_ref[...]
    remote = remote_ref[...]
    values = (local >> 7, local & 127, remote >> 7, remote & 127, kind_ref[...], jnp.ones_like(local))
    spread = jnp.concatenate([jnp.where(in_tile, v.astype(f32), 0.0) for v in values], axis=0).astype(bf16)
    got = lax.dot_general(spread, in_lane, (((1,), (1,)), ((), ())), preferred_element_type=f32)
    got = [got[24 * k : 24 * (k + 1)] for k in range(6)]
    empty = got[5] - 1.0
    return got[0] * 128.0 + got[1] + empty, got[2] * 128.0 + got[3] + empty, got[4]


def picks(idx_ref, k):
    idx = jnp.concatenate([idx_ref[pl.ds(2 * k, 1), :], idx_ref[pl.ds(2 * k + 1, 1), :]], axis=1)
    code = ((idx >> 12) << 7) | (idx & 127)
    pick = (lax.broadcasted_iota(i32, (512, 256), 0) == code).astype(f32).astype(bf16)
    return pick, lax.broadcasted_iota(i32, (32, 256), 0) == ((idx >> 7) & 31)


def split_fields(disp_ref, dir_ref, parts_ref):
    for field, ref in enumerate((disp_ref, dir_ref)):
        for x in range(4):
            value = ref[:, x].reshape(6 * 32, 128)
            hi = value.astype(bf16)
            cols = slice(128 * x, 128 * (x + 1))
            parts_ref[192 * field : 192 * (field + 1), cols] = hi
            parts_ref[384 + 192 * field : 384 + 192 * (field + 1), cols] = (value - hi.astype(f32)).astype(bf16)


def split_kernel(disp_ref, dir_ref, parts_ref):
    split_fields(disp_ref, dir_ref, parts_ref)


def gather_rows(parts_ref, idx_ref, here_ref, first, last):
    def step(k, carry):
        pick, in_y = picks(idx_ref, k)
        rows = jnp.dot(parts_ref[...], pick, preferred_element_type=f32)
        rows = (rows[:384] + rows[384:]).reshape(12, 32, 256)
        got = jnp.sum(jnp.where(in_y[None], rows, 0.0), axis=1)
        here_ref[2 * k, 0:12, :] = got[:, :128]
        here_ref[2 * k + 1, 0:12, :] = got[:, 128:]
        return carry

    lax.fori_loop(first, last, step, 0, unroll=3)


def scatter_rows(val_ref, idx_ref, sum_ref):
    dims = (((1,), (1,)), ((), ()))
    total = None
    for group in range(3):
        held, high, low = [], [], []
        for k in range(group * SIDE // 2 // 3, (group + 1) * SIDE // 2 // 3):
            pick, in_y = picks(idx_ref, k)
            value = jnp.concatenate([val_ref[2 * k], val_ref[2 * k + 1]], axis=1)
            hi = value.astype(bf16).astype(f32)
            held.append(pick)
            for out, part in ((high, hi), (low, value - hi)):
                out.append(jnp.where(in_y[None], part[:, None, :], 0.0).reshape(384, 256).astype(bf16))
        held = jnp.concatenate(held, axis=1)
        got = lax.dot_general(jnp.concatenate(high, axis=1), held, dims, preferred_element_type=f32)
        got = got + lax.dot_general(jnp.concatenate(low, axis=1), held, dims, preferred_element_type=f32)
        total = got if total is None else total + got
    sum_ref[...] = total


def list_kernel(p_ref, me_ref, owner_hbm, local_hbm, remote_hbm, kind_hbm, disp_hbm, dir_hbm, ids_hbm,
                idx_ref, chunk_hbm, up_hbm, down_hbm, self_ref, same_hbm, other_hbm,
                parts_ref, rows_ref, owner_ref, local_ref, remote_ref, kind_ref, disp_ref, dir_ref, ids_ref, near_ref,
                chunk_ref, sems, more_sems):
    p = p_ref[0]
    pairs = ((owner_hbm, owner_ref), (local_hbm, local_ref), (remote_hbm, remote_ref), (kind_hbm, kind_ref),
             (disp_hbm, disp_ref), (dir_hbm, dir_ref), (ids_hbm, ids_ref))
    copies = [pltpu.make_async_copy(a, b, sems.at[k]) for k, (a, b) in enumerate(pairs)]
    for copy in copies:
        copy.start()
    for copy in copies[:4]:
        copy.wait()
    mine, theirs, kind = slot_tables(p, owner_ref, local_ref, remote_ref, kind_ref)
    idx_ref[...] = mine.astype(i32)
    for tile in range(SIDE):
        rows_ref[tile, 12:13, :] = theirs[tile : tile + 1]
        rows_ref[tile, 13:14, :] = kind[tile : tile + 1]
        rows_ref[tile, 14:16, :] = jnp.zeros((2, 128), f32)
    for copy in copies[4:]:
        copy.wait()
    moves = []
    for field, ref in enumerate((disp_ref, dir_ref)):
        part = pl.ds(6 * field, 6)
        for k in range(PARTS):
            block = me_ref[0] ^ k
            rows = pl.ds(pl.multiple_of(16 * (block & 1), 16), 16)
            moves.append((ref.at[:, block >> 1, rows, :], (same_hbm, other_hbm)[k % 2].at[k // 2, part]))
        moves.append((ref.at[:, 3], up_hbm.at[pl.ds(1 + 6 * field, 6)]))
        moves.append((ref.at[:, 0], down_hbm.at[pl.ds(1 + 6 * field, 6)]))
    moves = [pltpu.make_async_copy(a, b, more_sems.at[k]) for k, (a, b) in enumerate(moves)]
    for move in moves:
        move.start()
    split_fields(disp_ref, dir_ref, parts_ref)
    near_ref[2] = (ids_ref[3] + 1).astype(f32)
    near_ref[3] = (ids_ref[0] + 1).astype(f32)
    for d in (0, 1, SLABS - 1):
        chunk_ref[(p + d) & (SLABS - 1)] = jnp.zeros((16, 128), f32)
    gather_rows(parts_ref, idx_ref, rows_ref, 3, SIDE // 2)
    for d, tile in ((2, 6), (SLABS - 2, 7)):
        chunk_ref[(p + d) & (SLABS - 1)] = rows_ref[tile]
    for d in range(3, SLABS - 2):
        tile = far_tile(d)
        chunk_ref[(p + d) & (SLABS - 1)] = rows_ref[tile]
    ends = [pltpu.make_async_copy(chunk_ref, chunk_hbm, sems.at[11])]
    ends[0].start()
    gather_rows(parts_ref, idx_ref, rows_ref, 0, 3)
    for k in range(2):
        near_ref[k] = rows_ref[2 + 2 * k : 4 + 2 * k].reshape(32, 128)
    pairs = ((near_ref.at[0], up_hbm.at[0]), (near_ref.at[1], down_hbm.at[0]),
             (near_ref.at[2], up_hbm.at[13]), (near_ref.at[3], down_hbm.at[13]))
    for k, (a, b) in enumerate(pairs):
        ends.append(pltpu.make_async_copy(a, b, sems.at[7 + k]))
        ends[-1].start()
    self_ref[...] = rows_ref[0:2]
    for move in moves + ends:
        move.wait()


def gap_kernel(p_ref, chunk_ref, up_ref, down_ref, self_ref, parts_ref, after_ref,
               idx_ref, kind_ref, gap_ref, here_ref):
    p = p_ref[0]

    def asked(d):
        return chunk_ref[(p - d) & (SLABS - 1)]

    near = [ref[0, 16 * k : 16 * (k + 1), :] for ref in (up_ref, down_ref) for k in range(2)]
    tiles = [self_ref[0], self_ref[1]] + near + [asked(2), asked(SLABS - 2)]
    tiles += merge_far(asked, 16, 0.0)
    beyond = lanes(1) >= 3 * SEG
    rows = [t[12:13] for t in tiles[:8]] + [jnp.where(beyond, -1.0, t[12:13]) for t in tiles[8:]]
    idx_ref[...] = jnp.concatenate(rows + [jnp.full((7, 128), -1.0, f32)], axis=0).astype(i32)
    kind_ref[...] = jnp.concatenate([t[13:14] for t in tiles] + [jnp.zeros((7, 128), f32)], axis=0)
    gather_rows(parts_ref, idx_ref, here_ref, 0, SIDE // 2)
    for tile in range(24):
        gap = tiles[tile][0:12] - here_ref[tile] if tile < 17 else jnp.zeros((12, 128), f32)
        at = 128 * (tile % 3)
        for k in range(3):
            gap_ref[tile // 3, :, 384 * k + at : 384 * k + at + 128] = gap[4 * k : 4 * k + 4]


def force_kernel(me_ref, kind_ref, spread_ref, gap_ref, after_ref, out_ref, r_ref, d_ref, f_ref, t_ref):
    me = me_ref[0]
    for k in range(PARTS):
        gap = unfold(gap_ref[k])
        r_ref[6 * k : 6 * k + 6] = gap[0:6]
        d_ref[6 * k : 6 * k + 6] = gap[6:12]
    r = r_ref[...]
    dr = d_ref[...]
    w = jnp.dot(spread_ref[...], r, precision=lax.Precision.HIGHEST, preferred_element_type=f32)
    dw = jnp.dot(spread_ref[...], dr, precision=lax.Precision.HIGHEST, preferred_element_type=f32)
    bolted = jnp.concatenate([kind_ref[pl.ds(3 * me + k, 1), :] for k in range(3)], axis=1)
    slide = jnp.tanh(w / slip_speed)
    opened = jnp.tanh(r / clearance)
    friction = bolt_stiff * r + slip_force * slide
    contact = stop_stiff * (r - clearance * opened)
    f_ref[...] = bolted * friction + (1.0 - bolted) * contact
    tangent_friction = bolt_stiff * dr + slip_force * (1.0 - slide * slide) / slip_speed * dw
    tangent_contact = stop_stiff * opened * opened * dr
    t_ref[...] = bolted * tangent_friction + (1.0 - bolted) * tangent_contact
    for k in range(PARTS):
        out_ref[k] = fold(jnp.concatenate([f_ref[6 * k : 6 * k + 6], t_ref[6 * k : 6 * k + 6]], axis=0))


def reply_kernel(p_ref, force_ref, after_ref, chunk_ref, up_ref, down_ref, self_ref):
    p = p_ref[0]
    for d in (0, 1, SLABS - 1):
        chunk_ref[(p - d) & (SLABS - 1)] = jnp.zeros((4, 384), f32)
    for d, tile in ((2, 6), (SLABS - 2, 7)):
        chunk_ref[(p - d) & (SLABS - 1)] = fold(part_tile(force_ref, tile))
    for d in range(3, SLABS - 2):
        tile = far_tile(d)
        chunk_ref[(p - d) & (SLABS - 1)] = fold(part_tile(force_ref, tile))
    for k in range(2):
        self_ref[k] = part_tile(force_ref, k)
        down_ref[k] = part_tile(force_ref, 2 + k)
        up_ref[k] = part_tile(force_ref, 4 + k)


def partner_kernel(idx_ref, force_ref, lin_ref, out_ref, val_ref, sum_ref):
    for tile in range(17):
        val_ref[tile] = -part_tile(force_ref, tile)
    val_ref[17] = jnp.zeros((12, 128), f32)
    scatter_rows(val_ref, idx_ref, sum_ref)
    for x in range(4):
        out_ref[:, x] = lin_ref[:, x] + sum_ref[:, 128 * x : 128 * (x + 1)].reshape(12, 32, 128)


def final_kernel(p_ref, me_ref, idx_ref, chunk_ref, up_ref, down_ref, self_ref, part_ref, mass_ref,
                 keep_ref, cross_ref, y1_ref, y2_ref, y3_ref, res_ref, jac_ref, val_ref, sum_ref, acc_ref):
    p = p_ref[0]
    for k in range(PARTS):
        acc = (y1_ref, y2_ref, y3_ref)[k // 2 - 1][k % 2] if k > 1 else (keep_ref, cross_ref)[k][0]
        acc_ref[me_ref[0] ^ k] = acc

    def listed(d):
        return unfold(chunk_ref[(p + d) & (SLABS - 1)])

    tiles = [self_ref[0], self_ref[1], down_ref[0], down_ref[1], up_ref[0], up_ref[1], listed(2), listed(SLABS - 2)]
    tiles += merge_far(listed, 12, 0.0) + [jnp.zeros((12, 128), f32)]
    for k, tile in enumerate(tiles):
        val_ref[k] = tile
    scatter_rows(val_ref, idx_ref, sum_ref)
    for x in range(4):
        acc = jnp.concatenate([acc_ref[2 * x], acc_ref[2 * x + 1]], axis=1)
        added = sum_ref[:, 128 * x : 128 * (x + 1)].reshape(12, 32, 128)
        out = part_ref[:, x] + mass_ref[x][None] * acc + added
        res_ref[:, x] = out[0:6]
        jac_ref[:, x] = out[6:12]


def join_kernel(same_ref, other_ref, *out_refs):
    for k, out in enumerate(out_refs):
        out[0] = same_ref[k + 1]
        out[1] = other_ref[k + 1]


def rejoin_kernel(keep_ref, cross1_ref, cross2_ref, *out_refs):
    for k, out in enumerate(out_refs):
        out[0] = keep_ref[k + 1]
        out[1] = (cross1_ref, cross2_ref)[(k + 1) // 2][(k + 1) % 2]


def time_kernel(me_ref, same_ref, other_ref, y1_ref, y2_ref, y3_ref, *refs):
    keep_ref, cross1_ref, cross2_ref, in_ref, out_ref = refs
    me = me_ref[0]
    in_ref[0] = same_ref[0]
    in_ref[1] = other_ref[0]
    for k, ref in enumerate((y1_ref, y2_ref, y3_ref)):
        in_ref[2 * k + 2 : 2 * k + 4] = ref[...]
    at = [me ^ ((me + k) & (PARTS - 1)) for k in range(PARTS)]
    count = 2 * PARTS

    def step(g, carry):
        field = g // 3
        row = 6 * field + (g - 3 * field)
        x = [in_ref[at[t // 2], row + 3 * (t % 2)] for t in range(count)]
        for t in range(count):
            acc = x[0] * float(MIXED[t, 0])
            for s in range(1, count):
                acc = acc + x[s] * float(MIXED[(t - s) % count, 0])
            out_ref[at[t // 2], row + 3 * (t % 2)] = acc
        return carry

    lax.fori_loop(0, 6, step, 0)
    for k in range(PARTS):
        ref, at = (keep_ref, k // 2) if k % 2 == 0 else ((cross1_ref, cross2_ref)[k // 4], k // 2 % 2)
        ref[at] = out_ref[k]


def lookup(ids, mat_ref, column, count):
    out = jnp.zeros(ids.shape, f32)
    for m in range(count):
        out = jnp.where(ids == m, mat_ref[m, column], out)
    return out


def stiff_kernel(p_ref, mat_ref, ids_ref, disp_ref, dir_ref, forcing_ref, up_ref, down_ref, after_ref, out_ref, mass_ref, *, materials):
    p = p_ref[0]
    low = jnp.where(p > 0, up_ref[1:14], 0.0)
    high = jnp.where(p < SLABS - 1, down_ref[1:14], 0.0)
    ids = ids_ref[...]
    kx, ky, kz, mass = [lookup(ids, mat_ref, col, materials) for col in range(4)]
    mass_ref[...] = mass
    kx_low = lookup(low[12].astype(i32) - 1, mat_ref, 0, materials)
    kx_high = lookup(high[12].astype(i32) - 1, mat_ref, 0, materials)
    shape = ids.shape
    y = lax.broadcasted_iota(i32, shape, 1)
    z = lax.broadcasted_iota(i32, shape, 2)
    xm = 0.5 * (kx + jnp.concatenate([kx_low[None], kx[:-1]], axis=0))
    xp = 0.5 * (kx + jnp.concatenate([kx[1:], kx_high[None]], axis=0))
    total = xm + xp
    sides = []
    for k, pos, axis in ((ky, y, 1), (kz, z, 2)):
        size = shape[axis]
        for shift, edge in ((1, 0), (size - 1, size - 1)):
            inside = pos != edge
            near = jnp.where(inside, pltpu.roll(k, shift, axis), 0.0)
            side = 0.5 * (k + near)
            total = total + side
            sides.append((jnp.where(inside, side, 0.0), shift, axis))
    for field, ref in enumerate((disp_ref, dir_ref)):
        for c in range(6):
            w = ref[c]
            down = jnp.concatenate([low[6 * field + c][None], w[:-1]], axis=0)
            up = jnp.concatenate([w[1:], high[6 * field + c][None]], axis=0)
            out = total * w - xm * down - xp * up
            for side, shift, axis in sides:
                out = out - side * pltpu.roll(w, shift, axis)
            if field == 0:
                out = out - forcing_ref[c]
            out_ref[6 * field + c] = out


VMEM = 16 * 1024 * 1024


def call(kernel, outs, *args, smem=(0,), away=(), scratch=(), kept=(), limit=VMEM):
    spaces = [pltpu.SMEM if k in smem else pl.ANY if k in away else pltpu.VMEM for k in range(len(args))]
    specs = [pl.BlockSpec(memory_space=space) for space in spaces]
    return pl.pallas_call(
        kernel,
        out_shape=[jax.ShapeDtypeStruct(s, d) for s, d in outs],
        in_specs=specs,
        out_specs=[pl.BlockSpec(memory_space=pltpu.HBM if k in kept else pltpu.VMEM) for k in range(len(outs))],
        scratch_shapes=list(scratch),
        compiler_params=pltpu.CompilerParams(vmem_limit_bytes=limit),
    )(*args)


def shift(x, by):
    return lax.ppermute(x, "mesh", [(i, (i + by) % SLABS) for i in range(SLABS)])


def exchange(chunk, up, down):
    up, down = shift(up, 1), shift(down, -1)
    return lax.all_to_all(chunk, "mesh", split_axis=0, concat_axis=0, tiled=True), up, down


def swap(x, bit):
    return lax.ppermute(x, "inst", [(i, i ^ bit) for i in range(PARTS)])


def inst_split(x):
    return lax.all_to_all(x, "inst", split_axis=0, concat_axis=0, tiled=True)


def on_device(displacement, direction, forcing, material_ids, materials, joint_owner, joint_local, joint_remote, joint_kind):
    shape = displacement.shape
    fields = (6, 4, 32, 128)
    whole = (12, 4, 32, 128)
    disp = displacement.reshape(fields)
    dire = direction.reshape(fields)
    count = joint_local.shape[0]
    p = lax.axis_index("mesh").astype(i32).reshape(1)
    me = lax.axis_index("inst").astype(i32).reshape(1)
    parts = (768, 512)
    index = ((24, 128), i32)
    half = ((4, 12, 16, 128), f32)
    near = ((14, 32, 128), f32)

    own_idx, chunk, up, down, own, same, other = call(
        list_kernel,
        [index, ((SLABS, 16, 128), f32), near, near, ((2, 16, 128), f32), half, half],
        p,
        me,
        joint_owner.reshape(1, count),
        joint_local.reshape(1, count),
        joint_remote.reshape(1, count),
        joint_kind.reshape(1, count),
        disp,
        dire,
        material_ids,
        smem=(0, 1),
        away=range(2, 9),
        limit=60 * 1024 * 1024,
        kept=(1, 2, 3, 5, 6),
        scratch=[pltpu.VMEM(parts, bf16), pltpu.VMEM((SIDE, 16, 128), f32)]
        + [pltpu.VMEM((1, count), i32)] * 4
        + [pltpu.VMEM(fields, f32)] * 2
        + [pltpu.VMEM((4, 32, 128), i32), pltpu.VMEM((4, 32, 128), f32)]
        + [pltpu.VMEM((SLABS, 16, 128), f32), pltpu.SemaphoreType.DMA((12,)), pltpu.SemaphoreType.DMA((20,))],
    )
    chunk, up, down = exchange(chunk, up, down)

    pair = ((2, 12, 16, 128), f32)
    other = swap(other, 1)
    joined = call(join_kernel, [pair] * 3, same, other, smem=())
    turned = [swap(x, 2 * k + 2) for k, x in enumerate(joined)]
    blocks = [pltpu.VMEM((PARTS, 12, 16, 128), f32)] * 2
    keep, *cross = call(time_kernel, [half, pair, pair], me, same, other, *turned, scratch=blocks)

    part = ((PARTS, 4, 1152), f32)
    fields_parts = call(split_kernel, [(parts, bf16)], disp, dire, smem=())[0]
    far_idx, kind, gap = call(
        gap_kernel,
        [index, ((24, 128), f32), part],
        p, chunk, up, down, own, fields_parts, joined[0],
        away=(6,),
        scratch=[pltpu.VMEM((SIDE, 12, 128), f32)],
    )
    force = call(
        force_kernel,
        [part],
        me, kind, jnp.asarray(SPREAD), inst_split(gap), keep,
        away=(4,),
        scratch=[pltpu.VMEM((48, 384), f32)] * 4,
    )[0]
    force = inst_split(force)
    cross = [swap(x, 1) for x in cross]
    joined = call(rejoin_kernel, [pair] * 3, keep, *cross, smem=())
    turned = [swap(x, 2 * k + 2) for k, x in enumerate(joined)]
    lin, mass = call(
        lambda *refs: stiff_kernel(*refs, materials=materials.shape[0]),
        [(whole, f32), ((4, 32, 128), f32)],
        p, materials, material_ids, disp, dire, forcing.reshape(fields), up, down, joined[0],
        smem=(0, 1),
        away=(8,),
    )
    two = ((2, 12, 128), f32)
    chunk, up2, down2, own = call(reply_kernel, [((SLABS, 4, 384), f32), two, two, two], p, force, mass, away=(2,))
    chunk, up2, down2 = exchange(chunk, up2, down2)

    adding = [pltpu.VMEM((SIDE, 12, 128), f32), pltpu.VMEM((384, 512), f32)]
    partial = call(partner_kernel, [(whole, f32)], far_idx, force, lin, smem=(), scratch=adding)[0]
    residual, jacobian = call(
        final_kernel,
        [(fields, f32)] * 2,
        p, me, own_idx, chunk, up2, down2, own, partial, mass, keep, cross[0], *turned,
        smem=(0, 1),
        scratch=adding + blocks[:1],
    )
    return residual.reshape(shape), jacobian.reshape(shape)


def solution(mesh):
    field = P("inst", None, "mesh", None, None)
    placed = (field, field, field, P("mesh", None, None), P(), P("mesh", None), P("mesh"), P("mesh"), P("mesh"))
    return jax.shard_map(on_device, mesh=mesh, in_specs=placed, out_specs=(field, field), check_vma=False)
```

```python
import jax
import jax.numpy as jnp
import numpy as np
from jax import lax
from jax.experimental import pallas as pl
from jax.experimental.pallas import tpu as pltpu
from jax.sharding import PartitionSpec as P

frequency = 0.6
damping = 0.3
bolt_stiff = 2.0
slip_force = 1.0
slip_speed = 0.5
stop_stiff = 3.0
clearance = 0.3

SLABS = 32
PARTS = 8
SIDE = 18
SEG = 42
f32 = jnp.float32
bf16 = jnp.bfloat16
i32 = jnp.int32


def tables(count):
    offsets = np.arange(count)[:, None] - np.arange(count)[None, :]
    tangent = np.where(offsets == 0, 1.0, np.tan(np.pi * offsets / count))
    first = np.where(offsets == 0, 0.0, 0.5 * np.where(offsets % 2 == 0, 1.0, -1.0) / tangent) * frequency
    return first, first @ first


FIRST, SECOND = tables(2 * PARTS)
MIXED = (SECOND + damping * FIRST).astype(np.float32)
SPREAD = np.kron(FIRST, np.eye(3)).astype(np.float32)


def far_tile(offset):
    return 8 + (offset - 3) // 3


def fold(rows):
    return jnp.concatenate([rows[0:4], rows[4:8], rows[8:12]], axis=1)


def unfold(rows):
    width = rows.shape[1] // 3
    return jnp.concatenate([rows[:, width * k : width * (k + 1)] for k in range(3)], axis=0)


def part_tile(ref, tile):
    at = 128 * (tile % 3)
    return jnp.concatenate([ref[tile // 3, :, 384 * k + at : 384 * k + at + 128] for k in range(3)], axis=0)


def lanes(rows):
    return lax.broadcasted_iota(i32, (rows, 128), 1)


def merge_far(read, rows, fill):
    lane = lanes(rows)
    tiles = []
    for k in range(9):
        parts = [read(3 + 3 * k + s) for s in range(3)]
        tile = jnp.where(lane < SEG, parts[0], jnp.where(lane < 2 * SEG, parts[1], parts[2]))
        tiles.append(jnp.where(lane < 3 * SEG, tile, fill))
    return tiles


def slot_tables(p, owner_ref, local_ref, remote_ref, kind_ref):
    count = owner_ref.shape[1]
    offset = (owner_ref[...] - p) & (SLABS - 1)
    hit = (lax.broadcasted_iota(i32, (SLABS, count), 0) == offset).astype(f32)
    hit16 = hit.astype(bf16)
    before = (lax.broadcasted_iota(i32, (128, 128), 0) < lax.broadcasted_iota(i32, (128, 128), 1)).astype(f32).astype(bf16)
    row = lax.broadcasted_iota(i32, (SLABS, 1), 0)
    far = row - 3
    group = (far * 171) >> 9
    start = 1024 + group * 128 + (far - 3 * group) * SEG
    for value, at in ((0, 0), (1, 256), (SLABS - 1, 512), (2, 768), (SLABS - 2, 896)):
        start = jnp.where(row == value, at, start)
    run = start.astype(f32)
    places = []
    for b in range(count // 128):
        block = hit[:, 128 * b : 128 * (b + 1)]
        earlier = jnp.dot(hit16[:, 128 * b : 128 * (b + 1)], before, preferred_element_type=f32)
        places.append(jnp.sum(block * (earlier + run), axis=0, keepdims=True))
        run = run + jnp.sum(block, axis=1, keepdims=True)
    slot = jnp.concatenate(places, axis=1).astype(i32)
    in_tile = lax.broadcasted_iota(i32, (24, count), 0) == (slot >> 7)
    in_lane = (lax.broadcasted_iota(i32, (128, count), 0) == (slot & 127)).astype(f32).astype(bf16)
    local = local_ref[...]
    remote = remote_ref[...]
    values = (local >> 7, local & 127, remote >> 7, remote & 127, kind_ref[...], jnp.ones_like(local))
    spread = jnp.concatenate([jnp.where(in_tile, v.astype(f32), 0.0) for v in values], axis=0).astype(bf16)
    got = lax.dot_general(spread, in_lane, (((1,), (1,)), ((), ())), preferred_element_type=f32)
    got = [got[24 * k : 24 * (k + 1)] for k in range(6)]
    empty = got[5] - 1.0
    return got[0] * 128.0 + got[1] + empty, got[2] * 128.0 + got[3] + empty, got[4]


def picks(idx_ref, k):
    idx = jnp.concatenate([idx_ref[pl.ds(2 * k, 1), :], idx_ref[pl.ds(2 * k + 1, 1), :]], axis=1)
    code = ((idx >> 12) << 7) | (idx & 127)
    pick = (lax.broadcasted_iota(i32, (512, 256), 0) == code).astype(f32).astype(bf16)
    return pick, lax.broadcasted_iota(i32, (32, 256), 0) == ((idx >> 7) & 31)


def split_fields(disp_ref, dir_ref, parts_ref):
    for field, ref in enumerate((disp_ref, dir_ref)):
        for x in range(4):
            value = ref[:, x].reshape(6 * 32, 128)
            hi = value.astype(bf16)
            cols = slice(128 * x, 128 * (x + 1))
            parts_ref[192 * field : 192 * (field + 1), cols] = hi
            parts_ref[384 + 192 * field : 384 + 192 * (field + 1), cols] = (value - hi.astype(f32)).astype(bf16)


def split_kernel(disp_ref, dir_ref, parts_ref):
    split_fields(disp_ref, dir_ref, parts_ref)


def gather_rows(parts_ref, idx_ref, here_ref, first, last):
    def step(k, carry):
        pick, in_y = picks(idx_ref, k)
        rows = jnp.dot(parts_ref[...], pick, preferred_element_type=f32)
        rows = (rows[:384] + rows[384:]).reshape(12, 32, 256)
        got = jnp.sum(jnp.where(in_y[None], rows, 0.0), axis=1)
        here_ref[2 * k, 0:12, :] = got[:, :128]
        here_ref[2 * k + 1, 0:12, :] = got[:, 128:]
        return carry

    lax.fori_loop(first, last, step, 0, unroll=3)


def scatter_rows(val_ref, idx_ref, sum_ref):
    dims = (((1,), (1,)), ((), ()))
    total = None
    for group in range(3):
        held, high, low = [], [], []
        for k in range(group * SIDE // 2 // 3, (group + 1) * SIDE // 2 // 3):
            pick, in_y = picks(idx_ref, k)
            value = jnp.concatenate([val_ref[2 * k], val_ref[2 * k + 1]], axis=1)
            hi = value.astype(bf16).astype(f32)
            held.append(pick)
            for out, part in ((high, hi), (low, value - hi)):
                out.append(jnp.where(in_y[None], part[:, None, :], 0.0).reshape(384, 256).astype(bf16))
        held = jnp.concatenate(held, axis=1)
        got = lax.dot_general(jnp.concatenate(high, axis=1), held, dims, preferred_element_type=f32)
        got = got + lax.dot_general(jnp.concatenate(low, axis=1), held, dims, preferred_element_type=f32)
        total = got if total is None else total + got
    sum_ref[...] = total


def list_kernel(p_ref, me_ref, owner_hbm, local_hbm, remote_hbm, kind_hbm, disp_hbm, dir_hbm, ids_hbm,
                idx_ref, chunk_hbm, up_hbm, down_hbm, self_ref, same_hbm, other_hbm,
                parts_ref, rows_ref, owner_ref, local_ref, remote_ref, kind_ref, disp_ref, dir_ref, ids_ref, near_ref,
                chunk_ref, sems, more_sems):
    p = p_ref[0]
    pairs = ((owner_hbm, owner_ref), (local_hbm, local_ref), (remote_hbm, remote_ref), (kind_hbm, kind_ref),
             (disp_hbm, disp_ref), (dir_hbm, dir_ref), (ids_hbm, ids_ref))
    copies = [pltpu.make_async_copy(a, b, sems.at[k]) for k, (a, b) in enumerate(pairs)]
    for copy in copies:
        copy.start()
    for copy in copies[:4]:
        copy.wait()
    mine, theirs, kind = slot_tables(p, owner_ref, local_ref, remote_ref, kind_ref)
    idx_ref[...] = mine.astype(i32)
    for tile in range(SIDE):
        rows_ref[tile, 12:13, :] = theirs[tile : tile + 1]
        rows_ref[tile, 13:14, :] = kind[tile : tile + 1]
        rows_ref[tile, 14:16, :] = jnp.zeros((2, 128), f32)
    for copy in copies[4:]:
        copy.wait()
    moves = []
    for field, ref in enumerate((disp_ref, dir_ref)):
        part = pl.ds(6 * field, 6)
        for k in range(PARTS):
            block = me_ref[0] ^ k
            rows = pl.ds(pl.multiple_of(16 * (block & 1), 16), 16)
            moves.append((ref.at[:, block >> 1, rows, :], (same_hbm, other_hbm)[k % 2].at[k // 2, part]))
        moves.append((ref.at[:, 3], up_hbm.at[pl.ds(1 + 6 * field, 6)]))
        moves.append((ref.at[:, 0], down_hbm.at[pl.ds(1 + 6 * field, 6)]))
    moves = [pltpu.make_async_copy(a, b, more_sems.at[k]) for k, (a, b) in enumerate(moves)]
    for move in moves:
        move.start()
    split_fields(disp_ref, dir_ref, parts_ref)
    near_ref[2] = (ids_ref[3] + 1).astype(f32)
    near_ref[3] = (ids_ref[0] + 1).astype(f32)
    for d in (0, 1, SLABS - 1):
        chunk_ref[(p + d) & (SLABS - 1)] = jnp.zeros((16, 128), f32)
    gather_rows(parts_ref, idx_ref, rows_ref, 3, SIDE // 2)
    for d, tile in ((2, 6), (SLABS - 2, 7)):
        chunk_ref[(p + d) & (SLABS - 1)] = rows_ref[tile]
    for d in range(3, SLABS - 2):
        tile = far_tile(d)
        chunk_ref[(p + d) & (SLABS - 1)] = rows_ref[tile]
    ends = [pltpu.make_async_copy(chunk_ref, chunk_hbm, sems.at[11])]
    ends[0].start()
    gather_rows(parts_ref, idx_ref, rows_ref, 0, 3)
    for k in range(2):
        near_ref[k] = rows_ref[2 + 2 * k : 4 + 2 * k].reshape(32, 128)
    pairs = ((near_ref.at[0], up_hbm.at[0]), (near_ref.at[1], down_hbm.at[0]),
             (near_ref.at[2], up_hbm.at[13]), (near_ref.at[3], down_hbm.at[13]))
    for k, (a, b) in enumerate(pairs):
        ends.append(pltpu.make_async_copy(a, b, sems.at[7 + k]))
        ends[-1].start()
    self_ref[...] = rows_ref[0:2]
    for move in moves + ends:
        move.wait()


def gap_kernel(p_ref, chunk_ref, up_ref, down_ref, self_ref, parts_ref, after_ref,
               idx_ref, kind_ref, gap_ref, here_ref):
    p = p_ref[0]

    def asked(d):
        return chunk_ref[(p - d) & (SLABS - 1)]

    near = [ref[0, 16 * k : 16 * (k + 1), :] for ref in (up_ref, down_ref) for k in range(2)]
    tiles = [self_ref[0], self_ref[1]] + near + [asked(2), asked(SLABS - 2)]
    tiles += merge_far(asked, 16, 0.0)
    beyond = lanes(1) >= 3 * SEG
    rows = [t[12:13] for t in tiles[:8]] + [jnp.where(beyond, -1.0, t[12:13]) for t in tiles[8:]]
    idx_ref[...] = jnp.concatenate(rows + [jnp.full((7, 128), -1.0, f32)], axis=0).astype(i32)
    kind_ref[...] = jnp.concatenate([t[13:14] for t in tiles] + [jnp.zeros((7, 128), f32)], axis=0)
    gather_rows(parts_ref, idx_ref, here_ref, 0, SIDE // 2)
    for tile in range(24):
        gap = tiles[tile][0:12] - here_ref[tile] if tile < 17 else jnp.zeros((12, 128), f32)
        at = 128 * (tile % 3)
        for k in range(3):
            gap_ref[tile // 3, :, 384 * k + at : 384 * k + at + 128] = gap[4 * k : 4 * k + 4]


def force_kernel(me_ref, kind_ref, spread_ref, gap_ref, after_ref, out_ref, r_ref, d_ref, f_ref, t_ref):
    me = me_ref[0]
    for k in range(PARTS):
        gap = unfold(gap_ref[k])
        r_ref[6 * k : 6 * k + 6] = gap[0:6]
        d_ref[6 * k : 6 * k + 6] = gap[6:12]
    r = r_ref[...]
    dr = d_ref[...]
    w = jnp.dot(spread_ref[...], r, precision=lax.Precision.HIGHEST, preferred_element_type=f32)
    dw = jnp.dot(spread_ref[...], dr, precision=lax.Precision.HIGHEST, preferred_element_type=f32)
    bolted = jnp.concatenate([kind_ref[pl.ds(3 * me + k, 1), :] for k in range(3)], axis=1)
    slide = jnp.tanh(w / slip_speed)
    opened = jnp.tanh(r / clearance)
    friction = bolt_stiff * r + slip_force * slide
    contact = stop_stiff * (r - clearance * opened)
    f_ref[...] = bolted * friction + (1.0 - bolted) * contact
    tangent_friction = bolt_stiff * dr + slip_force * (1.0 - slide * slide) / slip_speed * dw
    tangent_contact = stop_stiff * opened * opened * dr
    t_ref[...] = bolted * tangent_friction + (1.0 - bolted) * tangent_contact
    for k in range(PARTS):
        out_ref[k] = fold(jnp.concatenate([f_ref[6 * k : 6 * k + 6], t_ref[6 * k : 6 * k + 6]], axis=0))


def reply_kernel(p_ref, force_ref, after_ref, chunk_ref, up_ref, down_ref, self_ref):
    p = p_ref[0]
    for d in (0, 1, SLABS - 1):
        chunk_ref[(p - d) & (SLABS - 1)] = jnp.zeros((4, 384), f32)
    for d, tile in ((2, 6), (SLABS - 2, 7)):
        chunk_ref[(p - d) & (SLABS - 1)] = fold(part_tile(force_ref, tile))
    for d in range(3, SLABS - 2):
        tile = far_tile(d)
        chunk_ref[(p - d) & (SLABS - 1)] = fold(part_tile(force_ref, tile))
    for k in range(2):
        self_ref[k] = part_tile(force_ref, k)
        down_ref[k] = part_tile(force_ref, 2 + k)
        up_ref[k] = part_tile(force_ref, 4 + k)


def partner_kernel(idx_ref, force_ref, lin_ref, out_ref, val_ref, sum_ref):
    for tile in range(17):
        val_ref[tile] = -part_tile(force_ref, tile)
    val_ref[17] = jnp.zeros((12, 128), f32)
    scatter_rows(val_ref, idx_ref, sum_ref)
    for x in range(4):
        out_ref[:, x] = lin_ref[:, x] + sum_ref[:, 128 * x : 128 * (x + 1)].reshape(12, 32, 128)


def final_kernel(p_ref, me_ref, idx_ref, chunk_ref, up_ref, down_ref, self_ref, part_ref, mass_ref,
                 keep_ref, cross_ref, early_ref, y1_ref, y2_ref, y3_ref, res_ref, jac_ref, val_ref, sum_ref, acc_ref):
    p = p_ref[0]
    for k in range(PARTS):
        acc = ((keep_ref, 0), (cross_ref, 0), (y1_ref, 0), (y1_ref, 1), (early_ref, ...), (y2_ref, ...), (y3_ref, 0), (y3_ref, 1))[k]
        acc_ref[me_ref[0] ^ k] = acc[0][acc[1]]

    def listed(d):
        return unfold(chunk_ref[(p + d) & (SLABS - 1)])

    tiles = [self_ref[0], self_ref[1], down_ref[0], down_ref[1], up_ref[0], up_ref[1], listed(2), listed(SLABS - 2)]
    tiles += merge_far(listed, 12, 0.0) + [jnp.zeros((12, 128), f32)]
    for k, tile in enumerate(tiles):
        val_ref[k] = tile
    scatter_rows(val_ref, idx_ref, sum_ref)
    for x in range(4):
        acc = jnp.concatenate([acc_ref[2 * x], acc_ref[2 * x + 1]], axis=1)
        added = sum_ref[:, 128 * x : 128 * (x + 1)].reshape(12, 32, 128)
        out = part_ref[:, x] + mass_ref[x][None] * acc + added
        res_ref[:, x] = out[0:6]
        jac_ref[:, x] = out[6:12]


def join_kernel(same_ref, other_ref, *out_refs):
    for k, out in enumerate(out_refs):
        out[0] = same_ref[k + 1]
        out[1] = other_ref[k + 1]


def rejoin_kernel(keep_ref, cross1_ref, cross2_ref, out1_ref, out2_ref, out3_ref):
    out1_ref[0] = keep_ref[1]
    out1_ref[1] = cross1_ref[1]
    out2_ref[...] = cross2_ref[0]
    out3_ref[0] = keep_ref[3]
    out3_ref[1] = cross2_ref[1]


def time_kernel(me_ref, same_ref, other_ref, y1_ref, y2_ref, y3_ref, *refs):
    keep_ref, cross1_ref, cross2_ref, early_ref, in_ref, out_ref = refs
    me = me_ref[0]
    in_ref[0] = same_ref[0]
    in_ref[1] = other_ref[0]
    for k, ref in enumerate((y1_ref, y2_ref, y3_ref)):
        in_ref[2 * k + 2 : 2 * k + 4] = ref[...]
    at = [me ^ ((me + k) & (PARTS - 1)) for k in range(PARTS)]
    count = 2 * PARTS

    def step(g, carry):
        field = g // 3
        row = 6 * field + (g - 3 * field)
        x = [in_ref[at[t // 2], row + 3 * (t % 2)] for t in range(count)]
        for t in range(count):
            acc = x[0] * float(MIXED[t, 0])
            for s in range(1, count):
                acc = acc + x[s] * float(MIXED[(t - s) % count, 0])
            out_ref[at[t // 2], row + 3 * (t % 2)] = acc
        return carry

    lax.fori_loop(0, 6, step, 0)
    for k in range(PARTS):
        ref, at = (keep_ref, k // 2) if k % 2 == 0 else ((cross1_ref, cross2_ref)[k // 4], k // 2 % 2)
        ref[at] = out_ref[k]
    early_ref[...] = out_ref[4]


def lookup(ids, mat_ref, column, count):
    out = jnp.zeros(ids.shape, f32)
    for m in range(count):
        out = jnp.where(ids == m, mat_ref[m, column], out)
    return out


def stiff_kernel(p_ref, mat_ref, ids_ref, disp_ref, dir_ref, forcing_ref, up_ref, down_ref, after1, after2, out_ref, mass_ref, *, materials):
    p = p_ref[0]
    low = jnp.where(p > 0, up_ref[1:14], 0.0)
    high = jnp.where(p < SLABS - 1, down_ref[1:14], 0.0)
    ids = ids_ref[...]
    kx, ky, kz, mass = [lookup(ids, mat_ref, col, materials) for col in range(4)]
    mass_ref[...] = mass
    kx_low = lookup(low[12].astype(i32) - 1, mat_ref, 0, materials)
    kx_high = lookup(high[12].astype(i32) - 1, mat_ref, 0, materials)
    shape = ids.shape
    y = lax.broadcasted_iota(i32, shape, 1)
    z = lax.broadcasted_iota(i32, shape, 2)
    xm = 0.5 * (kx + jnp.concatenate([kx_low[None], kx[:-1]], axis=0))
    xp = 0.5 * (kx + jnp.concatenate([kx[1:], kx_high[None]], axis=0))
    total = xm + xp
    sides = []
    for k, pos, axis in ((ky, y, 1), (kz, z, 2)):
        size = shape[axis]
        for shift, edge in ((1, 0), (size - 1, size - 1)):
            inside = pos != edge
            near = jnp.where(inside, pltpu.roll(k, shift, axis), 0.0)
            side = 0.5 * (k + near)
            total = total + side
            sides.append((jnp.where(inside, side, 0.0), shift, axis))
    for field, ref in enumerate((disp_ref, dir_ref)):
        for c in range(6):
            w = ref[c]
            down = jnp.concatenate([low[6 * field + c][None], w[:-1]], axis=0)
            up = jnp.concatenate([w[1:], high[6 * field + c][None]], axis=0)
            out = total * w - xm * down - xp * up
            for side, shift, axis in sides:
                out = out - side * pltpu.roll(w, shift, axis)
            if field == 0:
                out = out - forcing_ref[c]
            out_ref[6 * field + c] = out


VMEM = 16 * 1024 * 1024


def call(kernel, outs, *args, smem=(0,), away=(), scratch=(), kept=(), limit=VMEM):
    spaces = [pltpu.SMEM if k in smem else pl.ANY if k in away else pltpu.VMEM for k in range(len(args))]
    specs = [pl.BlockSpec(memory_space=space) for space in spaces]
    return pl.pallas_call(
        kernel,
        out_shape=[jax.ShapeDtypeStruct(s, d) for s, d in outs],
        in_specs=specs,
        out_specs=[pl.BlockSpec(memory_space=pltpu.HBM if k in kept else pltpu.VMEM) for k in range(len(outs))],
        scratch_shapes=list(scratch),
        compiler_params=pltpu.CompilerParams(vmem_limit_bytes=limit),
    )(*args)


def shift(x, by):
    return lax.ppermute(x, "mesh", [(i, (i + by) % SLABS) for i in range(SLABS)])


def exchange(chunk, up, down):
    up, down = shift(up, 1), shift(down, -1)
    return lax.all_to_all(chunk, "mesh", split_axis=0, concat_axis=0, tiled=True), up, down


def swap(x, bit):
    return lax.ppermute(x, "inst", [(i, i ^ bit) for i in range(PARTS)])


def inst_split(x):
    return lax.all_to_all(x, "inst", split_axis=0, concat_axis=0, tiled=True)


def on_device(displacement, direction, forcing, material_ids, materials, joint_owner, joint_local, joint_remote, joint_kind):
    shape = displacement.shape
    fields = (6, 4, 32, 128)
    whole = (12, 4, 32, 128)
    disp = displacement.reshape(fields)
    dire = direction.reshape(fields)
    count = joint_local.shape[0]
    p = lax.axis_index("mesh").astype(i32).reshape(1)
    me = lax.axis_index("inst").astype(i32).reshape(1)
    parts = (768, 512)
    index = ((24, 128), i32)
    half = ((4, 12, 16, 128), f32)
    near = ((14, 32, 128), f32)

    own_idx, chunk, up, down, own, same, other = call(
        list_kernel,
        [index, ((SLABS, 16, 128), f32), near, near, ((2, 16, 128), f32), half, half],
        p,
        me,
        joint_owner.reshape(1, count),
        joint_local.reshape(1, count),
        joint_remote.reshape(1, count),
        joint_kind.reshape(1, count),
        disp,
        dire,
        material_ids,
        smem=(0, 1),
        away=range(2, 9),
        limit=60 * 1024 * 1024,
        kept=(1, 2, 3, 5, 6),
        scratch=[pltpu.VMEM(parts, bf16), pltpu.VMEM((SIDE, 16, 128), f32)]
        + [pltpu.VMEM((1, count), i32)] * 4
        + [pltpu.VMEM(fields, f32)] * 2
        + [pltpu.VMEM((4, 32, 128), i32), pltpu.VMEM((4, 32, 128), f32)]
        + [pltpu.VMEM((SLABS, 16, 128), f32), pltpu.SemaphoreType.DMA((12,)), pltpu.SemaphoreType.DMA((20,))],
    )
    chunk, up, down = exchange(chunk, up, down)

    pair = ((2, 12, 16, 128), f32)
    block = ((12, 16, 128), f32)
    other = swap(other, 1)
    joined = call(join_kernel, [pair] * 3, same, other, smem=())
    turned = [swap(x, 2 * k + 2) for k, x in enumerate(joined)]
    blocks = [pltpu.VMEM((PARTS, 12, 16, 128), f32)] * 2
    keep, *cross, early = call(time_kernel, [half, pair, pair, block], me, same, other, *turned, scratch=blocks)

    part = ((PARTS, 4, 1152), f32)
    fields_parts = call(split_kernel, [(parts, bf16)], disp, dire, smem=())[0]
    far_idx, kind, gap = call(
        gap_kernel,
        [index, ((24, 128), f32), part],
        p, chunk, up, down, own, fields_parts, joined[0],
        away=(6,),
        scratch=[pltpu.VMEM((SIDE, 12, 128), f32)],
    )
    force = call(
        force_kernel,
        [part],
        me, kind, jnp.asarray(SPREAD), inst_split(gap), keep,
        away=(4,),
        scratch=[pltpu.VMEM((48, 384), f32)] * 4,
    )[0]
    force = inst_split(force)
    cross = [swap(x, 1) for x in cross]
    early = swap(early, 4)
    joined = call(rejoin_kernel, [pair, block, pair], keep, *cross, smem=())
    turned = [swap(x, 2 * k + 2) for k, x in enumerate(joined)]
    lin, mass = call(
        lambda *refs: stiff_kernel(*refs, materials=materials.shape[0]),
        [(whole, f32), ((4, 32, 128), f32)],
        p, materials, material_ids, disp, dire, forcing.reshape(fields), up, down, joined[0], early,
        smem=(0, 1),
        away=(8, 9),
    )
    two = ((2, 12, 128), f32)
    chunk, up2, down2, own = call(reply_kernel, [((SLABS, 4, 384), f32), two, two, two], p, force, mass, away=(2,))
    chunk, up2, down2 = exchange(chunk, up2, down2)

    adding = [pltpu.VMEM((SIDE, 12, 128), f32), pltpu.VMEM((384, 512), f32)]
    partial = call(partner_kernel, [(whole, f32)], far_idx, force, lin, smem=(), scratch=adding)[0]
    residual, jacobian = call(
        final_kernel,
        [(fields, f32)] * 2,
        p, me, own_idx, chunk, up2, down2, own, partial, mass, keep, cross[0], early, *turned,
        smem=(0, 1),
        scratch=adding + blocks[:1],
    )
    return residual.reshape(shape), jacobian.reshape(shape)


def solution(mesh):
    field = P("inst", None, "mesh", None, None)
    placed = (field, field, field, P("mesh", None, None), P(), P("mesh", None), P("mesh"), P("mesh"), P("mesh"))
    return jax.shard_map(on_device, mesh=mesh, in_specs=placed, out_specs=(field, field), check_vma=False)
```

```python
import jax
import jax.numpy as jnp
import numpy as np
from jax import lax
from jax.experimental import pallas as pl
from jax.experimental.pallas import tpu as pltpu
from jax.sharding import PartitionSpec as P

frequency = 0.6
damping = 0.3
bolt_stiff = 2.0
slip_force = 1.0
slip_speed = 0.5
stop_stiff = 3.0
clearance = 0.3

SLABS = 32
PARTS = 8
SIDE = 18
SEG = 42
f32 = jnp.float32
bf16 = jnp.bfloat16
i32 = jnp.int32


def tables(count):
    offsets = np.arange(count)[:, None] - np.arange(count)[None, :]
    tangent = np.where(offsets == 0, 1.0, np.tan(np.pi * offsets / count))
    first = np.where(offsets == 0, 0.0, 0.5 * np.where(offsets % 2 == 0, 1.0, -1.0) / tangent) * frequency
    return first, first @ first


FIRST, SECOND = tables(2 * PARTS)
MIXED = (SECOND + damping * FIRST).astype(np.float32)
SPREAD = np.kron(FIRST, np.eye(3)).astype(np.float32)


def far_tile(offset):
    return 8 + (offset - 3) // 3


def fold(rows):
    return jnp.concatenate([rows[0:4], rows[4:8], rows[8:12]], axis=1)


def unfold(rows):
    width = rows.shape[1] // 3
    return jnp.concatenate([rows[:, width * k : width * (k + 1)] for k in range(3)], axis=0)


def part_tile(ref, tile):
    at = 128 * (tile % 3)
    return jnp.concatenate([ref[tile // 3, :, 384 * k + at : 384 * k + at + 128] for k in range(3)], axis=0)


def lanes(rows):
    return lax.broadcasted_iota(i32, (rows, 128), 1)


def merge_far(read, rows, fill):
    lane = lanes(rows)
    tiles = []
    for k in range(9):
        parts = [read(3 + 3 * k + s) for s in range(3)]
        tile = jnp.where(lane < SEG, parts[0], jnp.where(lane < 2 * SEG, parts[1], parts[2]))
        tiles.append(jnp.where(lane < 3 * SEG, tile, fill))
    return tiles


def slot_tables(p, owner_ref, local_ref, remote_ref, kind_ref):
    count = owner_ref.shape[1]
    offset = (owner_ref[...] - p) & (SLABS - 1)
    hit = (lax.broadcasted_iota(i32, (SLABS, count), 0) == offset).astype(f32)
    hit16 = hit.astype(bf16)
    before = (lax.broadcasted_iota(i32, (128, 128), 0) < lax.broadcasted_iota(i32, (128, 128), 1)).astype(f32).astype(bf16)
    row = lax.broadcasted_iota(i32, (SLABS, 1), 0)
    far = row - 3
    group = (far * 171) >> 9
    start = 1024 + group * 128 + (far - 3 * group) * SEG
    for value, at in ((0, 0), (1, 256), (SLABS - 1, 512), (2, 768), (SLABS - 2, 896)):
        start = jnp.where(row == value, at, start)
    run = start.astype(f32)
    places = []
    for b in range(count // 128):
        block = hit[:, 128 * b : 128 * (b + 1)]
        earlier = jnp.dot(hit16[:, 128 * b : 128 * (b + 1)], before, preferred_element_type=f32)
        places.append(jnp.sum(block * (earlier + run), axis=0, keepdims=True))
        run = run + jnp.sum(block, axis=1, keepdims=True)
    slot = jnp.concatenate(places, axis=1).astype(i32)
    in_tile = lax.broadcasted_iota(i32, (24, count), 0) == (slot >> 7)
    in_lane = (lax.broadcasted_iota(i32, (128, count), 0) == (slot & 127)).astype(f32).astype(bf16)
    local = local_ref[...]
    remote = remote_ref[...]
    values = (local >> 7, local & 127, remote >> 7, remote & 127, kind_ref[...], jnp.ones_like(local))
    spread = jnp.concatenate([jnp.where(in_tile, v.astype(f32), 0.0) for v in values], axis=0).astype(bf16)
    got = lax.dot_general(spread, in_lane, (((1,), (1,)), ((), ())), preferred_element_type=f32)
    got = [got[24 * k : 24 * (k + 1)] for k in range(6)]
    empty = got[5] - 1.0
    return got[0] * 128.0 + got[1] + empty, got[2] * 128.0 + got[3] + empty, got[4]


def picks(idx_ref, k):
    idx = jnp.concatenate([idx_ref[pl.ds(2 * k, 1), :], idx_ref[pl.ds(2 * k + 1, 1), :]], axis=1)
    code = ((idx >> 12) << 7) | (idx & 127)
    pick = (lax.broadcasted_iota(i32, (512, 256), 0) == code).astype(f32).astype(bf16)
    return pick, lax.broadcasted_iota(i32, (32, 256), 0) == ((idx >> 7) & 31)


def split_fields(disp_ref, dir_ref, parts_ref):
    for field, ref in enumerate((disp_ref, dir_ref)):
        for x in range(4):
            value = ref[:, x].reshape(6 * 32, 128)
            hi = value.astype(bf16)
            cols = slice(128 * x, 128 * (x + 1))
            parts_ref[192 * field : 192 * (field + 1), cols] = hi
            parts_ref[384 + 192 * field : 384 + 192 * (field + 1), cols] = (value - hi.astype(f32)).astype(bf16)


def split_kernel(disp_ref, dir_ref, parts_ref):
    split_fields(disp_ref, dir_ref, parts_ref)


def gather_rows(parts_ref, idx_ref, here_ref, first, last):
    def step(k, carry):
        pick, in_y = picks(idx_ref, k)
        rows = jnp.dot(parts_ref[...], pick, preferred_element_type=f32)
        rows = (rows[:384] + rows[384:]).reshape(12, 32, 256)
        got = jnp.sum(jnp.where(in_y[None], rows, 0.0), axis=1)
        here_ref[2 * k, 0:12, :] = got[:, :128]
        here_ref[2 * k + 1, 0:12, :] = got[:, 128:]
        return carry

    lax.fori_loop(first, last, step, 0, unroll=3)


def scatter_rows(val_ref, idx_ref, sum_ref):
    dims = (((1,), (1,)), ((), ()))
    total = None
    for group in range(3):
        held, high, low = [], [], []
        for k in range(group * SIDE // 2 // 3, (group + 1) * SIDE // 2 // 3):
            pick, in_y = picks(idx_ref, k)
            value = jnp.concatenate([val_ref[2 * k], val_ref[2 * k + 1]], axis=1)
            hi = value.astype(bf16).astype(f32)
            held.append(pick)
            for out, part in ((high, hi), (low, value - hi)):
                out.append(jnp.where(in_y[None], part[:, None, :], 0.0).reshape(384, 256).astype(bf16))
        held = jnp.concatenate(held, axis=1)
        got = lax.dot_general(jnp.concatenate(high, axis=1), held, dims, preferred_element_type=f32)
        got = got + lax.dot_general(jnp.concatenate(low, axis=1), held, dims, preferred_element_type=f32)
        total = got if total is None else total + got
    sum_ref[...] = total


def list_kernel(p_ref, me_ref, owner_hbm, local_hbm, remote_hbm, kind_hbm, disp_hbm, dir_hbm, ids_hbm,
                idx_ref, chunk_hbm, up_hbm, down_hbm, self_ref, same_hbm, other_hbm,
                parts_ref, rows_ref, owner_ref, local_ref, remote_ref, kind_ref, disp_ref, dir_ref, ids_ref, near_ref,
                chunk_ref, sems, more_sems):
    p = p_ref[0]
    pairs = ((owner_hbm, owner_ref), (local_hbm, local_ref), (remote_hbm, remote_ref), (kind_hbm, kind_ref),
             (disp_hbm, disp_ref), (dir_hbm, dir_ref), (ids_hbm, ids_ref))
    copies = [pltpu.make_async_copy(a, b, sems.at[k]) for k, (a, b) in enumerate(pairs)]
    for copy in copies:
        copy.start()
    for copy in copies[:4]:
        copy.wait()
    mine, theirs, kind = slot_tables(p, owner_ref, local_ref, remote_ref, kind_ref)
    idx_ref[...] = mine.astype(i32)
    for tile in range(SIDE):
        rows_ref[tile, 12:13, :] = theirs[tile : tile + 1]
        rows_ref[tile, 13:14, :] = kind[tile : tile + 1]
        rows_ref[tile, 14:16, :] = jnp.zeros((2, 128), f32)
    for copy in copies[4:]:
        copy.wait()
    moves = []
    for field, ref in enumerate((disp_ref, dir_ref)):
        part = pl.ds(6 * field, 6)
        for k in range(PARTS):
            block = me_ref[0] ^ k
            rows = pl.ds(pl.multiple_of(16 * (block & 1), 16), 16)
            moves.append((ref.at[:, block >> 1, rows, :], (same_hbm, other_hbm)[k % 2].at[k // 2, part]))
        moves.append((ref.at[:, 3], up_hbm.at[pl.ds(1 + 6 * field, 6)]))
        moves.append((ref.at[:, 0], down_hbm.at[pl.ds(1 + 6 * field, 6)]))
    moves = [pltpu.make_async_copy(a, b, more_sems.at[k]) for k, (a, b) in enumerate(moves)]
    for move in moves:
        move.start()
    split_fields(disp_ref, dir_ref, parts_ref)
    near_ref[2] = (ids_ref[3] + 1).astype(f32)
    near_ref[3] = (ids_ref[0] + 1).astype(f32)
    for d in (0, 1, SLABS - 1):
        chunk_ref[(p + d) & (SLABS - 1)] = jnp.zeros((16, 128), f32)
    gather_rows(parts_ref, idx_ref, rows_ref, 3, SIDE // 2)
    for d, tile in ((2, 6), (SLABS - 2, 7)):
        chunk_ref[(p + d) & (SLABS - 1)] = rows_ref[tile]
    for d in range(3, SLABS - 2):
        tile = far_tile(d)
        chunk_ref[(p + d) & (SLABS - 1)] = rows_ref[tile]
    ends = [pltpu.make_async_copy(chunk_ref, chunk_hbm, sems.at[11])]
    ends[0].start()
    gather_rows(parts_ref, idx_ref, rows_ref, 0, 3)
    for k in range(2):
        near_ref[k] = rows_ref[2 + 2 * k : 4 + 2 * k].reshape(32, 128)
    pairs = ((near_ref.at[0], up_hbm.at[0]), (near_ref.at[1], down_hbm.at[0]),
             (near_ref.at[2], up_hbm.at[13]), (near_ref.at[3], down_hbm.at[13]))
    for k, (a, b) in enumerate(pairs):
        ends.append(pltpu.make_async_copy(a, b, sems.at[7 + k]))
        ends[-1].start()
    self_ref[...] = rows_ref[0:2]
    for move in moves + ends:
        move.wait()


def gap_kernel(p_ref, chunk_ref, up_ref, down_ref, self_ref, parts_ref, after_ref,
               idx_ref, kind_ref, gap_ref, here_ref):
    p = p_ref[0]

    def asked(d):
        return chunk_ref[(p - d) & (SLABS - 1)]

    near = [ref[0, 16 * k : 16 * (k + 1), :] for ref in (up_ref, down_ref) for k in range(2)]
    tiles = [self_ref[0], self_ref[1]] + near + [asked(2), asked(SLABS - 2)]
    tiles += merge_far(asked, 16, 0.0)
    beyond = lanes(1) >= 3 * SEG
    rows = [t[12:13] for t in tiles[:8]] + [jnp.where(beyond, -1.0, t[12:13]) for t in tiles[8:]]
    idx_ref[...] = jnp.concatenate(rows + [jnp.full((7, 128), -1.0, f32)], axis=0).astype(i32)
    kind_ref[...] = jnp.concatenate([t[13:14] for t in tiles] + [jnp.zeros((7, 128), f32)], axis=0)
    gather_rows(parts_ref, idx_ref, here_ref, 0, SIDE // 2)
    for tile in range(24):
        gap = tiles[tile][0:12] - here_ref[tile] if tile < 17 else jnp.zeros((12, 128), f32)
        at = 128 * (tile % 3)
        for k in range(3):
            gap_ref[tile // 3, :, 384 * k + at : 384 * k + at + 128] = gap[4 * k : 4 * k + 4]


def force_kernel(me_ref, kind_ref, spread_ref, gap_ref, after_ref, out_ref, r_ref, d_ref, f_ref, t_ref):
    me = me_ref[0]
    for k in range(PARTS):
        gap = unfold(gap_ref[k])
        r_ref[6 * k : 6 * k + 6] = gap[0:6]
        d_ref[6 * k : 6 * k + 6] = gap[6:12]
    r = r_ref[...]
    dr = d_ref[...]
    w = jnp.dot(spread_ref[...], r, precision=lax.Precision.HIGHEST, preferred_element_type=f32)
    dw = jnp.dot(spread_ref[...], dr, precision=lax.Precision.HIGHEST, preferred_element_type=f32)
    bolted = jnp.concatenate([kind_ref[pl.ds(3 * me + k, 1), :] for k in range(3)], axis=1)
    slide = jnp.tanh(w / slip_speed)
    opened = jnp.tanh(r / clearance)
    friction = bolt_stiff * r + slip_force * slide
    contact = stop_stiff * (r - clearance * opened)
    f_ref[...] = bolted * friction + (1.0 - bolted) * contact
    tangent_friction = bolt_stiff * dr + slip_force * (1.0 - slide * slide) / slip_speed * dw
    tangent_contact = stop_stiff * opened * opened * dr
    t_ref[...] = bolted * tangent_friction + (1.0 - bolted) * tangent_contact
    for k in range(PARTS):
        out_ref[k] = fold(jnp.concatenate([f_ref[6 * k : 6 * k + 6], t_ref[6 * k : 6 * k + 6]], axis=0))


def reply_kernel(p_ref, force_ref, after_ref, chunk_ref, up_ref, down_ref, self_ref):
    p = p_ref[0]
    for d in (0, 1, SLABS - 1):
        chunk_ref[(p - d) & (SLABS - 1)] = jnp.zeros((4, 384), f32)
    for d, tile in ((2, 6), (SLABS - 2, 7)):
        chunk_ref[(p - d) & (SLABS - 1)] = fold(part_tile(force_ref, tile))
    for d in range(3, SLABS - 2):
        tile = far_tile(d)
        chunk_ref[(p - d) & (SLABS - 1)] = fold(part_tile(force_ref, tile))
    for k in range(2):
        self_ref[k] = part_tile(force_ref, k)
        down_ref[k] = part_tile(force_ref, 2 + k)
        up_ref[k] = part_tile(force_ref, 4 + k)


def partner_kernel(idx_ref, force_ref, lin_ref, out_ref, val_ref, sum_ref):
    for tile in range(17):
        val_ref[tile] = -part_tile(force_ref, tile)
    val_ref[17] = jnp.zeros((12, 128), f32)
    scatter_rows(val_ref, idx_ref, sum_ref)
    for x in range(4):
        out_ref[:, x] = lin_ref[:, x] + sum_ref[:, 128 * x : 128 * (x + 1)].reshape(12, 32, 128)


def listed_kernel(p_ref, idx_ref, chunk_ref, up_ref, down_ref, self_ref, part_ref, out_ref, val_ref, sum_ref):
    p = p_ref[0]

    def listed(d):
        return unfold(chunk_ref[(p + d) & (SLABS - 1)])

    tiles = [self_ref[0], self_ref[1], down_ref[0], down_ref[1], up_ref[0], up_ref[1], listed(2), listed(SLABS - 2)]
    tiles += merge_far(listed, 12, 0.0) + [jnp.zeros((12, 128), f32)]
    for k, tile in enumerate(tiles):
        val_ref[k] = tile
    scatter_rows(val_ref, idx_ref, sum_ref)
    for x in range(4):
        out_ref[:, x] = part_ref[:, x] + sum_ref[:, 128 * x : 128 * (x + 1)].reshape(12, 32, 128)


def final_kernel(me_ref, part_ref, mass_ref, keep_ref, cross_ref, y1_ref, y2_ref, y3_ref, res_ref, jac_ref):
    for k in range(PARTS):
        acc = (y1_ref, y2_ref, y3_ref)[k // 2 - 1][k % 2] if k > 1 else (keep_ref, cross_ref)[k][0]
        block = me_ref[0] ^ k
        x = block >> 1
        rows = pl.ds(pl.multiple_of(16 * (block & 1), 16), 16)
        out = part_ref[:, x, rows, :] + mass_ref[x, rows, :][None] * acc
        res_ref[:, x, rows, :] = out[0:6]
        jac_ref[:, x, rows, :] = out[6:12]


def join_kernel(same_ref, other_ref, *out_refs):
    for k, out in enumerate(out_refs):
        out[0] = same_ref[k + 1]
        out[1] = other_ref[k + 1]


def rejoin_kernel(keep_ref, cross1_ref, cross2_ref, *out_refs):
    for k, out in enumerate(out_refs):
        out[0] = keep_ref[k + 1]
        out[1] = (cross1_ref, cross2_ref)[(k + 1) // 2][(k + 1) % 2]


def time_kernel(me_ref, same_ref, other_ref, y1_ref, y2_ref, y3_ref, *refs):
    keep_ref, cross1_ref, cross2_ref, in_ref, out_ref = refs
    me = me_ref[0]
    in_ref[0] = same_ref[0]
    in_ref[1] = other_ref[0]
    for k, ref in enumerate((y1_ref, y2_ref, y3_ref)):
        in_ref[2 * k + 2 : 2 * k + 4] = ref[...]
    at = [me ^ ((me + k) & (PARTS - 1)) for k in range(PARTS)]
    count = 2 * PARTS

    def step(g, carry):
        field = g // 3
        row = 6 * field + (g - 3 * field)
        x = [in_ref[at[t // 2], row + 3 * (t % 2)] for t in range(count)]
        for t in range(count):
            acc = x[0] * float(MIXED[t, 0])
            for s in range(1, count):
                acc = acc + x[s] * float(MIXED[(t - s) % count, 0])
            out_ref[at[t // 2], row + 3 * (t % 2)] = acc
        return carry

    lax.fori_loop(0, 6, step, 0)
    for k in range(PARTS):
        ref, at = (keep_ref, k // 2) if k % 2 == 0 else ((cross1_ref, cross2_ref)[k // 4], k // 2 % 2)
        ref[at] = out_ref[k]


def lookup(ids, mat_ref, column, count):
    out = jnp.zeros(ids.shape, f32)
    for m in range(count):
        out = jnp.where(ids == m, mat_ref[m, column], out)
    return out


def stiff_kernel(p_ref, mat_ref, ids_ref, disp_ref, dir_ref, forcing_ref, up_ref, down_ref, after_ref, out_ref, mass_ref, *, materials):
    p = p_ref[0]
    low = jnp.where(p > 0, up_ref[1:14], 0.0)
    high = jnp.where(p < SLABS - 1, down_ref[1:14], 0.0)
    ids = ids_ref[...]
    kx, ky, kz, mass = [lookup(ids, mat_ref, col, materials) for col in range(4)]
    mass_ref[...] = mass
    kx_low = lookup(low[12].astype(i32) - 1, mat_ref, 0, materials)
    kx_high = lookup(high[12].astype(i32) - 1, mat_ref, 0, materials)
    shape = ids.shape
    y = lax.broadcasted_iota(i32, shape, 1)
    z = lax.broadcasted_iota(i32, shape, 2)
    xm = 0.5 * (kx + jnp.concatenate([kx_low[None], kx[:-1]], axis=0))
    xp = 0.5 * (kx + jnp.concatenate([kx[1:], kx_high[None]], axis=0))
    total = xm + xp
    sides = []
    for k, pos, axis in ((ky, y, 1), (kz, z, 2)):
        size = shape[axis]
        for shift, edge in ((1, 0), (size - 1, size - 1)):
            inside = pos != edge
            near = jnp.where(inside, pltpu.roll(k, shift, axis), 0.0)
            side = 0.5 * (k + near)
            total = total + side
            sides.append((jnp.where(inside, side, 0.0), shift, axis))
    for field, ref in enumerate((disp_ref, dir_ref)):
        for c in range(6):
            w = ref[c]
            down = jnp.concatenate([low[6 * field + c][None], w[:-1]], axis=0)
            up = jnp.concatenate([w[1:], high[6 * field + c][None]], axis=0)
            out = total * w - xm * down - xp * up
            for side, shift, axis in sides:
                out = out - side * pltpu.roll(w, shift, axis)
            if field == 0:
                out = out - forcing_ref[c]
            out_ref[6 * field + c] = out


VMEM = 16 * 1024 * 1024


def call(kernel, outs, *args, smem=(0,), away=(), scratch=(), kept=(), limit=VMEM):
    spaces = [pltpu.SMEM if k in smem else pl.ANY if k in away else pltpu.VMEM for k in range(len(args))]
    specs = [pl.BlockSpec(memory_space=space) for space in spaces]
    return pl.pallas_call(
        kernel,
        out_shape=[jax.ShapeDtypeStruct(s, d) for s, d in outs],
        in_specs=specs,
        out_specs=[pl.BlockSpec(memory_space=pltpu.HBM if k in kept else pltpu.VMEM) for k in range(len(outs))],
        scratch_shapes=list(scratch),
        compiler_params=pltpu.CompilerParams(vmem_limit_bytes=limit),
    )(*args)


def shift(x, by):
    return lax.ppermute(x, "mesh", [(i, (i + by) % SLABS) for i in range(SLABS)])


def exchange(chunk, up, down):
    up, down = shift(up, 1), shift(down, -1)
    return lax.all_to_all(chunk, "mesh", split_axis=0, concat_axis=0, tiled=True), up, down


def swap(x, bit):
    return lax.ppermute(x, "inst", [(i, i ^ bit) for i in range(PARTS)])


def inst_split(x):
    return lax.all_to_all(x, "inst", split_axis=0, concat_axis=0, tiled=True)


def on_device(displacement, direction, forcing, material_ids, materials, joint_owner, joint_local, joint_remote, joint_kind):
    shape = displacement.shape
    fields = (6, 4, 32, 128)
    whole = (12, 4, 32, 128)
    disp = displacement.reshape(fields)
    dire = direction.reshape(fields)
    count = joint_local.shape[0]
    p = lax.axis_index("mesh").astype(i32).reshape(1)
    me = lax.axis_index("inst").astype(i32).reshape(1)
    parts = (768, 512)
    index = ((24, 128), i32)
    half = ((4, 12, 16, 128), f32)
    near = ((14, 32, 128), f32)

    own_idx, chunk, up, down, own, same, other = call(
        list_kernel,
        [index, ((SLABS, 16, 128), f32), near, near, ((2, 16, 128), f32), half, half],
        p,
        me,
        joint_owner.reshape(1, count),
        joint_local.reshape(1, count),
        joint_remote.reshape(1, count),
        joint_kind.reshape(1, count),
        disp,
        dire,
        material_ids,
        smem=(0, 1),
        away=range(2, 9),
        limit=60 * 1024 * 1024,
        kept=(1, 2, 3, 5, 6),
        scratch=[pltpu.VMEM(parts, bf16), pltpu.VMEM((SIDE, 16, 128), f32)]
        + [pltpu.VMEM((1, count), i32)] * 4
        + [pltpu.VMEM(fields, f32)] * 2
        + [pltpu.VMEM((4, 32, 128), i32), pltpu.VMEM((4, 32, 128), f32)]
        + [pltpu.VMEM((SLABS, 16, 128), f32), pltpu.SemaphoreType.DMA((12,)), pltpu.SemaphoreType.DMA((20,))],
    )
    chunk, up, down = exchange(chunk, up, down)

    pair = ((2, 12, 16, 128), f32)
    other = swap(other, 1)
    joined = call(join_kernel, [pair] * 3, same, other, smem=())
    turned = [swap(x, 2 * k + 2) for k, x in enumerate(joined)]
    blocks = [pltpu.VMEM((PARTS, 12, 16, 128), f32)] * 2
    keep, *cross = call(time_kernel, [half, pair, pair], me, same, other, *turned, scratch=blocks)

    part = ((PARTS, 4, 1152), f32)
    fields_parts = call(split_kernel, [(parts, bf16)], disp, dire, smem=())[0]
    far_idx, kind, gap = call(
        gap_kernel,
        [index, ((24, 128), f32), part],
        p, chunk, up, down, own, fields_parts, joined[0],
        away=(6,),
        scratch=[pltpu.VMEM((SIDE, 12, 128), f32)],
    )
    force = call(
        force_kernel,
        [part],
        me, kind, jnp.asarray(SPREAD), inst_split(gap), keep,
        away=(4,),
        scratch=[pltpu.VMEM((48, 384), f32)] * 4,
    )[0]
    force = inst_split(force)
    cross = [swap(x, 1) for x in cross]
    joined = call(rejoin_kernel, [pair] * 3, keep, *cross, smem=())
    turned = [swap(x, 2 * k + 2) for k, x in enumerate(joined)]
    lin, mass = call(
        lambda *refs: stiff_kernel(*refs, materials=materials.shape[0]),
        [(whole, f32), ((4, 32, 128), f32)],
        p, materials, material_ids, disp, dire, forcing.reshape(fields), up, down, joined[0],
        smem=(0, 1),
        away=(8,),
    )
    two = ((2, 12, 128), f32)
    chunk, up2, down2, own = call(reply_kernel, [((SLABS, 4, 384), f32), two, two, two], p, force, mass, away=(2,))
    chunk, up2, down2 = exchange(chunk, up2, down2)

    adding = [pltpu.VMEM((SIDE, 12, 128), f32), pltpu.VMEM((384, 512), f32)]
    partial = call(partner_kernel, [(whole, f32)], far_idx, force, lin, smem=(), scratch=adding)[0]
    partial = call(
        listed_kernel, [(whole, f32)], p, own_idx, chunk, up2, down2, own, partial, scratch=adding
    )[0]
    residual, jacobian = call(final_kernel, [(fields, f32)] * 2, me, partial, mass, keep, cross[0], *turned)
    return residual.reshape(shape), jacobian.reshape(shape)


def solution(mesh):
    field = P("inst", None, "mesh", None, None)
    placed = (field, field, field, P("mesh", None, None), P(), P("mesh", None), P("mesh"), P("mesh"), P("mesh"))
    return jax.shard_map(on_device, mesh=mesh, in_specs=placed, out_specs=(field, field), check_vma=False)
```

```python
import jax
import jax.numpy as jnp
import numpy as np
from jax import lax
from jax.experimental import pallas as pl
from jax.experimental.pallas import tpu as pltpu
from jax.sharding import PartitionSpec as P

frequency = 0.6
damping = 0.3
bolt_stiff = 2.0
slip_force = 1.0
slip_speed = 0.5
stop_stiff = 3.0
clearance = 0.3

SLABS = 32
PARTS = 8
SIDE = 18
SEG = 42
f32 = jnp.float32
bf16 = jnp.bfloat16
i32 = jnp.int32


def tables(count):
    offsets = np.arange(count)[:, None] - np.arange(count)[None, :]
    tangent = np.where(offsets == 0, 1.0, np.tan(np.pi * offsets / count))
    first = np.where(offsets == 0, 0.0, 0.5 * np.where(offsets % 2 == 0, 1.0, -1.0) / tangent) * frequency
    return first, first @ first


FIRST, SECOND = tables(2 * PARTS)
MIXED = (SECOND + damping * FIRST).astype(np.float32)
SPREAD = np.kron(FIRST, np.eye(3)).astype(np.float32)


def far_tile(offset):
    return 8 + (offset - 3) // 3


def fold(rows):
    return jnp.concatenate([rows[0:4], rows[4:8], rows[8:12]], axis=1)


def unfold(rows):
    width = rows.shape[1] // 3
    return jnp.concatenate([rows[:, width * k : width * (k + 1)] for k in range(3)], axis=0)


def part_tile(ref, tile):
    at = 128 * (tile % 3)
    return jnp.concatenate([ref[tile // 3, :, 384 * k + at : 384 * k + at + 128] for k in range(3)], axis=0)


def lanes(rows):
    return lax.broadcasted_iota(i32, (rows, 128), 1)


def merge_far(read, rows, fill):
    lane = lanes(rows)
    tiles = []
    for k in range(9):
        parts = [read(3 + 3 * k + s) for s in range(3)]
        tile = jnp.where(lane < SEG, parts[0], jnp.where(lane < 2 * SEG, parts[1], parts[2]))
        tiles.append(jnp.where(lane < 3 * SEG, tile, fill))
    return tiles


def slot_tables(p, owner_ref, local_ref, remote_ref, kind_ref):
    count = owner_ref.shape[1]
    offset = (owner_ref[...] - p) & (SLABS - 1)
    hit = (lax.broadcasted_iota(i32, (SLABS, count), 0) == offset).astype(f32)
    hit16 = hit.astype(bf16)
    before = (lax.broadcasted_iota(i32, (128, 128), 0) < lax.broadcasted_iota(i32, (128, 128), 1)).astype(f32).astype(bf16)
    row = lax.broadcasted_iota(i32, (SLABS, 1), 0)
    far = row - 3
    group = (far * 171) >> 9
    start = 1024 + group * 128 + (far - 3 * group) * SEG
    for value, at in ((0, 0), (1, 256), (SLABS - 1, 512), (2, 768), (SLABS - 2, 896)):
        start = jnp.where(row == value, at, start)
    run = start.astype(f32)
    places = []
    for b in range(count // 128):
        block = hit[:, 128 * b : 128 * (b + 1)]
        earlier = jnp.dot(hit16[:, 128 * b : 128 * (b + 1)], before, preferred_element_type=f32)
        places.append(jnp.sum(block * (earlier + run), axis=0, keepdims=True))
        run = run + jnp.sum(block, axis=1, keepdims=True)
    slot = jnp.concatenate(places, axis=1).astype(i32)
    in_tile = lax.broadcasted_iota(i32, (24, count), 0) == (slot >> 7)
    in_lane = (lax.broadcasted_iota(i32, (128, count), 0) == (slot & 127)).astype(f32).astype(bf16)
    local = local_ref[...]
    remote = remote_ref[...]
    values = (local >> 7, local & 127, remote >> 7, remote & 127, kind_ref[...], jnp.ones_like(local))
    spread = jnp.concatenate([jnp.where(in_tile, v.astype(f32), 0.0) for v in values], axis=0).astype(bf16)
    got = lax.dot_general(spread, in_lane, (((1,), (1,)), ((), ())), preferred_element_type=f32)
    got = [got[24 * k : 24 * (k + 1)] for k in range(6)]
    empty = got[5] - 1.0
    return got[0] * 128.0 + got[1] + empty, got[2] * 128.0 + got[3] + empty, got[4]


def picks(idx_ref, k):
    idx = jnp.concatenate([idx_ref[pl.ds(2 * k, 1), :], idx_ref[pl.ds(2 * k + 1, 1), :]], axis=1)
    code = ((idx >> 12) << 7) | (idx & 127)
    pick = (lax.broadcasted_iota(i32, (512, 256), 0) == code).astype(f32).astype(bf16)
    return pick, lax.broadcasted_iota(i32, (32, 256), 0) == ((idx >> 7) & 31)


def split_fields(disp_ref, dir_ref, parts_ref):
    for field, ref in enumerate((disp_ref, dir_ref)):
        for x in range(4):
            value = ref[:, x].reshape(6 * 32, 128)
            hi = value.astype(bf16)
            cols = slice(128 * x, 128 * (x + 1))
            parts_ref[192 * field : 192 * (field + 1), cols] = hi
            parts_ref[384 + 192 * field : 384 + 192 * (field + 1), cols] = (value - hi.astype(f32)).astype(bf16)


def split_kernel(disp_ref, dir_ref, parts_ref):
    split_fields(disp_ref, dir_ref, parts_ref)


def gather_rows(parts_ref, idx_ref, here_ref, first, last):
    def step(k, carry):
        pick, in_y = picks(idx_ref, k)
        rows = jnp.dot(parts_ref[...], pick, preferred_element_type=f32)
        rows = (rows[:384] + rows[384:]).reshape(12, 32, 256)
        got = jnp.sum(jnp.where(in_y[None], rows, 0.0), axis=1)
        here_ref[2 * k, 0:12, :] = got[:, :128]
        here_ref[2 * k + 1, 0:12, :] = got[:, 128:]
        return carry

    lax.fori_loop(first, last, step, 0, unroll=True)


def scatter_rows(val_ref, idx_ref, sum_ref):
    dims = (((1,), (1,)), ((), ()))
    total = None
    for group in range(3):
        held, high, low = [], [], []
        for k in range(group * SIDE // 2 // 3, (group + 1) * SIDE // 2 // 3):
            pick, in_y = picks(idx_ref, k)
            value = jnp.concatenate([val_ref[2 * k], val_ref[2 * k + 1]], axis=1)
            hi = value.astype(bf16).astype(f32)
            held.append(pick)
            for out, part in ((high, hi), (low, value - hi)):
                out.append(jnp.where(in_y[None], part[:, None, :], 0.0).reshape(384, 256).astype(bf16))
        held = jnp.concatenate(held, axis=1)
        got = lax.dot_general(jnp.concatenate(high, axis=1), held, dims, preferred_element_type=f32)
        got = got + lax.dot_general(jnp.concatenate(low, axis=1), held, dims, preferred_element_type=f32)
        total = got if total is None else total + got
    sum_ref[...] = total


def list_kernel(p_ref, me_ref, owner_hbm, local_hbm, remote_hbm, kind_hbm, disp_hbm, dir_hbm, ids_hbm,
                idx_ref, chunk_hbm, up_hbm, down_hbm, self_ref, same_hbm, other_hbm,
                parts_ref, rows_ref, owner_ref, local_ref, remote_ref, kind_ref, disp_ref, dir_ref, ids_ref, near_ref,
                chunk_ref, sems, more_sems):
    p = p_ref[0]
    pairs = ((owner_hbm, owner_ref), (local_hbm, local_ref), (remote_hbm, remote_ref), (kind_hbm, kind_ref),
             (disp_hbm, disp_ref), (dir_hbm, dir_ref), (ids_hbm, ids_ref))
    copies = [pltpu.make_async_copy(a, b, sems.at[k]) for k, (a, b) in enumerate(pairs)]
    for copy in copies:
        copy.start()
    for copy in copies[:4]:
        copy.wait()
    mine, theirs, kind = slot_tables(p, owner_ref, local_ref, remote_ref, kind_ref)
    idx_ref[...] = mine.astype(i32)
    for tile in range(SIDE):
        rows_ref[tile, 12:13, :] = theirs[tile : tile + 1]
        rows_ref[tile, 13:14, :] = kind[tile : tile + 1]
        rows_ref[tile, 14:16, :] = jnp.zeros((2, 128), f32)
    for copy in copies[4:]:
        copy.wait()
    moves = []
    for field, ref in enumerate((disp_ref, dir_ref)):
        part = pl.ds(6 * field, 6)
        for k in range(PARTS):
            block = me_ref[0] ^ k
            rows = pl.ds(pl.multiple_of(16 * (block & 1), 16), 16)
            moves.append((ref.at[:, block >> 1, rows, :], (same_hbm, other_hbm)[k % 2].at[k // 2, part]))
        moves.append((ref.at[:, 3], up_hbm.at[pl.ds(1 + 6 * field, 6)]))
        moves.append((ref.at[:, 0], down_hbm.at[pl.ds(1 + 6 * field, 6)]))
    moves = [pltpu.make_async_copy(a, b, more_sems.at[k]) for k, (a, b) in enumerate(moves)]
    for move in moves:
        move.start()
    split_fields(disp_ref, dir_ref, parts_ref)
    near_ref[2] = (ids_ref[3] + 1).astype(f32)
    near_ref[3] = (ids_ref[0] + 1).astype(f32)
    for d in (0, 1, SLABS - 1):
        chunk_ref[(p + d) & (SLABS - 1)] = jnp.zeros((16, 128), f32)
    gather_rows(parts_ref, idx_ref, rows_ref, 3, SIDE // 2)
    for d, tile in ((2, 6), (SLABS - 2, 7)):
        chunk_ref[(p + d) & (SLABS - 1)] = rows_ref[tile]
    for d in range(3, SLABS - 2):
        tile = far_tile(d)
        chunk_ref[(p + d) & (SLABS - 1)] = rows_ref[tile]
    ends = [pltpu.make_async_copy(chunk_ref, chunk_hbm, sems.at[11])]
    ends[0].start()
    gather_rows(parts_ref, idx_ref, rows_ref, 0, 3)
    for k in range(2):
        near_ref[k] = rows_ref[2 + 2 * k : 4 + 2 * k].reshape(32, 128)
    pairs = ((near_ref.at[0], up_hbm.at[0]), (near_ref.at[1], down_hbm.at[0]),
             (near_ref.at[2], up_hbm.at[13]), (near_ref.at[3], down_hbm.at[13]))
    for k, (a, b) in enumerate(pairs):
        ends.append(pltpu.make_async_copy(a, b, sems.at[7 + k]))
        ends[-1].start()
    self_ref[...] = rows_ref[0:2]
    for move in moves + ends:
        move.wait()


def gap_kernel(p_ref, chunk_ref, up_ref, down_ref, self_ref, parts_ref, after_ref,
               idx_ref, kind_ref, gap_ref, here_ref):
    p = p_ref[0]

    def asked(d):
        return chunk_ref[(p - d) & (SLABS - 1)]

    near = [ref[0, 16 * k : 16 * (k + 1), :] for ref in (up_ref, down_ref) for k in range(2)]
    tiles = [self_ref[0], self_ref[1]] + near + [asked(2), asked(SLABS - 2)]
    tiles += merge_far(asked, 16, 0.0)
    beyond = lanes(1) >= 3 * SEG
    rows = [t[12:13] for t in tiles[:8]] + [jnp.where(beyond, -1.0, t[12:13]) for t in tiles[8:]]
    idx_ref[...] = jnp.concatenate(rows + [jnp.full((7, 128), -1.0, f32)], axis=0).astype(i32)
    kind_ref[...] = jnp.concatenate([t[13:14] for t in tiles] + [jnp.zeros((7, 128), f32)], axis=0)
    gather_rows(parts_ref, idx_ref, here_ref, 0, SIDE // 2)
    for tile in range(24):
        gap = tiles[tile][0:12] - here_ref[tile] if tile < 17 else jnp.zeros((12, 128), f32)
        at = 128 * (tile % 3)
        for k in range(3):
            gap_ref[tile // 3, :, 384 * k + at : 384 * k + at + 128] = gap[4 * k : 4 * k + 4]


def force_kernel(me_ref, kind_ref, spread_ref, gap_ref, after_ref, out_ref, r_ref, d_ref, f_ref, t_ref):
    me = me_ref[0]
    for k in range(PARTS):
        gap = unfold(gap_ref[k])
        r_ref[6 * k : 6 * k + 6] = gap[0:6]
        d_ref[6 * k : 6 * k + 6] = gap[6:12]
    r = r_ref[...]
    dr = d_ref[...]
    w = jnp.dot(spread_ref[...], r, precision=lax.Precision.HIGHEST, preferred_element_type=f32)
    dw = jnp.dot(spread_ref[...], dr, precision=lax.Precision.HIGHEST, preferred_element_type=f32)
    bolted = jnp.concatenate([kind_ref[pl.ds(3 * me + k, 1), :] for k in range(3)], axis=1)
    slide = jnp.tanh(w / slip_speed)
    opened = jnp.tanh(r / clearance)
    friction = bolt_stiff * r + slip_force * slide
    contact = stop_stiff * (r - clearance * opened)
    f_ref[...] = bolted * friction + (1.0 - bolted) * contact
    tangent_friction = bolt_stiff * dr + slip_force * (1.0 - slide * slide) / slip_speed * dw
    tangent_contact = stop_stiff * opened * opened * dr
    t_ref[...] = bolted * tangent_friction + (1.0 - bolted) * tangent_contact
    for k in range(PARTS):
        out_ref[k] = fold(jnp.concatenate([f_ref[6 * k : 6 * k + 6], t_ref[6 * k : 6 * k + 6]], axis=0))


def reply_kernel(p_ref, force_ref, after_ref, chunk_ref, up_ref, down_ref, self_ref):
    p = p_ref[0]
    for d in (0, 1, SLABS - 1):
        chunk_ref[(p - d) & (SLABS - 1)] = jnp.zeros((4, 384), f32)
    for d, tile in ((2, 6), (SLABS - 2, 7)):
        chunk_ref[(p - d) & (SLABS - 1)] = fold(part_tile(force_ref, tile))
    for d in range(3, SLABS - 2):
        tile = far_tile(d)
        chunk_ref[(p - d) & (SLABS - 1)] = fold(part_tile(force_ref, tile))
    for k in range(2):
        self_ref[k] = part_tile(force_ref, k)
        down_ref[k] = part_tile(force_ref, 2 + k)
        up_ref[k] = part_tile(force_ref, 4 + k)


def partner_kernel(idx_ref, force_ref, lin_ref, out_ref, val_ref, sum_ref):
    for tile in range(17):
        val_ref[tile] = -part_tile(force_ref, tile)
    val_ref[17] = jnp.zeros((12, 128), f32)
    scatter_rows(val_ref, idx_ref, sum_ref)
    for x in range(4):
        out_ref[:, x] = lin_ref[:, x] + sum_ref[:, 128 * x : 128 * (x + 1)].reshape(12, 32, 128)


def listed_kernel(p_ref, idx_ref, chunk_ref, up_ref, down_ref, self_ref, part_ref, out_ref, val_ref, sum_ref):
    p = p_ref[0]

    def listed(d):
        return unfold(chunk_ref[(p + d) & (SLABS - 1)])

    tiles = [self_ref[0], self_ref[1], down_ref[0], down_ref[1], up_ref[0], up_ref[1], listed(2), listed(SLABS - 2)]
    tiles += merge_far(listed, 12, 0.0) + [jnp.zeros((12, 128), f32)]
    for k, tile in enumerate(tiles):
        val_ref[k] = tile
    scatter_rows(val_ref, idx_ref, sum_ref)
    for x in range(4):
        out_ref[:, x] = part_ref[:, x] + sum_ref[:, 128 * x : 128 * (x + 1)].reshape(12, 32, 128)


def final_kernel(me_ref, part_ref, mass_ref, keep_ref, cross_ref, y1_ref, y2_ref, y3_ref, res_ref, jac_ref):
    for k in range(PARTS):
        acc = (y1_ref, y2_ref, y3_ref)[k // 2 - 1][k % 2] if k > 1 else (keep_ref, cross_ref)[k][0]
        block = me_ref[0] ^ k
        x = block >> 1
        rows = pl.ds(pl.multiple_of(16 * (block & 1), 16), 16)
        out = part_ref[:, x, rows, :] + mass_ref[x, rows, :][None] * acc
        res_ref[:, x, rows, :] = out[0:6]
        jac_ref[:, x, rows, :] = out[6:12]


def join_kernel(same_ref, other_ref, *out_refs):
    for k, out in enumerate(out_refs):
        out[0] = same_ref[k + 1]
        out[1] = other_ref[k + 1]


def rejoin_kernel(keep_ref, cross1_ref, cross2_ref, *out_refs):
    for k, out in enumerate(out_refs):
        out[0] = keep_ref[k + 1]
        out[1] = (cross1_ref, cross2_ref)[(k + 1) // 2][(k + 1) % 2]


def time_kernel(me_ref, same_ref, other_ref, y1_ref, y2_ref, y3_ref, *refs):
    keep_ref, cross1_ref, cross2_ref, in_ref, out_ref = refs
    me = me_ref[0]
    in_ref[0] = same_ref[0]
    in_ref[1] = other_ref[0]
    for k, ref in enumerate((y1_ref, y2_ref, y3_ref)):
        in_ref[2 * k + 2 : 2 * k + 4] = ref[...]
    at = [me ^ ((me + k) & (PARTS - 1)) for k in range(PARTS)]
    count = 2 * PARTS

    def step(g, carry):
        field = g // 3
        row = 6 * field + (g - 3 * field)
        x = [in_ref[at[t // 2], row + 3 * (t % 2)] for t in range(count)]
        for t in range(count):
            acc = x[0] * float(MIXED[t, 0])
            for s in range(1, count):
                acc = acc + x[s] * float(MIXED[(t - s) % count, 0])
            out_ref[at[t // 2], row + 3 * (t % 2)] = acc
        return carry

    lax.fori_loop(0, 6, step, 0)
    for k in range(PARTS):
        ref, at = (keep_ref, k // 2) if k % 2 == 0 else ((cross1_ref, cross2_ref)[k // 4], k // 2 % 2)
        ref[at] = out_ref[k]


def lookup(ids, mat_ref, column, count):
    out = jnp.zeros(ids.shape, f32)
    for m in range(count):
        out = jnp.where(ids == m, mat_ref[m, column], out)
    return out


def stiff_kernel(p_ref, mat_ref, ids_ref, disp_ref, dir_ref, forcing_ref, up_ref, down_ref, after_ref, out_ref, mass_ref, *, materials):
    p = p_ref[0]
    low = jnp.where(p > 0, up_ref[1:14], 0.0)
    high = jnp.where(p < SLABS - 1, down_ref[1:14], 0.0)
    ids = ids_ref[...]
    kx, ky, kz, mass = [lookup(ids, mat_ref, col, materials) for col in range(4)]
    mass_ref[...] = mass
    kx_low = lookup(low[12].astype(i32) - 1, mat_ref, 0, materials)
    kx_high = lookup(high[12].astype(i32) - 1, mat_ref, 0, materials)
    shape = ids.shape
    y = lax.broadcasted_iota(i32, shape, 1)
    z = lax.broadcasted_iota(i32, shape, 2)
    xm = 0.5 * (kx + jnp.concatenate([kx_low[None], kx[:-1]], axis=0))
    xp = 0.5 * (kx + jnp.concatenate([kx[1:], kx_high[None]], axis=0))
    total = xm + xp
    sides = []
    for k, pos, axis in ((ky, y, 1), (kz, z, 2)):
        size = shape[axis]
        for shift, edge in ((1, 0), (size - 1, size - 1)):
            inside = pos != edge
            near = jnp.where(inside, pltpu.roll(k, shift, axis), 0.0)
            side = 0.5 * (k + near)
            total = total + side
            sides.append((jnp.where(inside, side, 0.0), shift, axis))
    for field, ref in enumerate((disp_ref, dir_ref)):
        for c in range(6):
            w = ref[c]
            down = jnp.concatenate([low[6 * field + c][None], w[:-1]], axis=0)
            up = jnp.concatenate([w[1:], high[6 * field + c][None]], axis=0)
            out = total * w - xm * down - xp * up
            for side, shift, axis in sides:
                out = out - side * pltpu.roll(w, shift, axis)
            if field == 0:
                out = out - forcing_ref[c]
            out_ref[6 * field + c] = out


VMEM = 16 * 1024 * 1024


def call(kernel, outs, *args, smem=(0,), away=(), scratch=(), kept=(), limit=VMEM):
    spaces = [pltpu.SMEM if k in smem else pl.ANY if k in away else pltpu.VMEM for k in range(len(args))]
    specs = [pl.BlockSpec(memory_space=space) for space in spaces]
    return pl.pallas_call(
        kernel,
        out_shape=[jax.ShapeDtypeStruct(s, d) for s, d in outs],
        in_specs=specs,
        out_specs=[pl.BlockSpec(memory_space=pltpu.HBM if k in kept else pltpu.VMEM) for k in range(len(outs))],
        scratch_shapes=list(scratch),
        compiler_params=pltpu.CompilerParams(vmem_limit_bytes=limit),
    )(*args)


def shift(x, by):
    return lax.ppermute(x, "mesh", [(i, (i + by) % SLABS) for i in range(SLABS)])


def exchange(chunk, up, down):
    up, down = shift(up, 1), shift(down, -1)
    return lax.all_to_all(chunk, "mesh", split_axis=0, concat_axis=0, tiled=True), up, down


def swap(x, bit):
    return lax.ppermute(x, "inst", [(i, i ^ bit) for i in range(PARTS)])


def inst_split(x):
    return lax.all_to_all(x, "inst", split_axis=0, concat_axis=0, tiled=True)


def on_device(displacement, direction, forcing, material_ids, materials, joint_owner, joint_local, joint_remote, joint_kind):
    shape = displacement.shape
    fields = (6, 4, 32, 128)
    whole = (12, 4, 32, 128)
    disp = displacement.reshape(fields)
    dire = direction.reshape(fields)
    count = joint_local.shape[0]
    p = lax.axis_index("mesh").astype(i32).reshape(1)
    me = lax.axis_index("inst").astype(i32).reshape(1)
    parts = (768, 512)
    index = ((24, 128), i32)
    half = ((4, 12, 16, 128), f32)
    near = ((14, 32, 128), f32)

    own_idx, chunk, up, down, own, same, other = call(
        list_kernel,
        [index, ((SLABS, 16, 128), f32), near, near, ((2, 16, 128), f32), half, half],
        p,
        me,
        joint_owner.reshape(1, count),
        joint_local.reshape(1, count),
        joint_remote.reshape(1, count),
        joint_kind.reshape(1, count),
        disp,
        dire,
        material_ids,
        smem=(0, 1),
        away=range(2, 9),
        limit=60 * 1024 * 1024,
        kept=(1, 2, 3, 5, 6),
        scratch=[pltpu.VMEM(parts, bf16), pltpu.VMEM((SIDE, 16, 128), f32)]
        + [pltpu.VMEM((1, count), i32)] * 4
        + [pltpu.VMEM(fields, f32)] * 2
        + [pltpu.VMEM((4, 32, 128), i32), pltpu.VMEM((4, 32, 128), f32)]
        + [pltpu.VMEM((SLABS, 16, 128), f32), pltpu.SemaphoreType.DMA((12,)), pltpu.SemaphoreType.DMA((20,))],
    )
    chunk, up, down = exchange(chunk, up, down)

    pair = ((2, 12, 16, 128), f32)
    other = swap(other, 1)
    joined = call(join_kernel, [pair] * 3, same, other, smem=())
    turned = [swap(x, 2 * k + 2) for k, x in enumerate(joined)]
    blocks = [pltpu.VMEM((PARTS, 12, 16, 128), f32)] * 2
    keep, *cross = call(time_kernel, [half, pair, pair], me, same, other, *turned, scratch=blocks)

    part = ((PARTS, 4, 1152), f32)
    fields_parts = call(split_kernel, [(parts, bf16)], disp, dire, smem=())[0]
    far_idx, kind, gap = call(
        gap_kernel,
        [index, ((24, 128), f32), part],
        p, chunk, up, down, own, fields_parts, joined[0],
        away=(6,),
        scratch=[pltpu.VMEM((SIDE, 12, 128), f32)],
    )
    force = call(
        force_kernel,
        [part],
        me, kind, jnp.asarray(SPREAD), inst_split(gap), keep,
        away=(4,),
        scratch=[pltpu.VMEM((48, 384), f32)] * 4,
    )[0]
    force = inst_split(force)
    cross = [swap(x, 1) for x in cross]
    joined = call(rejoin_kernel, [pair] * 3, keep, *cross, smem=())
    turned = [swap(x, 2 * k + 2) for k, x in enumerate(joined)]
    lin, mass = call(
        lambda *refs: stiff_kernel(*refs, materials=materials.shape[0]),
        [(whole, f32), ((4, 32, 128), f32)],
        p, materials, material_ids, disp, dire, forcing.reshape(fields), up, down, joined[0],
        smem=(0, 1),
        away=(8,),
    )
    two = ((2, 12, 128), f32)
    chunk, up2, down2, own = call(reply_kernel, [((SLABS, 4, 384), f32), two, two, two], p, force, mass, away=(2,))
    chunk, up2, down2 = exchange(chunk, up2, down2)

    adding = [pltpu.VMEM((SIDE, 12, 128), f32), pltpu.VMEM((384, 512), f32)]
    partial = call(partner_kernel, [(whole, f32)], far_idx, force, lin, smem=(), scratch=adding)[0]
    partial = call(
        listed_kernel, [(whole, f32)], p, own_idx, chunk, up2, down2, own, partial, scratch=adding
    )[0]
    residual, jacobian = call(final_kernel, [(fields, f32)] * 2, me, partial, mass, keep, cross[0], *turned)
    return residual.reshape(shape), jacobian.reshape(shape)


def solution(mesh):
    field = P("inst", None, "mesh", None, None)
    placed = (field, field, field, P("mesh", None, None), P(), P("mesh", None), P("mesh"), P("mesh"), P("mesh"))
    return jax.shard_map(on_device, mesh=mesh, in_specs=placed, out_specs=(field, field), check_vma=False)
```

```python
import jax
import jax.numpy as jnp
import numpy as np
from jax import lax
from jax.experimental import pallas as pl
from jax.experimental.pallas import tpu as pltpu
from jax.sharding import PartitionSpec as P

frequency = 0.6
damping = 0.3
bolt_stiff = 2.0
slip_force = 1.0
slip_speed = 0.5
stop_stiff = 3.0
clearance = 0.3

SLABS = 32
PARTS = 8
SIDE = 18
SEG = 42
f32 = jnp.float32
bf16 = jnp.bfloat16
i32 = jnp.int32


def tables(count):
    offsets = np.arange(count)[:, None] - np.arange(count)[None, :]
    tangent = np.where(offsets == 0, 1.0, np.tan(np.pi * offsets / count))
    first = np.where(offsets == 0, 0.0, 0.5 * np.where(offsets % 2 == 0, 1.0, -1.0) / tangent) * frequency
    return first, first @ first


FIRST, SECOND = tables(2 * PARTS)
MIXED = (SECOND + damping * FIRST).astype(np.float32)
SPREAD = np.kron(FIRST, np.eye(3)).astype(np.float32)


def far_tile(offset):
    return 8 + (offset - 3) // 3


def fold(rows):
    return jnp.concatenate([rows[0:4], rows[4:8], rows[8:12]], axis=1)


def unfold(rows):
    width = rows.shape[1] // 3
    return jnp.concatenate([rows[:, width * k : width * (k + 1)] for k in range(3)], axis=0)


def part_tile(ref, tile):
    at = 128 * (tile % 3)
    return jnp.concatenate([ref[tile // 3, :, 384 * k + at : 384 * k + at + 128] for k in range(3)], axis=0)


def lanes(rows):
    return lax.broadcasted_iota(i32, (rows, 128), 1)


def merge_far(read, rows, fill):
    lane = lanes(rows)
    tiles = []
    for k in range(9):
        parts = [read(3 + 3 * k + s) for s in range(3)]
        tile = jnp.where(lane < SEG, parts[0], jnp.where(lane < 2 * SEG, parts[1], parts[2]))
        tiles.append(jnp.where(lane < 3 * SEG, tile, fill))
    return tiles


def slot_tables(p, owner_ref, local_ref, remote_ref, kind_ref):
    count = owner_ref.shape[1]
    offset = (owner_ref[...] - p) & (SLABS - 1)
    hit = (lax.broadcasted_iota(i32, (SLABS, count), 0) == offset).astype(f32)
    hit16 = hit.astype(bf16)
    before = (lax.broadcasted_iota(i32, (128, 128), 0) < lax.broadcasted_iota(i32, (128, 128), 1)).astype(f32).astype(bf16)
    row = lax.broadcasted_iota(i32, (SLABS, 1), 0)
    far = row - 3
    group = (far * 171) >> 9
    start = 1024 + group * 128 + (far - 3 * group) * SEG
    for value, at in ((0, 0), (1, 256), (SLABS - 1, 512), (2, 768), (SLABS - 2, 896)):
        start = jnp.where(row == value, at, start)
    run = start.astype(f32)
    places = []
    for b in range(count // 128):
        block = hit[:, 128 * b : 128 * (b + 1)]
        earlier = jnp.dot(hit16[:, 128 * b : 128 * (b + 1)], before, preferred_element_type=f32)
        places.append(jnp.sum(block * (earlier + run), axis=0, keepdims=True))
        run = run + jnp.sum(block, axis=1, keepdims=True)
    slot = jnp.concatenate(places, axis=1).astype(i32)
    in_tile = lax.broadcasted_iota(i32, (24, count), 0) == (slot >> 7)
    in_lane = (lax.broadcasted_iota(i32, (128, count), 0) == (slot & 127)).astype(f32).astype(bf16)
    local = local_ref[...]
    remote = remote_ref[...]
    values = (local >> 7, local & 127, remote >> 7, remote & 127, kind_ref[...], jnp.ones_like(local))
    spread = jnp.concatenate([jnp.where(in_tile, v.astype(f32), 0.0) for v in values], axis=0).astype(bf16)
    got = lax.dot_general(spread, in_lane, (((1,), (1,)), ((), ())), preferred_element_type=f32)
    got = [got[24 * k : 24 * (k + 1)] for k in range(6)]
    empty = got[5] - 1.0
    return got[0] * 128.0 + got[1] + empty, got[2] * 128.0 + got[3] + empty, got[4]


def picks(idx_ref, k):
    idx = jnp.concatenate([idx_ref[pl.ds(2 * k, 1), :], idx_ref[pl.ds(2 * k + 1, 1), :]], axis=1)
    code = ((idx >> 12) << 7) | (idx & 127)
    pick = (lax.broadcasted_iota(i32, (512, 256), 0) == code).astype(f32).astype(bf16)
    return pick, lax.broadcasted_iota(i32, (32, 256), 0) == ((idx >> 7) & 31)


def split_fields(disp_ref, dir_ref, parts_ref):
    for field, ref in enumerate((disp_ref, dir_ref)):
        for x in range(4):
            value = ref[:, x].reshape(6 * 32, 128)
            hi = value.astype(bf16)
            cols = slice(128 * x, 128 * (x + 1))
            parts_ref[192 * field : 192 * (field + 1), cols] = hi
            parts_ref[384 + 192 * field : 384 + 192 * (field + 1), cols] = (value - hi.astype(f32)).astype(bf16)


def split_kernel(disp_ref, dir_ref, parts_ref):
    split_fields(disp_ref, dir_ref, parts_ref)


def gather_rows(parts_ref, idx_ref, here_ref, first, last):
    def step(k, carry):
        pick, in_y = picks(idx_ref, k)
        rows = jnp.dot(parts_ref[...], pick, preferred_element_type=f32)
        rows = (rows[:384] + rows[384:]).reshape(12, 32, 256)
        got = jnp.sum(jnp.where(in_y[None], rows, 0.0), axis=1)
        here_ref[2 * k, 0:12, :] = got[:, :128]
        here_ref[2 * k + 1, 0:12, :] = got[:, 128:]
        return carry

    lax.fori_loop(first, last, step, 0, unroll=True)


def scatter_rows(val_ref, idx_ref, sum_ref):
    dims = (((1,), (1,)), ((), ()))
    total = None
    for group in range(3):
        held, high, low = [], [], []
        for k in range(group * SIDE // 2 // 3, (group + 1) * SIDE // 2 // 3):
            pick, in_y = picks(idx_ref, k)
            value = jnp.concatenate([val_ref[2 * k], val_ref[2 * k + 1]], axis=1)
            hi = value.astype(bf16).astype(f32)
            held.append(pick)
            for out, part in ((high, hi), (low, value - hi)):
                out.append(jnp.where(in_y[None], part[:, None, :], 0.0).reshape(384, 256).astype(bf16))
        held = jnp.concatenate(held, axis=1)
        got = lax.dot_general(jnp.concatenate(high, axis=1), held, dims, preferred_element_type=f32)
        got = got + lax.dot_general(jnp.concatenate(low, axis=1), held, dims, preferred_element_type=f32)
        total = got if total is None else total + got
    sum_ref[...] = total


def list_kernel(p_ref, me_ref, owner_hbm, local_hbm, remote_hbm, kind_hbm, disp_hbm, dir_hbm, ids_hbm,
                idx_ref, chunk_hbm, up_hbm, down_hbm, self_ref, same_hbm, other_hbm,
                parts_ref, rows_ref, owner_ref, local_ref, remote_ref, kind_ref, disp_ref, dir_ref, ids_ref, near_ref,
                chunk_ref, sems, more_sems):
    p = p_ref[0]
    pairs = ((owner_hbm, owner_ref), (local_hbm, local_ref), (remote_hbm, remote_ref), (kind_hbm, kind_ref),
             (disp_hbm, disp_ref), (dir_hbm, dir_ref), (ids_hbm, ids_ref))
    copies = [pltpu.make_async_copy(a, b, sems.at[k]) for k, (a, b) in enumerate(pairs)]
    for copy in copies:
        copy.start()
    for copy in copies[:4]:
        copy.wait()
    mine, theirs, kind = slot_tables(p, owner_ref, local_ref, remote_ref, kind_ref)
    idx_ref[...] = mine.astype(i32)
    for tile in range(SIDE):
        rows_ref[tile, 12:13, :] = theirs[tile : tile + 1]
        rows_ref[tile, 13:14, :] = kind[tile : tile + 1]
        rows_ref[tile, 14:16, :] = jnp.zeros((2, 128), f32)
    for copy in copies[4:]:
        copy.wait()
    moves = []
    for field, ref in enumerate((disp_ref, dir_ref)):
        part = pl.ds(6 * field, 6)
        for k in range(PARTS):
            block = me_ref[0] ^ k
            rows = pl.ds(pl.multiple_of(16 * (block & 1), 16), 16)
            moves.append((ref.at[:, block >> 1, rows, :], (same_hbm, other_hbm)[k % 2].at[k // 2, part]))
        moves.append((ref.at[:, 3], up_hbm.at[pl.ds(1 + 6 * field, 6)]))
        moves.append((ref.at[:, 0], down_hbm.at[pl.ds(1 + 6 * field, 6)]))
    moves = [pltpu.make_async_copy(a, b, more_sems.at[k]) for k, (a, b) in enumerate(moves)]
    for move in moves:
        move.start()
    split_fields(disp_ref, dir_ref, parts_ref)
    near_ref[2] = (ids_ref[3] + 1).astype(f32)
    near_ref[3] = (ids_ref[0] + 1).astype(f32)
    for d in (0, 1, SLABS - 1):
        chunk_ref[(p + d) & (SLABS - 1)] = jnp.zeros((16, 128), f32)
    gather_rows(parts_ref, idx_ref, rows_ref, 0, SIDE // 2)
    for d, tile in ((2, 6), (SLABS - 2, 7)):
        chunk_ref[(p + d) & (SLABS - 1)] = rows_ref[tile]
    for d in range(3, SLABS - 2):
        tile = far_tile(d)
        chunk_ref[(p + d) & (SLABS - 1)] = rows_ref[tile]
    ends = [pltpu.make_async_copy(chunk_ref, chunk_hbm, sems.at[11])]
    ends[0].start()
    for k in range(2):
        near_ref[k] = rows_ref[2 + 2 * k : 4 + 2 * k].reshape(32, 128)
    pairs = ((near_ref.at[0], up_hbm.at[0]), (near_ref.at[1], down_hbm.at[0]),
             (near_ref.at[2], up_hbm.at[13]), (near_ref.at[3], down_hbm.at[13]))
    for k, (a, b) in enumerate(pairs):
        ends.append(pltpu.make_async_copy(a, b, sems.at[7 + k]))
        ends[-1].start()
    self_ref[...] = rows_ref[0:2]
    for move in moves + ends:
        move.wait()


def gap_kernel(p_ref, chunk_ref, up_ref, down_ref, self_ref, parts_ref, after_ref,
               idx_ref, kind_ref, gap_ref, here_ref):
    p = p_ref[0]

    def asked(d):
        return chunk_ref[(p - d) & (SLABS - 1)]

    near = [ref[0, 16 * k : 16 * (k + 1), :] for ref in (up_ref, down_ref) for k in range(2)]
    tiles = [self_ref[0], self_ref[1]] + near + [asked(2), asked(SLABS - 2)]
    tiles += merge_far(asked, 16, 0.0)
    beyond = lanes(1) >= 3 * SEG
    rows = [t[12:13] for t in tiles[:8]] + [jnp.where(beyond, -1.0, t[12:13]) for t in tiles[8:]]
    idx_ref[...] = jnp.concatenate(rows + [jnp.full((7, 128), -1.0, f32)], axis=0).astype(i32)
    kind_ref[...] = jnp.concatenate([t[13:14] for t in tiles] + [jnp.zeros((7, 128), f32)], axis=0)
    gather_rows(parts_ref, idx_ref, here_ref, 0, SIDE // 2)
    for tile in range(24):
        gap = tiles[tile][0:12] - here_ref[tile] if tile < 17 else jnp.zeros((12, 128), f32)
        at = 128 * (tile % 3)
        for k in range(3):
            gap_ref[tile // 3, :, 384 * k + at : 384 * k + at + 128] = gap[4 * k : 4 * k + 4]


def force_kernel(me_ref, kind_ref, spread_ref, gap_ref, after_ref, out_ref, r_ref, d_ref, f_ref, t_ref):
    me = me_ref[0]
    for k in range(PARTS):
        gap = unfold(gap_ref[k])
        r_ref[6 * k : 6 * k + 6] = gap[0:6]
        d_ref[6 * k : 6 * k + 6] = gap[6:12]
    r = r_ref[...]
    dr = d_ref[...]
    w = jnp.dot(spread_ref[...], r, precision=lax.Precision.HIGHEST, preferred_element_type=f32)
    dw = jnp.dot(spread_ref[...], dr, precision=lax.Precision.HIGHEST, preferred_element_type=f32)
    bolted = jnp.concatenate([kind_ref[pl.ds(3 * me + k, 1), :] for k in range(3)], axis=1)
    slide = jnp.tanh(w / slip_speed)
    opened = jnp.tanh(r / clearance)
    friction = bolt_stiff * r + slip_force * slide
    contact = stop_stiff * (r - clearance * opened)
    f_ref[...] = bolted * friction + (1.0 - bolted) * contact
    tangent_friction = bolt_stiff * dr + slip_force * (1.0 - slide * slide) / slip_speed * dw
    tangent_contact = stop_stiff * opened * opened * dr
    t_ref[...] = bolted * tangent_friction + (1.0 - bolted) * tangent_contact
    for k in range(PARTS):
        out_ref[k] = fold(jnp.concatenate([f_ref[6 * k : 6 * k + 6], t_ref[6 * k : 6 * k + 6]], axis=0))


def reply_kernel(p_ref, force_ref, after_ref, chunk_ref, up_ref, down_ref, self_ref):
    p = p_ref[0]
    for d in (0, 1, SLABS - 1):
        chunk_ref[(p - d) & (SLABS - 1)] = jnp.zeros((4, 384), f32)
    for d, tile in ((2, 6), (SLABS - 2, 7)):
        chunk_ref[(p - d) & (SLABS - 1)] = fold(part_tile(force_ref, tile))
    for d in range(3, SLABS - 2):
        tile = far_tile(d)
        chunk_ref[(p - d) & (SLABS - 1)] = fold(part_tile(force_ref, tile))
    for k in range(2):
        self_ref[k] = part_tile(force_ref, k)
        down_ref[k] = part_tile(force_ref, 2 + k)
        up_ref[k] = part_tile(force_ref, 4 + k)


def partner_kernel(idx_ref, force_ref, lin_ref, out_ref, val_ref, sum_ref):
    for tile in range(17):
        val_ref[tile] = -part_tile(force_ref, tile)
    val_ref[17] = jnp.zeros((12, 128), f32)
    scatter_rows(val_ref, idx_ref, sum_ref)
    for x in range(4):
        out_ref[:, x] = lin_ref[:, x] + sum_ref[:, 128 * x : 128 * (x + 1)].reshape(12, 32, 128)


def listed_kernel(p_ref, idx_ref, chunk_ref, up_ref, down_ref, self_ref, part_ref, out_ref, val_ref, sum_ref):
    p = p_ref[0]

    def listed(d):
        return unfold(chunk_ref[(p + d) & (SLABS - 1)])

    tiles = [self_ref[0], self_ref[1], down_ref[0], down_ref[1], up_ref[0], up_ref[1], listed(2), listed(SLABS - 2)]
    tiles += merge_far(listed, 12, 0.0) + [jnp.zeros((12, 128), f32)]
    for k, tile in enumerate(tiles):
        val_ref[k] = tile
    scatter_rows(val_ref, idx_ref, sum_ref)
    for x in range(4):
        out_ref[:, x] = part_ref[:, x] + sum_ref[:, 128 * x : 128 * (x + 1)].reshape(12, 32, 128)


def final_kernel(me_ref, part_ref, mass_ref, keep_ref, cross_ref, y1_ref, y2_ref, y3_ref, res_ref, jac_ref):
    for k in range(PARTS):
        acc = (y1_ref, y2_ref, y3_ref)[k // 2 - 1][k % 2] if k > 1 else (keep_ref, cross_ref)[k][0]
        block = me_ref[0] ^ k
        x = block >> 1
        rows = pl.ds(pl.multiple_of(16 * (block & 1), 16), 16)
        out = part_ref[:, x, rows, :] + mass_ref[x, rows, :][None] * acc
        res_ref[:, x, rows, :] = out[0:6]
        jac_ref[:, x, rows, :] = out[6:12]


def join_kernel(same_ref, other_ref, *out_refs):
    for k, out in enumerate(out_refs):
        out[0] = same_ref[k + 1]
        out[1] = other_ref[k + 1]


def rejoin_kernel(keep_ref, cross1_ref, cross2_ref, *out_refs):
    for k, out in enumerate(out_refs):
        out[0] = keep_ref[k + 1]
        out[1] = (cross1_ref, cross2_ref)[(k + 1) // 2][(k + 1) % 2]


def time_kernel(me_ref, same_ref, other_ref, y1_ref, y2_ref, y3_ref, *refs):
    keep_ref, cross1_ref, cross2_ref, in_ref, out_ref = refs
    me = me_ref[0]
    in_ref[0] = same_ref[0]
    in_ref[1] = other_ref[0]
    for k, ref in enumerate((y1_ref, y2_ref, y3_ref)):
        in_ref[2 * k + 2 : 2 * k + 4] = ref[...]
    at = [me ^ ((me + k) & (PARTS - 1)) for k in range(PARTS)]
    count = 2 * PARTS

    def step(g, carry):
        field = g // 3
        row = 6 * field + (g - 3 * field)
        x = [in_ref[at[t // 2], row + 3 * (t % 2)] for t in range(count)]
        for t in range(count):
            acc = x[0] * float(MIXED[t, 0])
            for s in range(1, count):
                acc = acc + x[s] * float(MIXED[(t - s) % count, 0])
            out_ref[at[t // 2], row + 3 * (t % 2)] = acc
        return carry

    lax.fori_loop(0, 6, step, 0)
    for k in range(PARTS):
        ref, at = (keep_ref, k // 2) if k % 2 == 0 else ((cross1_ref, cross2_ref)[k // 4], k // 2 % 2)
        ref[at] = out_ref[k]


def lookup(ids, mat_ref, column, count):
    out = jnp.zeros(ids.shape, f32)
    for m in range(count):
        out = jnp.where(ids == m, mat_ref[m, column], out)
    return out


def stiff_kernel(p_ref, mat_ref, ids_ref, disp_ref, dir_ref, forcing_ref, up_ref, down_ref, after_ref, out_ref, mass_ref, *, materials):
    p = p_ref[0]
    low = jnp.where(p > 0, up_ref[1:14], 0.0)
    high = jnp.where(p < SLABS - 1, down_ref[1:14], 0.0)
    ids = ids_ref[...]
    kx, ky, kz, mass = [lookup(ids, mat_ref, col, materials) for col in range(4)]
    mass_ref[...] = mass
    kx_low = lookup(low[12].astype(i32) - 1, mat_ref, 0, materials)
    kx_high = lookup(high[12].astype(i32) - 1, mat_ref, 0, materials)
    shape = ids.shape
    y = lax.broadcasted_iota(i32, shape, 1)
    z = lax.broadcasted_iota(i32, shape, 2)
    xm = 0.5 * (kx + jnp.concatenate([kx_low[None], kx[:-1]], axis=0))
    xp = 0.5 * (kx + jnp.concatenate([kx[1:], kx_high[None]], axis=0))
    total = xm + xp
    sides = []
    for k, pos, axis in ((ky, y, 1), (kz, z, 2)):
        size = shape[axis]
        for shift, edge in ((1, 0), (size - 1, size - 1)):
            inside = pos != edge
            near = jnp.where(inside, pltpu.roll(k, shift, axis), 0.0)
            side = 0.5 * (k + near)
            total = total + side
            sides.append((jnp.where(inside, side, 0.0), shift, axis))
    for field, ref in enumerate((disp_ref, dir_ref)):
        for c in range(6):
            w = ref[c]
            down = jnp.concatenate([low[6 * field + c][None], w[:-1]], axis=0)
            up = jnp.concatenate([w[1:], high[6 * field + c][None]], axis=0)
            out = total * w - xm * down - xp * up
            for side, shift, axis in sides:
                out = out - side * pltpu.roll(w, shift, axis)
            if field == 0:
                out = out - forcing_ref[c]
            out_ref[6 * field + c] = out


VMEM = 16 * 1024 * 1024


def call(kernel, outs, *args, smem=(0,), away=(), scratch=(), kept=(), limit=VMEM):
    spaces = [pltpu.SMEM if k in smem else pl.ANY if k in away else pltpu.VMEM for k in range(len(args))]
    specs = [pl.BlockSpec(memory_space=space) for space in spaces]
    return pl.pallas_call(
        kernel,
        out_shape=[jax.ShapeDtypeStruct(s, d) for s, d in outs],
        in_specs=specs,
        out_specs=[pl.BlockSpec(memory_space=pltpu.HBM if k in kept else pltpu.VMEM) for k in range(len(outs))],
        scratch_shapes=list(scratch),
        compiler_params=pltpu.CompilerParams(vmem_limit_bytes=limit),
    )(*args)


def shift(x, by):
    return lax.ppermute(x, "mesh", [(i, (i + by) % SLABS) for i in range(SLABS)])


def exchange(chunk, up, down):
    up, down = shift(up, 1), shift(down, -1)
    return lax.all_to_all(chunk, "mesh", split_axis=0, concat_axis=0, tiled=True), up, down


def swap(x, bit):
    return lax.ppermute(x, "inst", [(i, i ^ bit) for i in range(PARTS)])


def inst_split(x):
    return lax.all_to_all(x, "inst", split_axis=0, concat_axis=0, tiled=True)


def on_device(displacement, direction, forcing, material_ids, materials, joint_owner, joint_local, joint_remote, joint_kind):
    shape = displacement.shape
    fields = (6, 4, 32, 128)
    whole = (12, 4, 32, 128)
    disp = displacement.reshape(fields)
    dire = direction.reshape(fields)
    count = joint_local.shape[0]
    p = lax.axis_index("mesh").astype(i32).reshape(1)
    me = lax.axis_index("inst").astype(i32).reshape(1)
    parts = (768, 512)
    index = ((24, 128), i32)
    half = ((4, 12, 16, 128), f32)
    near = ((14, 32, 128), f32)

    own_idx, chunk, up, down, own, same, other = call(
        list_kernel,
        [index, ((SLABS, 16, 128), f32), near, near, ((2, 16, 128), f32), half, half],
        p,
        me,
        joint_owner.reshape(1, count),
        joint_local.reshape(1, count),
        joint_remote.reshape(1, count),
        joint_kind.reshape(1, count),
        disp,
        dire,
        material_ids,
        smem=(0, 1),
        away=range(2, 9),
        limit=60 * 1024 * 1024,
        kept=(1, 2, 3, 5, 6),
        scratch=[pltpu.VMEM(parts, bf16), pltpu.VMEM((SIDE, 16, 128), f32)]
        + [pltpu.VMEM((1, count), i32)] * 4
        + [pltpu.VMEM(fields, f32)] * 2
        + [pltpu.VMEM((4, 32, 128), i32), pltpu.VMEM((4, 32, 128), f32)]
        + [pltpu.VMEM((SLABS, 16, 128), f32), pltpu.SemaphoreType.DMA((12,)), pltpu.SemaphoreType.DMA((20,))],
    )
    chunk, up, down = exchange(chunk, up, down)

    pair = ((2, 12, 16, 128), f32)
    other = swap(other, 1)
    joined = call(join_kernel, [pair] * 3, same, other, smem=())
    turned = [swap(x, 2 * k + 2) for k, x in enumerate(joined)]
    blocks = [pltpu.VMEM((PARTS, 12, 16, 128), f32)] * 2
    keep, *cross = call(time_kernel, [half, pair, pair], me, same, other, *turned, scratch=blocks)

    part = ((PARTS, 4, 1152), f32)
    fields_parts = call(split_kernel, [(parts, bf16)], disp, dire, smem=())[0]
    far_idx, kind, gap = call(
        gap_kernel,
        [index, ((24, 128), f32), part],
        p, chunk, up, down, own, fields_parts, joined[0],
        away=(6,),
        scratch=[pltpu.VMEM((SIDE, 12, 128), f32)],
    )
    force = call(
        force_kernel,
        [part],
        me, kind, jnp.asarray(SPREAD), inst_split(gap), keep,
        away=(4,),
        scratch=[pltpu.VMEM((48, 384), f32)] * 4,
    )[0]
    force = inst_split(force)
    cross = [swap(x, 1) for x in cross]
    joined = call(rejoin_kernel, [pair] * 3, keep, *cross, smem=())
    turned = [swap(x, 2 * k + 2) for k, x in enumerate(joined)]
    lin, mass = call(
        lambda *refs: stiff_kernel(*refs, materials=materials.shape[0]),
        [(whole, f32), ((4, 32, 128), f32)],
        p, materials, material_ids, disp, dire, forcing.reshape(fields), up, down, joined[0],
        smem=(0, 1),
        away=(8,),
    )
    two = ((2, 12, 128), f32)
    chunk, up2, down2, own = call(reply_kernel, [((SLABS, 4, 384), f32), two, two, two], p, force, mass, away=(2,))
    chunk, up2, down2 = exchange(chunk, up2, down2)

    adding = [pltpu.VMEM((SIDE, 12, 128), f32), pltpu.VMEM((384, 512), f32)]
    partial = call(partner_kernel, [(whole, f32)], far_idx, force, lin, smem=(), scratch=adding)[0]
    partial = call(
        listed_kernel, [(whole, f32)], p, own_idx, chunk, up2, down2, own, partial, scratch=adding
    )[0]
    residual, jacobian = call(final_kernel, [(fields, f32)] * 2, me, partial, mass, keep, cross[0], *turned)
    return residual.reshape(shape), jacobian.reshape(shape)


def solution(mesh):
    field = P("inst", None, "mesh", None, None)
    placed = (field, field, field, P("mesh", None, None), P(), P("mesh", None), P("mesh"), P("mesh"), P("mesh"))
    return jax.shard_map(on_device, mesh=mesh, in_specs=placed, out_specs=(field, field), check_vma=False)
```
